32 devices in a mesh: seq: 8 (over z, x), wt: 4 (over y, core).
Axes of the slice: x: 2, y: 2, z: 4, core: 2. Of those that a mesh axis runs over, the one named last changes fastest.
Arguments:
- tokens: bfloat16 [4, 4096, 1536], P('wt', 'seq'), may hold values from -6 to 6
- teacher: bfloat16 [4, 4096, 1536], P('wt', 'seq'), may hold values from -6 to 6
- seq_lengths: int32 [4, 1], P('wt'), may hold values from 1024 to 4096, as said below
- w_attn: bfloat16 [1536, 1792], P('wt'), may hold values from -0.15625 to 0.15625
- w_out: bfloat16 [1536, 1536], P('wt'), may hold values from -1.25 to 1.25
- w_in: bfloat16 [1536, 2, 4608], P(None, None, 'wt'), may hold values from -0.15625 to 0.15625
- w_down: bfloat16 [4608, 1536], P('wt'), may hold values from -0.09375 to 0.09375
- gain_attn: float32 [1536], replicated, may hold values from 0.25 to 1.75
- gain_ffn: float32 [1536], replicated, may hold values from 0.25 to 1.75
Outputs:
- block_out: bfloat16 [4, 4096, 1536], P('wt', 'seq')
- loss: float32 [], replicated
- input_grad: float32 [4, 4096, 1536], P('wt', 'seq')
- grad_queries: float32 [1536, 1536], P('wt', 'seq')
- grad_keyvals: float32 [1536, 2, 128], P('wt', None, 'seq')
- grad_out: float32 [1536, 1536], P('wt', 'seq')
- grad_in: float32 [1536, 2, 4608], P('seq', None, 'wt')
- grad_down: float32 [4608, 1536], P('wt', 'seq')
- grad_gain_attn: float32 [1536], replicated
- grad_gain_ffn: float32 [1536], replicated
The draws below stay inside these ranges and needn't reach their ends.
Inputs may be any that keep to these rules, and one draw needn't show every extreme that they name: `seq_lengths`: each stream packs its sequences from position 0 on; the positions after their sum are padding, fewer than 512 of them.
All inputs are finite; a program needn't handle non-finite values.
Results may differ from the reference program's by a relative error of at most 0.012.
Values may be sent and summed in bfloat16 or wider, within the bound.
A program may use at most 320 MiB of HBM per device.

```python
import math
import jax
import jax.numpy as jnp
from jax import lax

D = 1536
HEADS = 12
HD = 128
FF = 4608
WINDOW = 1024
QBLK = 512
LEN_MIN = 1024
LEN_MAX = 4096
TOK_DEV = 512
STREAM = 4096
N_WT = 4


def draw_seq_lengths(key, part):
    key = jax.random.fold_in(key, 11)
    short_key, pick_key, cut_key, flip_key = jax.random.split(key, 4)
    groups = STREAM // LEN_MAX
    short = jax.random.randint(short_key, (N_WT, groups), LEN_MIN, LEN_MAX // 2 + 1)
    chosen = jax.random.randint(pick_key, (N_WT, 1), 0, groups)
    places = jnp.arange(groups, dtype=jnp.int32)[None, :]
    target = (chosen + 1) % groups
    if groups > 1:
        short = jnp.where(places == target, LEN_MIN, short)
    longer = LEN_MAX - short
    reach = min(TOK_DEV, LEN_MAX // 2 - LEN_MIN + 1)
    cut = jax.random.randint(cut_key, (N_WT, 1), reach // 2, reach)
    removed = jnp.where(places == target, cut, 0)
    longer = longer - removed
    flip = jax.random.randint(flip_key, (N_WT, groups), 0, 2)
    first = jnp.where(flip == 1, longer, short)
    second = jnp.where(flip == 1, short, longer)
    first = jnp.where(places == chosen, LEN_MAX - removed, first)
    second = jnp.where(places == chosen, 0, second)
    joined = jnp.stack([first, second], axis=-1).reshape(N_WT, 2 * groups)
    slots = jnp.arange(2 * groups, dtype=jnp.int32)[None, :]
    scores = jnp.where(joined > 0, slots, 2 * groups + slots)
    order = jnp.argsort(scores, axis=1, stable=True)
    packed = jnp.take_along_axis(joined, order, axis=1)
    return packed[:, :2 * groups - 1].astype(jnp.int32)


def shard_levels(own_key, shape, cuts, low, top_value):
    level = 1.0
    for dim, parts in cuts:
        draws = jax.random.uniform(jax.random.fold_in(jax.random.fold_in(own_key, 6), dim), (parts,), jnp.float32, low / len(cuts), top_value / len(cuts))
        level = level * jnp.repeat(jnp.exp(draws), shape[dim] // parts).reshape((-1,) + (1,) * (len(shape) - 1 - dim))
    return level


def normal_values(own_key, shape, width, limit, cuts=(), held_as=jnp.bfloat16):
    array = jax.random.normal(own_key, shape, jnp.float32) * width
    if len(cuts) > 0:
        array = shard_levels(own_key, shape, cuts, -0.22, 0.18) * array
    return jnp.clip(array, min=-limit, max=limit).astype(held_as)


def setup_inputs(seed: int = 0) -> dict:
    key_list = jax.random.split(jax.random.key(seed), 10)
    tokens = normal_values(key_list[0], (N_WT, STREAM, D), 1.0, 6.0, ((0, 4), (1, 8)))
    teacher = normal_values(key_list[1], (N_WT, STREAM, D), 1.0, 6.0, ((0, 4), (1, 8)))
    seq_lengths = draw_seq_lengths(jax.random.fold_in(key_list[9], 71), 0)
    w_attn = normal_values(key_list[3], (D, D + 2 * HD), D ** -0.5, 0.15625, ((0, 4),))
    w_out = normal_values(key_list[4], (D, D), (D // 64) ** -0.5, 1.25, ((0, 4),))
    w_in = normal_values(key_list[5], (D, 2, FF), D ** -0.5, 0.15625, ((2, 4),))
    w_down = normal_values(key_list[6], (FF, D), FF ** -0.5, 0.09375, ((0, 4),))
    gain_attn = jnp.clip(1.0 + 0.15 * jax.random.normal(key_list[7], (D,), jnp.float32), 0.25, 1.75)
    gain_ffn = jnp.clip(1.0 + 0.15 * jax.random.normal(key_list[8], (D,), jnp.float32), 0.25, 1.75)
    return {"tokens": tokens, "teacher": teacher, "seq_lengths": seq_lengths, "w_attn": w_attn, "w_out": w_out, "w_in": w_in, "w_down": w_down, "gain_attn": gain_attn, "gain_ffn": gain_ffn}


EPSILON = 1e-06
NEGATIVE = -1e+30
HIGHEST = lax.Precision.HIGHEST

@jax.custom_vjp
def low(v):
    return lax.optimization_barrier(v.astype(jnp.bfloat16)).astype(jnp.float32)

@jax.custom_vjp
def low_back(v):
    return v

def low_keep(v):
    return (low(v), None)

def low_pass(kept, grad):
    return (grad,)

def back_keep(v):
    return (v, None)

def back_low(kept, grad):
    return (low(grad),)
low.defvjp(low_keep, low_pass)
low_back.defvjp(back_keep, back_low)

def rms_scale(values, gain):
    return values * lax.rsqrt(lax.optimization_barrier(jnp.mean(values * values, axis=-1, keepdims=True)) + EPSILON) * gain

def stream_ids(positions, lengths, stream_len):
    seq_ends = jnp.cumsum(lengths).astype(jnp.int32)
    seq_starts = seq_ends - lengths
    inside = (positions >= 0) & (positions < seq_ends[-1])
    number = lax.optimization_barrier(jnp.sum((positions[:, None] >= seq_starts[None, :]).astype(jnp.int32), axis=1)) - 1
    return jnp.where(inside, number, -(positions + 2 * stream_len)).astype(jnp.int32)

def window_mask(query_ids, key_ids):
    query_pos = lax.broadcasted_iota(jnp.int32, (QBLK, WINDOW + QBLK), 0)
    key_pos = lax.broadcasted_iota(jnp.int32, (QBLK, WINDOW + QBLK), 1)
    offset = key_pos - WINDOW - query_pos
    return (offset <= 0) & (offset > -WINDOW) & (query_ids[:, None] == key_ids[None, :])

def attention(queries, keys_values, seq_ids):
    scale = 1.0 / math.sqrt(HD)
    padded = jnp.concatenate([jnp.zeros((N_WT, WINDOW, 2 * HD), jnp.float32), keys_values], axis=1)
    blocks_per = STREAM // QBLK

    def one_block(index):
        stream_at = (index // blocks_per).astype(jnp.int32)
        start = (index % blocks_per * QBLK).astype(jnp.int32)
        zero = jnp.zeros((), jnp.int32)
        q_blk = lax.dynamic_slice(queries, (stream_at, start, zero, zero), (1, QBLK, HEADS, HD))[0]
        window = lax.dynamic_slice(padded, (stream_at, start, zero), (1, WINDOW + QBLK, 2 * HD))[0]
        id_row = lax.dynamic_index_in_dim(seq_ids, stream_at, 0, keepdims=False)
        query_ids = lax.dynamic_slice_in_dim(id_row, start + WINDOW, QBLK)
        key_ids = lax.dynamic_slice_in_dim(id_row, start, WINDOW + QBLK)
        raw = jnp.einsum('qhe,ke->hqk', q_blk, window[:, :HD], precision=HIGHEST)
        scores = low_back(raw * scale)
        allowed = window_mask(query_ids, key_ids)
        masked = jnp.where(allowed[None], scores, NEGATIVE)
        top = lax.optimization_barrier(jnp.max(masked, axis=-1, keepdims=True))
        log_total = top + jnp.log(lax.optimization_barrier(jnp.sum(jnp.exp(masked - top), axis=-1, keepdims=True)))
        weights = low(jnp.exp(masked - log_total))
        return jnp.einsum('hqk,ke->qhe', weights, window[:, HD:], precision=HIGHEST)
    result = lax.map(jax.checkpoint(one_block), jnp.arange(N_WT * blocks_per, dtype=jnp.int32))
    return result.reshape(N_WT, STREAM, HEADS * HD)

def forward(inputs, w_qkv, w_proj, w_gate_up, w_shrink, gain_one, gain_two, seq_ids):
    normed = low(rms_scale(inputs, gain_one))
    qkv = low_back(low(jnp.einsum('wsd,de->wse', normed, w_qkv, precision=HIGHEST)))
    queries = qkv[..., :D].reshape(N_WT, STREAM, HEADS, HD)
    mixed = low_back(low(attention(queries, qkv[..., D:], seq_ids)))
    middle = inputs + low_back(jnp.einsum('wsd,de->wse', mixed, w_proj, precision=HIGHEST))
    normed_two = low(rms_scale(middle, gain_two))
    gate_up = low_back(jnp.einsum('wsd,dgf->wsgf', normed_two, w_gate_up, precision=HIGHEST))
    hidden = low(jax.nn.gelu(gate_up[..., 0, :]) * gate_up[..., 1, :])
    return middle + low_back(jnp.einsum('wsf,fd->wsd', hidden, w_shrink, precision=HIGHEST))

def reference(tokens, teacher, seq_lengths, w_attn, w_out, w_in, w_down, gain_attn, gain_ffn):
    positions = jnp.arange(STREAM + WINDOW, dtype=jnp.int32) - WINDOW
    seq_ids = jnp.stack([stream_ids(positions, seq_lengths[index], STREAM) for index in range(N_WT)])
    inputs = tokens.astype(jnp.float32)

    def closed(first, second, third, fourth, fifth, sixth, seventh):
        return forward(first, second, third, fourth, fifth, sixth, seventh, seq_ids)
    output, pull = jax.vjp(closed, inputs, w_attn.astype(jnp.float32), w_out.astype(jnp.float32), w_in.astype(jnp.float32), w_down.astype(jnp.float32), gain_attn, gain_ffn)
    valid = (seq_ids[:, WINDOW:] >= 0).astype(jnp.float32)
    count = jnp.sum(valid)
    diff = output - teacher.astype(jnp.float32)
    masked_diff = valid[..., None] * diff
    cotangent = masked_diff * (N_WT * STREAM / count)
    grads = pull(cotangent)
    loss = jnp.sum(masked_diff * diff) / (count * D)
    grad_queries = grads[1][:, :D]
    grad_keyvals = grads[1][:, D:].reshape(D, 2, HD)
    return (output.astype(jnp.bfloat16), loss, grads[0], grad_queries, grad_keyvals, grads[2], grads[3], grads[4], grads[5], grads[6])
```

```python
import math

import jax
import jax.numpy as jnp
from jax import lax
from jax.sharding import PartitionSpec as P

HEADS = 12
HD = 128
WINDOW = 1024
QBLK = 512


EPSILON = 1e-06
NEGATIVE = -1e30


def passed_along(block, axis, distance):
    devices = range(lax.axis_size(axis))
    route = [(i - distance, i) for i in devices if i - distance in devices]
    return lax.ppermute(block, axis, route)


def rms_scale(values, gain):
    return values * lax.rsqrt(jnp.mean(values * values, axis=-1, keepdims=True) + EPSILON) * gain


def stream_ids(positions, lengths, stream_len):
    seq_ends = jnp.cumsum(lengths)
    seq_starts = seq_ends - lengths
    inside = (positions >= 0) & (positions < seq_ends[-1])
    number = jnp.sum((positions[:, None] >= seq_starts[None, :]).astype(jnp.int32), axis=1) - 1
    return jnp.where(inside, number, -(positions + 2 * stream_len))


def window_mask(query_ids, key_ids):
    query_pos = lax.broadcasted_iota(jnp.int32, (QBLK, WINDOW + QBLK), 0)
    key_pos = lax.broadcasted_iota(jnp.int32, (QBLK, WINDOW + QBLK), 1)
    offset = key_pos - WINDOW - query_pos
    return (offset <= 0) & (offset > -WINDOW) & (query_ids[:, None] == key_ids[None, :])


def gated_act(gate_up):
    return jax.nn.gelu(gate_up[:, 0, :]) * gate_up[:, 1, :]


def per_device(tokens, teacher, seq_lengths, w_attn, w_out, w_in, w_down, gain_attn, gain_ffn):
    tok_rows = tokens.shape[1]
    model_width = tokens.shape[2]
    seq_devices = lax.axis_size("seq")
    seq_place = lax.axis_index("seq")
    stream_len = tok_rows * seq_devices
    all_slots = stream_len * lax.axis_size("wt")
    reach_count = (WINDOW + tok_rows - 1) // tok_rows
    edge_rows = reach_count * tok_rows
    scale = 1.0 / math.sqrt(HD)
    inputs = tokens[0].astype(jnp.float32)
    target = teacher[0].astype(jnp.float32)
    positions = seq_place * tok_rows - edge_rows + jnp.arange(edge_rows + tok_rows, dtype=jnp.int32)
    seq_ids = stream_ids(positions, seq_lengths[0], stream_len)
    valid = (seq_ids[edge_rows:] >= 0).astype(jnp.float32)
    valid_total = lax.psum(jnp.sum(seq_lengths[0]).astype(jnp.float32), "wt")
    attn_full, out_full = (
        lax.all_gather(w_attn, "wt", axis=0, tiled=True),
        lax.all_gather(w_out, "wt", axis=0, tiled=True),
    )
    normed_f, norm_one_pull = jax.vjp(rms_scale, inputs, gain_attn)
    normed = normed_f.astype(jnp.bfloat16)
    qkv = jnp.dot(normed, attn_full, preferred_element_type=jnp.float32).astype(jnp.bfloat16)
    queries = qkv[:, :model_width].reshape(tok_rows, HEADS, HD)
    key_value = qkv[:, model_width:]
    earlier = [passed_along(key_value, "seq", back_step) for back_step in range(reach_count, 0, -1)]
    extended = jnp.concatenate(earlier + [key_value], axis=0)
    block_count = tok_rows // QBLK

    def block_scores(block):
        start = block * QBLK
        query_ids = lax.dynamic_slice_in_dim(seq_ids, start + edge_rows, QBLK)
        raw = jnp.einsum(
            "qhe,ke->hqk", queries, extended[:, :HD], preferred_element_type=jnp.float32
        )
        allowed = window_mask(query_ids, seq_ids)
        masked = jnp.where(allowed[None], raw * scale, NEGATIVE)
        return (queries, extended, masked)

    def forward_block(block):
        q_blk, window, masked = block_scores(block)
        top = jnp.max(masked, axis=-1, keepdims=True)
        log_total = top + jnp.log(jnp.sum(jnp.exp(masked - top), axis=-1, keepdims=True))
        weights = jnp.exp(masked - log_total).astype(jnp.bfloat16)
        mixed = jnp.einsum(
            "hqk,ke->qhe", weights, window[:, HD:], preferred_element_type=jnp.float32
        )
        return (mixed, log_total)

    mixed_blocks, log_totals = lax.map(forward_block, jnp.arange(block_count, dtype=jnp.int32))
    mixed_b = mixed_blocks.reshape(tok_rows, model_width).astype(jnp.bfloat16)
    middle = inputs + jnp.dot(mixed_b, out_full, preferred_element_type=jnp.float32)
    normed_two_f, norm_two_pull = jax.vjp(rms_scale, middle, gain_ffn)
    normed_two = normed_two_f.astype(jnp.bfloat16)
    normed_all = lax.all_gather(normed_two, "wt", axis=0, tiled=True)
    gate_up = jnp.einsum("td,dgf->tgf", normed_all, w_in, preferred_element_type=jnp.float32)
    hidden_f, act_pull = jax.vjp(gated_act, gate_up)
    hidden = hidden_f.astype(jnp.bfloat16)
    ffn_low = jnp.dot(hidden, w_down, preferred_element_type=jnp.float32).astype(jnp.bfloat16)
    ffn_part = lax.psum_scatter(ffn_low, "wt", scatter_dimension=0, tiled=True)
    output = middle + ffn_part.astype(jnp.float32)
    diff = output - target
    masked_diff = valid[:, None] * diff
    squares = jnp.sum(masked_diff * diff)
    cotangent = masked_diff * (all_slots / valid_total)
    cot_all = lax.all_gather(cotangent.astype(jnp.bfloat16), "wt", axis=0, tiled=True)
    grad_down = jnp.einsum("td,tf->df", cot_all, hidden, preferred_element_type=jnp.float32)
    grad_down = lax.psum_scatter(grad_down.astype(jnp.bfloat16), "seq", scatter_dimension=0, tiled=True)
    grad_hidden = jnp.einsum("td,fd->tf", cot_all, w_down, preferred_element_type=jnp.float32)
    grad_gu = act_pull(grad_hidden)[0].astype(jnp.bfloat16)
    norm_two_low = jnp.einsum("tgf,dgf->td", grad_gu, w_in, preferred_element_type=jnp.float32).astype(jnp.bfloat16)
    grad_norm_two = lax.psum_scatter(norm_two_low, "wt", scatter_dimension=0, tiled=True).astype(jnp.float32)
    grad_in = jnp.einsum("td,tgf->dgf", normed_all, grad_gu, preferred_element_type=jnp.float32)
    grad_in = lax.psum_scatter(grad_in.astype(jnp.bfloat16), "seq", scatter_dimension=0, tiled=True)
    grad_middle_norm, grad_gain_ffn = norm_two_pull(grad_norm_two)
    grad_middle = cotangent + grad_middle_norm
    grad_mid_low = grad_middle.astype(jnp.bfloat16)
    grad_out = jnp.einsum("te,td->ed", grad_mid_low, mixed_b, preferred_element_type=jnp.float32)
    grad_mixed = jnp.einsum("te,de->td", grad_mid_low, out_full, preferred_element_type=jnp.float32)
    grad_mixed = grad_mixed.astype(jnp.bfloat16).reshape(tok_rows, HEADS, HD)

    def backward_block(grad_ext, block):
        q_blk, window, masked = block_scores(block)
        log_total = lax.dynamic_index_in_dim(log_totals, block, 0, keepdims=False)
        probs = jnp.exp(masked - log_total)
        weights = probs.astype(jnp.bfloat16)
        grad_weights = jnp.einsum(
            "qhe,ke->hqk", grad_mixed, window[:, HD:], preferred_element_type=jnp.float32
        )
        grad_scores = probs * (grad_weights - jnp.sum(probs * grad_weights, axis=-1, keepdims=True))
        grad_scores_low = grad_scores.astype(jnp.bfloat16)
        grad_query = (
            jnp.einsum(
                "hqk,ke->qhe", grad_scores_low, window[:, :HD], preferred_element_type=jnp.float32
            )
            * scale
        )
        grad_key = (
            jnp.einsum("hqk,qhe->ke", grad_scores_low, q_blk, preferred_element_type=jnp.float32)
            * scale
        )
        grad_value = jnp.einsum(
            "hqk,qhe->ke", weights, grad_mixed, preferred_element_type=jnp.float32
        )
        updated = grad_ext + jnp.concatenate([grad_key, grad_value], axis=1)
        return (updated, grad_query)

    grad_ext, grad_query_blocks = lax.scan(
        backward_block,
        jnp.zeros((edge_rows + tok_rows, 2 * HD), jnp.float32),
        jnp.arange(block_count, dtype=jnp.int32),
    )
    grad_kv = grad_ext[edge_rows:]
    for back_step in range(1, reach_count + 1):
        slab_rows = grad_ext[
            edge_rows - back_step * tok_rows : edge_rows - (back_step - 1) * tok_rows
        ]
        grad_kv = grad_kv + passed_along(slab_rows, "seq", -back_step)
    grad_qkv = jnp.concatenate(
        [grad_query_blocks.reshape(tok_rows, model_width), grad_kv], axis=1
    ).astype(jnp.bfloat16)
    grad_attn = jnp.einsum("te,td->ed", grad_qkv, normed, preferred_element_type=jnp.float32)
    grad_normed = jnp.einsum("te,de->td", grad_qkv, attn_full, preferred_element_type=jnp.float32)
    grad_input_norm, grad_gain_attn = norm_one_pull(grad_normed)
    grad_inputs = grad_middle + grad_input_norm
    grad_keyvals = jnp.swapaxes(grad_attn[model_width:].reshape(2, seq_devices, HD // seq_devices, model_width), 0, 1)
    slot = model_width // seq_devices
    packed = jnp.concatenate(
        [
            grad_attn[:model_width].reshape(seq_devices, slot, model_width),
            grad_keyvals.reshape(seq_devices, 2 * HD // seq_devices, model_width),
            grad_out.reshape(seq_devices, slot, model_width),
        ],
        axis=1,
    ).astype(jnp.bfloat16)
    packed = packed.reshape(seq_devices, 2 * slot + 2 * HD // seq_devices, lax.axis_size("wt"), -1)
    packed = lax.psum_scatter(packed, "seq", scatter_dimension=0, tiled=False)
    packed = lax.psum_scatter(packed, "wt", scatter_dimension=1, tiled=False).astype(jnp.float32)
    grad_queries = packed[:slot].T
    grad_keyvals = packed[slot:-slot].T.reshape(-1, 2, HD // seq_devices)
    grad_out = packed[-slot:].T
    grad_down = grad_down.astype(jnp.float32).T
    grad_in = grad_in.astype(jnp.float32)
    squares_all, gain_attn_all, gain_ffn_all = lax.psum(
        (squares, grad_gain_attn, grad_gain_ffn), ("seq", "wt")
    )
    loss = squares_all / (valid_total * model_width)
    return (
        output.astype(jnp.bfloat16)[None],
        loss,
        grad_inputs[None],
        grad_queries,
        grad_keyvals,
        grad_out,
        grad_in,
        grad_down,
        gain_attn_all,
        gain_ffn_all,
    )


def solution(mesh):
    in_specs = (
        P("wt", "seq", None),
        P("wt", "seq", None),
        P("wt", None),
        P("wt", None),
        P("wt", None),
        P(None, None, "wt"),
        P("wt", None),
        P(),
        P(),
    )
    out_specs = (
        P("wt", "seq", None),
        P(),
        P("wt", "seq", None),
        P("wt", "seq"),
        P("wt", None, "seq"),
        P("wt", "seq"),
        P("seq", None, "wt"),
        P("wt", "seq"),
        P(),
        P(),
    )
    return jax.shard_map(
        per_device, mesh=mesh, in_specs=in_specs, out_specs=out_specs, check_vma=False
    )
```

```python
import math

import jax
import jax.numpy as jnp
from jax import lax
from jax.experimental import pallas as pl
from jax.experimental.pallas import tpu as pltpu
from jax.sharding import PartitionSpec as P

HEADS = 12
HD = 128
WINDOW = 1024
QBLK = 512


EPSILON = 1e-06
NEGATIVE = -1e30

MESH = pl.DeviceIdType.MESH
F32 = jnp.float32
BF16 = jnp.bfloat16


def places():
    seq, wt = lax.axis_index("seq"), lax.axis_index("wt")
    return seq // 2, seq % 2, wt // 2, wt % 2


def device(z, x, y, c):
    return (z * 2 + x, y * 2 + c)


def remote(src, dst, send, recv, to):
    copy = pltpu.make_async_remote_copy(
        src_ref=src, dst_ref=dst, send_sem=send, recv_sem=recv, device_id=to, device_id_type=MESH
    )
    copy.start()
    return copy


def greet(devices):
    barrier = pltpu.get_barrier_semaphore()
    for one in devices:
        pl.semaphore_signal(barrier, inc=1, device_id=one, device_id_type=MESH)
    pl.semaphore_wait(barrier, len(devices))


def reduce_kernel(depth, widths, g_refs, p_ref, v_ref, g_outs, p_out, v_out, gx, gt, gz, pc, py, px, pt, pz, vb,
                  gxs, gxr, gzs, gzr, pcs, pcr, pys, pyr, pxs, pxr, pzs, pzr, vs, vr):
    z, x, y, c = places()
    width = gx.shape[-1]
    cols = pc.shape[-1]
    sib, ypeer, xpeer = device(z, x, y, 1 - c), device(z, x, 1 - y, c), device(z, 1 - x, y, c)
    zs = [lax.rem(z + d, depth) for d in range(depth)]
    zpeers = [device(zs[d], x, y, c) for d in range(depth)]
    greet([sib, ypeer, xpeer] + zpeers[1:])
    places_of = [(i, k * width) for i, total in enumerate(widths) for k in range(total // width)]
    chunks = len(places_of)
    started = []

    def go(*args):
        started.append(remote(*args))
        return started[-1]

    order = list(range(1, depth)) + [0]
    core = {}
    for d in order:
        for h in range(2):
            at = pl.multiple_of((2 * h + 1 - c) * cols, cols)
            core[d, h] = go(p_ref.at[zs[d], :, :, pl.ds(at, cols)], pc.at[d, h], pcs.at[d, h], pcr.at[d, h], sib)
    gxc, gzc, pyc, pxc, pzc, vc = {}, {}, {}, {}, {}, {}

    def g_send(k):
        if k < chunks:
            i, at = places_of[k]
            gxc[k] = go(g_refs[i].at[:, 1 - x, :, pl.ds(at, width)], gx.at[k], gxs.at[k], gxr.at[k], xpeer)

    for k in range(2):
        g_send(k)
    vc[0] = go(v_ref, vb.at[0], vs.at[0], vr.at[0], sib)

    def p_y(d):
        for h in range(2):
            core[d, h].wait_recv()
        mine = pl.multiple_of((2 * (1 - y) + c) * cols, cols)
        pt[d] = (p_ref[zs[d], :, :, pl.ds(mine, cols)].astype(F32) + pc[d, 1 - y].astype(F32)).astype(BF16)
        pyc[d] = go(pt.at[d], py.at[d], pys.at[d], pyr.at[d], ypeer)

    def g_step(k):
        gxc[k].wait_recv()
        g_send(k + 2)
        i, at = places_of[k]
        for d in range(depth):
            own = g_refs[i][zs[d], x, :, at : at + width].astype(F32)
            gt[k, d] = (own + gx[k, zs[d]].astype(F32)).astype(BF16)
            if d:
                gzc[k, d] = go(gt.at[k, d], gz.at[k, d - 1], gzs.at[k, d - 1], gzr.at[k, d - 1], zpeers[d])

    def g_end(k):
        total = gt[k, 0].astype(F32)
        for d in range(1, depth):
            gzc[k, d].wait_recv()
            total += gz[k, d - 1].astype(F32)
        i, at = places_of[k]
        g_outs[i][:, at : at + width] = total

    def p_half(d, side):
        mine = pl.multiple_of((2 * y + c) * cols, cols)
        own = p_ref[zs[d], side, :, pl.ds(mine, cols)].astype(F32)
        return own + pc[d, y, side].astype(F32) + py[d, side].astype(F32)

    def p_x(d):
        pyc[d].wait_recv()
        pt[depth + d, 0] = p_half(d, 1 - x).astype(BF16)
        pxc[d] = go(pt.at[depth + d, 0], px.at[d], pxs.at[d], pxr.at[d], xpeer)

    def p_z(d):
        pxc[d].wait_recv()
        pt[depth + d, 1] = (p_half(d, x) + px[d].astype(F32)).astype(BF16)
        if d:
            pzc[d] = go(pt.at[depth + d, 1], pz.at[d - 1], pzs.at[d - 1], pzr.at[d - 1], zpeers[d])

    def v_y():
        vc[0].wait_recv()
        vb[4] = v_ref[...] + vb[0]
        vc[1] = go(vb.at[4], vb.at[1], vs.at[1], vr.at[1], ypeer)

    def v_x():
        vc[1].wait_recv()
        vb[5] = vb[4] + vb[1]
        vc[2] = go(vb.at[5], vb.at[2], vs.at[2], vr.at[2], xpeer)

    def v_z():
        vc[2].wait_recv()
        vb[6] = vb[5] + vb[2]
        for d in range(1, depth):
            vc[2 + d] = go(vb.at[6], vb.at[6 + d], vs.at[2 + d], vr.at[2 + d], zpeers[d])

    def v_end():
        for d in range(1, depth):
            vc[2 + d].wait_recv()
        total = vb[6 + lax.rem(z, depth)]
        for n in range(1, depth):
            total += vb[6 + lax.rem(z - n + depth, depth)]
        v_out[...] = total

    todo = [lambda d=d: p_y(d) for d in order] + [v_y]
    late = [lambda: p_x(order[0]), v_x, lambda: p_x(order[1]), lambda: p_z(order[0]), v_z]
    late += [lambda: p_x(order[2]), lambda: p_z(order[1]), lambda: p_x(order[3]), lambda: p_z(order[2]), lambda: p_z(order[3]), v_end]
    for k in range(chunks):
        g_step(k)
        if k >= 2:
            g_end(k - 2)
        for _ in range(2):
            if todo:
                todo.pop(0)()
            elif k >= 4 and late:
                late.pop(0)()
    for step in todo + late:
        step()
    g_end(chunks - 2)
    g_end(chunks - 1)
    total = pt[depth, 1].astype(F32)
    for d in range(1, depth):
        pzc[d].wait_recv()
        total += pz[d - 1].astype(F32)
    p_out[...] = total
    for copy in started:
        copy.wait_send()


def reduce_all(gs, p, v, width):
    seq, slot = gs[0].shape[:2]
    depth = seq // 2
    rows, model_width = p.shape[1:]
    cols = model_width // 4
    widths = tuple(g.shape[2] for g in gs)
    chunks = sum(widths) // width
    dma = pltpu.SemaphoreType.DMA
    n = len(gs)

    def kernel(*refs):
        reduce_kernel(depth, widths, refs[:n], refs[n], refs[n + 1], refs[n + 2 : 2 * n + 2], *refs[2 * n + 2 :])

    vm = pl.BlockSpec(memory_space=pltpu.VMEM)
    out = pl.pallas_call(
        kernel,
        name="reduce_all",
        out_shape=[jax.ShapeDtypeStruct((slot, total), F32) for total in widths]
        + [jax.ShapeDtypeStruct((rows, cols), F32), jax.ShapeDtypeStruct(v.shape, F32)],
        in_specs=[vm] * (n + 2),
        out_specs=[vm] * (n + 2),
        scratch_shapes=[
            pltpu.VMEM((chunks, depth, slot, width), BF16),
            pltpu.VMEM((chunks, depth, slot, width), BF16),
            pltpu.VMEM((chunks, depth - 1, slot, width), BF16),
            pltpu.VMEM((depth, 2, 2, rows, cols), BF16),
            pltpu.VMEM((depth, 2, rows, cols), BF16),
            pltpu.VMEM((depth, rows, cols), BF16),
            pltpu.VMEM((2 * depth, 2, rows, cols), BF16),
            pltpu.VMEM((depth - 1, rows, cols), BF16),
            pltpu.VMEM((6 + depth,) + v.shape, F32),
            dma((chunks,)), dma((chunks,)), dma((chunks, depth - 1)), dma((chunks, depth - 1)),
            dma((depth, 2)), dma((depth, 2)), dma((depth,)), dma((depth,)), dma((depth,)), dma((depth,)),
            dma((depth - 1,)), dma((depth - 1,)), dma((2 + depth,)), dma((2 + depth,)),
        ],
        compiler_params=pltpu.CompilerParams(collective_id=1, has_side_effects=True, vmem_limit_bytes=60 << 20),
    )(*[g.reshape(depth, 2, slot, -1) for g in gs], p.reshape(depth, 2, rows, model_width), v)
    return out[:n], out[n], out[n + 1]


def reduce_plain(gs, p, v, width):
    gs = [lax.psum_scatter(g, "seq", scatter_dimension=0, tiled=False).astype(F32) for g in gs]
    p = lax.psum_scatter(p, "seq", scatter_dimension=0, tiled=False)
    p = lax.psum_scatter(p, "wt", scatter_dimension=1, tiled=True).astype(F32)
    return gs, p, lax.psum(v, ("seq", "wt"))


def passed_along(block, axis, distance):
    devices = range(lax.axis_size(axis))
    route = [(i - distance, i) for i in devices if i - distance in devices]
    return lax.ppermute(block, axis, route)


def rms_scale(values, gain):
    return values * lax.rsqrt(jnp.mean(values * values, axis=-1, keepdims=True) + EPSILON) * gain


def stream_ids(positions, lengths, stream_len):
    seq_ends = jnp.cumsum(lengths)
    seq_starts = seq_ends - lengths
    inside = (positions >= 0) & (positions < seq_ends[-1])
    number = jnp.sum((positions[:, None] >= seq_starts[None, :]).astype(jnp.int32), axis=1) - 1
    return jnp.where(inside, number, -(positions + 2 * stream_len))


def window_mask(query_ids, key_ids):
    query_pos = lax.broadcasted_iota(jnp.int32, (QBLK, WINDOW + QBLK), 0)
    key_pos = lax.broadcasted_iota(jnp.int32, (QBLK, WINDOW + QBLK), 1)
    offset = key_pos - WINDOW - query_pos
    return (offset <= 0) & (offset > -WINDOW) & (query_ids[:, None] == key_ids[None, :])


def gated_act(gate_up):
    return jax.nn.gelu(gate_up[:, 0, :]) * gate_up[:, 1, :]


def per_device(tokens, teacher, seq_lengths, w_attn, w_out, w_in, w_down, gain_attn, gain_ffn):
    tok_rows = tokens.shape[1]
    model_width = tokens.shape[2]
    seq_devices = lax.axis_size("seq")
    seq_place = lax.axis_index("seq")
    stream_len = tok_rows * seq_devices
    all_slots = stream_len * lax.axis_size("wt")
    reach_count = (WINDOW + tok_rows - 1) // tok_rows
    edge_rows = reach_count * tok_rows
    scale = 1.0 / math.sqrt(HD)
    inputs = tokens[0].astype(jnp.float32)
    target = teacher[0].astype(jnp.float32)
    positions = seq_place * tok_rows - edge_rows + jnp.arange(edge_rows + tok_rows, dtype=jnp.int32)
    seq_ids = stream_ids(positions, seq_lengths[0], stream_len)
    valid = (seq_ids[edge_rows:] >= 0).astype(jnp.float32)
    valid_total = lax.psum(jnp.sum(seq_lengths[0]).astype(jnp.float32), "wt")
    attn_full, out_full = (
        lax.all_gather(w_attn, "wt", axis=0, tiled=True),
        lax.all_gather(w_out, "wt", axis=0, tiled=True),
    )
    normed_f, norm_one_pull = jax.vjp(rms_scale, inputs, gain_attn)
    normed = normed_f.astype(jnp.bfloat16)
    qkv = jnp.dot(normed, attn_full, preferred_element_type=jnp.float32).astype(jnp.bfloat16)
    queries = qkv[:, :model_width].reshape(tok_rows, HEADS, HD)
    key_value = qkv[:, model_width:]
    earlier = [passed_along(key_value, "seq", back_step) for back_step in range(reach_count, 0, -1)]
    extended = jnp.concatenate(earlier + [key_value], axis=0)
    block_count = tok_rows // QBLK

    def block_scores(block):
        start = block * QBLK
        query_ids = lax.dynamic_slice_in_dim(seq_ids, start + edge_rows, QBLK)
        raw = jnp.einsum(
            "qhe,ke->hqk", queries, extended[:, :HD], preferred_element_type=jnp.float32
        )
        allowed = window_mask(query_ids, seq_ids)
        masked = jnp.where(allowed[None], raw * scale, NEGATIVE)
        return (queries, extended, masked)

    def forward_block(block):
        q_blk, window, masked = block_scores(block)
        top = jnp.max(masked, axis=-1, keepdims=True)
        log_total = top + jnp.log(jnp.sum(jnp.exp(masked - top), axis=-1, keepdims=True))
        weights = jnp.exp(masked - log_total).astype(jnp.bfloat16)
        mixed = jnp.einsum(
            "hqk,ke->qhe", weights, window[:, HD:], preferred_element_type=jnp.float32
        )
        return (mixed, log_total)

    mixed_blocks, log_totals = lax.map(forward_block, jnp.arange(block_count, dtype=jnp.int32))
    mixed_b = mixed_blocks.reshape(tok_rows, model_width).astype(jnp.bfloat16)
    middle = inputs + jnp.dot(mixed_b, out_full, preferred_element_type=jnp.float32)
    normed_two_f, norm_two_pull = jax.vjp(rms_scale, middle, gain_ffn)
    normed_two = normed_two_f.astype(jnp.bfloat16)
    normed_all = lax.all_gather(normed_two, "wt", axis=0, tiled=True)
    gate_up = jnp.einsum("td,dgf->tgf", normed_all, w_in, preferred_element_type=jnp.float32)
    hidden_f, act_pull = jax.vjp(gated_act, gate_up)
    hidden = hidden_f.astype(jnp.bfloat16)
    ffn_low = jnp.dot(hidden, w_down, preferred_element_type=jnp.float32).astype(jnp.bfloat16)
    ffn_part = lax.psum_scatter(ffn_low, "wt", scatter_dimension=0, tiled=True)
    output = middle + ffn_part.astype(jnp.float32)
    diff = output - target
    masked_diff = valid[:, None] * diff
    squares = jnp.sum(masked_diff * diff)
    cotangent = masked_diff * (all_slots / valid_total)
    cot_all = lax.all_gather(cotangent.astype(jnp.bfloat16), "wt", axis=0, tiled=True)
    grad_down = jnp.einsum("td,tf->df", cot_all, hidden, preferred_element_type=jnp.float32)
    grad_down = grad_down.astype(jnp.bfloat16)
    grad_hidden = jnp.einsum("td,fd->tf", cot_all, w_down, preferred_element_type=jnp.float32)
    grad_gu = act_pull(grad_hidden)[0].astype(jnp.bfloat16)
    norm_two_low = jnp.einsum("tgf,dgf->td", grad_gu, w_in, preferred_element_type=jnp.float32).astype(jnp.bfloat16)
    grad_norm_two = lax.psum_scatter(norm_two_low, "wt", scatter_dimension=0, tiled=True).astype(jnp.float32)
    grad_gate, grad_up = (
        jnp.einsum("td,tf->df", normed_all, grad_gu[:, half], preferred_element_type=jnp.float32).astype(jnp.bfloat16)
        for half in range(2)
    )
    grad_middle_norm, grad_gain_ffn = norm_two_pull(grad_norm_two)
    grad_middle = cotangent + grad_middle_norm
    grad_mid_low = grad_middle.astype(jnp.bfloat16)
    grad_out = jnp.einsum("te,td->ed", grad_mid_low, mixed_b, preferred_element_type=jnp.float32)
    grad_mixed = jnp.einsum("te,de->td", grad_mid_low, out_full, preferred_element_type=jnp.float32)
    grad_mixed = grad_mixed.astype(jnp.bfloat16).reshape(tok_rows, HEADS, HD)

    def backward_block(grad_ext, block):
        q_blk, window, masked = block_scores(block)
        log_total = lax.dynamic_index_in_dim(log_totals, block, 0, keepdims=False)
        probs = jnp.exp(masked - log_total)
        weights = probs.astype(jnp.bfloat16)
        grad_weights = jnp.einsum(
            "qhe,ke->hqk", grad_mixed, window[:, HD:], preferred_element_type=jnp.float32
        )
        grad_scores = probs * (grad_weights - jnp.sum(probs * grad_weights, axis=-1, keepdims=True))
        grad_scores_low = grad_scores.astype(jnp.bfloat16)
        grad_query = (
            jnp.einsum(
                "hqk,ke->qhe", grad_scores_low, window[:, :HD], preferred_element_type=jnp.float32
            )
            * scale
        )
        grad_key = (
            jnp.einsum("hqk,qhe->ke", grad_scores_low, q_blk, preferred_element_type=jnp.float32)
            * scale
        )
        grad_value = jnp.einsum(
            "hqk,qhe->ke", weights, grad_mixed, preferred_element_type=jnp.float32
        )
        updated = grad_ext + jnp.concatenate([grad_key, grad_value], axis=1)
        return (updated, grad_query)

    grad_ext, grad_query_blocks = lax.scan(
        backward_block,
        jnp.zeros((edge_rows + tok_rows, 2 * HD), jnp.float32),
        jnp.arange(block_count, dtype=jnp.int32),
    )
    grad_kv = grad_ext[edge_rows:]
    for back_step in range(1, reach_count + 1):
        slab_rows = grad_ext[
            edge_rows - back_step * tok_rows : edge_rows - (back_step - 1) * tok_rows
        ]
        grad_kv = grad_kv + passed_along(slab_rows, "seq", -back_step)
    grad_qkv = jnp.concatenate(
        [grad_query_blocks.reshape(tok_rows, model_width), grad_kv], axis=1
    ).astype(jnp.bfloat16)
    grad_attn = jnp.einsum("te,td->ed", grad_qkv, normed, preferred_element_type=jnp.float32)
    grad_normed = jnp.einsum("te,de->td", grad_qkv, attn_full, preferred_element_type=jnp.float32)
    grad_input_norm, grad_gain_attn = norm_one_pull(grad_normed)
    grad_inputs = grad_middle + grad_input_norm
    slot, kv_slot = model_width // seq_devices, HD // seq_devices
    grad_attn = grad_attn.astype(jnp.bfloat16)
    grad_key, grad_value = (
        grad_attn[model_width + at : model_width + at + HD].reshape(seq_devices, kv_slot, model_width) for at in (0, HD)
    )
    packed = jnp.concatenate(
        [
            grad_attn[:model_width].reshape(seq_devices, slot, model_width),
            grad_key,
            grad_value,
            grad_out.astype(jnp.bfloat16).reshape(seq_devices, slot, model_width),
        ],
        axis=1,
    )
    small = jnp.stack([grad_gain_attn, grad_gain_ffn, jnp.full((model_width,), squares)] + [jnp.zeros_like(grad_gain_attn)] * 5)
    ffn_grads = [part.reshape(seq_devices, slot, -1) for part in (grad_down, grad_gate, grad_up)]
    reduce = reduce_all if slot % 16 == 0 and kv_slot % 16 == 0 else reduce_plain
    (grad_down, grad_gate, grad_up), packed, small = reduce(ffn_grads, packed, small, 384)
    grad_queries = packed[:slot].T
    grad_keyvals = packed[slot:-slot].T.reshape(-1, 2, kv_slot)
    grad_out = packed[-slot:].T
    grad_down = grad_down.T
    grad_in = jnp.stack([grad_gate, grad_up], axis=1)
    gain_attn_all, gain_ffn_all, squares_all = small[0], small[1], small[2, 0]
    loss = squares_all / (valid_total * model_width)
    return (
        output.astype(jnp.bfloat16)[None],
        loss,
        grad_inputs[None],
        grad_queries,
        grad_keyvals,
        grad_out,
        grad_in,
        grad_down,
        gain_attn_all,
        gain_ffn_all,
    )


def solution(mesh):
    in_specs = (
        P("wt", "seq", None),
        P("wt", "seq", None),
        P("wt", None),
        P("wt", None),
        P("wt", None),
        P(None, None, "wt"),
        P("wt", None),
        P(),
        P(),
    )
    out_specs = (
        P("wt", "seq", None),
        P(),
        P("wt", "seq", None),
        P("wt", "seq"),
        P("wt", None, "seq"),
        P("wt", "seq"),
        P("seq", None, "wt"),
        P("wt", "seq"),
        P(),
        P(),
    )
    return jax.shard_map(
        per_device, mesh=mesh, in_specs=in_specs, out_specs=out_specs, check_vma=False
    )
```

```python
import math

import jax
import jax.numpy as jnp
from jax import lax
from jax.experimental import pallas as pl
from jax.experimental.pallas import tpu as pltpu
from jax.sharding import PartitionSpec as P

HEADS = 12
HD = 128
WINDOW = 1024
QBLK = 512


EPSILON = 1e-06
NEGATIVE = -1e30

MESH = pl.DeviceIdType.MESH
F32 = jnp.float32
BF16 = jnp.bfloat16


def places():
    seq, wt = lax.axis_index("seq"), lax.axis_index("wt")
    return seq // 2, seq % 2, wt // 2, wt % 2


def device(z, x, y, c):
    return (z * 2 + x, y * 2 + c)


def remote(src, dst, send, recv, to):
    copy = pltpu.make_async_remote_copy(
        src_ref=src, dst_ref=dst, send_sem=send, recv_sem=recv, device_id=to, device_id_type=MESH
    )
    copy.start()
    return copy


def greet(devices):
    barrier = pltpu.get_barrier_semaphore()
    for one in devices:
        pl.semaphore_signal(barrier, inc=1, device_id=one, device_id_type=MESH)
    pl.semaphore_wait(barrier, len(devices))


def reduce_kernel(depth, widths, g_refs, p_ref, v_ref, g_outs, p_out, v_out, gx, gt, gz, pc, py, px, pt, pz, vb,
                  gxs, gxr, gzs, gzr, pcs, pcr, pys, pyr, pxs, pxr, pzs, pzr, vs, vr):
    z, x, y, c = places()
    width = gx.shape[-1]
    cols = pc.shape[-1]
    sib, ypeer, xpeer = device(z, x, y, 1 - c), device(z, x, 1 - y, c), device(z, 1 - x, y, c)
    zs = [lax.rem(z + d, depth) for d in range(depth)]
    zpeers = [device(zs[d], x, y, c) for d in range(depth)]
    greet([sib, ypeer, xpeer] + zpeers[1:])
    places_of = [(i, k * width) for i, total in enumerate(widths) for k in range(total // width)]
    chunks = len(places_of)
    started = []

    def go(*args):
        started.append(remote(*args))
        return started[-1]

    order = list(range(1, depth)) + [0]
    core = {}
    for d in order:
        for h in range(2):
            at = pl.multiple_of((2 * h + 1 - c) * cols, cols)
            core[d, h] = go(p_ref.at[zs[d], :, :, pl.ds(at, cols)], pc.at[d, h], pcs.at[d, h], pcr.at[d, h], sib)
    gxc, gzc, pyc, pxc, pzc, vc = {}, {}, {}, {}, {}, {}

    def g_send(k):
        if k < chunks:
            i, at = places_of[k]
            gxc[k] = go(g_refs[i].at[:, 1 - x, :, pl.ds(at, width)], gx.at[k], gxs.at[k], gxr.at[k], xpeer)

    for k in range(2):
        g_send(k)
    vc[0] = go(v_ref, vb.at[0], vs.at[0], vr.at[0], sib)

    def p_y(d):
        for h in range(2):
            core[d, h].wait_recv()
        mine = pl.multiple_of((2 * (1 - y) + c) * cols, cols)
        pt[d] = (p_ref[zs[d], :, :, pl.ds(mine, cols)].astype(F32) + pc[d, 1 - y].astype(F32)).astype(BF16)
        pyc[d] = go(pt.at[d], py.at[d], pys.at[d], pyr.at[d], ypeer)

    def g_step(k):
        gxc[k].wait_recv()
        g_send(k + 2)
        i, at = places_of[k]
        for d in range(depth):
            own = g_refs[i][zs[d], x, :, at : at + width].astype(F32)
            gt[k, d] = (own + gx[k, zs[d]].astype(F32)).astype(BF16)
            if d:
                gzc[k, d] = go(gt.at[k, d], gz.at[k, d - 1], gzs.at[k, d - 1], gzr.at[k, d - 1], zpeers[d])

    def g_end(k):
        total = gt[k, 0].astype(F32)
        for d in range(1, depth):
            gzc[k, d].wait_recv()
            total += gz[k, d - 1].astype(F32)
        i, at = places_of[k]
        g_outs[i][:, at : at + width] = total

    def p_half(d, side):
        mine = pl.multiple_of((2 * y + c) * cols, cols)
        own = p_ref[zs[d], side, :, pl.ds(mine, cols)].astype(F32)
        return own + pc[d, y, side].astype(F32) + py[d, side].astype(F32)

    def p_x(d):
        pyc[d].wait_recv()
        pt[depth + d, 0] = p_half(d, 1 - x).astype(BF16)
        pxc[d] = go(pt.at[depth + d, 0], px.at[d], pxs.at[d], pxr.at[d], xpeer)

    def p_z(d):
        pxc[d].wait_recv()
        pt[depth + d, 1] = (p_half(d, x) + px[d].astype(F32)).astype(BF16)
        if d:
            pzc[d] = go(pt.at[depth + d, 1], pz.at[d - 1], pzs.at[d - 1], pzr.at[d - 1], zpeers[d])

    def v_y():
        vc[0].wait_recv()
        vb[4] = v_ref[...] + vb[0]
        vc[1] = go(vb.at[4], vb.at[1], vs.at[1], vr.at[1], ypeer)

    def v_x():
        vc[1].wait_recv()
        vb[5] = vb[4] + vb[1]
        vc[2] = go(vb.at[5], vb.at[2], vs.at[2], vr.at[2], xpeer)

    def v_z():
        vc[2].wait_recv()
        vb[6] = vb[5] + vb[2]
        for d in range(1, depth):
            vc[2 + d] = go(vb.at[6], vb.at[6 + d], vs.at[2 + d], vr.at[2 + d], zpeers[d])

    def v_end():
        for d in range(1, depth):
            vc[2 + d].wait_recv()
        total = vb[6 + lax.rem(z, depth)]
        for n in range(1, depth):
            total += vb[6 + lax.rem(z - n + depth, depth)]
        v_out[...] = total

    todo = [lambda d=d: p_y(d) for d in order] + [v_y]
    late = [lambda: p_x(order[0]), v_x, lambda: p_x(order[1]), lambda: p_z(order[0]), v_z]
    late += [lambda: p_x(order[2]), lambda: p_z(order[1]), lambda: p_x(order[3]), lambda: p_z(order[2]), lambda: p_z(order[3]), v_end]
    for k in range(chunks):
        g_step(k)
        if k >= 2:
            g_end(k - 2)
        for _ in range(2):
            if todo:
                todo.pop(0)()
            elif k >= 4 and late:
                late.pop(0)()
    for step in todo + late:
        step()
    g_end(chunks - 2)
    g_end(chunks - 1)
    total = pt[depth, 1].astype(F32)
    for d in range(1, depth):
        pzc[d].wait_recv()
        total += pz[d - 1].astype(F32)
    p_out[...] = total
    for copy in started:
        copy.wait_send()


def reduce_all(gd, gi, p, v, width):
    seq, slot, units = gd.shape
    depth = seq // 2
    rows, model_width = p.shape[1:]
    cols = model_width // 4
    chunks = 3 * units // width
    dma = pltpu.SemaphoreType.DMA

    def kernel(gd_ref, gi_ref, p_ref, v_ref, gd_out, gi_out, *refs):
        g_refs = (gd_ref, gi_ref.at[0], gi_ref.at[1])
        reduce_kernel(depth, (units,) * 3, g_refs, p_ref, v_ref, (gd_out, gi_out.at[0], gi_out.at[1]), *refs)

    vm = pl.BlockSpec(memory_space=pltpu.VMEM)
    return pl.pallas_call(
        kernel,
        name="reduce_all",
        out_shape=[
            jax.ShapeDtypeStruct((slot, units), F32),
            jax.ShapeDtypeStruct((2, slot, units), F32),
            jax.ShapeDtypeStruct((rows, cols), F32),
            jax.ShapeDtypeStruct(v.shape, F32),
        ],
        in_specs=[vm] * 4,
        out_specs=[vm] * 4,
        scratch_shapes=[
            pltpu.VMEM((chunks, depth, slot, width), BF16),
            pltpu.VMEM((chunks, depth, slot, width), BF16),
            pltpu.VMEM((chunks, depth - 1, slot, width), BF16),
            pltpu.VMEM((depth, 2, 2, rows, cols), BF16),
            pltpu.VMEM((depth, 2, rows, cols), BF16),
            pltpu.VMEM((depth, rows, cols), BF16),
            pltpu.VMEM((2 * depth, 2, rows, cols), BF16),
            pltpu.VMEM((depth - 1, rows, cols), BF16),
            pltpu.VMEM((6 + depth,) + v.shape, F32),
            dma((chunks,)), dma((chunks,)), dma((chunks, depth - 1)), dma((chunks, depth - 1)),
            dma((depth, 2)), dma((depth, 2)), dma((depth,)), dma((depth,)), dma((depth,)), dma((depth,)),
            dma((depth - 1,)), dma((depth - 1,)), dma((2 + depth,)), dma((2 + depth,)),
        ],
        compiler_params=pltpu.CompilerParams(collective_id=1, has_side_effects=True, vmem_limit_bytes=60 << 20),
    )(gd.reshape(depth, 2, slot, units), gi.reshape(2, depth, 2, slot, units), p.reshape(depth, 2, rows, model_width), v)


def reduce_plain(gd, gi, p, v, width):
    gd = lax.psum_scatter(gd, "seq", scatter_dimension=0, tiled=False).astype(F32)
    gi = lax.psum_scatter(gi, "seq", scatter_dimension=1, tiled=False).astype(F32)
    p = lax.psum_scatter(p, "seq", scatter_dimension=0, tiled=False)
    p = lax.psum_scatter(p, "wt", scatter_dimension=1, tiled=True).astype(F32)
    return gd, gi, p, lax.psum(v, ("seq", "wt"))


def contract(a, b, dim_a, dim_b):
    return lax.dot_general(a, b, (((dim_a,), (dim_b,)), ((), ())), preferred_element_type=F32)


def tiles(total, width, body):
    def step(i, _):
        body(pl.ds(pl.multiple_of(i * width, width), width))
        return 0

    lax.fori_loop(0, total // width, step, 0)


def flat(block):
    return block.reshape(-1, block.shape[-1])


def ffn_kernel(h, wi_hbm, wd_hbm, mid_hbm, teacher_hbm, valid, scale, out, cot, dh, gd, gi, squares,
               wi, wd, mid, teacher, hall, dall, act, hid, acc, far, out_low, sent, got, stage,
               load, h_send, h_recv, d_send, d_recv, p_send, p_recv, store, g_store):
    seq, wt = lax.axis_index("seq"), lax.axis_index("wt")
    y, c = wt // 2, wt % 2
    sib, peer = (seq, y * 2 + 1 - c), (seq, (1 - y) * 2 + c)
    half, width = h.shape[1:]
    units = wd.shape[0]

    def fetch(src, dst, sem):
        copy = pltpu.make_async_copy(src, dst, sem)
        copy.start()
        return copy

    loads = [fetch(*pair, load.at[n]) for n, pair in enumerate(
        ((h, hall.at[0]), (wi_hbm, wi), (wd_hbm, wd), (mid_hbm, mid), (teacher_hbm, teacher)))]
    greet([sib, peer])
    pending = []

    def go(*args):
        nonlocal pending
        pending.append(remote(*args))
        return pending[-1]

    def spread(src, dst, send, recv, j):
        a = go(src.at[j], dst.at[2, j], send.at[0, j], recv.at[0, j], peer)
        b = go(src.at[j], dst.at[1, j], send.at[1, j], recv.at[1, j], sib)
        return a, b

    def relay(dst, send, recv, j):
        return go(dst.at[2, j], dst.at[3, j], send.at[2, j], recv.at[2, j], sib)

    def group(ref, g):
        return ref.at[2:4, g - 2] if g >= 2 else ref.at[g]

    h_copies = [spread(h, hall, h_send, h_recv, j) for j in range(2)]

    def gated(g):
        rows = flat(group(hall, g)[...])

        def body(cols):
            gate = contract(rows, wi[0, :, cols], 1, 0)
            up = contract(rows, wi[1, :, cols], 1, 0)
            square = gate * gate
            turn = jnp.tanh(gate * (0.7978845608028654 + 0.035677408136300125 * square))
            upper = 0.5 + 0.5 * turn
            value = gate * upper
            slope = upper + 0.5 * gate * (1.0 - turn * turn) * (0.7978845608028654 + 0.10703222440890038 * square)
            shape = (2, half, up.shape[-1])
            group(hid, g)[:, :, cols] = (value * up).astype(BF16).reshape(shape)
            group(act.at[0], g)[:, :, cols] = (slope * up).astype(BF16).reshape(shape)
            group(act.at[1], g)[:, :, cols] = value.astype(BF16).reshape(shape)

        tiles(units, 384, body)

    def emit(g, cols, part):
        if g == 0:
            acc[:, :, cols] = part.reshape(2, half, -1)
        elif g == 1:
            sent[0, :, :, cols] = part.astype(BF16).reshape(2, half, -1)
        else:
            far[:, cols] = part[:half]
            sent[1, g - 2, :, cols] = part[half:].astype(BF16)

    def down(g):
        rows = flat(group(hid, g)[...])
        tiles(width, 512, lambda cols: emit(g, cols, contract(rows, wd[:, cols], 1, 0)))

    def push(phase, kind, j):
        return go(sent.at[kind, j], got.at[kind, j], p_send.at[phase, kind, j], p_recv.at[phase, kind, j], peer if kind == 2 else sib)

    def sums(phase, compute, copies, buffer, send, recv, before):
        kept = {}
        compute(0)
        for j in range(2):
            copies[j][1].wait_recv()
        compute(1)
        for j in range(2):
            kept[0, j] = push(phase, 0, j)
        for j in range(2):
            copies[j][0].wait_recv()
            passed = relay(buffer, send, recv, j)
            passed.wait_recv()
            compute(2 + j)
            kept[1, j] = push(phase, 1, j)
            kept[1, j].wait_recv()
            sent[2, j] = (far[...] + got[1, j].astype(F32)).astype(BF16)
            kept[2, j] = push(phase, 2, j)
        return kept

    def forward(g):
        gated(g)
        down(g)

    for one in loads[:3]:
        one.wait()
    kept = sums(0, forward, h_copies, hall, h_send, h_recv, None)
    first, pending = pending, []
    loads[3].wait()
    loads[4].wait()
    total = jnp.zeros((), F32)
    d_copies, saves = [], []
    factor = scale[0, 0]
    for j in range(2):
        kept[0, j].wait_recv()
        kept[2, j].wait_recv()
        step = half // 4

        def rows_of(i, so_far):
            r = pl.ds(pl.multiple_of(i * step, step), step)
            value = mid[j, r, :] + acc[j, r, :] + got[0, j, r, :].astype(F32) + got[2, j, r, :].astype(F32)
            out_low[j, r, :] = value.astype(BF16)
            diff = value - teacher[j, r, :].astype(F32)
            masked = valid[j, r, :] * diff
            grad = masked * factor
            mid[j, r, :] = grad
            dall[0, j, r, :] = grad.astype(BF16)
            return so_far + jnp.sum(masked * diff)

        total = lax.fori_loop(0, 4, rows_of, total)
        d_copies.append(spread(dall.at[0], dall, d_send, d_recv, j))
        saves.append(fetch(out_low.at[j], out.at[j], store.at[0, j]))
        saves.append(fetch(mid.at[j], cot.at[j], store.at[1, j]))
    squares[...] = jnp.full(squares.shape, total)

    def backward(g):
        rows = flat(group(dall, g)[...])

        def body(cols):
            grad = contract(rows, wd[cols, :], 1, 1).reshape(2, half, -1)
            for n in range(2):
                part = group(act.at[n], g)
                part[:, :, cols] = (grad * part[:, :, cols].astype(F32)).astype(BF16)

        tiles(units, 384, body)
        gate, up = flat(group(act.at[0], g)[...]), flat(group(act.at[1], g)[...])
        tiles(width, 512, lambda cols: emit(g, cols, contract(gate, wi[0, cols, :], 1, 1) + contract(up, wi[1, cols, :], 1, 1)))

    for copy in first:
        copy.wait_send()
    kept = sums(1, backward, d_copies, dall, d_send, d_recv, None)
    count = 0
    blocks = width // 256
    left, right = {}, {}

    def weight(left, right, target):
        def body(i, _):
            for n in range(2):
                at = pl.ds(pl.multiple_of(i * 512 + n * 256, 256), 256)

                @pl.when(i > 0)
                def _():
                    pltpu.make_async_copy(stage.at[n], target.at[at], g_store.at[n]).wait()

                stage[n] = contract(left(at), right(), 0, 0).astype(BF16)
                pltpu.make_async_copy(stage.at[n], target.at[at], g_store.at[n]).start()
            return 0

        lax.fori_loop(0, width // 512, body, 0)
        for n in range(2):
            pltpu.make_async_copy(stage.at[n], target.at[pl.ds(0, 256)], g_store.at[n]).wait()

    weight(lambda at: flat(dall[:, :, :, at].reshape(4, 2 * half, 256)), lambda: flat(hid[...].reshape(4, 2 * half, units)), gd)
    for n in range(2):
        weight(lambda at: flat(hall[:, :, :, at].reshape(4, 2 * half, 256)), lambda n=n: flat(act[n].reshape(4, 2 * half, units)), gi.at[n])
    for j in range(2):
        kept[0, j].wait_recv()
        kept[2, j].wait_recv()
        saves[2 * j + 1].wait()

        def sum_rows(i, _):
            r = pl.ds(pl.multiple_of(i * step, step), step)
            mid[j, r, :] = acc[j, r, :] + got[0, j, r, :].astype(F32) + got[2, j, r, :].astype(F32)
            return 0

        lax.fori_loop(0, 4, sum_rows, 0)
        saves.append(fetch(mid.at[j], dh.at[j], store.at[2, j]))
    for copy in pending:
        copy.wait_send()
    for n in (0, 2, 4, 5):
        saves[n].wait()


def ffn(h, wi, wd, mid, teacher, valid, scale):
    rows, width = h.shape
    units = wd.shape[0]
    half = rows // 2
    split = lambda a: a.reshape(2, half, a.shape[-1])
    dma = pltpu.SemaphoreType.DMA
    hbm, vm = pl.BlockSpec(memory_space=pl.ANY), pl.BlockSpec(memory_space=pltpu.VMEM)
    out, cot, dh, gd, gi, squares = pl.pallas_call(
        ffn_kernel,
        name="ffn",
        out_shape=[
            jax.ShapeDtypeStruct((2, half, width), BF16),
            jax.ShapeDtypeStruct((2, half, width), F32),
            jax.ShapeDtypeStruct((2, half, width), F32),
            jax.ShapeDtypeStruct((width, units), BF16),
            jax.ShapeDtypeStruct((2, width, units), BF16),
            jax.ShapeDtypeStruct((8, 128), F32),
        ],
        in_specs=[hbm] * 5 + [vm, pl.BlockSpec(memory_space=pltpu.SMEM)],
        out_specs=[hbm] * 5 + [vm],
        scratch_shapes=[
            pltpu.VMEM((2, width, units), BF16),
            pltpu.VMEM((units, width), BF16),
            pltpu.VMEM((2, half, width), F32),
            pltpu.VMEM((2, half, width), BF16),
            pltpu.VMEM((4, 2, half, width), BF16),
            pltpu.VMEM((4, 2, half, width), BF16),
            pltpu.VMEM((2, 4, 2, half, units), BF16),
            pltpu.VMEM((4, 2, half, units), BF16),
            pltpu.VMEM((2, half, width), F32),
            pltpu.VMEM((half, width), F32),
            pltpu.VMEM((2, half, width), BF16),
            pltpu.VMEM((3, 2, half, width), BF16),
            pltpu.VMEM((3, 2, half, width), BF16),
            pltpu.VMEM((2, 256, units), BF16),
            dma((5,)), dma((3, 2)), dma((3, 2)), dma((3, 2)), dma((3, 2)),
            dma((2, 3, 2)), dma((2, 3, 2)), dma((3, 2)), dma((2,)),
        ],
        compiler_params=pltpu.CompilerParams(collective_id=2, has_side_effects=True, vmem_limit_bytes=63 << 20),
    )(split(h), wi, wd, split(mid), split(teacher), split(valid), scale)
    return out.reshape(rows, width), cot.reshape(rows, width), dh.reshape(rows, width), gd, gi, squares[0, 0]


def passed_along(block, axis, distance):
    devices = range(lax.axis_size(axis))
    route = [(i - distance, i) for i in devices if i - distance in devices]
    return lax.ppermute(block, axis, route)


def rms_scale(values, gain):
    return values * lax.rsqrt(jnp.mean(values * values, axis=-1, keepdims=True) + EPSILON) * gain


def stream_ids(positions, lengths, stream_len):
    seq_ends = jnp.cumsum(lengths)
    seq_starts = seq_ends - lengths
    inside = (positions >= 0) & (positions < seq_ends[-1])
    number = jnp.sum((positions[:, None] >= seq_starts[None, :]).astype(jnp.int32), axis=1) - 1
    return jnp.where(inside, number, -(positions + 2 * stream_len))


def window_mask(query_ids, key_ids):
    query_pos = lax.broadcasted_iota(jnp.int32, (QBLK, WINDOW + QBLK), 0)
    key_pos = lax.broadcasted_iota(jnp.int32, (QBLK, WINDOW + QBLK), 1)
    offset = key_pos - WINDOW - query_pos
    return (offset <= 0) & (offset > -WINDOW) & (query_ids[:, None] == key_ids[None, :])


def gated_act(gate_up):
    return jax.nn.gelu(gate_up[:, 0, :]) * gate_up[:, 1, :]


def per_device(tokens, teacher, seq_lengths, w_attn, w_out, w_in, w_down, gain_attn, gain_ffn):
    tok_rows = tokens.shape[1]
    model_width = tokens.shape[2]
    seq_devices = lax.axis_size("seq")
    seq_place = lax.axis_index("seq")
    stream_len = tok_rows * seq_devices
    all_slots = stream_len * lax.axis_size("wt")
    reach_count = (WINDOW + tok_rows - 1) // tok_rows
    edge_rows = reach_count * tok_rows
    scale = 1.0 / math.sqrt(HD)
    inputs = tokens[0].astype(jnp.float32)
    positions = seq_place * tok_rows - edge_rows + jnp.arange(edge_rows + tok_rows, dtype=jnp.int32)
    seq_ids = stream_ids(positions, seq_lengths[0], stream_len)
    valid = (seq_ids[edge_rows:] >= 0).astype(jnp.float32)
    valid_total = lax.psum(jnp.sum(seq_lengths[0]).astype(jnp.float32), "wt")
    attn_full, out_full = (
        lax.all_gather(w_attn, "wt", axis=0, tiled=True),
        lax.all_gather(w_out, "wt", axis=0, tiled=True),
    )
    normed_f, norm_one_pull = jax.vjp(rms_scale, inputs, gain_attn)
    normed = normed_f.astype(jnp.bfloat16)
    qkv = jnp.dot(normed, attn_full, preferred_element_type=jnp.float32).astype(jnp.bfloat16)
    queries = qkv[:, :model_width].reshape(tok_rows, HEADS, HD)
    key_value = qkv[:, model_width:]
    earlier = [passed_along(key_value, "seq", back_step) for back_step in range(reach_count, 0, -1)]
    extended = jnp.concatenate(earlier + [key_value], axis=0)
    block_count = tok_rows // QBLK

    def block_scores(block):
        start = block * QBLK
        query_ids = lax.dynamic_slice_in_dim(seq_ids, start + edge_rows, QBLK)
        raw = jnp.einsum(
            "qhe,ke->hqk", queries, extended[:, :HD], preferred_element_type=jnp.float32
        )
        allowed = window_mask(query_ids, seq_ids)
        masked = jnp.where(allowed[None], raw * scale, NEGATIVE)
        return (queries, extended, masked)

    def forward_block(block):
        q_blk, window, masked = block_scores(block)
        top = jnp.max(masked, axis=-1, keepdims=True)
        log_total = top + jnp.log(jnp.sum(jnp.exp(masked - top), axis=-1, keepdims=True))
        weights = jnp.exp(masked - log_total).astype(jnp.bfloat16)
        mixed = jnp.einsum(
            "hqk,ke->qhe", weights, window[:, HD:], preferred_element_type=jnp.float32
        )
        return (mixed, log_total)

    mixed_blocks, log_totals = lax.map(forward_block, jnp.arange(block_count, dtype=jnp.int32))
    mixed_b = mixed_blocks.reshape(tok_rows, model_width).astype(jnp.bfloat16)
    middle = inputs + jnp.dot(mixed_b, out_full, preferred_element_type=jnp.float32)
    normed_two_f, norm_two_pull = jax.vjp(rms_scale, middle, gain_ffn)
    normed_two = normed_two_f.astype(jnp.bfloat16)
    scale_up = (all_slots / valid_total).reshape(1, 1)
    w_pair = jnp.swapaxes(w_in, 0, 1)
    output, cotangent, grad_norm_two, grad_down, grad_in, squares = ffn(
        normed_two, w_pair, w_down, middle, teacher[0], valid[:, None], scale_up
    )
    grad_middle_norm, grad_gain_ffn = norm_two_pull(grad_norm_two)
    grad_middle = cotangent + grad_middle_norm
    grad_mid_low = grad_middle.astype(jnp.bfloat16)
    grad_out = jnp.einsum("te,td->ed", grad_mid_low, mixed_b, preferred_element_type=jnp.float32)
    grad_mixed = jnp.einsum("te,de->td", grad_mid_low, out_full, preferred_element_type=jnp.float32)
    grad_mixed = grad_mixed.astype(jnp.bfloat16).reshape(tok_rows, HEADS, HD)

    def backward_block(grad_ext, block):
        q_blk, window, masked = block_scores(block)
        log_total = lax.dynamic_index_in_dim(log_totals, block, 0, keepdims=False)
        probs = jnp.exp(masked - log_total)
        weights = probs.astype(jnp.bfloat16)
        grad_weights = jnp.einsum(
            "qhe,ke->hqk", grad_mixed, window[:, HD:], preferred_element_type=jnp.float32
        )
        grad_scores = probs * (grad_weights - jnp.sum(probs * grad_weights, axis=-1, keepdims=True))
        grad_scores_low = grad_scores.astype(jnp.bfloat16)
        grad_query = (
            jnp.einsum(
                "hqk,ke->qhe", grad_scores_low, window[:, :HD], preferred_element_type=jnp.float32
            )
            * scale
        )
        grad_key = (
            jnp.einsum("hqk,qhe->ke", grad_scores_low, q_blk, preferred_element_type=jnp.float32)
            * scale
        )
        grad_value = jnp.einsum(
            "hqk,qhe->ke", weights, grad_mixed, preferred_element_type=jnp.float32
        )
        updated = grad_ext + jnp.concatenate([grad_key, grad_value], axis=1)
        return (updated, grad_query)

    grad_ext, grad_query_blocks = lax.scan(
        backward_block,
        jnp.zeros((edge_rows + tok_rows, 2 * HD), jnp.float32),
        jnp.arange(block_count, dtype=jnp.int32),
    )
    grad_kv = grad_ext[edge_rows:]
    for back_step in range(1, reach_count + 1):
        slab_rows = grad_ext[
            edge_rows - back_step * tok_rows : edge_rows - (back_step - 1) * tok_rows
        ]
        grad_kv = grad_kv + passed_along(slab_rows, "seq", -back_step)
    grad_qkv = jnp.concatenate(
        [grad_query_blocks.reshape(tok_rows, model_width), grad_kv], axis=1
    ).astype(jnp.bfloat16)
    grad_attn = jnp.einsum("te,td->ed", grad_qkv, normed, preferred_element_type=jnp.float32)
    grad_normed = jnp.einsum("te,de->td", grad_qkv, attn_full, preferred_element_type=jnp.float32)
    grad_input_norm, grad_gain_attn = norm_one_pull(grad_normed)
    grad_inputs = grad_middle + grad_input_norm
    slot, kv_slot = model_width // seq_devices, HD // seq_devices
    grad_attn = grad_attn.astype(jnp.bfloat16)
    grad_key, grad_value = (
        grad_attn[model_width + at : model_width + at + HD].reshape(seq_devices, kv_slot, model_width) for at in (0, HD)
    )
    packed = jnp.concatenate(
        [
            grad_attn[:model_width].reshape(seq_devices, slot, model_width),
            grad_key,
            grad_value,
            grad_out.astype(jnp.bfloat16).reshape(seq_devices, slot, model_width),
        ],
        axis=1,
    )
    small = jnp.stack([grad_gain_attn, grad_gain_ffn, jnp.full((model_width,), squares)] + [jnp.zeros_like(grad_gain_attn)] * 5)
    grad_down, grad_in = grad_down.reshape(seq_devices, slot, -1), grad_in.reshape(2, seq_devices, slot, -1)
    reduce = reduce_all if slot % 16 == 0 and kv_slot % 16 == 0 else reduce_plain
    grad_down, grad_in, packed, small = reduce(grad_down, grad_in, packed, small, 384)
    grad_queries = packed[:slot].T
    grad_keyvals = packed[slot:-slot].T.reshape(-1, 2, kv_slot)
    grad_out = packed[-slot:].T
    grad_down = grad_down.T
    grad_in = jnp.swapaxes(grad_in, 0, 1)
    gain_attn_all, gain_ffn_all, squares_all = small[0], small[1], small[2, 0]
    loss = squares_all / (valid_total * model_width)
    return (
        output[None],
        loss,
        grad_inputs[None],
        grad_queries,
        grad_keyvals,
        grad_out,
        grad_in,
        grad_down,
        gain_attn_all,
        gain_ffn_all,
    )


def solution(mesh):
    in_specs = (
        P("wt", "seq", None),
        P("wt", "seq", None),
        P("wt", None),
        P("wt", None),
        P("wt", None),
        P(None, None, "wt"),
        P("wt", None),
        P(),
        P(),
    )
    out_specs = (
        P("wt", "seq", None),
        P(),
        P("wt", "seq", None),
        P("wt", "seq"),
        P("wt", None, "seq"),
        P("wt", "seq"),
        P("seq", None, "wt"),
        P("wt", "seq"),
        P(),
        P(),
    )
    return jax.shard_map(
        per_device, mesh=mesh, in_specs=in_specs, out_specs=out_specs, check_vma=False
    )
```

```python
import math

import jax
import jax.numpy as jnp
from jax import lax
from jax.experimental import pallas as pl
from jax.experimental.pallas import tpu as pltpu
from jax.sharding import PartitionSpec as P

HEADS = 12
HD = 128
WINDOW = 1024
QROWS = 256


EPSILON = 1e-06
NEGATIVE = -1e30

MESH = pl.DeviceIdType.MESH
F32 = jnp.float32
BF16 = jnp.bfloat16


def places():
    seq, wt = lax.axis_index("seq"), lax.axis_index("wt")
    return seq // 2, seq % 2, wt // 2, wt % 2


def device(z, x, y, c):
    return (z * 2 + x, y * 2 + c)


def remote(src, dst, send, recv, to):
    copy = pltpu.make_async_remote_copy(
        src_ref=src, dst_ref=dst, send_sem=send, recv_sem=recv, device_id=to, device_id_type=MESH
    )
    copy.start()
    return copy


def greet(devices):
    barrier = pltpu.get_barrier_semaphore()
    for one in devices:
        pl.semaphore_signal(barrier, inc=1, device_id=one, device_id_type=MESH)
    pl.semaphore_wait(barrier, len(devices))


def reduce_kernel(depth, widths, g_refs, p_ref, v_ref, g_outs, p_out, v_out, gx, gt, gz, pc, py, px, pt, pz, vb,
                  gxs, gxr, gzs, gzr, pcs, pcr, pys, pyr, pxs, pxr, pzs, pzr, vs, vr):
    z, x, y, c = places()
    width = gx.shape[-1]
    cols = pc.shape[-1]
    sib, ypeer, xpeer = device(z, x, y, 1 - c), device(z, x, 1 - y, c), device(z, 1 - x, y, c)
    zs = [lax.rem(z + d, depth) for d in range(depth)]
    zpeers = [device(zs[d], x, y, c) for d in range(depth)]
    greet([sib, ypeer, xpeer] + zpeers[1:])
    places_of = [(i, k * width) for i, total in enumerate(widths) for k in range(total // width)]
    chunks = len(places_of)
    started = []

    def go(*args):
        started.append(remote(*args))
        return started[-1]

    order = list(range(1, depth)) + [0]
    core = {}
    for d in order:
        for h in range(2):
            at = pl.multiple_of((2 * h + 1 - c) * cols, cols)
            core[d, h] = go(p_ref.at[zs[d], :, :, pl.ds(at, cols)], pc.at[d, h], pcs.at[d, h], pcr.at[d, h], sib)
    gxc, gzc, pyc, pxc, pzc, vc = {}, {}, {}, {}, {}, {}

    def g_send(k):
        if k < chunks:
            i, at = places_of[k]
            gxc[k] = go(g_refs[i].at[:, 1 - x, :, pl.ds(at, width)], gx.at[k], gxs.at[k], gxr.at[k], xpeer)

    for k in range(2):
        g_send(k)
    vc[0] = go(v_ref, vb.at[0], vs.at[0], vr.at[0], sib)

    def p_y(d):
        for h in range(2):
            core[d, h].wait_recv()
        mine = pl.multiple_of((2 * (1 - y) + c) * cols, cols)
        pt[d] = (p_ref[zs[d], :, :, pl.ds(mine, cols)].astype(F32) + pc[d, 1 - y].astype(F32)).astype(BF16)
        pyc[d] = go(pt.at[d], py.at[d], pys.at[d], pyr.at[d], ypeer)

    def g_step(k):
        gxc[k].wait_recv()
        g_send(k + 2)
        i, at = places_of[k]
        for d in range(depth):
            own = g_refs[i][zs[d], x, :, at : at + width].astype(F32)
            gt[k, d] = (own + gx[k, zs[d]].astype(F32)).astype(BF16)
            if d:
                gzc[k, d] = go(gt.at[k, d], gz.at[k, d - 1], gzs.at[k, d - 1], gzr.at[k, d - 1], zpeers[d])

    def g_end(k):
        total = gt[k, 0].astype(F32)
        for d in range(1, depth):
            gzc[k, d].wait_recv()
            total += gz[k, d - 1].astype(F32)
        i, at = places_of[k]
        g_outs[i][:, at : at + width] = total

    def p_half(d, side):
        mine = pl.multiple_of((2 * y + c) * cols, cols)
        own = p_ref[zs[d], side, :, pl.ds(mine, cols)].astype(F32)
        return own + pc[d, y, side].astype(F32) + py[d, side].astype(F32)

    def p_x(d):
        pyc[d].wait_recv()
        pt[depth + d, 0] = p_half(d, 1 - x).astype(BF16)
        pxc[d] = go(pt.at[depth + d, 0], px.at[d], pxs.at[d], pxr.at[d], xpeer)

    def p_z(d):
        pxc[d].wait_recv()
        pt[depth + d, 1] = (p_half(d, x) + px[d].astype(F32)).astype(BF16)
        if d:
            pzc[d] = go(pt.at[depth + d, 1], pz.at[d - 1], pzs.at[d - 1], pzr.at[d - 1], zpeers[d])

    def v_y():
        vc[0].wait_recv()
        vb[4] = v_ref[...] + vb[0]
        vc[1] = go(vb.at[4], vb.at[1], vs.at[1], vr.at[1], ypeer)

    def v_x():
        vc[1].wait_recv()
        vb[5] = vb[4] + vb[1]
        vc[2] = go(vb.at[5], vb.at[2], vs.at[2], vr.at[2], xpeer)

    def v_z():
        vc[2].wait_recv()
        vb[6] = vb[5] + vb[2]
        for d in range(1, depth):
            vc[2 + d] = go(vb.at[6], vb.at[6 + d], vs.at[2 + d], vr.at[2 + d], zpeers[d])

    def v_end():
        for d in range(1, depth):
            vc[2 + d].wait_recv()
        total = vb[6 + lax.rem(z, depth)]
        for n in range(1, depth):
            total += vb[6 + lax.rem(z - n + depth, depth)]
        v_out[...] = total

    todo = [lambda d=d: p_y(d) for d in order] + [v_y]
    late = [lambda: p_x(order[0]), v_x, lambda: p_x(order[1]), lambda: p_z(order[0]), v_z]
    late += [lambda: p_x(order[2]), lambda: p_z(order[1]), lambda: p_x(order[3]), lambda: p_z(order[2]), lambda: p_z(order[3]), v_end]
    for k in range(chunks):
        g_step(k)
        if k >= 2:
            g_end(k - 2)
        for _ in range(2):
            if todo:
                todo.pop(0)()
            elif k >= 4 and late:
                late.pop(0)()
    for step in todo + late:
        step()
    g_end(chunks - 2)
    g_end(chunks - 1)
    total = pt[depth, 1].astype(F32)
    for d in range(1, depth):
        pzc[d].wait_recv()
        total += pz[d - 1].astype(F32)
    p_out[...] = total
    for copy in started:
        copy.wait_send()


def reduce_all(gd, gi, p, v, width):
    seq, slot, units = gd.shape
    depth = seq // 2
    rows, model_width = p.shape[1:]
    cols = model_width // 4
    chunks = 3 * units // width
    dma = pltpu.SemaphoreType.DMA

    def kernel(gd_ref, gi_ref, p_ref, v_ref, gd_out, gi_out, *refs):
        g_refs = (gd_ref, gi_ref.at[0], gi_ref.at[1])
        reduce_kernel(depth, (units,) * 3, g_refs, p_ref, v_ref, (gd_out, gi_out.at[0], gi_out.at[1]), *refs)

    vm = pl.BlockSpec(memory_space=pltpu.VMEM)
    return pl.pallas_call(
        kernel,
        name="reduce_all",
        out_shape=[
            jax.ShapeDtypeStruct((slot, units), F32),
            jax.ShapeDtypeStruct((2, slot, units), F32),
            jax.ShapeDtypeStruct((rows, cols), F32),
            jax.ShapeDtypeStruct(v.shape, F32),
        ],
        in_specs=[vm] * 4,
        out_specs=[vm] * 4,
        scratch_shapes=[
            pltpu.VMEM((chunks, depth, slot, width), BF16),
            pltpu.VMEM((chunks, depth, slot, width), BF16),
            pltpu.VMEM((chunks, depth - 1, slot, width), BF16),
            pltpu.VMEM((depth, 2, 2, rows, cols), BF16),
            pltpu.VMEM((depth, 2, rows, cols), BF16),
            pltpu.VMEM((depth, rows, cols), BF16),
            pltpu.VMEM((2 * depth, 2, rows, cols), BF16),
            pltpu.VMEM((depth - 1, rows, cols), BF16),
            pltpu.VMEM((6 + depth,) + v.shape, F32),
            dma((chunks,)), dma((chunks,)), dma((chunks, depth - 1)), dma((chunks, depth - 1)),
            dma((depth, 2)), dma((depth, 2)), dma((depth,)), dma((depth,)), dma((depth,)), dma((depth,)),
            dma((depth - 1,)), dma((depth - 1,)), dma((2 + depth,)), dma((2 + depth,)),
        ],
        compiler_params=pltpu.CompilerParams(collective_id=1, has_side_effects=True, vmem_limit_bytes=60 << 20),
    )(gd.reshape(depth, 2, slot, units), gi.reshape(2, depth, 2, slot, units), p.reshape(depth, 2, rows, model_width), v)


def reduce_plain(gd, gi, p, v, width):
    gd = lax.psum_scatter(gd, "seq", scatter_dimension=0, tiled=False).astype(F32)
    gi = lax.psum_scatter(gi, "seq", scatter_dimension=1, tiled=False).astype(F32)
    p = lax.psum_scatter(p, "seq", scatter_dimension=0, tiled=False)
    p = lax.psum_scatter(p, "wt", scatter_dimension=1, tiled=True).astype(F32)
    return gd, gi, p, lax.psum(v, ("seq", "wt"))


def contract(a, b, dim_a, dim_b):
    return lax.dot_general(a, b, (((dim_a,), (dim_b,)), ((), ())), preferred_element_type=F32)


def tiles(total, width, body):
    def step(i, _):
        body(pl.ds(pl.multiple_of(i * width, width), width))
        return 0

    lax.fori_loop(0, total // width, step, 0)


def flat(block):
    return block.reshape(-1, block.shape[-1])


def ffn_kernel(h, wi_hbm, wd_hbm, mid_hbm, teacher_hbm, valid, scale, out, cot, dh, gd, gi, squares,
               wi, wd, mid, teacher, hall, dall, act, hid, acc, far, out_low, sent, got, stage,
               load, h_send, h_recv, d_send, d_recv, p_send, p_recv, store, g_store):
    seq, wt = lax.axis_index("seq"), lax.axis_index("wt")
    y, c = wt // 2, wt % 2
    sib, peer = (seq, y * 2 + 1 - c), (seq, (1 - y) * 2 + c)
    half, width = h.shape[1:]
    units = wd.shape[0]

    def fetch(src, dst, sem):
        copy = pltpu.make_async_copy(src, dst, sem)
        copy.start()
        return copy

    loads = [fetch(*pair, load.at[n]) for n, pair in enumerate(
        ((h, hall.at[0]), (wi_hbm, wi), (wd_hbm, wd), (mid_hbm, mid), (teacher_hbm, teacher)))]
    greet([sib, peer])
    pending = []

    def go(*args):
        nonlocal pending
        pending.append(remote(*args))
        return pending[-1]

    def spread(src, dst, send, recv, j):
        a = go(src.at[j], dst.at[2, j], send.at[0, j], recv.at[0, j], peer)
        b = go(src.at[j], dst.at[1, j], send.at[1, j], recv.at[1, j], sib)
        return a, b

    def relay(dst, send, recv, j):
        return go(dst.at[2, j], dst.at[3, j], send.at[2, j], recv.at[2, j], sib)

    def group(ref, g):
        return ref.at[2:4, g - 2] if g >= 2 else ref.at[g]

    h_copies = [spread(h, hall, h_send, h_recv, j) for j in range(2)]

    def gated(g):
        rows = flat(group(hall, g)[...])

        def body(cols):
            gate = contract(rows, wi[0, :, cols], 1, 0)
            up = contract(rows, wi[1, :, cols], 1, 0)
            square = gate * gate
            turn = jnp.tanh(gate * (0.7978845608028654 + 0.035677408136300125 * square))
            upper = 0.5 + 0.5 * turn
            value = gate * upper
            slope = upper + 0.5 * gate * (1.0 - turn * turn) * (0.7978845608028654 + 0.10703222440890038 * square)
            shape = (2, half, up.shape[-1])
            group(hid, g)[:, :, cols] = (value * up).astype(BF16).reshape(shape)
            group(act.at[0], g)[:, :, cols] = (slope * up).astype(BF16).reshape(shape)
            group(act.at[1], g)[:, :, cols] = value.astype(BF16).reshape(shape)

        tiles(units, 384, body)

    def emit(g, cols, part):
        if g == 0:
            acc[:, :, cols] = part.reshape(2, half, -1)
        elif g == 1:
            sent[0, :, :, cols] = part.astype(BF16).reshape(2, half, -1)
        else:
            far[:, cols] = part[:half]
            sent[1, g - 2, :, cols] = part[half:].astype(BF16)

    def down(g):
        rows = flat(group(hid, g)[...])
        tiles(width, 512, lambda cols: emit(g, cols, contract(rows, wd[:, cols], 1, 0)))

    def push(phase, kind, j):
        return go(sent.at[kind, j], got.at[kind, j], p_send.at[phase, kind, j], p_recv.at[phase, kind, j], peer if kind == 2 else sib)

    def sums(phase, compute, copies, buffer, send, recv, before):
        kept = {}
        compute(0)
        for j in range(2):
            copies[j][1].wait_recv()
        compute(1)
        for j in range(2):
            kept[0, j] = push(phase, 0, j)
        for j in range(2):
            copies[j][0].wait_recv()
            passed = relay(buffer, send, recv, j)
            passed.wait_recv()
            compute(2 + j)
            kept[1, j] = push(phase, 1, j)
            kept[1, j].wait_recv()
            sent[2, j] = (far[...] + got[1, j].astype(F32)).astype(BF16)
            kept[2, j] = push(phase, 2, j)
        return kept

    def forward(g):
        gated(g)
        down(g)

    for one in loads[:3]:
        one.wait()
    kept = sums(0, forward, h_copies, hall, h_send, h_recv, None)
    first, pending = pending, []
    loads[3].wait()
    loads[4].wait()
    total = jnp.zeros((), F32)
    d_copies, saves = [], []
    factor = scale[0, 0]
    for j in range(2):
        kept[0, j].wait_recv()
        kept[2, j].wait_recv()
        step = half // 4

        def rows_of(i, so_far):
            r = pl.ds(pl.multiple_of(i * step, step), step)
            value = mid[j, r, :] + acc[j, r, :] + got[0, j, r, :].astype(F32) + got[2, j, r, :].astype(F32)
            out_low[j, r, :] = value.astype(BF16)
            diff = value - teacher[j, r, :].astype(F32)
            masked = valid[j, r, :] * diff
            grad = masked * factor
            mid[j, r, :] = grad
            dall[0, j, r, :] = grad.astype(BF16)
            return so_far + jnp.sum(masked * diff)

        total = lax.fori_loop(0, 4, rows_of, total)
        d_copies.append(spread(dall.at[0], dall, d_send, d_recv, j))
        saves.append(fetch(out_low.at[j], out.at[j], store.at[0, j]))
        saves.append(fetch(mid.at[j], cot.at[j], store.at[1, j]))
    squares[...] = jnp.full(squares.shape, total)

    def backward(g):
        rows = flat(group(dall, g)[...])

        def body(cols):
            grad = contract(rows, wd[cols, :], 1, 1).reshape(2, half, -1)
            for n in range(2):
                part = group(act.at[n], g)
                part[:, :, cols] = (grad * part[:, :, cols].astype(F32)).astype(BF16)

        tiles(units, 384, body)
        gate, up = flat(group(act.at[0], g)[...]), flat(group(act.at[1], g)[...])
        tiles(width, 512, lambda cols: emit(g, cols, contract(gate, wi[0, cols, :], 1, 1) + contract(up, wi[1, cols, :], 1, 1)))

    for copy in first:
        copy.wait_send()
    kept = sums(1, backward, d_copies, dall, d_send, d_recv, None)
    count = 0
    blocks = width // 256
    left, right = {}, {}

    def weight(left, right, target):
        def body(i, _):
            for n in range(2):
                at = pl.ds(pl.multiple_of(i * 512 + n * 256, 256), 256)

                @pl.when(i > 0)
                def _():
                    pltpu.make_async_copy(stage.at[n], target.at[at], g_store.at[n]).wait()

                stage[n] = contract(left(at), right(), 0, 0).astype(BF16)
                pltpu.make_async_copy(stage.at[n], target.at[at], g_store.at[n]).start()
            return 0

        lax.fori_loop(0, width // 512, body, 0)
        for n in range(2):
            pltpu.make_async_copy(stage.at[n], target.at[pl.ds(0, 256)], g_store.at[n]).wait()

    weight(lambda at: flat(dall[:, :, :, at].reshape(4, 2 * half, 256)), lambda: flat(hid[...].reshape(4, 2 * half, units)), gd)
    for n in range(2):
        weight(lambda at: flat(hall[:, :, :, at].reshape(4, 2 * half, 256)), lambda n=n: flat(act[n].reshape(4, 2 * half, units)), gi.at[n])
    for j in range(2):
        kept[0, j].wait_recv()
        kept[2, j].wait_recv()
        saves[2 * j + 1].wait()

        def sum_rows(i, _):
            r = pl.ds(pl.multiple_of(i * step, step), step)
            mid[j, r, :] = acc[j, r, :] + got[0, j, r, :].astype(F32) + got[2, j, r, :].astype(F32)
            return 0

        lax.fori_loop(0, 4, sum_rows, 0)
        saves.append(fetch(mid.at[j], dh.at[j], store.at[2, j]))
    for copy in pending:
        copy.wait_send()
    for n in (0, 2, 4, 5):
        saves[n].wait()


def ffn(h, wi, wd, mid, teacher, valid, scale):
    rows, width = h.shape
    units = wd.shape[0]
    half = rows // 2
    split = lambda a: a.reshape(2, half, a.shape[-1])
    dma = pltpu.SemaphoreType.DMA
    hbm, vm = pl.BlockSpec(memory_space=pl.ANY), pl.BlockSpec(memory_space=pltpu.VMEM)
    out, cot, dh, gd, gi, squares = pl.pallas_call(
        ffn_kernel,
        name="ffn",
        out_shape=[
            jax.ShapeDtypeStruct((2, half, width), BF16),
            jax.ShapeDtypeStruct((2, half, width), F32),
            jax.ShapeDtypeStruct((2, half, width), F32),
            jax.ShapeDtypeStruct((width, units), BF16),
            jax.ShapeDtypeStruct((2, width, units), BF16),
            jax.ShapeDtypeStruct((8, 128), F32),
        ],
        in_specs=[hbm] * 5 + [vm, pl.BlockSpec(memory_space=pltpu.SMEM)],
        out_specs=[hbm] * 5 + [vm],
        scratch_shapes=[
            pltpu.VMEM((2, width, units), BF16),
            pltpu.VMEM((units, width), BF16),
            pltpu.VMEM((2, half, width), F32),
            pltpu.VMEM((2, half, width), BF16),
            pltpu.VMEM((4, 2, half, width), BF16),
            pltpu.VMEM((4, 2, half, width), BF16),
            pltpu.VMEM((2, 4, 2, half, units), BF16),
            pltpu.VMEM((4, 2, half, units), BF16),
            pltpu.VMEM((2, half, width), F32),
            pltpu.VMEM((half, width), F32),
            pltpu.VMEM((2, half, width), BF16),
            pltpu.VMEM((3, 2, half, width), BF16),
            pltpu.VMEM((3, 2, half, width), BF16),
            pltpu.VMEM((2, 256, units), BF16),
            dma((5,)), dma((3, 2)), dma((3, 2)), dma((3, 2)), dma((3, 2)),
            dma((2, 3, 2)), dma((2, 3, 2)), dma((3, 2)), dma((2,)),
        ],
        compiler_params=pltpu.CompilerParams(collective_id=2, has_side_effects=True, vmem_limit_bytes=63 << 20),
    )(split(h), wi, wd, split(mid), split(teacher), split(valid), scale)
    return out.reshape(rows, width), cot.reshape(rows, width), dh.reshape(rows, width), gd, gi, squares[0, 0]

def pair_rows(block):
    return jnp.concatenate([block[:, :HD], block[:, HD:]], axis=0)


def pair_columns(block):
    rows = block.shape[0] // 2
    return jnp.concatenate([block[:rows], block[rows:]], axis=1)


def attend_kernel(q, kv, q_ids, k_ids, out, probs, bias):
    i, pair = pl.program_id(0), pl.program_id(1)
    reach = WINDOW + QROWS
    keys = pl.ds(pl.multiple_of(i * QROWS, QROWS), reach)

    @pl.when(pair == 0)
    def _():
        row = lax.broadcasted_iota(jnp.int32, (QROWS, reach), 0)
        offset = lax.broadcasted_iota(jnp.int32, (QROWS, reach), 1) - WINDOW - row
        allowed = (offset <= 0) & (offset > -WINDOW) & (q_ids[...] == k_ids[:, keys])
        bias[...] = jnp.where(allowed, 0.0, NEGATIVE)

    scores = contract(pair_rows(q[...]), kv[keys, :HD], 1, 1) * (math.log2(math.e) / math.sqrt(HD))
    shifted = scores.reshape(2, QROWS, reach) + bias[...][None]
    powers = jnp.exp2(shifted - jnp.max(shifted, axis=-1, keepdims=True))
    weights = (powers * (1.0 / jnp.sum(powers, axis=-1, keepdims=True))).astype(BF16)
    probs[0] = weights
    mixed = contract(weights.reshape(2 * QROWS, reach), kv[keys, HD:], 1, 0)
    out[...] = pair_columns(mixed).astype(BF16)


def attend(queries, width, extended, q_ids, k_ids):
    rows = queries.shape[0]
    blocks, pairs, reach = rows // QROWS, width // (2 * HD), WINDOW + QROWS
    return pl.pallas_call(
        attend_kernel,
        name="attend",
        grid=(blocks, pairs),
        out_shape=[
            jax.ShapeDtypeStruct((rows, width), BF16),
            jax.ShapeDtypeStruct((blocks, 2 * pairs, QROWS, reach), BF16),
        ],
        in_specs=[
            pl.BlockSpec((QROWS, 2 * HD), lambda i, p: (i, p)),
            pl.BlockSpec(extended.shape, lambda i, p: (0, 0)),
            pl.BlockSpec((QROWS, 1), lambda i, p: (i, 0)),
            pl.BlockSpec(k_ids.shape, lambda i, p: (0, 0)),
        ],
        out_specs=[
            pl.BlockSpec((QROWS, 2 * HD), lambda i, p: (i, p)),
            pl.BlockSpec((1, 2, QROWS, reach), lambda i, p: (i, p, 0, 0)),
        ],
        scratch_shapes=[pltpu.VMEM((QROWS, reach), F32)],
        compiler_params=pltpu.CompilerParams(vmem_limit_bytes=48 << 20),
    )(queries, extended, q_ids, k_ids)


def attend_back_kernel(q, kv, grad, mixed, probs, grad_q, grad_kv):
    i, pair = pl.program_id(0), pl.program_id(1)
    reach = WINDOW + QROWS
    keys = pl.ds(pl.multiple_of(i * QROWS, QROWS), reach)

    @pl.when((i == 0) & (pair == 0))
    def _():
        grad_kv[...] = jnp.zeros_like(grad_kv)

    queries, grads = pair_rows(q[...]), pair_rows(grad[...])
    weights = probs[0].reshape(2 * QROWS, reach)
    dots = jnp.sum(grads.astype(F32) * pair_rows(mixed[...]).astype(F32), axis=-1, keepdims=True)
    steep = contract(grads, kv[keys, HD:], 1, 1) - dots
    steep = (weights.astype(F32) * steep).astype(BF16)
    grad_q[...] = (pair_columns(contract(steep, kv[keys, :HD], 1, 0)) * (1.0 / math.sqrt(HD))).astype(BF16)
    grad_kv[keys, :HD] += contract(steep, queries, 0, 0)
    grad_kv[keys, HD:] += contract(weights, grads, 0, 0)


def attend_back(queries, extended, grad_mixed, mixed, probs):
    rows, width = mixed.shape
    blocks, pairs, reach = rows // QROWS, width // (2 * HD), WINDOW + QROWS
    block = pl.BlockSpec((QROWS, 2 * HD), lambda i, p: (i, p))
    whole = pl.BlockSpec(extended.shape, lambda i, p: (0, 0))
    return pl.pallas_call(
        attend_back_kernel,
        name="attend_back",
        grid=(blocks, pairs),
        out_shape=[jax.ShapeDtypeStruct((rows, width), BF16), jax.ShapeDtypeStruct(extended.shape, F32)],
        in_specs=[block, whole, block, block, pl.BlockSpec((1, 2, QROWS, reach), lambda i, p: (i, p, 0, 0))],
        out_specs=[block, whole],
        compiler_params=pltpu.CompilerParams(vmem_limit_bytes=48 << 20),
    )(queries, extended, grad_mixed, mixed, probs)


def passed_along(block, axis, distance):
    devices = range(lax.axis_size(axis))
    route = [(i - distance, i) for i in devices if i - distance in devices]
    return lax.ppermute(block, axis, route)


def rms_scale(values, gain):
    return values * lax.rsqrt(jnp.mean(values * values, axis=-1, keepdims=True) + EPSILON) * gain


def stream_ids(positions, lengths, stream_len):
    seq_ends = jnp.cumsum(lengths)
    seq_starts = seq_ends - lengths
    inside = (positions >= 0) & (positions < seq_ends[-1])
    number = jnp.sum((positions[:, None] >= seq_starts[None, :]).astype(jnp.int32), axis=1) - 1
    return jnp.where(inside, number, -(positions + 2 * stream_len))


def per_device(tokens, teacher, seq_lengths, w_attn, w_out, w_in, w_down, gain_attn, gain_ffn):
    tok_rows = tokens.shape[1]
    model_width = tokens.shape[2]
    seq_devices = lax.axis_size("seq")
    seq_place = lax.axis_index("seq")
    stream_len = tok_rows * seq_devices
    all_slots = stream_len * lax.axis_size("wt")
    reach_count = (WINDOW + tok_rows - 1) // tok_rows
    edge_rows = reach_count * tok_rows
    inputs = tokens[0].astype(jnp.float32)
    positions = seq_place * tok_rows - edge_rows + jnp.arange(edge_rows + tok_rows, dtype=jnp.int32)
    seq_ids = stream_ids(positions, seq_lengths[0], stream_len)
    valid = (seq_ids[edge_rows:] >= 0).astype(jnp.float32)
    valid_total = lax.psum(jnp.sum(seq_lengths[0]).astype(jnp.float32), "wt")
    attn_full, out_full = (
        lax.all_gather(w_attn, "wt", axis=0, tiled=True),
        lax.all_gather(w_out, "wt", axis=0, tiled=True),
    )
    normed_f, norm_one_pull = jax.vjp(rms_scale, inputs, gain_attn)
    normed = normed_f.astype(jnp.bfloat16)
    qkv = jnp.dot(normed, attn_full, preferred_element_type=jnp.float32).astype(jnp.bfloat16)
    key_value = qkv[:, model_width:]
    earlier = [passed_along(key_value, "seq", back_step) for back_step in range(reach_count, 0, -1)]
    extended = jnp.concatenate(earlier + [key_value], axis=0)
    mixed_b, probs = attend(qkv, model_width, extended, seq_ids[edge_rows:, None], seq_ids[None, :])
    middle = inputs + jnp.dot(mixed_b, out_full, preferred_element_type=jnp.float32)
    normed_two_f, norm_two_pull = jax.vjp(rms_scale, middle, gain_ffn)
    normed_two = normed_two_f.astype(jnp.bfloat16)
    scale_up = (all_slots / valid_total).reshape(1, 1)
    w_pair = jnp.swapaxes(w_in, 0, 1)
    output, cotangent, grad_norm_two, grad_down, grad_in, squares = ffn(
        normed_two, w_pair, w_down, middle, teacher[0], valid[:, None], scale_up
    )
    grad_middle_norm, grad_gain_ffn = norm_two_pull(grad_norm_two)
    grad_middle = cotangent + grad_middle_norm
    grad_mid_low = grad_middle.astype(jnp.bfloat16)
    grad_out = jnp.einsum("te,td->ed", grad_mid_low, mixed_b, preferred_element_type=jnp.float32)
    grad_mixed = jnp.einsum("te,de->td", grad_mid_low, out_full, preferred_element_type=jnp.float32)
    grad_query, grad_ext = attend_back(qkv, extended, grad_mixed.astype(jnp.bfloat16), mixed_b, probs)
    grad_kv = grad_ext[edge_rows:]
    for back_step in range(1, reach_count + 1):
        slab_rows = grad_ext[
            edge_rows - back_step * tok_rows : edge_rows - (back_step - 1) * tok_rows
        ]
        grad_kv = grad_kv + passed_along(slab_rows, "seq", -back_step)
    grad_key = (grad_kv[:, :HD] * (1.0 / math.sqrt(HD))).astype(jnp.bfloat16)
    grad_qkv = jnp.concatenate([grad_query, grad_key, grad_kv[:, HD:].astype(jnp.bfloat16)], axis=1)
    grad_attn = jnp.einsum("te,td->ed", grad_qkv, normed, preferred_element_type=jnp.float32)
    grad_normed = jnp.einsum("te,de->td", grad_qkv, attn_full, preferred_element_type=jnp.float32)
    grad_input_norm, grad_gain_attn = norm_one_pull(grad_normed)
    grad_inputs = grad_middle + grad_input_norm
    slot, kv_slot = model_width // seq_devices, HD // seq_devices
    grad_attn = grad_attn.astype(jnp.bfloat16)
    grad_key, grad_value = (
        grad_attn[model_width + at : model_width + at + HD].reshape(seq_devices, kv_slot, model_width) for at in (0, HD)
    )
    packed = jnp.concatenate(
        [
            grad_attn[:model_width].reshape(seq_devices, slot, model_width),
            grad_key,
            grad_value,
            grad_out.astype(jnp.bfloat16).reshape(seq_devices, slot, model_width),
        ],
        axis=1,
    )
    small = jnp.stack([grad_gain_attn, grad_gain_ffn, jnp.full((model_width,), squares)] + [jnp.zeros_like(grad_gain_attn)] * 5)
    grad_down, grad_in = grad_down.reshape(seq_devices, slot, -1), grad_in.reshape(2, seq_devices, slot, -1)
    reduce = reduce_all if slot % 16 == 0 and kv_slot % 16 == 0 else reduce_plain
    grad_down, grad_in, packed, small = reduce(grad_down, grad_in, packed, small, 384)
    grad_queries = packed[:slot].T
    grad_keyvals = packed[slot:-slot].T.reshape(-1, 2, kv_slot)
    grad_out = packed[-slot:].T
    grad_down = grad_down.T
    grad_in = jnp.swapaxes(grad_in, 0, 1)
    gain_attn_all, gain_ffn_all, squares_all = small[0], small[1], small[2, 0]
    loss = squares_all / (valid_total * model_width)
    return (
        output[None],
        loss,
        grad_inputs[None],
        grad_queries,
        grad_keyvals,
        grad_out,
        grad_in,
        grad_down,
        gain_attn_all,
        gain_ffn_all,
    )


def solution(mesh):
    in_specs = (
        P("wt", "seq", None),
        P("wt", "seq", None),
        P("wt", None),
        P("wt", None),
        P("wt", None),
        P(None, None, "wt"),
        P("wt", None),
        P(),
        P(),
    )
    out_specs = (
        P("wt", "seq", None),
        P(),
        P("wt", "seq", None),
        P("wt", "seq"),
        P("wt", None, "seq"),
        P("wt", "seq"),
        P("seq", None, "wt"),
        P("wt", "seq"),
        P(),
        P(),
    )
    return jax.shard_map(
        per_device, mesh=mesh, in_specs=in_specs, out_specs=out_specs, check_vma=False
    )
```

```python
import math

import jax
import jax.numpy as jnp
from jax import lax
from jax.experimental import pallas as pl
from jax.experimental.pallas import tpu as pltpu
from jax.sharding import PartitionSpec as P

HEADS = 12
HD = 128
WINDOW = 1024
QROWS = 256


EPSILON = 1e-06
NEGATIVE = -1e30

MESH = pl.DeviceIdType.MESH
F32 = jnp.float32
BF16 = jnp.bfloat16


def places():
    seq, wt = lax.axis_index("seq"), lax.axis_index("wt")
    return seq // 2, seq % 2, wt // 2, wt % 2


def device(z, x, y, c):
    return (z * 2 + x, y * 2 + c)


def remote(src, dst, send, recv, to):
    copy = pltpu.make_async_remote_copy(
        src_ref=src, dst_ref=dst, send_sem=send, recv_sem=recv, device_id=to, device_id_type=MESH
    )
    copy.start()
    return copy


def greet(devices):
    barrier = pltpu.get_barrier_semaphore()
    for one in devices:
        pl.semaphore_signal(barrier, inc=1, device_id=one, device_id_type=MESH)
    pl.semaphore_wait(barrier, len(devices))


def reduce_plain(gd, gi, p, v):
    gd = lax.psum_scatter(gd, "seq", scatter_dimension=0, tiled=False).astype(F32)
    gi = lax.psum_scatter(gi, "seq", scatter_dimension=1, tiled=False).astype(F32)
    p = lax.psum_scatter(p, "seq", scatter_dimension=0, tiled=False)
    p = lax.psum_scatter(p, "wt", scatter_dimension=1, tiled=True).astype(F32)
    return gd, gi, p, lax.psum(v, ("seq", "wt"))


def contract(a, b, dim_a, dim_b):
    return lax.dot_general(a, b, (((dim_a,), (dim_b,)), ((), ())), preferred_element_type=F32)


def tiles(total, width, body):
    def step(i, _):
        body(pl.ds(pl.multiple_of(i * width, width), width))
        return 0

    lax.fori_loop(0, total // width, step, 0)


def flat(block):
    return block.reshape(-1, block.shape[-1])


def ffn_kernel(h, wi_hbm, wd_hbm, mid_hbm, teacher_hbm, valid, scale, out, cot, dh, gd, gi, squares,
               wi, wd, mid, teacher, hall, dall, act, hid, acc, far, out_low, sent, got, stage,
               load, h_send, h_recv, d_send, d_recv, p_send, p_recv, store, g_store):
    seq, wt = lax.axis_index("seq"), lax.axis_index("wt")
    y, c = wt // 2, wt % 2
    sib, peer = (seq, y * 2 + 1 - c), (seq, (1 - y) * 2 + c)
    half, width = h.shape[1:]
    units = wd.shape[0]

    def fetch(src, dst, sem):
        copy = pltpu.make_async_copy(src, dst, sem)
        copy.start()
        return copy

    loads = [fetch(*pair, load.at[n]) for n, pair in enumerate(
        ((h, hall.at[0]), (wi_hbm, wi), (wd_hbm, wd), (mid_hbm, mid), (teacher_hbm, teacher)))]
    greet([sib, peer])
    pending = []

    def go(*args):
        nonlocal pending
        pending.append(remote(*args))
        return pending[-1]

    def spread(src, dst, send, recv, j):
        a = go(src.at[j], dst.at[2, j], send.at[0, j], recv.at[0, j], peer)
        b = go(src.at[j], dst.at[1, j], send.at[1, j], recv.at[1, j], sib)
        return a, b

    def relay(dst, send, recv, j):
        return go(dst.at[2, j], dst.at[3, j], send.at[2, j], recv.at[2, j], sib)

    def group(ref, g):
        return ref.at[2:4, g - 2] if g >= 2 else ref.at[g]

    h_copies = [spread(h, hall, h_send, h_recv, j) for j in range(2)]

    def gated(g):
        rows = flat(group(hall, g)[...])

        def body(cols):
            gate = contract(rows, wi[0, :, cols], 1, 0)
            up = contract(rows, wi[1, :, cols], 1, 0)
            square = gate * gate
            turn = jnp.tanh(gate * (0.7978845608028654 + 0.035677408136300125 * square))
            upper = 0.5 + 0.5 * turn
            value = gate * upper
            slope = upper + 0.5 * gate * (1.0 - turn * turn) * (0.7978845608028654 + 0.10703222440890038 * square)
            shape = (2, half, up.shape[-1])
            group(hid, g)[:, :, cols] = (value * up).astype(BF16).reshape(shape)
            group(act.at[0], g)[:, :, cols] = (slope * up).astype(BF16).reshape(shape)
            group(act.at[1], g)[:, :, cols] = value.astype(BF16).reshape(shape)

        tiles(units, 384, body)

    def emit(g, cols, part):
        if g == 0:
            acc[:, :, cols] = part.reshape(2, half, -1)
        elif g == 1:
            sent[0, :, :, cols] = part.astype(BF16).reshape(2, half, -1)
        else:
            far[:, cols] = part[:half]
            sent[1, g - 2, :, cols] = part[half:].astype(BF16)

    def down(g):
        rows = flat(group(hid, g)[...])
        tiles(width, 512, lambda cols: emit(g, cols, contract(rows, wd[:, cols], 1, 0)))

    def push(phase, kind, j):
        return go(sent.at[kind, j], got.at[kind, j], p_send.at[phase, kind, j], p_recv.at[phase, kind, j], peer if kind == 2 else sib)

    def sums(phase, compute, copies, buffer, send, recv, before):
        kept = {}
        compute(0)
        for j in range(2):
            copies[j][1].wait_recv()
        compute(1)
        for j in range(2):
            kept[0, j] = push(phase, 0, j)
        for j in range(2):
            copies[j][0].wait_recv()
            passed = relay(buffer, send, recv, j)
            passed.wait_recv()
            compute(2 + j)
            kept[1, j] = push(phase, 1, j)
            kept[1, j].wait_recv()
            sent[2, j] = (far[...] + got[1, j].astype(F32)).astype(BF16)
            kept[2, j] = push(phase, 2, j)
        return kept

    def forward(g):
        gated(g)
        down(g)

    for one in loads[:3]:
        one.wait()
    kept = sums(0, forward, h_copies, hall, h_send, h_recv, None)
    first, pending = pending, []
    loads[3].wait()
    loads[4].wait()
    total = jnp.zeros((), F32)
    d_copies, saves = [], []
    factor = scale[0, 0]
    for j in range(2):
        kept[0, j].wait_recv()
        kept[2, j].wait_recv()
        step = half // 4

        def rows_of(i, so_far):
            r = pl.ds(pl.multiple_of(i * step, step), step)
            value = mid[j, r, :] + acc[j, r, :] + got[0, j, r, :].astype(F32) + got[2, j, r, :].astype(F32)
            out_low[j, r, :] = value.astype(BF16)
            diff = value - teacher[j, r, :].astype(F32)
            masked = valid[j, r, :] * diff
            grad = masked * factor
            mid[j, r, :] = grad
            dall[0, j, r, :] = grad.astype(BF16)
            return so_far + jnp.sum(masked * diff)

        total = lax.fori_loop(0, 4, rows_of, total)
        d_copies.append(spread(dall.at[0], dall, d_send, d_recv, j))
        saves.append(fetch(out_low.at[j], out.at[j], store.at[0, j]))
        saves.append(fetch(mid.at[j], cot.at[j], store.at[1, j]))
    squares[...] = jnp.full(squares.shape, total)

    def backward(g):
        rows = flat(group(dall, g)[...])

        def body(cols):
            grad = contract(rows, wd[cols, :], 1, 1).reshape(2, half, -1)
            for n in range(2):
                part = group(act.at[n], g)
                part[:, :, cols] = (grad * part[:, :, cols].astype(F32)).astype(BF16)

        tiles(units, 384, body)
        gate, up = flat(group(act.at[0], g)[...]), flat(group(act.at[1], g)[...])
        tiles(width, 512, lambda cols: emit(g, cols, contract(gate, wi[0, cols, :], 1, 1) + contract(up, wi[1, cols, :], 1, 1)))

    for copy in first:
        copy.wait_send()
    kept = sums(1, backward, d_copies, dall, d_send, d_recv, None)
    count = 0
    blocks = width // 256
    left, right = {}, {}

    def weight(left, right, target):
        def body(i, _):
            for n in range(2):
                at = pl.ds(pl.multiple_of(i * 512 + n * 256, 256), 256)

                @pl.when(i > 0)
                def _():
                    pltpu.make_async_copy(stage.at[n], target.at[at], g_store.at[n]).wait()

                stage[n] = contract(left(at), right(), 0, 0).astype(BF16)
                pltpu.make_async_copy(stage.at[n], target.at[at], g_store.at[n]).start()
            return 0

        lax.fori_loop(0, width // 512, body, 0)
        for n in range(2):
            pltpu.make_async_copy(stage.at[n], target.at[pl.ds(0, 256)], g_store.at[n]).wait()

    weight(lambda at: flat(dall[:, :, :, at].reshape(4, 2 * half, 256)), lambda: flat(hid[...].reshape(4, 2 * half, units)), gd)
    for n in range(2):
        weight(lambda at: flat(hall[:, :, :, at].reshape(4, 2 * half, 256)), lambda n=n: flat(act[n].reshape(4, 2 * half, units)), gi.at[n])
    for j in range(2):
        kept[0, j].wait_recv()
        kept[2, j].wait_recv()
        saves[2 * j + 1].wait()

        def sum_rows(i, _):
            r = pl.ds(pl.multiple_of(i * step, step), step)
            mid[j, r, :] = acc[j, r, :] + got[0, j, r, :].astype(F32) + got[2, j, r, :].astype(F32)
            return 0

        lax.fori_loop(0, 4, sum_rows, 0)
        saves.append(fetch(mid.at[j], dh.at[j], store.at[2, j]))
    for copy in pending:
        copy.wait_send()
    for n in (0, 2, 4, 5):
        saves[n].wait()


def ffn(h, wi, wd, mid, teacher, valid, scale):
    rows, width = h.shape
    units = wd.shape[0]
    half = rows // 2
    split = lambda a: a.reshape(2, half, a.shape[-1])
    dma = pltpu.SemaphoreType.DMA
    hbm, vm = pl.BlockSpec(memory_space=pl.ANY), pl.BlockSpec(memory_space=pltpu.VMEM)
    out, cot, dh, gd, gi, squares = pl.pallas_call(
        ffn_kernel,
        name="ffn",
        out_shape=[
            jax.ShapeDtypeStruct((2, half, width), BF16),
            jax.ShapeDtypeStruct((2, half, width), F32),
            jax.ShapeDtypeStruct((2, half, width), F32),
            jax.ShapeDtypeStruct((width, units), BF16),
            jax.ShapeDtypeStruct((2, width, units), BF16),
            jax.ShapeDtypeStruct((8, 128), F32),
        ],
        in_specs=[hbm] * 5 + [vm, pl.BlockSpec(memory_space=pltpu.SMEM)],
        out_specs=[hbm] * 5 + [vm],
        scratch_shapes=[
            pltpu.VMEM((2, width, units), BF16),
            pltpu.VMEM((units, width), BF16),
            pltpu.VMEM((2, half, width), F32),
            pltpu.VMEM((2, half, width), BF16),
            pltpu.VMEM((4, 2, half, width), BF16),
            pltpu.VMEM((4, 2, half, width), BF16),
            pltpu.VMEM((2, 4, 2, half, units), BF16),
            pltpu.VMEM((4, 2, half, units), BF16),
            pltpu.VMEM((2, half, width), F32),
            pltpu.VMEM((half, width), F32),
            pltpu.VMEM((2, half, width), BF16),
            pltpu.VMEM((3, 2, half, width), BF16),
            pltpu.VMEM((3, 2, half, width), BF16),
            pltpu.VMEM((2, 256, units), BF16),
            dma((5,)), dma((3, 2)), dma((3, 2)), dma((3, 2)), dma((3, 2)),
            dma((2, 3, 2)), dma((2, 3, 2)), dma((3, 2)), dma((2,)),
        ],
        compiler_params=pltpu.CompilerParams(collective_id=2, has_side_effects=True, vmem_limit_bytes=63 << 20),
    )(split(h), wi, wd, split(mid), split(teacher), split(valid), scale)
    return out.reshape(rows, width), cot.reshape(rows, width), dh.reshape(rows, width), gd, gi, squares

def pair_rows(block):
    return jnp.concatenate([block[:, :HD], block[:, HD:]], axis=0)


def pair_columns(block):
    rows = block.shape[0] // 2
    return jnp.concatenate([block[:rows], block[rows:]], axis=1)


def attend_kernel(q, kv, q_ids, k_ids, out, probs, bias):
    i, pair = pl.program_id(0), pl.program_id(1)
    reach = WINDOW + QROWS
    keys = pl.ds(pl.multiple_of(i * QROWS, QROWS), reach)

    @pl.when(pair == 0)
    def _():
        row = lax.broadcasted_iota(jnp.int32, (QROWS, reach), 0)
        offset = lax.broadcasted_iota(jnp.int32, (QROWS, reach), 1) - WINDOW - row
        allowed = (offset <= 0) & (offset > -WINDOW) & (q_ids[...] == k_ids[:, keys])
        bias[...] = jnp.where(allowed, 0.0, NEGATIVE)

    scores = contract(pair_rows(q[...]), kv[keys, :HD], 1, 1) * (math.log2(math.e) / math.sqrt(HD))
    shifted = scores.reshape(2, QROWS, reach) + bias[...][None]
    powers = jnp.exp2(shifted - jnp.max(shifted, axis=-1, keepdims=True))
    weights = (powers * (1.0 / jnp.sum(powers, axis=-1, keepdims=True))).astype(BF16)
    probs[0] = weights
    mixed = contract(weights.reshape(2 * QROWS, reach), kv[keys, HD:], 1, 0)
    out[...] = pair_columns(mixed).astype(BF16)


def attend(queries, width, extended, q_ids, k_ids):
    rows = queries.shape[0]
    blocks, pairs, reach = rows // QROWS, width // (2 * HD), WINDOW + QROWS
    return pl.pallas_call(
        attend_kernel,
        name="attend",
        grid=(blocks, pairs),
        out_shape=[
            jax.ShapeDtypeStruct((rows, width), BF16),
            jax.ShapeDtypeStruct((blocks, 2 * pairs, QROWS, reach), BF16),
        ],
        in_specs=[
            pl.BlockSpec((QROWS, 2 * HD), lambda i, p: (i, p)),
            pl.BlockSpec(extended.shape, lambda i, p: (0, 0)),
            pl.BlockSpec((QROWS, 1), lambda i, p: (i, 0)),
            pl.BlockSpec(k_ids.shape, lambda i, p: (0, 0)),
        ],
        out_specs=[
            pl.BlockSpec((QROWS, 2 * HD), lambda i, p: (i, p)),
            pl.BlockSpec((1, 2, QROWS, reach), lambda i, p: (i, p, 0, 0)),
        ],
        scratch_shapes=[pltpu.VMEM((QROWS, reach), F32)],
        compiler_params=pltpu.CompilerParams(vmem_limit_bytes=48 << 20),
    )(queries, extended, q_ids, k_ids)


def attend_back_kernel(q, kv, grad, mixed, probs, grad_q, grad_kv):
    i, pair = pl.program_id(0), pl.program_id(1)
    reach = WINDOW + QROWS
    keys = pl.ds(pl.multiple_of(i * QROWS, QROWS), reach)

    @pl.when((i == 0) & (pair == 0))
    def _():
        grad_kv[...] = jnp.zeros_like(grad_kv)

    queries, grads = pair_rows(q[...]), pair_rows(grad[...])
    weights = probs[0].reshape(2 * QROWS, reach)
    dots = jnp.sum(grads.astype(F32) * pair_rows(mixed[...]).astype(F32), axis=-1, keepdims=True)
    steep = contract(grads, kv[keys, HD:], 1, 1) - dots
    steep = (weights.astype(F32) * steep).astype(BF16)
    grad_q[...] = (pair_columns(contract(steep, kv[keys, :HD], 1, 0)) * (1.0 / math.sqrt(HD))).astype(BF16)
    grad_kv[keys, :HD] += contract(steep, queries, 0, 0)
    grad_kv[keys, HD:] += contract(weights, grads, 0, 0)


def attend_back(queries, extended, grad_mixed, mixed, probs):
    rows, width = mixed.shape
    blocks, pairs, reach = rows // QROWS, width // (2 * HD), WINDOW + QROWS
    block = pl.BlockSpec((QROWS, 2 * HD), lambda i, p: (i, p))
    whole = pl.BlockSpec(extended.shape, lambda i, p: (0, 0))
    return pl.pallas_call(
        attend_back_kernel,
        name="attend_back",
        grid=(blocks, pairs),
        out_shape=[jax.ShapeDtypeStruct((rows, width), BF16), jax.ShapeDtypeStruct(extended.shape, F32)],
        in_specs=[block, whole, block, block, pl.BlockSpec((1, 2, QROWS, reach), lambda i, p: (i, p, 0, 0))],
        out_specs=[block, whole],
        compiler_params=pltpu.CompilerParams(vmem_limit_bytes=48 << 20),
    )(queries, extended, grad_mixed, mixed, probs)


GRAD_COLS = 384
AHEAD = 3


class RowSum:
    def __init__(self, source, buffers, sems, where, go):
        self.source, self.go = source, go
        self.core, self.side, self.cross, self.along = buffers
        self.cs, self.cr, self.ys, self.yr, self.xs, self.xr, self.zs_, self.zr = sems
        self.x, self.y, self.c, self.zs, self.sib, self.ypeer, self.xpeer, self.zpeers = where
        self.depth, self.cols = len(self.zs), self.core.shape[-1]
        self.order = list(range(1, self.depth)) + [0]
        self.moved = {}

    def columns(self, y, c):
        return pl.ds(pl.multiple_of((2 * y + c) * self.cols, self.cols), self.cols)

    def first(self, d):
        for h in range(2):
            part = self.source.at[self.zs[d], :, :, self.columns(h, 1 - self.c)]
            self.moved["c", d, h] = self.go(part, self.core.at[d, h], self.cs.at[d, h], self.cr.at[d, h], self.sib)

    def second(self, d):
        for h in range(2):
            self.moved["c", d, h].wait_recv()
        far = 1 - self.y
        own = self.source[self.zs[d], :, :, self.columns(far, self.c)].astype(F32)
        self.core[d, far] = (own + self.core[d, far].astype(F32)).astype(BF16)
        self.moved["y", d] = self.go(self.core.at[d, far], self.side.at[d], self.ys.at[d], self.yr.at[d], self.ypeer)

    def kept(self, d, x):
        own = self.source[self.zs[d], x, :, self.columns(self.y, self.c)].astype(F32)
        return own + self.core[d, self.y, x].astype(F32) + self.side[d, x].astype(F32)

    def third(self, d):
        self.moved["y", d].wait_recv()
        self.side[d, 1 - self.x] = self.kept(d, 1 - self.x).astype(BF16)
        self.moved["x", d] = self.go(self.side.at[d, 1 - self.x], self.cross.at[d], self.xs.at[d], self.xr.at[d], self.xpeer)

    def fourth(self, d):
        self.moved["x", d].wait_recv()
        self.cross[d] = (self.kept(d, self.x) + self.cross[d].astype(F32)).astype(BF16)
        if d:
            self.moved["z", d] = self.go(
                self.cross.at[d], self.along.at[d - 1], self.zs_.at[d - 1], self.zr.at[d - 1], self.zpeers[d]
            )

    def total(self):
        value = self.cross[0].astype(F32)
        for d in range(1, self.depth):
            self.moved["z", d].wait_recv()
            value += self.along[d - 1].astype(F32)
        return value


def norm_back(values, grad, gain):
    r = lax.rsqrt(jnp.mean(values * values, axis=-1, keepdims=True) + EPSILON)
    scaled = grad * gain
    slope = r * r * r * jnp.mean(values * scaled, axis=-1, keepdims=True)
    return r * scaled - values * slope, jnp.sum(grad * values * r, axis=0, keepdims=True)


def finish_kernel(dh_hbm, cot_hbm, middle_hbm, w_out_hbm, w_attn_hbm, mixed_hbm, probs_hbm, qkv_hbm, ext_hbm, normed_hbm,
                  tokens_hbm, gd_hbm, gi_hbm, gain_attn, gain_ffn, squares,
                  grad_x, grad_d, grad_i, grad_qkv_out, grad_o, small_out,
                  dh, cot, middle, weight, mixed, probs, qkv, ext, normed, low, dmix, dkv, slabs, slabs_in,
                  gx, gz, own, staged, po, pa, ocore, oside, ocross, oalong, acore, aside, across, aalong, vb,
                  load, p_load, own_load, out_sem, slab_s, slab_r, gxs, gxr, gzs, gzr, o_sems, a_sems, vs, vr):
    z, x, y, c = places()
    depth, width = own.shape[1], own.shape[-1]
    rows, model_width = dh.shape
    units = gd_hbm.shape[-1]
    seq = 2 * depth
    me = 2 * z + x
    sib, ypeer, xpeer = device(z, x, y, 1 - c), device(z, x, 1 - y, c), device(z, 1 - x, y, c)
    zs = [lax.rem(z + d, depth) for d in range(depth)]
    zpeers = [device(zs[d], x, y, c) for d in range(depth)]
    wt = 2 * y + c
    diagonal = (lax.rem(me + seq - 1 + 2 * x, seq), wt)
    back = [(lax.rem(me + seq - step, seq), wt) for step in (1, 2)]

    def fetch(src, dst, sem):
        copy = pltpu.make_async_copy(src, dst, sem)
        copy.start()
        return copy

    loads = {}
    for n, (name, src, dst) in enumerate((
        ("dh", dh_hbm, dh), ("cot", cot_hbm, cot), ("w_out", w_out_hbm, weight.at[:, :model_width]), ("mixed", mixed_hbm, mixed),
        ("qkv", qkv_hbm, qkv), ("ext", ext_hbm, ext), ("normed", normed_hbm, normed))):
        loads[name] = fetch(src, dst, load.at[n])
    greet([sib, ypeer, xpeer, diagonal] + zpeers[1:])
    started = []

    def go(*args):
        started.append(remote(*args))
        return started[-1]

    spots = [(n, at) for n in range(3) for at in range(0, units, width)]
    chunks = len(spots)
    gxc, gzc, owned = {}, {}, {}

    def g_ref(k, side):
        n, at = spots[k]
        ref = gd_hbm if n == 0 else gi_hbm.at[n - 1]
        return ref.at[:, side, :, pl.ds(at, width)]

    def g_send(k):
        if k < chunks:
            gxc[k] = go(g_ref(k, 1 - x), gx.at[k], gxs.at[k], gxr.at[k], xpeer)

    def g_load(k):
        if k < chunks:
            owned[k] = fetch(g_ref(k, x), own.at[k % 2], own_load.at[k % 2])

    def g_step(k):
        gxc[k].wait_recv()
        g_send(k + AHEAD)
        owned[k].wait()
        for d in range(depth):
            gx[k, zs[d]] = (own[k % 2, zs[d]].astype(F32) + gx[k, zs[d]].astype(F32)).astype(BF16)
            if d:
                gzc[k, d] = go(gx.at[k, zs[d]], gz.at[k, d - 1], gzs.at[k, d - 1], gzr.at[k, d - 1], zpeers[d])
        g_load(k + 2)

    stores = {}

    def g_end(k):
        total = gx[k, z].astype(F32)
        for d in range(1, depth):
            gzc[k, d].wait_recv()
            total += gz[k, d - 1].astype(F32)
        if k >= 2:
            stores[k - 2].wait()
        staged[k % 2] = total
        n, at = spots[k]
        target = grad_d if n == 0 else grad_i.at[n - 1]
        stores[k] = fetch(staged.at[k % 2], target.at[:, pl.ds(at, width)], out_sem.at[k % 2])

    for k in range(AHEAD):
        g_send(k)
    g_load(0)
    g_load(1)
    where = (x, y, c, zs, sib, ypeer, xpeer, zpeers)
    sum_o = RowSum(po, (ocore, oside, ocross, oalong), o_sems, where, go)
    sum_a = RowSum(pa, (acore, aside, across, aalong), a_sems, where, go)

    step = middle.shape[1]
    steps = rows // step
    mids = [None] * steps

    def mid_load(n):
        if n < steps:
            mids[n] = fetch(middle_hbm.at[pl.ds(n * step, step)], middle.at[n % 2], load.at[8 + n % 2])

    mid_load(0)
    mid_load(1)
    loads["dh"].wait()
    loads["cot"].wait()
    gain_grad = jnp.zeros((1, model_width), F32)
    for n in range(steps):
        mids[n].wait()
        r = pl.ds(n * step, step)
        grad, part = norm_back(middle[n % 2], dh[r, :], gain_ffn[...])
        grad = cot[r, :] + grad
        cot[r, :] = grad
        low[r, :model_width] = grad.astype(BF16)
        gain_grad += part
        mid_load(n + 2)
    vb[0] = jnp.zeros(vb.shape[1:], F32)
    vb[0, 1:2] = gain_grad
    vb[0, 2:3] = jnp.broadcast_to(squares[0:1, 0:1], (1, model_width))
    loads["w_out"].wait()
    loads["mixed"].wait()
    rows_low = lambda: low[:, :model_width]

    def out_back(cols):
        dmix[:, cols] = contract(rows_low(), weight[cols, :model_width], 1, 1).astype(BF16)

    tiles(model_width, 512, out_back)
    loads["w_attn"] = fetch(w_attn_hbm, weight, load.at[7])

    def out_grad(d, _):
        cols = pl.ds(pl.multiple_of(d * 2 * po.shape[2], 128), 2 * po.shape[2])
        po[d] = contract(low[:, cols], mixed[...], 0, 0).astype(BF16).reshape(po.shape[1:])
        return 0

    lax.fori_loop(0, depth, out_grad, 0)
    for d in sum_o.order:
        sum_o.first(d)
    g_step(0)
    blocks, pairs, reach = probs_hbm.shape[0], probs_hbm.shape[1], probs.shape[-1]
    count = blocks * pairs

    def p_fetch(t):
        return pltpu.make_async_copy(probs_hbm.at[t // pairs, t % pairs], probs.at[t % 2], p_load.at[t % 2])

    p_fetch(0).start()
    p_fetch(1).start()
    dkv[...] = jnp.zeros_like(dkv)
    loads["qkv"].wait()
    loads["ext"].wait()
    for i in range(blocks):
        q_rows, keys = pl.ds(i * QROWS, QROWS), pl.ds(i * QROWS, reach)

        def one(pair, _):
            t = i * pairs + pair
            cols = pl.ds(pl.multiple_of(pair * 2 * HD, 2 * HD), 2 * HD)
            queries, grads = pair_rows(qkv[q_rows, cols]), pair_rows(dmix[q_rows, cols])
            outs = pair_rows(mixed[q_rows, cols])
            dots = jnp.sum(grads.astype(F32) * outs.astype(F32), axis=-1, keepdims=True)
            slot = lax.rem(t, 2)
            p_fetch(t).wait()
            weights = flat(probs[slot])
            steep = contract(grads, ext[keys, HD:], 1, 1) - dots
            steep = (weights.astype(F32) * steep).astype(BF16)
            low[q_rows, cols] = (pair_columns(contract(steep, ext[keys, :HD], 1, 0)) * (1.0 / math.sqrt(HD))).astype(BF16)
            dkv[keys, :HD] += contract(steep, queries, 0, 0)
            dkv[keys, HD:] += contract(weights, grads, 0, 0)

            @pl.when(t + 2 < count)
            def _():
                p_fetch(t + 2).start()

            return 0

        lax.fori_loop(0, pairs, one, 0)
        if i == 0:
            for d in sum_o.order:
                sum_o.second(d)
            g_step(1)
    for n in range(2):
        slabs[n] = dkv[(1 - n) * rows : (2 - n) * rows, :].astype(BF16)
    returned = [go(slabs.at[n], slabs_in.at[n], slab_s.at[n], slab_r.at[n], back[n]) for n in range(2)]
    loads["normed"].wait()
    slot_rows = model_width // seq

    def query_grad(d, _):
        cols = pl.ds(pl.multiple_of(d * 2 * slot_rows, 128), 2 * slot_rows)
        pa[d, :, :slot_rows] = contract(low[:, cols], normed[...], 0, 0).astype(BF16).reshape(2, slot_rows, model_width)
        return 0

    lax.fori_loop(0, depth, query_grad, 0)
    g_step(2)
    for one in returned:
        one.wait_recv()
    summed = dkv[2 * rows :, :] + slabs_in[0].astype(F32) + slabs_in[1].astype(F32)
    low[:, model_width : model_width + HD] = (summed[:, :HD] * (1.0 / math.sqrt(HD))).astype(BF16)
    low[:, model_width + HD :] = summed[:, HD:].astype(BF16)
    kv_grad = contract(low[:, model_width:], normed[...], 0, 0).astype(BF16)
    kv_rows = HD // seq
    for n in range(2):
        part = kv_grad[n * HD : (n + 1) * HD].reshape(depth, 2, kv_rows, model_width)
        pa[:, :, slot_rows + n * kv_rows : slot_rows + (n + 1) * kv_rows] = part
    for d in sum_a.order:
        sum_a.first(d)
    loads["tokens"] = fetch(tokens_hbm, mixed, load.at[3])
    loads["w_attn"].wait()

    def attn_back(cols):
        dh[:, cols] = contract(low[...], weight[cols, :], 1, 1)

    tiles(model_width, 512, attn_back)
    for d in sum_a.order:
        sum_a.second(d)
    g_step(3)
    loads["tokens"].wait()

    def last_norm(n, so_far):
        r = pl.ds(pl.multiple_of(n * step, step), step)
        grad, part = norm_back(mixed[r, :].astype(F32), dh[r, :], gain_attn[...])
        cot[r, :] += grad
        return so_far + part

    vb[0, 0:1] = lax.fori_loop(0, steps, last_norm, jnp.zeros((1, model_width), F32))
    saved = fetch(cot, grad_x, load.at[0])

    vc = {}

    def v_first():
        vc[0] = go(vb.at[0], vb.at[1], vs.at[0], vr.at[0], sib)

    def v_swap(n, to):
        vc[n - 1].wait_recv()
        vb[2 * n] = vb[2 * n - 2] + vb[2 * n - 1]
        vc[n] = go(vb.at[2 * n], vb.at[2 * n + 1], vs.at[n], vr.at[n], to)

    def v_along():
        vc[2].wait_recv()
        vb[6] = vb[4] + vb[5]
        for d in range(1, depth):
            vc[2 + d] = go(vb.at[6], vb.at[6 + d], vs.at[2 + d], vr.at[2 + d], zpeers[d])

    def v_end():
        for d in range(1, depth):
            vc[2 + d].wait_recv()
        total = vb[6 + z]
        for n in range(1, depth):
            total += vb[6 + lax.rem(z - n + depth, depth)]
        small_out[...] = total

    v_first()
    o, a = sum_o.order, sum_a.order
    g_end(0)
    for d in o:
        sum_o.third(d)
    v_swap(1, ypeer)
    g_step(4)
    g_end(1)
    for d in o:
        sum_o.fourth(d)
    v_swap(2, xpeer)
    g_step(5)
    g_end(2)
    sum_a.third(a[0])
    sum_a.third(a[1])
    v_along()
    g_step(6)
    g_end(3)
    sum_a.third(a[2])
    sum_a.third(a[3])
    sum_a.fourth(a[0])
    grad_o[...] = sum_o.total()
    g_step(7)
    g_end(4)
    for d in a[1:]:
        sum_a.fourth(d)
    v_end()
    for k in range(8, chunks):
        g_step(k)
        g_end(k - 3)
    g_end(chunks - 3)
    grad_qkv_out[...] = sum_a.total()
    g_end(chunks - 2)
    g_end(chunks - 1)
    for copy in started:
        copy.wait_send()
    saved.wait()
    stores[chunks - 2].wait()
    stores[chunks - 1].wait()


def finish(dh, cot, middle, w_out, w_attn, mixed, probs, qkv, ext, normed, tokens, gd, gi, gain_attn, gain_ffn, squares, seq):
    rows, model_width = dh.shape
    depth, slot, units = seq // 2, model_width // seq, gd.shape[-1]
    kv_rows, cols = 2 * HD // seq, model_width // 4
    blocks, heads, _, reach = probs.shape
    chunks = 3 * units // GRAD_COLS
    qkv_slot = slot + kv_rows
    step = 128
    dma = pltpu.SemaphoreType.DMA
    hbm, vm = pl.BlockSpec(memory_space=pl.ANY), pl.BlockSpec(memory_space=pltpu.VMEM)

    def sum_buffers(n):
        return [
            pltpu.VMEM((depth, 2, 2, n, cols), BF16),
            pltpu.VMEM((depth, 2, n, cols), BF16),
            pltpu.VMEM((depth, n, cols), BF16),
            pltpu.VMEM((depth - 1, n, cols), BF16),
        ]

    sum_sems = [dma((depth, 2)), dma((depth, 2)), dma((depth,)), dma((depth,)), dma((depth,)), dma((depth,)), dma((depth - 1,)), dma((depth - 1,))]

    def kernel(*refs):
        refs = list(refs)
        at = len(refs) - 18
        o_sems, a_sems = refs[at : at + 8], refs[at + 8 : at + 16]
        finish_kernel(*refs[:at], o_sems, a_sems, *refs[at + 16 :])

    return pl.pallas_call(
        kernel,
        name="finish",
        out_shape=[
            jax.ShapeDtypeStruct((rows, model_width), F32),
            jax.ShapeDtypeStruct((slot, units), F32),
            jax.ShapeDtypeStruct((2, slot, units), F32),
            jax.ShapeDtypeStruct((qkv_slot, cols), F32),
            jax.ShapeDtypeStruct((slot, cols), F32),
            jax.ShapeDtypeStruct((8, model_width), F32),
        ],
        in_specs=[hbm] * 13 + [vm] * 3,
        out_specs=[hbm] * 3 + [vm] * 3,
        scratch_shapes=[
            pltpu.VMEM((rows, model_width), F32),
            pltpu.VMEM((rows, model_width), F32),
            pltpu.VMEM((2, step, model_width), F32),
            pltpu.VMEM(w_attn.shape, BF16),
            pltpu.VMEM((rows, model_width), BF16),
            pltpu.VMEM((2, 2, QROWS, reach), BF16),
            pltpu.VMEM(qkv.shape, BF16),
            pltpu.VMEM(ext.shape, BF16),
            pltpu.VMEM((rows, model_width), BF16),
            pltpu.VMEM(qkv.shape, BF16),
            pltpu.VMEM((rows, model_width), BF16),
            pltpu.VMEM(ext.shape, F32),
            pltpu.VMEM((2, rows, 2 * HD), BF16),
            pltpu.VMEM((2, rows, 2 * HD), BF16),
            pltpu.VMEM((chunks, depth, slot, GRAD_COLS), BF16),
            pltpu.VMEM((chunks, depth - 1, slot, GRAD_COLS), BF16),
            pltpu.VMEM((2, depth, slot, GRAD_COLS), BF16),
            pltpu.VMEM((2, slot, GRAD_COLS), F32),
            pltpu.VMEM((depth, 2, slot, model_width), BF16),
            pltpu.VMEM((depth, 2, qkv_slot, model_width), BF16),
        ]
        + sum_buffers(slot)
        + sum_buffers(qkv_slot)
        + [pltpu.VMEM((6 + depth, 8, model_width), F32)]
        + [
            dma((10,)), dma((2,)), dma((2,)), dma((2,)), dma((2,)), dma((2,)),
            dma((chunks,)), dma((chunks,)), dma((chunks, depth - 1)), dma((chunks, depth - 1)),
        ]
        + sum_sems
        + sum_sems
        + [dma((2 + depth,)), dma((2 + depth,))],
        compiler_params=pltpu.CompilerParams(collective_id=1, has_side_effects=True, vmem_limit_bytes=63 << 20),
    )(
        dh, cot, middle, w_out, w_attn, mixed, probs.reshape(blocks, heads // 2, 2, QROWS, reach), qkv, ext, normed, tokens,
        gd.reshape(depth, 2, slot, units), gi.reshape(2, depth, 2, slot, units),
        gain_attn.reshape(1, -1), gain_ffn.reshape(1, -1), squares,
    )


def passed_along(block, axis, distance):
    devices = range(lax.axis_size(axis))
    route = [(i - distance, i) for i in devices if i - distance in devices]
    return lax.ppermute(block, axis, route)


def rms_scale(values, gain):
    return values * lax.rsqrt(jnp.mean(values * values, axis=-1, keepdims=True) + EPSILON) * gain


def stream_ids(positions, lengths, stream_len):
    seq_ends = jnp.cumsum(lengths)
    seq_starts = seq_ends - lengths
    inside = (positions >= 0) & (positions < seq_ends[-1])
    number = jnp.sum((positions[:, None] >= seq_starts[None, :]).astype(jnp.int32), axis=1) - 1
    return jnp.where(inside, number, -(positions + 2 * stream_len))


def per_device(tokens, teacher, seq_lengths, w_attn, w_out, w_in, w_down, gain_attn, gain_ffn):
    tok_rows = tokens.shape[1]
    model_width = tokens.shape[2]
    seq_devices = lax.axis_size("seq")
    seq_place = lax.axis_index("seq")
    stream_len = tok_rows * seq_devices
    all_slots = stream_len * lax.axis_size("wt")
    reach_count = (WINDOW + tok_rows - 1) // tok_rows
    edge_rows = reach_count * tok_rows
    inputs = tokens[0].astype(jnp.float32)
    positions = seq_place * tok_rows - edge_rows + jnp.arange(edge_rows + tok_rows, dtype=jnp.int32)
    seq_ids = stream_ids(positions, seq_lengths[0], stream_len)
    valid = (seq_ids[edge_rows:] >= 0).astype(jnp.float32)
    valid_total = lax.psum(jnp.sum(seq_lengths[0]).astype(jnp.float32), "wt")
    attn_full, out_full = (
        lax.all_gather(w_attn, "wt", axis=0, tiled=True),
        lax.all_gather(w_out, "wt", axis=0, tiled=True),
    )
    normed_f, norm_one_pull = jax.vjp(rms_scale, inputs, gain_attn)
    normed = normed_f.astype(jnp.bfloat16)
    qkv = jnp.dot(normed, attn_full, preferred_element_type=jnp.float32).astype(jnp.bfloat16)
    key_value = qkv[:, model_width:]
    earlier = [passed_along(key_value, "seq", back_step) for back_step in range(reach_count, 0, -1)]
    extended = jnp.concatenate(earlier + [key_value], axis=0)
    mixed_b, probs = attend(qkv, model_width, extended, seq_ids[edge_rows:, None], seq_ids[None, :])
    middle = inputs + jnp.dot(mixed_b, out_full, preferred_element_type=jnp.float32)
    normed_two_f, norm_two_pull = jax.vjp(rms_scale, middle, gain_ffn)
    normed_two = normed_two_f.astype(jnp.bfloat16)
    scale_up = (all_slots / valid_total).reshape(1, 1)
    w_pair = jnp.swapaxes(w_in, 0, 1)
    output, cotangent, grad_norm_two, grad_down, grad_in, squares = ffn(
        normed_two, w_pair, w_down, middle, teacher[0], valid[:, None], scale_up
    )
    slot, kv_slot = model_width // seq_devices, HD // seq_devices
    if slot % 16 == 0 and kv_slot % 16 == 0:
        grad_inputs, grad_down, grad_in, grad_attn, grad_out, small = finish(
            grad_norm_two, cotangent, middle, out_full, attn_full, mixed_b, probs, qkv, extended, normed, tokens[0],
            grad_down, grad_in, gain_attn, gain_ffn, squares, seq_devices,
        )
    else:
        grad_middle_norm, grad_gain_ffn = norm_two_pull(grad_norm_two)
        grad_middle = cotangent + grad_middle_norm
        grad_mid_low = grad_middle.astype(jnp.bfloat16)
        grad_out = jnp.einsum("te,td->ed", grad_mid_low, mixed_b, preferred_element_type=jnp.float32)
        grad_mixed = jnp.einsum("te,de->td", grad_mid_low, out_full, preferred_element_type=jnp.float32)
        grad_query, grad_ext = attend_back(qkv, extended, grad_mixed.astype(jnp.bfloat16), mixed_b, probs)
        grad_kv = grad_ext[edge_rows:]
        for back_step in range(1, reach_count + 1):
            slab_rows = grad_ext[
                edge_rows - back_step * tok_rows : edge_rows - (back_step - 1) * tok_rows
            ]
            grad_kv = grad_kv + passed_along(slab_rows, "seq", -back_step)
        grad_key = (grad_kv[:, :HD] * (1.0 / math.sqrt(HD))).astype(jnp.bfloat16)
        grad_qkv = jnp.concatenate([grad_query, grad_key, grad_kv[:, HD:].astype(jnp.bfloat16)], axis=1)
        grad_attn = jnp.einsum("te,td->ed", grad_qkv, normed, preferred_element_type=jnp.float32)
        grad_normed = jnp.einsum("te,de->td", grad_qkv, attn_full, preferred_element_type=jnp.float32)
        grad_input_norm, grad_gain_attn = norm_one_pull(grad_normed)
        grad_inputs = grad_middle + grad_input_norm
        grad_attn = grad_attn.astype(jnp.bfloat16)
        grad_key, grad_value = (
            grad_attn[model_width + at : model_width + at + HD].reshape(seq_devices, kv_slot, model_width) for at in (0, HD)
        )
        packed = jnp.concatenate(
            [
                grad_attn[:model_width].reshape(seq_devices, slot, model_width),
                grad_key,
                grad_value,
                grad_out.astype(jnp.bfloat16).reshape(seq_devices, slot, model_width),
            ],
            axis=1,
        )
        small = jnp.stack([grad_gain_attn, grad_gain_ffn, jnp.full((model_width,), squares[0, 0])] + [jnp.zeros_like(grad_gain_attn)] * 5)
        grad_down, grad_in = grad_down.reshape(seq_devices, slot, -1), grad_in.reshape(2, seq_devices, slot, -1)
        grad_down, grad_in, packed, small = reduce_plain(grad_down, grad_in, packed, small)
        grad_attn, grad_out = packed[:-slot], packed[-slot:]
    grad_queries = grad_attn[:slot].T
    grad_keyvals = grad_attn[slot:].T.reshape(-1, 2, kv_slot)
    grad_out = grad_out.T
    grad_down = grad_down.T
    grad_in = jnp.swapaxes(grad_in, 0, 1)
    gain_attn_all, gain_ffn_all, squares_all = small[0], small[1], small[2, 0]
    loss = squares_all / (valid_total * model_width)
    return (
        output[None],
        loss,
        grad_inputs[None],
        grad_queries,
        grad_keyvals,
        grad_out,
        grad_in,
        grad_down,
        gain_attn_all,
        gain_ffn_all,
    )


def solution(mesh):
    in_specs = (
        P("wt", "seq", None),
        P("wt", "seq", None),
        P("wt", None),
        P("wt", None),
        P("wt", None),
        P(None, None, "wt"),
        P("wt", None),
        P(),
        P(),
    )
    out_specs = (
        P("wt", "seq", None),
        P(),
        P("wt", "seq", None),
        P("wt", "seq"),
        P("wt", None, "seq"),
        P("wt", "seq"),
        P("seq", None, "wt"),
        P("wt", "seq"),
        P(),
        P(),
    )
    return jax.shard_map(
        per_device, mesh=mesh, in_specs=in_specs, out_specs=out_specs, check_vma=False
    )
```

```python
import math

import jax
import jax.numpy as jnp
from jax import lax
from jax.experimental import pallas as pl
from jax.experimental.pallas import tpu as pltpu
from jax.sharding import PartitionSpec as P

HEADS = 12
HD = 128
WINDOW = 1024
QROWS = 256


EPSILON = 1e-06
NEGATIVE = -1e30

MESH = pl.DeviceIdType.MESH
F32 = jnp.float32
BF16 = jnp.bfloat16


def places():
    seq, wt = lax.axis_index("seq"), lax.axis_index("wt")
    return seq // 2, seq % 2, wt // 2, wt % 2


def device(z, x, y, c):
    return (z * 2 + x, y * 2 + c)


def remote(src, dst, send, recv, to):
    copy = pltpu.make_async_remote_copy(
        src_ref=src, dst_ref=dst, send_sem=send, recv_sem=recv, device_id=to, device_id_type=MESH
    )
    copy.start()
    return copy


def greet(devices):
    barrier = pltpu.get_barrier_semaphore()
    for one in devices:
        pl.semaphore_signal(barrier, inc=1, device_id=one, device_id_type=MESH)
    pl.semaphore_wait(barrier, len(devices))


def reduce_plain(gd, gi, p, v):
    gd = lax.psum_scatter(gd, "seq", scatter_dimension=0, tiled=False).astype(F32)
    gi = lax.psum_scatter(gi, "seq", scatter_dimension=1, tiled=False).astype(F32)
    p = lax.psum_scatter(p, "seq", scatter_dimension=0, tiled=False)
    p = lax.psum_scatter(p, "wt", scatter_dimension=1, tiled=True).astype(F32)
    return gd, gi, p, lax.psum(v, ("seq", "wt"))


def contract(a, b, dim_a, dim_b):
    return lax.dot_general(a, b, (((dim_a,), (dim_b,)), ((), ())), preferred_element_type=F32)


def tiles(total, width, body):
    def step(i, _):
        body(pl.ds(pl.multiple_of(i * width, width), width))
        return 0

    lax.fori_loop(0, total // width, step, 0)


def flat(block):
    return block.reshape(-1, block.shape[-1])


def ffn_kernel(h, wi_hbm, wd_hbm, mid_hbm, teacher_hbm, valid, scale, out, cot, dh, gd, gi, squares,
               wi, wd, mid, teacher, hall, dall, act, hid, acc, far, out_low, sent, got, stage,
               load, h_send, h_recv, d_send, d_recv, p_send, p_recv, store, g_store):
    seq, wt = lax.axis_index("seq"), lax.axis_index("wt")
    y, c = wt // 2, wt % 2
    sib, peer = (seq, y * 2 + 1 - c), (seq, (1 - y) * 2 + c)
    half, width = h.shape[1:]
    units = wd.shape[0]

    def fetch(src, dst, sem):
        copy = pltpu.make_async_copy(src, dst, sem)
        copy.start()
        return copy

    loads = [fetch(*pair, load.at[n]) for n, pair in enumerate(
        ((h, hall.at[0]), (wi_hbm, wi), (wd_hbm, wd), (mid_hbm, mid), (teacher_hbm, teacher)))]
    greet([sib, peer])
    pending = []

    def go(*args):
        nonlocal pending
        pending.append(remote(*args))
        return pending[-1]

    def spread(src, dst, send, recv, j):
        a = go(src.at[j], dst.at[2, j], send.at[0, j], recv.at[0, j], peer)
        b = go(src.at[j], dst.at[1, j], send.at[1, j], recv.at[1, j], sib)
        return a, b

    def relay(dst, send, recv, j):
        return go(dst.at[2, j], dst.at[3, j], send.at[2, j], recv.at[2, j], sib)

    def group(ref, g):
        return ref.at[2:4, g - 2] if g >= 2 else ref.at[g]

    h_copies = [spread(h, hall, h_send, h_recv, j) for j in range(2)]

    def gated(g):
        rows = flat(group(hall, g)[...])

        def body(cols):
            gate = contract(rows, wi[0, :, cols], 1, 0)
            up = contract(rows, wi[1, :, cols], 1, 0)
            square = gate * gate
            turn = jnp.tanh(gate * (0.7978845608028654 + 0.035677408136300125 * square))
            upper = 0.5 + 0.5 * turn
            value = gate * upper
            slope = upper + 0.5 * gate * (1.0 - turn * turn) * (0.7978845608028654 + 0.10703222440890038 * square)
            shape = (2, half, up.shape[-1])
            group(hid, g)[:, :, cols] = (value * up).astype(BF16).reshape(shape)
            group(act.at[0], g)[:, :, cols] = (slope * up).astype(BF16).reshape(shape)
            group(act.at[1], g)[:, :, cols] = value.astype(BF16).reshape(shape)

        tiles(units, 384, body)

    def emit(g, cols, part):
        if g == 0:
            acc[:, :, cols] = part.reshape(2, half, -1)
        elif g == 1:
            sent[0, :, :, cols] = part.astype(BF16).reshape(2, half, -1)
        else:
            far[:, cols] = part[:half]
            sent[1, g - 2, :, cols] = part[half:].astype(BF16)

    def down(g):
        rows = flat(group(hid, g)[...])
        tiles(width, 512, lambda cols: emit(g, cols, contract(rows, wd[:, cols], 1, 0)))

    def push(phase, kind, j):
        return go(sent.at[kind, j], got.at[kind, j], p_send.at[phase, kind, j], p_recv.at[phase, kind, j], peer if kind == 2 else sib)

    def sums(phase, compute, copies, buffer, send, recv, before):
        kept = {}
        compute(0)
        for j in range(2):
            copies[j][1].wait_recv()
        compute(1)
        for j in range(2):
            kept[0, j] = push(phase, 0, j)
        for j in range(2):
            copies[j][0].wait_recv()
            passed = relay(buffer, send, recv, j)
            passed.wait_recv()
            compute(2 + j)
            kept[1, j] = push(phase, 1, j)
            kept[1, j].wait_recv()
            sent[2, j] = (far[...] + got[1, j].astype(F32)).astype(BF16)
            kept[2, j] = push(phase, 2, j)
        return kept

    def forward(g):
        gated(g)
        down(g)

    for one in loads[:3]:
        one.wait()
    kept = sums(0, forward, h_copies, hall, h_send, h_recv, None)
    first, pending = pending, []
    loads[3].wait()
    loads[4].wait()
    total = jnp.zeros((), F32)
    d_copies, saves = [], []
    factor = scale[0, 0]
    for j in range(2):
        kept[0, j].wait_recv()
        kept[2, j].wait_recv()
        step = half // 4

        def rows_of(i, so_far):
            r = pl.ds(pl.multiple_of(i * step, step), step)
            value = mid[j, r, :] + acc[j, r, :] + got[0, j, r, :].astype(F32) + got[2, j, r, :].astype(F32)
            out_low[j, r, :] = value.astype(BF16)
            diff = value - teacher[j, r, :].astype(F32)
            masked = valid[j, r, :] * diff
            grad = masked * factor
            mid[j, r, :] = grad
            dall[0, j, r, :] = grad.astype(BF16)
            return so_far + jnp.sum(masked * diff)

        total = lax.fori_loop(0, 4, rows_of, total)
        d_copies.append(spread(dall.at[0], dall, d_send, d_recv, j))
        saves.append(fetch(out_low.at[j], out.at[j], store.at[0, j]))
        saves.append(fetch(mid.at[j], cot.at[j], store.at[1, j]))
    squares[...] = jnp.full(squares.shape, total)

    def backward(g):
        rows = flat(group(dall, g)[...])

        def body(cols):
            grad = contract(rows, wd[cols, :], 1, 1).reshape(2, half, -1)
            for n in range(2):
                part = group(act.at[n], g)
                part[:, :, cols] = (grad * part[:, :, cols].astype(F32)).astype(BF16)

        tiles(units, 384, body)
        gate, up = flat(group(act.at[0], g)[...]), flat(group(act.at[1], g)[...])
        tiles(width, 512, lambda cols: emit(g, cols, contract(gate, wi[0, cols, :], 1, 1) + contract(up, wi[1, cols, :], 1, 1)))

    for copy in first:
        copy.wait_send()
    kept = sums(1, backward, d_copies, dall, d_send, d_recv, None)
    count = 0
    blocks = width // 256
    left, right = {}, {}

    def weight(left, right, target):
        def body(i, _):
            for n in range(2):
                at = pl.ds(pl.multiple_of(i * 512 + n * 256, 256), 256)

                @pl.when(i > 0)
                def _():
                    pltpu.make_async_copy(stage.at[n], target.at[at], g_store.at[n]).wait()

                stage[n] = contract(left(at), right(), 0, 0).astype(BF16)
                pltpu.make_async_copy(stage.at[n], target.at[at], g_store.at[n]).start()
            return 0

        lax.fori_loop(0, width // 512, body, 0)
        for n in range(2):
            pltpu.make_async_copy(stage.at[n], target.at[pl.ds(0, 256)], g_store.at[n]).wait()

    weight(lambda at: flat(dall[:, :, :, at].reshape(4, 2 * half, 256)), lambda: flat(hid[...].reshape(4, 2 * half, units)), gd)
    for n in range(2):
        weight(lambda at: flat(hall[:, :, :, at].reshape(4, 2 * half, 256)), lambda n=n: flat(act[n].reshape(4, 2 * half, units)), gi.at[n])
    for j in range(2):
        kept[0, j].wait_recv()
        kept[2, j].wait_recv()
        saves[2 * j + 1].wait()

        def sum_rows(i, _):
            r = pl.ds(pl.multiple_of(i * step, step), step)
            mid[j, r, :] = acc[j, r, :] + got[0, j, r, :].astype(F32) + got[2, j, r, :].astype(F32)
            return 0

        lax.fori_loop(0, 4, sum_rows, 0)
        saves.append(fetch(mid.at[j], dh.at[j], store.at[2, j]))
    for copy in pending:
        copy.wait_send()
    for n in (0, 2, 4, 5):
        saves[n].wait()


def ffn(h, wi, wd, mid, teacher, valid, scale):
    rows, width = h.shape
    units = wd.shape[0]
    half = rows // 2
    split = lambda a: a.reshape(2, half, a.shape[-1])
    dma = pltpu.SemaphoreType.DMA
    hbm, vm = pl.BlockSpec(memory_space=pl.ANY), pl.BlockSpec(memory_space=pltpu.VMEM)
    out, cot, dh, gd, gi, squares = pl.pallas_call(
        ffn_kernel,
        name="ffn",
        out_shape=[
            jax.ShapeDtypeStruct((2, half, width), BF16),
            jax.ShapeDtypeStruct((2, half, width), F32),
            jax.ShapeDtypeStruct((2, half, width), F32),
            jax.ShapeDtypeStruct((width, units), BF16),
            jax.ShapeDtypeStruct((2, width, units), BF16),
            jax.ShapeDtypeStruct((8, 128), F32),
        ],
        in_specs=[hbm] * 5 + [vm, pl.BlockSpec(memory_space=pltpu.SMEM)],
        out_specs=[hbm] * 5 + [vm],
        scratch_shapes=[
            pltpu.VMEM((2, width, units), BF16),
            pltpu.VMEM((units, width), BF16),
            pltpu.VMEM((2, half, width), F32),
            pltpu.VMEM((2, half, width), BF16),
            pltpu.VMEM((4, 2, half, width), BF16),
            pltpu.VMEM((4, 2, half, width), BF16),
            pltpu.VMEM((2, 4, 2, half, units), BF16),
            pltpu.VMEM((4, 2, half, units), BF16),
            pltpu.VMEM((2, half, width), F32),
            pltpu.VMEM((half, width), F32),
            pltpu.VMEM((2, half, width), BF16),
            pltpu.VMEM((3, 2, half, width), BF16),
            pltpu.VMEM((3, 2, half, width), BF16),
            pltpu.VMEM((2, 256, units), BF16),
            dma((5,)), dma((3, 2)), dma((3, 2)), dma((3, 2)), dma((3, 2)),
            dma((2, 3, 2)), dma((2, 3, 2)), dma((3, 2)), dma((2,)),
        ],
        compiler_params=pltpu.CompilerParams(collective_id=2, has_side_effects=True, vmem_limit_bytes=63 << 20),
    )(split(h), wi, wd, split(mid), split(teacher), split(valid), scale)
    return out.reshape(rows, width), cot.reshape(rows, width), dh.reshape(rows, width), gd, gi, squares

def pair_rows(block):
    return jnp.concatenate([block[:, :HD], block[:, HD:]], axis=0)


def pair_columns(block):
    rows = block.shape[0] // 2
    return jnp.concatenate([block[:rows], block[rows:]], axis=1)


def attend_back_kernel(q, kv, grad, mixed, probs, grad_q, grad_kv):
    i, pair = pl.program_id(0), pl.program_id(1)
    reach = WINDOW + QROWS
    keys = pl.ds(pl.multiple_of(i * QROWS, QROWS), reach)

    @pl.when((i == 0) & (pair == 0))
    def _():
        grad_kv[...] = jnp.zeros_like(grad_kv)

    queries, grads = pair_rows(q[...]), pair_rows(grad[...])
    weights = probs[0, 0].reshape(2 * QROWS, reach)
    dots = jnp.sum(grads.astype(F32) * pair_rows(mixed[...]).astype(F32), axis=-1, keepdims=True)
    steep = contract(grads, kv[keys, HD:], 1, 1) - dots
    steep = (weights.astype(F32) * steep).astype(BF16)
    grad_q[...] = (pair_columns(contract(steep, kv[keys, :HD], 1, 0)) * (1.0 / math.sqrt(HD))).astype(BF16)
    grad_kv[keys, :HD] += contract(steep, queries, 0, 0)
    grad_kv[keys, HD:] += contract(weights, grads, 0, 0)


def attend_back(queries, extended, grad_mixed, mixed, probs):
    rows, width = mixed.shape
    blocks, pairs, reach = rows // QROWS, width // (2 * HD), WINDOW + QROWS
    block = pl.BlockSpec((QROWS, 2 * HD), lambda i, p: (i, p))
    whole = pl.BlockSpec(extended.shape, lambda i, p: (0, 0))
    return pl.pallas_call(
        attend_back_kernel,
        name="attend_back",
        grid=(blocks, pairs),
        out_shape=[jax.ShapeDtypeStruct((rows, width), BF16), jax.ShapeDtypeStruct(extended.shape, F32)],
        in_specs=[block, whole, block, block, pl.BlockSpec((1, 1, 2, QROWS, reach), lambda i, p: (i, p, 0, 0, 0))],
        out_specs=[block, whole],
        compiler_params=pltpu.CompilerParams(vmem_limit_bytes=48 << 20),
    )(queries, extended, grad_mixed, mixed, probs)


GRAD_COLS = 384
AHEAD = 3


class RowSum:
    def __init__(self, source, buffers, sems, where, go):
        self.source, self.go = source, go
        self.core, self.side, self.cross, self.along = buffers
        self.cs, self.cr, self.ys, self.yr, self.xs, self.xr, self.zs_, self.zr = sems
        self.x, self.y, self.c, self.zs, self.sib, self.ypeer, self.xpeer, self.zpeers = where
        self.depth, self.cols = len(self.zs), self.core.shape[-1]
        self.order = list(range(1, self.depth)) + [0]
        self.moved = {}

    def columns(self, y, c):
        return pl.ds(pl.multiple_of((2 * y + c) * self.cols, self.cols), self.cols)

    def first(self, d):
        for h in range(2):
            part = self.source.at[self.zs[d], :, :, self.columns(h, 1 - self.c)]
            self.moved["c", d, h] = self.go(part, self.core.at[d, h], self.cs.at[d, h], self.cr.at[d, h], self.sib)

    def second(self, d):
        for h in range(2):
            self.moved["c", d, h].wait_recv()
        far = 1 - self.y
        own = self.source[self.zs[d], :, :, self.columns(far, self.c)].astype(F32)
        self.core[d, far] = (own + self.core[d, far].astype(F32)).astype(BF16)
        self.moved["y", d] = self.go(self.core.at[d, far], self.side.at[d], self.ys.at[d], self.yr.at[d], self.ypeer)

    def kept(self, d, x):
        own = self.source[self.zs[d], x, :, self.columns(self.y, self.c)].astype(F32)
        return own + self.core[d, self.y, x].astype(F32) + self.side[d, x].astype(F32)

    def third(self, d):
        self.moved["y", d].wait_recv()
        self.side[d, 1 - self.x] = self.kept(d, 1 - self.x).astype(BF16)
        self.moved["x", d] = self.go(self.side.at[d, 1 - self.x], self.cross.at[d], self.xs.at[d], self.xr.at[d], self.xpeer)

    def fourth(self, d):
        self.moved["x", d].wait_recv()
        self.cross[d] = (self.kept(d, self.x) + self.cross[d].astype(F32)).astype(BF16)
        if d:
            self.moved["z", d] = self.go(
                self.cross.at[d], self.along.at[d - 1], self.zs_.at[d - 1], self.zr.at[d - 1], self.zpeers[d]
            )

    def total(self):
        value = self.cross[0].astype(F32)
        for d in range(1, self.depth):
            self.moved["z", d].wait_recv()
            value += self.along[d - 1].astype(F32)
        return value


def norm_back(values, grad, gain):
    r = lax.rsqrt(jnp.mean(values * values, axis=-1, keepdims=True) + EPSILON)
    scaled = grad * gain
    slope = r * r * r * jnp.mean(values * scaled, axis=-1, keepdims=True)
    return r * scaled - values * slope, jnp.sum(grad * values * r, axis=0, keepdims=True)


def finish_kernel(dh_hbm, cot_hbm, middle_hbm, w_out_hbm, w_attn_hbm, mixed_hbm, probs_hbm, qkv_hbm, ext_hbm, normed_hbm,
                  tokens_hbm, gd_hbm, gi_hbm, gain_attn, gain_ffn, squares,
                  grad_x, grad_d, grad_i, grad_qkv_out, grad_o, small_out,
                  dh, cot, middle, weight, mixed, probs, qkv, ext, normed, low, dmix, dkv, slabs, slabs_in,
                  gx, gz, own, staged, po, pa, ocore, oside, ocross, oalong, acore, aside, across, aalong, vb,
                  load, p_load, own_load, out_sem, slab_s, slab_r, gxs, gxr, gzs, gzr, o_sems, a_sems, vs, vr):
    z, x, y, c = places()
    depth, width = own.shape[1], own.shape[-1]
    rows, model_width = dh.shape
    units = gd_hbm.shape[-1]
    seq = 2 * depth
    me = 2 * z + x
    sib, ypeer, xpeer = device(z, x, y, 1 - c), device(z, x, 1 - y, c), device(z, 1 - x, y, c)
    zs = [lax.rem(z + d, depth) for d in range(depth)]
    zpeers = [device(zs[d], x, y, c) for d in range(depth)]
    wt = 2 * y + c
    diagonal = (lax.rem(me + seq - 1 + 2 * x, seq), wt)
    back = [(lax.rem(me + seq - step, seq), wt) for step in (1, 2)]

    def fetch(src, dst, sem):
        copy = pltpu.make_async_copy(src, dst, sem)
        copy.start()
        return copy

    loads = {}
    for n, (name, src, dst) in enumerate((
        ("dh", dh_hbm, dh), ("cot", cot_hbm, cot), ("w_out", w_out_hbm, weight.at[:, :model_width]), ("mixed", mixed_hbm, mixed),
        ("qkv", qkv_hbm, qkv), ("ext", ext_hbm, ext), ("normed", normed_hbm, normed))):
        loads[name] = fetch(src, dst, load.at[n])
    greet([sib, ypeer, xpeer, diagonal] + zpeers[1:])
    started = []

    def go(*args):
        started.append(remote(*args))
        return started[-1]

    spots = [(n, at) for n in range(3) for at in range(0, units, width)]
    chunks = len(spots)
    gxc, gzc, owned = {}, {}, {}

    def g_ref(k, side):
        n, at = spots[k]
        ref = gd_hbm if n == 0 else gi_hbm.at[n - 1]
        return ref.at[:, side, :, pl.ds(at, width)]

    def g_send(k):
        if k < chunks:
            gxc[k] = go(g_ref(k, 1 - x), gx.at[k], gxs.at[k], gxr.at[k], xpeer)

    def g_load(k):
        if k < chunks:
            owned[k] = fetch(g_ref(k, x), own.at[k % 2], own_load.at[k % 2])

    def g_step(k):
        gxc[k].wait_recv()
        g_send(k + AHEAD)
        owned[k].wait()
        for d in range(depth):
            gx[k, zs[d]] = (own[k % 2, zs[d]].astype(F32) + gx[k, zs[d]].astype(F32)).astype(BF16)
            if d:
                gzc[k, d] = go(gx.at[k, zs[d]], gz.at[k, d - 1], gzs.at[k, d - 1], gzr.at[k, d - 1], zpeers[d])
        g_load(k + 2)

    stores = {}

    def g_end(k):
        total = gx[k, z].astype(F32)
        for d in range(1, depth):
            gzc[k, d].wait_recv()
            total += gz[k, d - 1].astype(F32)
        if k >= 2:
            stores[k - 2].wait()
        staged[k % 2] = total
        n, at = spots[k]
        target = grad_d if n == 0 else grad_i.at[n - 1]
        stores[k] = fetch(staged.at[k % 2], target.at[:, pl.ds(at, width)], out_sem.at[k % 2])

    for k in range(AHEAD):
        g_send(k)
    g_load(0)
    g_load(1)
    where = (x, y, c, zs, sib, ypeer, xpeer, zpeers)
    sum_o = RowSum(po, (ocore, oside, ocross, oalong), o_sems, where, go)
    sum_a = RowSum(pa, (acore, aside, across, aalong), a_sems, where, go)

    step = middle.shape[1]
    steps = rows // step
    mids = [None] * steps

    def mid_load(n):
        if n < steps:
            mids[n] = fetch(middle_hbm.at[pl.ds(n * step, step)], middle.at[n % 2], load.at[8 + n % 2])

    mid_load(0)
    mid_load(1)
    loads["dh"].wait()
    loads["cot"].wait()
    gain_grad = jnp.zeros((1, model_width), F32)
    for n in range(steps):
        mids[n].wait()
        r = pl.ds(n * step, step)
        grad, part = norm_back(middle[n % 2], dh[r, :], gain_ffn[...])
        grad = cot[r, :] + grad
        cot[r, :] = grad
        low[r, :model_width] = grad.astype(BF16)
        gain_grad += part
        mid_load(n + 2)
    vb[0] = jnp.zeros(vb.shape[1:], F32)
    vb[0, 1:2] = gain_grad
    vb[0, 2:3] = jnp.broadcast_to(squares[0:1, 0:1], (1, model_width))
    loads["w_out"].wait()
    loads["mixed"].wait()
    rows_low = lambda: low[:, :model_width]

    def out_back(cols):
        dmix[:, cols] = contract(rows_low(), weight[cols, :model_width], 1, 1).astype(BF16)

    tiles(model_width, 512, out_back)
    loads["w_attn"] = fetch(w_attn_hbm, weight, load.at[7])

    def out_grad(d, _):
        cols = pl.ds(pl.multiple_of(d * 2 * po.shape[2], 128), 2 * po.shape[2])
        po[d] = contract(low[:, cols], mixed[...], 0, 0).astype(BF16).reshape(po.shape[1:])
        return 0

    lax.fori_loop(0, depth, out_grad, 0)
    for d in sum_o.order:
        sum_o.first(d)
    g_step(0)
    blocks, pairs, reach = probs_hbm.shape[0], probs_hbm.shape[1], probs.shape[-1]
    count = blocks * pairs

    def p_fetch(t):
        return pltpu.make_async_copy(probs_hbm.at[t // pairs, t % pairs], probs.at[t % 2], p_load.at[t % 2])

    p_fetch(0).start()
    p_fetch(1).start()
    dkv[...] = jnp.zeros_like(dkv)
    loads["qkv"].wait()
    loads["ext"].wait()
    for i in range(blocks):
        q_rows, keys = pl.ds(i * QROWS, QROWS), pl.ds(i * QROWS, reach)

        def one(pair, _):
            t = i * pairs + pair
            cols = pl.ds(pl.multiple_of(pair * 2 * HD, 2 * HD), 2 * HD)
            queries, grads = pair_rows(qkv[q_rows, cols]), pair_rows(dmix[q_rows, cols])
            outs = pair_rows(mixed[q_rows, cols])
            dots = jnp.sum(grads.astype(F32) * outs.astype(F32), axis=-1, keepdims=True)
            slot = lax.rem(t, 2)
            p_fetch(t).wait()
            weights = flat(probs[slot])
            steep = contract(grads, ext[keys, HD:], 1, 1) - dots
            steep = (weights.astype(F32) * steep).astype(BF16)
            low[q_rows, cols] = (pair_columns(contract(steep, ext[keys, :HD], 1, 0)) * (1.0 / math.sqrt(HD))).astype(BF16)
            dkv[keys, :HD] += contract(steep, queries, 0, 0)
            dkv[keys, HD:] += contract(weights, grads, 0, 0)

            @pl.when(t + 2 < count)
            def _():
                p_fetch(t + 2).start()

            return 0

        lax.fori_loop(0, pairs, one, 0)
        if i == 0:
            for d in sum_o.order:
                sum_o.second(d)
            g_step(1)
    for n in range(2):
        slabs[n] = dkv[(1 - n) * rows : (2 - n) * rows, :].astype(BF16)
    returned = [go(slabs.at[n], slabs_in.at[n], slab_s.at[n], slab_r.at[n], back[n]) for n in range(2)]
    loads["normed"].wait()
    slot_rows = model_width // seq

    def query_grad(d, _):
        cols = pl.ds(pl.multiple_of(d * 2 * slot_rows, 128), 2 * slot_rows)
        pa[d, :, :slot_rows] = contract(low[:, cols], normed[...], 0, 0).astype(BF16).reshape(2, slot_rows, model_width)
        return 0

    lax.fori_loop(0, depth, query_grad, 0)
    g_step(2)
    for one in returned:
        one.wait_recv()
    summed = dkv[2 * rows :, :] + slabs_in[0].astype(F32) + slabs_in[1].astype(F32)
    low[:, model_width : model_width + HD] = (summed[:, :HD] * (1.0 / math.sqrt(HD))).astype(BF16)
    low[:, model_width + HD :] = summed[:, HD:].astype(BF16)
    kv_grad = contract(low[:, model_width:], normed[...], 0, 0).astype(BF16)
    kv_rows = HD // seq
    for n in range(2):
        part = kv_grad[n * HD : (n + 1) * HD].reshape(depth, 2, kv_rows, model_width)
        pa[:, :, slot_rows + n * kv_rows : slot_rows + (n + 1) * kv_rows] = part
    for d in sum_a.order:
        sum_a.first(d)
    loads["tokens"] = fetch(tokens_hbm, mixed, load.at[3])
    loads["w_attn"].wait()

    def attn_back(cols):
        dh[:, cols] = contract(low[...], weight[cols, :], 1, 1)

    tiles(model_width, 512, attn_back)
    for d in sum_a.order:
        sum_a.second(d)
    g_step(3)
    loads["tokens"].wait()

    def last_norm(n, so_far):
        r = pl.ds(pl.multiple_of(n * step, step), step)
        grad, part = norm_back(mixed[r, :].astype(F32), dh[r, :], gain_attn[...])
        cot[r, :] += grad
        return so_far + part

    vb[0, 0:1] = lax.fori_loop(0, steps, last_norm, jnp.zeros((1, model_width), F32))
    saved = fetch(cot, grad_x, load.at[0])

    vc = {}

    def v_first():
        vc[0] = go(vb.at[0], vb.at[1], vs.at[0], vr.at[0], sib)

    def v_swap(n, to):
        vc[n - 1].wait_recv()
        vb[2 * n] = vb[2 * n - 2] + vb[2 * n - 1]
        vc[n] = go(vb.at[2 * n], vb.at[2 * n + 1], vs.at[n], vr.at[n], to)

    def v_along():
        vc[2].wait_recv()
        vb[6] = vb[4] + vb[5]
        for d in range(1, depth):
            vc[2 + d] = go(vb.at[6], vb.at[6 + d], vs.at[2 + d], vr.at[2 + d], zpeers[d])

    def v_end():
        for d in range(1, depth):
            vc[2 + d].wait_recv()
        total = vb[6 + z]
        for n in range(1, depth):
            total += vb[6 + lax.rem(z - n + depth, depth)]
        small_out[...] = total

    v_first()
    o, a = sum_o.order, sum_a.order
    g_end(0)
    for d in o:
        sum_o.third(d)
    v_swap(1, ypeer)
    g_step(4)
    g_end(1)
    for d in o:
        sum_o.fourth(d)
    v_swap(2, xpeer)
    g_step(5)
    g_end(2)
    sum_a.third(a[0])
    sum_a.third(a[1])
    v_along()
    g_step(6)
    g_end(3)
    sum_a.third(a[2])
    sum_a.third(a[3])
    sum_a.fourth(a[0])
    grad_o[...] = sum_o.total()
    g_step(7)
    g_end(4)
    for d in a[1:]:
        sum_a.fourth(d)
    v_end()
    for k in range(8, chunks):
        g_step(k)
        g_end(k - 3)
    g_end(chunks - 3)
    grad_qkv_out[...] = sum_a.total()
    g_end(chunks - 2)
    g_end(chunks - 1)
    for copy in started:
        copy.wait_send()
    saved.wait()
    stores[chunks - 2].wait()
    stores[chunks - 1].wait()


def finish(dh, cot, middle, w_out, w_attn, mixed, probs, qkv, ext, normed, tokens, gd, gi, gain_attn, gain_ffn, squares, seq):
    rows, model_width = dh.shape
    depth, slot, units = seq // 2, model_width // seq, gd.shape[-1]
    kv_rows, cols = 2 * HD // seq, model_width // 4
    blocks, _, _, _, reach = probs.shape
    chunks = 3 * units // GRAD_COLS
    qkv_slot = slot + kv_rows
    step = 128
    dma = pltpu.SemaphoreType.DMA
    hbm, vm = pl.BlockSpec(memory_space=pl.ANY), pl.BlockSpec(memory_space=pltpu.VMEM)

    def sum_buffers(n):
        return [
            pltpu.VMEM((depth, 2, 2, n, cols), BF16),
            pltpu.VMEM((depth, 2, n, cols), BF16),
            pltpu.VMEM((depth, n, cols), BF16),
            pltpu.VMEM((depth - 1, n, cols), BF16),
        ]

    sum_sems = [dma((depth, 2)), dma((depth, 2)), dma((depth,)), dma((depth,)), dma((depth,)), dma((depth,)), dma((depth - 1,)), dma((depth - 1,))]

    def kernel(*refs):
        refs = list(refs)
        at = len(refs) - 18
        o_sems, a_sems = refs[at : at + 8], refs[at + 8 : at + 16]
        finish_kernel(*refs[:at], o_sems, a_sems, *refs[at + 16 :])

    return pl.pallas_call(
        kernel,
        name="finish",
        out_shape=[
            jax.ShapeDtypeStruct((rows, model_width), F32),
            jax.ShapeDtypeStruct((slot, units), F32),
            jax.ShapeDtypeStruct((2, slot, units), F32),
            jax.ShapeDtypeStruct((qkv_slot, cols), F32),
            jax.ShapeDtypeStruct((slot, cols), F32),
            jax.ShapeDtypeStruct((8, model_width), F32),
        ],
        in_specs=[hbm] * 13 + [vm] * 3,
        out_specs=[hbm] * 3 + [vm] * 3,
        scratch_shapes=[
            pltpu.VMEM((rows, model_width), F32),
            pltpu.VMEM((rows, model_width), F32),
            pltpu.VMEM((2, step, model_width), F32),
            pltpu.VMEM(w_attn.shape, BF16),
            pltpu.VMEM((rows, model_width), BF16),
            pltpu.VMEM((2, 2, QROWS, reach), BF16),
            pltpu.VMEM(qkv.shape, BF16),
            pltpu.VMEM(ext.shape, BF16),
            pltpu.VMEM((rows, model_width), BF16),
            pltpu.VMEM(qkv.shape, BF16),
            pltpu.VMEM((rows, model_width), BF16),
            pltpu.VMEM(ext.shape, F32),
            pltpu.VMEM((2, rows, 2 * HD), BF16),
            pltpu.VMEM((2, rows, 2 * HD), BF16),
            pltpu.VMEM((chunks, depth, slot, GRAD_COLS), BF16),
            pltpu.VMEM((chunks, depth - 1, slot, GRAD_COLS), BF16),
            pltpu.VMEM((2, depth, slot, GRAD_COLS), BF16),
            pltpu.VMEM((2, slot, GRAD_COLS), F32),
            pltpu.VMEM((depth, 2, slot, model_width), BF16),
            pltpu.VMEM((depth, 2, qkv_slot, model_width), BF16),
        ]
        + sum_buffers(slot)
        + sum_buffers(qkv_slot)
        + [pltpu.VMEM((6 + depth, 8, model_width), F32)]
        + [
            dma((10,)), dma((2,)), dma((2,)), dma((2,)), dma((2,)), dma((2,)),
            dma((chunks,)), dma((chunks,)), dma((chunks, depth - 1)), dma((chunks, depth - 1)),
        ]
        + sum_sems
        + sum_sems
        + [dma((2 + depth,)), dma((2 + depth,))],
        compiler_params=pltpu.CompilerParams(collective_id=1, has_side_effects=True, vmem_limit_bytes=63 << 20),
    )(
        dh, cot, middle, w_out, w_attn, mixed, probs, qkv, ext, normed, tokens,
        gd.reshape(depth, 2, slot, units), gi.reshape(2, depth, 2, slot, units),
        gain_attn.reshape(1, -1), gain_ffn.reshape(1, -1), squares,
    )


SHARERS = 8


def begin_kernel(lengths, tokens_hbm, w_attn_hbm, w_out_hbm, gain_attn, gain_ffn,
                 attn_out, out_out, qkv_out, ext_out, normed_out, mixed_out, probs_out, middle_out, low_out, valid_out, count_out,
                 tokens, normed, w_attn, w_out, qkv, ext, mixed, probs, bias, acc, counts,
                 load, c_send, c_recv, o_send, o_recv, s_send, s_recv, h_send, h_recv, n_send, n_recv, p_store, store):
    seq, wt = lax.axis_index("seq"), lax.axis_index("wt")
    n_seq = lax.axis_size("seq")
    y, c = wt // 2, wt % 2
    w_sib, w_peer, w_far = 2 * y + 1 - c, 2 * (1 - y) + c, 2 * (1 - y) + 1 - c
    sib, peer = (seq, w_sib), (seq, w_peer)
    rows, width = tokens.shape
    depth = w_attn_hbm.shape[0]
    pairs = width // (2 * HD)
    blocks, reach = rows // QROWS, WINDOW + QROWS
    slabs = WINDOW // rows
    first = seq // SHARERS * SHARERS
    place = lax.rem(seq, SHARERS)
    others = [(first + lax.rem(place + n, SHARERS), wt) for n in range(1, SHARERS)]
    ahead = [(lax.rem(seq + n, n_seq), wt) for n in range(1, slabs + 1)]
    behind = [(lax.rem(seq + n_seq - n, n_seq), wt) for n in range(1, slabs + 1)]

    def fetch(src, dst, sem):
        copy = pltpu.make_async_copy(src, dst, sem)
        copy.start()
        return copy

    def shard(w, size=None, at=0):
        return pl.ds(pl.multiple_of(w * depth + at, 16), depth if size is None else size)

    loads = [
        fetch(tokens_hbm, tokens, load.at[0]),
        fetch(w_attn_hbm, w_attn.at[shard(wt)], load.at[1]),
        fetch(w_out_hbm, w_out.at[shard(wt)], load.at[2]),
    ]
    greet([sib, peer] + others + (ahead + behind if n_seq > SHARERS else []))
    started = []

    def go(*args):
        started.append(remote(*args))
        return started[-1]

    def chunk(k):
        return pl.ds(pl.multiple_of(lax.rem(k + pairs, pairs + 1) * 2 * HD, 2 * HD), 2 * HD)

    def chunk_copy(kind, k):
        at = chunk(k)
        w, to = ((wt, peer), (wt, sib), (w_peer, sib))[kind]
        src = w_attn_hbm.at[:, at] if kind < 2 else w_attn.at[shard(w), at]
        return pltpu.make_async_remote_copy(
            src_ref=src, dst_ref=w_attn.at[shard(w), at], send_sem=c_send.at[kind, k], recv_sem=c_recv.at[kind, k],
            device_id=to, device_id_type=MESH)

    def arrived(kind, k):
        w = (w_peer, w_sib, w_far)[kind]
        at = chunk(k)
        here = w_attn.at[shard(w), at]
        pltpu.make_async_copy(here, here, c_recv.at[kind, k]).wait()

    chunk_copy(0, 0).start()
    slice_rows = depth // SHARERS

    def slice_at(w, n):
        return shard(w, slice_rows, n * slice_rows)

    mine = pl.ds(pl.multiple_of(place * slice_rows, 16), slice_rows)
    for k in range(pairs + 1):
        chunk_copy(1, k).start()
    whole = go(w_out_hbm, w_out.at[shard(wt)], o_send.at[1], o_recv.at[1], sib)

    def send_after(k):
        chunk_copy(0, k).wait_send()
        chunk_copy(0, k + 1).start()

    n_len = lengths.shape[1]
    ends = [lengths[0, 0]]
    for n in range(1, n_len):
        ends.append(ends[-1] + lengths[0, n])
    stream = n_seq * rows

    def ids(positions):
        number = jnp.zeros(positions.shape, jnp.int32) - 1
        for n in range(n_len):
            start = ends[n - 1] if n else 0
            number += (positions >= start).astype(jnp.int32)
        inside = (positions >= 0) & (positions < ends[-1])
        return jnp.where(inside, number, -(positions + 2 * stream))

    base = seq * rows
    q_ids = ids(lax.broadcasted_iota(jnp.int32, (rows, 1), 0) + base)
    k_ids = ids(lax.broadcasted_iota(jnp.int32, (1, rows + WINDOW), 1) + (base - WINDOW))
    valid_out[...] = (q_ids >= 0).astype(F32)
    counts[0] = jnp.full(counts.shape[1:], ends[-1]).astype(F32)
    number = go(counts.at[0], counts.at[1], n_send.at[0], n_recv.at[0], sib)

    loads[0].wait()
    part = 128

    def norm_rows(n, _):
        r = pl.ds(pl.multiple_of(n * part, part), part)
        values = tokens[r, :].astype(F32)
        scale = lax.rsqrt(jnp.mean(values * values, axis=-1, keepdims=True) + EPSILON)
        normed[r, :] = (values * scale * gain_attn[...]).astype(BF16)
        return 0

    lax.fori_loop(0, rows // part, norm_rows, 0)
    stores = [fetch(normed, normed_out, store.at[0])]
    for i in range(blocks):
        row = lax.broadcasted_iota(jnp.int32, (QROWS, reach), 0)
        offset = lax.broadcasted_iota(jnp.int32, (QROWS, reach), 1) - WINDOW - row
        here, there = q_ids[i * QROWS : (i + 1) * QROWS], k_ids[:, i * QROWS : i * QROWS + reach]
        bias[i] = jnp.where((offset <= 0) & (offset > -WINDOW) & (here == there), 0.0, NEGATIVE)
    number.wait_recv()
    counts[2] = counts[0] + counts[1]
    send_after(0)

    def relay(k):
        arrived(0, k)
        chunk_copy(2, k).start()

    loads[1].wait()
    relay(0)
    arrived(1, 0)
    arrived(2, 0)
    kv_cols = slice(width, width + 2 * HD)
    key_value = contract(normed[...], w_attn[:, kv_cols], 1, 0).astype(BF16)
    qkv[:, kv_cols] = key_value
    ext[WINDOW:, :] = key_value
    halo = {}

    def halo_send(half):
        for n in range(slabs):
            cols, at = pl.ds(half * HD, HD), half * slabs + n
            dst = ext.at[pl.ds(WINDOW - (n + 1) * rows, rows), cols]
            halo[half, n] = remote(ext.at[pl.ds(WINDOW, rows), cols], dst, h_send.at[at], h_recv.at[at], ahead[n])

    halo_send(0)

    def project_queries(p):
        cols = pl.ds(pl.multiple_of(p * 2 * HD, 2 * HD), 2 * HD)
        arrived(1, p + 1)
        arrived(2, p + 1)
        qkv[:, cols] = contract(normed[...], w_attn[:, cols], 1, 0).astype(BF16)

    send_after(1)
    relay(1)
    number = go(counts.at[2], counts.at[3], n_send.at[1], n_recv.at[1], peer)
    eighth = go(w_out_hbm.at[mine], w_out.at[slice_at(wt, place)], o_send.at[0], o_recv.at[0], peer)
    project_queries(0)
    for n in range(slabs):
        halo[0, n].wait_send()
    halo_send(1)
    send_after(2)
    relay(2)
    for n in range(slabs):
        halo[0, n].wait_recv()
    eighth.wait_recv()
    spread = [
        go(w_out.at[slice_at(w_peer, place)], w_out.at[slice_at(w_peer, place)], s_send.at[n], s_recv.at[n], others[n])
        for n in range(SHARERS - 1)
    ]
    number.wait_recv()
    count_out[...] = counts[2] + counts[3]
    factor = math.log2(math.e) / math.sqrt(HD)

    def p_copy(i, p):
        return pltpu.make_async_copy(probs.at[i], probs_out.at[i, p], p_store.at[i])

    def heads(p, _, values=None):
        @pl.when(jnp.asarray(p) + 3 <= pairs)
        def _():
            relay(p + 3)

        @pl.when(jnp.asarray(p) + 4 <= pairs)
        def _():
            send_after(p + 3)

        @pl.when(jnp.asarray(p) + 1 < pairs)
        def _():
            project_queries(p + 1)

        cols = pl.ds(pl.multiple_of(p * 2 * HD, 2 * HD), 2 * HD)
        for i in range(blocks):
            q_rows, keys = pl.ds(i * QROWS, QROWS), pl.ds(i * QROWS, reach)
            scores = contract(pair_rows(qkv[q_rows, cols]), ext[keys, :HD], 1, 1) * factor
            shifted = scores.reshape(2, QROWS, reach) + bias[i][None]
            powers = jnp.exp2(shifted - jnp.max(shifted, axis=-1, keepdims=True))
            weights = (powers * (1.0 / jnp.sum(powers, axis=-1, keepdims=True))).astype(BF16)

            @pl.when(jnp.asarray(p) > 0)
            def _():
                p_copy(i, p - 1).wait()

            probs[i] = weights
            p_copy(i, p).start()
            if values is not None and i == 0:
                for one in values:
                    one.wait_recv()
            outs = contract(weights.reshape(2 * QROWS, reach), ext[keys, HD:], 1, 0)
            mixed[q_rows, cols] = pair_columns(outs).astype(BF16)
        return 0

    heads(0, 0, [halo[1, n] for n in range(slabs)])
    stores.append(fetch(ext, ext_out, store.at[1]))
    lax.fori_loop(1, pairs - 1, heads, 0)
    for one in spread:
        one.wait_recv()
    passed = go(w_out.at[shard(w_peer)], w_out.at[shard(w_peer)], o_send.at[2], o_recv.at[2], sib)
    heads(pairs - 1, 0)
    stores += [fetch(qkv, qkv_out, store.at[2]), fetch(mixed, mixed_out, store.at[3]), fetch(w_attn, attn_out, store.at[4])]
    loads[2].wait()
    whole.wait_recv()
    passed.wait_recv()
    stores.append(fetch(w_out, out_out, store.at[5]))

    def project(cols):
        acc[:, cols] = tokens[:, cols].astype(F32) + contract(mixed[...], w_out[:, cols], 1, 0)

    tiles(width, 512, project)
    stores.append(fetch(acc, middle_out, store.at[6]))
    stores[0].wait()

    def norm_again(n, _):
        r = pl.ds(pl.multiple_of(n * part, part), part)
        values = acc[r, :]
        scale = lax.rsqrt(jnp.mean(values * values, axis=-1, keepdims=True) + EPSILON)
        normed[r, :] = (values * scale * gain_ffn[...]).astype(BF16)
        return 0

    lax.fori_loop(0, rows // part, norm_again, 0)
    stores.append(fetch(normed, low_out, store.at[0]))
    for i in range(blocks):
        p_copy(i, pairs - 1).wait()
    for one in stores[1:]:
        one.wait()
    chunk_copy(0, pairs).wait_send()
    for k in range(pairs + 1):
        for kind in range(1, 3):
            chunk_copy(kind, k).wait_send()
    for one in started + [halo[1, n] for n in range(slabs)]:
        one.wait_send()


def begin(lengths, tokens, w_attn, w_out, gain_attn, gain_ffn):
    rows, width = tokens.shape
    shards = 4
    depth = w_out.shape[0]
    pairs, blocks, reach = width // (2 * HD), rows // QROWS, WINDOW + QROWS
    columns = width + 2 * HD
    dma = pltpu.SemaphoreType.DMA
    hbm, vm = pl.BlockSpec(memory_space=pl.ANY), pl.BlockSpec(memory_space=pltpu.VMEM)
    shape = jax.ShapeDtypeStruct
    return pl.pallas_call(
        begin_kernel,
        name="begin",
        out_shape=[
            shape((width, columns), BF16),
            shape((width, width), BF16),
            shape((rows, columns), BF16),
            shape((rows + WINDOW, 2 * HD), BF16),
            shape((rows, width), BF16),
            shape((rows, width), BF16),
            shape((blocks, pairs, 2, QROWS, reach), BF16),
            shape((rows, width), F32),
            shape((rows, width), BF16),
            shape((rows, 1), F32),
            shape((8, 128), F32),
        ],
        in_specs=[pl.BlockSpec(memory_space=pltpu.SMEM)] + [hbm] * 3 + [vm] * 2,
        out_specs=[hbm] * 9 + [vm] * 2,
        scratch_shapes=[
            pltpu.VMEM((rows, width), BF16),
            pltpu.VMEM((rows, width), BF16),
            pltpu.VMEM((shards * depth, columns), BF16),
            pltpu.VMEM((shards * depth, width), BF16),
            pltpu.VMEM((rows, columns), BF16),
            pltpu.VMEM((rows + WINDOW, 2 * HD), BF16),
            pltpu.VMEM((rows, width), BF16),
            pltpu.VMEM((blocks, 2, QROWS, reach), BF16),
            pltpu.VMEM((blocks, QROWS, reach), F32),
            pltpu.VMEM((rows, width), F32),
            pltpu.VMEM((4, 8, 128), F32),
            dma((3,)), dma((3, pairs + 1)), dma((3, pairs + 1)), dma((3,)), dma((3,)), dma((SHARERS - 1,)), dma((SHARERS - 1,)),
            dma((2 * WINDOW // rows,)), dma((2 * WINDOW // rows,)), dma((2,)), dma((2,)), dma((blocks,)), dma((7,)),
        ],
        compiler_params=pltpu.CompilerParams(collective_id=3, has_side_effects=True, vmem_limit_bytes=60 << 20),
    )(lengths, tokens, w_attn, w_out, gain_attn.reshape(1, -1), gain_ffn.reshape(1, -1))


def passed_along(block, axis, distance):
    devices = range(lax.axis_size(axis))
    route = [(i - distance, i) for i in devices if i - distance in devices]
    return lax.ppermute(block, axis, route)


def rms_scale(values, gain):
    return values * lax.rsqrt(jnp.mean(values * values, axis=-1, keepdims=True) + EPSILON) * gain


def per_device(tokens, teacher, seq_lengths, w_attn, w_out, w_in, w_down, gain_attn, gain_ffn):
    tok_rows = tokens.shape[1]
    model_width = tokens.shape[2]
    seq_devices = lax.axis_size("seq")
    all_slots = tok_rows * seq_devices * lax.axis_size("wt")
    (attn_full, out_full, qkv, extended, normed, mixed_b, probs, middle, normed_two, valid, count) = begin(
        seq_lengths, tokens[0], w_attn, w_out, gain_attn, gain_ffn
    )
    valid_total = count[0, 0]
    scale_up = all_slots / count[:1, :1]
    w_pair = jnp.swapaxes(w_in, 0, 1)
    output, cotangent, grad_norm_two, grad_down, grad_in, squares = ffn(
        normed_two, w_pair, w_down, middle, teacher[0], valid, scale_up
    )
    slot, kv_slot = model_width // seq_devices, HD // seq_devices
    if slot % 16 == 0 and kv_slot % 16 == 0:
        grad_inputs, grad_down, grad_in, grad_attn, grad_out, small = finish(
            grad_norm_two, cotangent, middle, out_full, attn_full, mixed_b, probs, qkv, extended, normed, tokens[0],
            grad_down, grad_in, gain_attn, gain_ffn, squares, seq_devices,
        )
    else:
        _, norm_one_pull = jax.vjp(rms_scale, tokens[0].astype(jnp.float32), gain_attn)
        _, norm_two_pull = jax.vjp(rms_scale, middle, gain_ffn)
        grad_middle_norm, grad_gain_ffn = norm_two_pull(grad_norm_two)
        grad_middle = cotangent + grad_middle_norm
        grad_mid_low = grad_middle.astype(jnp.bfloat16)
        grad_out = jnp.einsum("te,td->ed", grad_mid_low, mixed_b, preferred_element_type=jnp.float32)
        grad_mixed = jnp.einsum("te,de->td", grad_mid_low, out_full, preferred_element_type=jnp.float32)
        grad_query, grad_ext = attend_back(qkv, extended, grad_mixed.astype(jnp.bfloat16), mixed_b, probs)
        edge_rows = WINDOW
        grad_kv = grad_ext[edge_rows:]
        for back_step in range(1, WINDOW // tok_rows + 1):
            slab_rows = grad_ext[
                edge_rows - back_step * tok_rows : edge_rows - (back_step - 1) * tok_rows
            ]
            grad_kv = grad_kv + passed_along(slab_rows, "seq", -back_step)
        grad_key = (grad_kv[:, :HD] * (1.0 / math.sqrt(HD))).astype(jnp.bfloat16)
        grad_qkv = jnp.concatenate([grad_query, grad_key, grad_kv[:, HD:].astype(jnp.bfloat16)], axis=1)
        grad_attn = jnp.einsum("te,td->ed", grad_qkv, normed, preferred_element_type=jnp.float32)
        grad_normed = jnp.einsum("te,de->td", grad_qkv, attn_full, preferred_element_type=jnp.float32)
        grad_input_norm, grad_gain_attn = norm_one_pull(grad_normed)
        grad_inputs = grad_middle + grad_input_norm
        grad_attn = grad_attn.astype(jnp.bfloat16)
        grad_key, grad_value = (
            grad_attn[model_width + at : model_width + at + HD].reshape(seq_devices, kv_slot, model_width) for at in (0, HD)
        )
        packed = jnp.concatenate(
            [
                grad_attn[:model_width].reshape(seq_devices, slot, model_width),
                grad_key,
                grad_value,
                grad_out.astype(jnp.bfloat16).reshape(seq_devices, slot, model_width),
            ],
            axis=1,
        )
        small = jnp.stack([grad_gain_attn, grad_gain_ffn, jnp.full((model_width,), squares[0, 0])] + [jnp.zeros_like(grad_gain_attn)] * 5)
        grad_down, grad_in = grad_down.reshape(seq_devices, slot, -1), grad_in.reshape(2, seq_devices, slot, -1)
        grad_down, grad_in, packed, small = reduce_plain(grad_down, grad_in, packed, small)
        grad_attn, grad_out = packed[:-slot], packed[-slot:]
    grad_queries = grad_attn[:slot].T
    grad_keyvals = grad_attn[slot:].T.reshape(-1, 2, kv_slot)
    grad_out = grad_out.T
    grad_down = grad_down.T
    grad_in = jnp.swapaxes(grad_in, 0, 1)
    gain_attn_all, gain_ffn_all, squares_all = small[0], small[1], small[2, 0]
    loss = squares_all / (valid_total * model_width)
    return (
        output[None],
        loss,
        grad_inputs[None],
        grad_queries,
        grad_keyvals,
        grad_out,
        grad_in,
        grad_down,
        gain_attn_all,
        gain_ffn_all,
    )


def solution(mesh):
    in_specs = (
        P("wt", "seq", None),
        P("wt", "seq", None),
        P("wt", None),
        P("wt", None),
        P("wt", None),
        P(None, None, "wt"),
        P("wt", None),
        P(),
        P(),
    )
    out_specs = (
        P("wt", "seq", None),
        P(),
        P("wt", "seq", None),
        P("wt", "seq"),
        P("wt", None, "seq"),
        P("wt", "seq"),
        P("seq", None, "wt"),
        P("wt", "seq"),
        P(),
        P(),
    )
    return jax.shard_map(
        per_device, mesh=mesh, in_specs=in_specs, out_specs=out_specs, check_vma=False
    )
```

```python
import functools
import math

import jax
import jax.numpy as jnp
from jax import lax
from jax.experimental import pallas as pl
from jax.experimental.pallas import tpu as pltpu
from jax.sharding import PartitionSpec as P

HEADS = 12
HD = 128
WINDOW = 1024
QROWS = 256


EPSILON = 1e-06
NEGATIVE = -1e30

MESH = pl.DeviceIdType.MESH
F32 = jnp.float32
BF16 = jnp.bfloat16


def places():
    seq, wt = lax.axis_index("seq"), lax.axis_index("wt")
    return seq // 2, seq % 2, wt // 2, wt % 2


def device(z, x, y, c):
    return (z * 2 + x, y * 2 + c)


def remote(src, dst, send, recv, to):
    copy = pltpu.make_async_remote_copy(
        src_ref=src, dst_ref=dst, send_sem=send, recv_sem=recv, device_id=to, device_id_type=MESH
    )
    copy.start()
    return copy


def greet(devices):
    barrier = pltpu.get_barrier_semaphore()
    for one in devices:
        pl.semaphore_signal(barrier, inc=1, device_id=one, device_id_type=MESH)
    pl.semaphore_wait(barrier, len(devices))


def reduce_plain(gd, gi, p, v):
    gd = lax.psum_scatter(gd, "seq", scatter_dimension=0, tiled=False).astype(F32)
    gi = lax.psum_scatter(gi, "seq", scatter_dimension=1, tiled=False).astype(F32)
    p = lax.psum_scatter(p, "seq", scatter_dimension=0, tiled=False)
    p = lax.psum_scatter(p, "wt", scatter_dimension=1, tiled=True).astype(F32)
    return gd, gi, p, lax.psum(v, ("seq", "wt"))


def contract(a, b, dim_a, dim_b):
    return lax.dot_general(a, b, (((dim_a,), (dim_b,)), ((), ())), preferred_element_type=F32)


def tiles(total, width, body):
    def step(i, _):
        body(pl.ds(pl.multiple_of(i * width, width), width))
        return 0

    lax.fori_loop(0, total // width, step, 0)


def flat(block):
    return block.reshape(-1, block.shape[-1])


def ffn_kernel(share, h, wi_hbm, wd_hbm, mid_hbm, teacher_hbm, lengths, scale, out, cot, dh, gd, gi, squares, gd_owner, gd_whole,
               wi, wd, mid, teacher, hall, dall, act, hid, acc, far, out_low, sent, got,
               load, h_send, h_recv, d_send, d_recv, p_send, p_recv, store, g_store, *sharing):
    z, x, y, c = places()
    sib, peer = device(z, x, y, 1 - c), device(z, x, 1 - y, c)
    half, width = h.shape[1:]
    units = wd.shape[0]

    def fetch(src, dst, sem):
        copy = pltpu.make_async_copy(src, dst, sem)
        copy.start()
        return copy

    loads = [fetch(*pair, load.at[n]) for n, pair in enumerate(
        ((h, hall.at[0]), (wi_hbm, wi), (wd_hbm, wd), (teacher_hbm, teacher)))]
    if share:
        gx, gz, gxs, gxr, gzs, gzr, end = sharing
        depth, slot = lax.axis_size("seq") // 2, gx.shape[1]
        zs = [lax.rem(z + d, depth) for d in range(depth)]
        xpeer, zpeers = device(z, 1 - x, y, c), [device(zs[d], x, y, c) for d in range(depth)]
    greet([sib, peer] + ([xpeer] + zpeers[1:] if share else []))
    pending = []

    def go(*args):
        nonlocal pending
        pending.append(remote(*args))
        return pending[-1]

    def spread(src, dst, send, recv, j):
        a = go(src.at[j], dst.at[2, j], send.at[0, j], recv.at[0, j], peer)
        b = go(src.at[j], dst.at[1, j], send.at[1, j], recv.at[1, j], sib)
        return a, b

    def relay(dst, send, recv, j):
        return go(dst.at[2, j], dst.at[3, j], send.at[2, j], recv.at[2, j], sib)

    def group(ref, g):
        return ref.at[2:4, g - 2] if g >= 2 else ref.at[g]

    h_copies = [spread(h, hall, h_send, h_recv, j) for j in range(2)]

    def gated(g):
        rows = flat(group(hall, g)[...])

        def body(cols):
            mid[:, :, :384] = contract(rows, wi[0, :, cols], 1, 0).reshape(2, half, -1)
            mid[:, :, 384:768] = contract(rows, wi[1, :, cols], 1, 0).reshape(2, half, -1)
            block = half // 2

            def finish_rows(i, _):
                j, r = i // 2, pl.ds(pl.multiple_of(lax.rem(i, 2) * block, block), block)
                gate, up = mid[j, r, :384], mid[j, r, 384:768]
                square = gate * gate
                turn = jnp.tanh(gate * (0.7978845608028654 + 0.035677408136300125 * square))
                upper = 0.5 + 0.5 * turn
                value = gate * upper
                slope = upper + 0.5 * gate * (1.0 - turn * turn) * (0.7978845608028654 + 0.10703222440890038 * square)
                group(hid, g)[j, r, cols] = (value * up).astype(BF16)
                group(act.at[0], g)[j, r, cols] = (slope * up).astype(BF16)
                group(act.at[1], g)[j, r, cols] = value.astype(BF16)
                return 0

            lax.fori_loop(0, 4, finish_rows, 0)

        tiles(units, 384, body)

    def emit(g, cols, part):
        if g == 0:
            acc[:, :, cols] = part.reshape(2, half, -1)
        elif g == 1:
            sent[0, :, :, cols] = part.astype(BF16).reshape(2, half, -1)
        else:
            far[:, cols] = part[:half]
            sent[1, g - 2, :, cols] = part[half:].astype(BF16)

    def down(g):
        rows = flat(group(hid, g)[...])
        tiles(width, 512, lambda cols: emit(g, cols, contract(rows, wd[:, cols], 1, 0)))

    def push(phase, kind, j):
        return go(sent.at[kind, j], got.at[kind, j], p_send.at[phase, kind, j], p_recv.at[phase, kind, j], peer if kind == 2 else sib)

    def sums(phase, compute, copies, buffer, send, recv, before):
        kept = {}
        compute(0)
        for j in range(2):
            copies[j][1].wait_recv()
        compute(1)
        for j in range(2):
            kept[0, j] = push(phase, 0, j)
        for j in range(2):
            copies[j][0].wait_recv()
            passed = relay(buffer, send, recv, j)
            passed.wait_recv()
            if phase == 1 and j == 1 and share:
                down_tile(0)
            compute(2 + j)
            kept[1, j] = push(phase, 1, j)
            kept[1, j].wait_recv()
            sent[2, j] = (far[...] + got[1, j].astype(F32)).astype(BF16)
            kept[2, j] = push(phase, 2, j)
        return kept

    def forward(g):
        gated(g)
        down(g)

    for one in loads[:3]:
        one.wait()
    kept = sums(0, forward, h_copies, hall, h_send, h_recv, None)
    first, pending = pending, []
    loads.append(fetch(mid_hbm, mid, load.at[4]))
    loads[3].wait()
    loads[4].wait()
    total = jnp.zeros((), F32)
    d_copies, saves = [], []
    factor = scale[0, 0]
    first_row = lax.axis_index("seq") * 2 * half
    used = lengths[0, 0]
    for n in range(1, lengths.shape[1]):
        used += lengths[0, n]
    for j in range(2):
        kept[0, j].wait_recv()
        kept[2, j].wait_recv()
        step = half // 4

        def rows_of(i, so_far):
            r = pl.ds(pl.multiple_of(i * step, step), step)
            value = mid[j, r, :] + acc[j, r, :] + got[0, j, r, :].astype(F32) + got[2, j, r, :].astype(F32)
            out_low[j, r, :] = value.astype(BF16)
            diff = value - teacher[j, r, :].astype(F32)
            place = lax.broadcasted_iota(jnp.int32, (step, 1), 0) + (first_row + j * half + i * step)
            masked = (place < used).astype(F32) * diff
            grad = masked * factor
            mid[j, r, :] = grad
            dall[0, j, r, :] = grad.astype(BF16)
            return so_far + jnp.sum(masked * diff)

        total = lax.fori_loop(0, 4, rows_of, total)
        d_copies.append(spread(dall.at[0], dall, d_send, d_recv, j))
        saves.append(fetch(out_low.at[j], out.at[j], store.at[0, j]))
        saves.append(fetch(mid.at[j], cot.at[j], store.at[1, j]))
    squares[...] = jnp.full(squares.shape, total)

    def backward(g):
        rows = flat(group(dall, g)[...])

        def body(cols):
            grad = contract(rows, wd[cols, :], 1, 1).reshape(2, half, -1)
            for n in range(2):
                part = group(act.at[n], g)
                part[:, :, cols] = (grad * part[:, :, cols].astype(F32)).astype(BF16)

        tiles(units, 384, body)
        gate, up = flat(group(act.at[0], g)[...]), flat(group(act.at[1], g)[...])
        tiles(width, 512, lambda cols: emit(g, cols, contract(gate, wi[0, cols, :], 1, 1) + contract(up, wi[1, cols, :], 1, 1)))

    for copy in first:
        copy.wait_send()
    order = sorted(range(depth), key=lambda d: (d == 0, abs(2 * d - depth))) if share else []
    parts = [teacher.at[:, :slot, :units], out_low.at[:, :slot, :units]] if share else []
    stage = [wd.at[pl.ds(n * 256, 256), :units] for n in range(2)]
    swaps, owners = {}, {}

    def down_tile(n):
        if n >= 2:
            swaps[n - 2].wait_send()
        else:
            saves[2 * n].wait()
        cols = pl.ds(pl.multiple_of(zs[order[n]] * 2 * slot, 128), 2 * slot)
        left = dall[:, :, :, cols].reshape(8 * half, 2 * slot)

        parts[n % 2][...] = contract(left, hid[...].reshape(8 * half, units), 0, 0).astype(BF16).reshape(2, slot, units)
        if n == 0:
            down_swap(0)

    def down_swap(n):
        swaps[n] = remote(parts[n % 2].at[1 - x], gx.at[n], gxs.at[n], gxr.at[n], xpeer)

    def down_owner(n):
        swaps[n].wait_recv()
        gx[n] = (parts[n % 2][x].astype(F32) + gx[n].astype(F32)).astype(BF16)
        if n < 2:
            owners[n] = go(gx.at[n], gz.at[n], gzs.at[n], gzr.at[n], zpeers[order[n]])

    kept = sums(1, backward, d_copies, dall, d_send, d_recv, None)
    count = 0
    blocks = width // 256
    left, right = {}, {}

    def weight(left, right, target):
        def body(i, _):
            for n in range(2):
                at = pl.ds(pl.multiple_of(i * 512 + n * 256, 256), 256)

                @pl.when(i > 0)
                def _():
                    pltpu.make_async_copy(stage[n], target.at[at], g_store.at[n]).wait()

                stage[n][...] = contract(left(at), right(), 0, 0).astype(BF16)
                pltpu.make_async_copy(stage[n], target.at[at], g_store.at[n]).start()
            return 0

        lax.fori_loop(0, width // 512, body, 0)
        for n in range(2):
            pltpu.make_async_copy(stage[n], target.at[pl.ds(0, 256)], g_store.at[n]).wait()

    if not share:
        weight(lambda at: flat(dall[:, :, :, at].reshape(4, 2 * half, 256)), lambda: flat(hid[...].reshape(4, 2 * half, units)), gd)
    for n in range(2):
        if share:
            down_tile(n + 1)
            down_swap(n + 1)
        weight(lambda at: flat(hall[:, :, :, at].reshape(4, 2 * half, 256)), lambda n=n: flat(act[n].reshape(4, 2 * half, units)), gi.at[n])
        if share:
            down_owner(n)
    if share:
        down_tile(3)
        ends = [fetch(parts[1], gd_whole, end.at[0])]
    for j in range(2):
        kept[0, j].wait_recv()
        kept[2, j].wait_recv()
        saves[2 * j + 1].wait()

        def sum_rows(i, _):
            r = pl.ds(pl.multiple_of(i * step, step), step)
            mid[j, r, :] = acc[j, r, :] + got[0, j, r, :].astype(F32) + got[2, j, r, :].astype(F32)
            return 0

        lax.fori_loop(0, 4, sum_rows, 0)
        saves.append(fetch(mid.at[j], dh.at[j], store.at[2, j]))
    if share:
        down_owner(2)
        ends.append(fetch(gx.at[2], gd_owner, end.at[1]))
        for n in range(2):
            owners[n].wait_recv()
        far[:slot, :units] = gz[0].astype(F32) + gz[1].astype(F32)
        ends.append(fetch(far.at[:slot, :units], gd, end.at[2]))
        swaps[2].wait_send()
        for one in ends:
            one.wait()
    for copy in pending:
        copy.wait_send()
    for n in (4, 5) if share else (0, 2, 4, 5):
        saves[n].wait()


def ffn(h, wi, wd, mid, teacher, lengths, scale, seq):
    rows, width = h.shape
    depth, slot = (seq // 2, width // seq) if seq else (0, 0)
    units = wd.shape[0]
    half = rows // 2
    split = lambda a: a.reshape(2, half, a.shape[-1])
    dma = pltpu.SemaphoreType.DMA
    hbm, vm = pl.BlockSpec(memory_space=pl.ANY), pl.BlockSpec(memory_space=pltpu.VMEM)
    def kernel(*refs):
        ffn_kernel(bool(seq), *(refs if seq else refs[:13] + (None, None) + refs[13:]))

    sharing = []
    if seq:
        sharing = [
            pltpu.VMEM((3, slot, units), BF16), pltpu.VMEM((2, slot, units), BF16),
            dma((3,)), dma((3,)), dma((2,)), dma((2,)), dma((3,)),
        ]
    out, cot, dh, gd, gi, squares, *rest = pl.pallas_call(
        kernel,
        name="ffn",
        out_shape=[
            jax.ShapeDtypeStruct((2, half, width), BF16),
            jax.ShapeDtypeStruct((2, half, width), F32),
            jax.ShapeDtypeStruct((2, half, width), F32),
            jax.ShapeDtypeStruct((slot, units), F32) if seq else jax.ShapeDtypeStruct((width, units), BF16),
            jax.ShapeDtypeStruct((2, width, units), BF16),
            jax.ShapeDtypeStruct((8, 128), F32),
        ]
        + [jax.ShapeDtypeStruct((slot, units), BF16), jax.ShapeDtypeStruct((2, slot, units), BF16)] * bool(seq),
        in_specs=[hbm] * 5 + [pl.BlockSpec(memory_space=pltpu.SMEM)] * 2,
        out_specs=[hbm] * 5 + [vm] + [hbm, hbm] * bool(seq),
        scratch_shapes=[
            pltpu.VMEM((2, width, units), BF16),
            pltpu.VMEM((units, width), BF16),
            pltpu.VMEM((2, half, width), F32),
            pltpu.VMEM((2, half, width), BF16),
            pltpu.VMEM((4, 2, half, width), BF16),
            pltpu.VMEM((4, 2, half, width), BF16),
            pltpu.VMEM((2, 4, 2, half, units), BF16),
            pltpu.VMEM((4, 2, half, units), BF16),
            pltpu.VMEM((2, half, width), F32),
            pltpu.VMEM((half, width), F32),
            pltpu.VMEM((2, half, width), BF16),
            pltpu.VMEM((3, 2, half, width), BF16),
            pltpu.VMEM((3, 2, half, width), BF16),
            dma((5,)), dma((3, 2)), dma((3, 2)), dma((3, 2)), dma((3, 2)),
            dma((2, 3, 2)), dma((2, 3, 2)), dma((3, 2)), dma((2,)),
        ]
        + sharing,
        compiler_params=pltpu.CompilerParams(collective_id=2, has_side_effects=True, vmem_limit_bytes=63 << 20),
    )(split(h), wi, wd, split(mid), split(teacher), lengths, scale)
    return out.reshape(rows, width), cot.reshape(rows, width), dh.reshape(rows, width), gd, gi, squares, rest


def pair_rows(block):
    return jnp.concatenate([block[:, :HD], block[:, HD:]], axis=0)


def pair_columns(block):
    rows = block.shape[0] // 2
    return jnp.concatenate([block[:rows], block[rows:]], axis=1)


def attend_back_kernel(q, kv, grad, mixed, probs, grad_q, grad_kv):
    i, pair = pl.program_id(0), pl.program_id(1)
    reach = WINDOW + QROWS
    keys = pl.ds(pl.multiple_of(i * QROWS, QROWS), reach)

    @pl.when((i == 0) & (pair == 0))
    def _():
        grad_kv[...] = jnp.zeros_like(grad_kv)

    queries, grads = pair_rows(q[...]), pair_rows(grad[...])
    weights = probs[0, 0].reshape(2 * QROWS, reach)
    dots = jnp.sum(grads.astype(F32) * pair_rows(mixed[...]).astype(F32), axis=-1, keepdims=True)
    steep = contract(grads, kv[keys, HD:], 1, 1) - dots
    steep = (weights.astype(F32) * steep).astype(BF16)
    grad_q[...] = (pair_columns(contract(steep, kv[keys, :HD], 1, 0)) * (1.0 / math.sqrt(HD))).astype(BF16)
    grad_kv[keys, :HD] += contract(steep, queries, 0, 0)
    grad_kv[keys, HD:] += contract(weights, grads, 0, 0)


def attend_back(queries, extended, grad_mixed, mixed, probs):
    rows, width = mixed.shape
    blocks, pairs, reach = rows // QROWS, width // (2 * HD), WINDOW + QROWS
    block = pl.BlockSpec((QROWS, 2 * HD), lambda i, p: (i, p))
    whole = pl.BlockSpec(extended.shape, lambda i, p: (0, 0))
    return pl.pallas_call(
        attend_back_kernel,
        name="attend_back",
        grid=(blocks, pairs),
        out_shape=[jax.ShapeDtypeStruct((rows, width), BF16), jax.ShapeDtypeStruct(extended.shape, F32)],
        in_specs=[block, whole, block, block, pl.BlockSpec((1, 1, 2, QROWS, reach), lambda i, p: (i, p, 0, 0, 0))],
        out_specs=[block, whole],
        compiler_params=pltpu.CompilerParams(vmem_limit_bytes=48 << 20),
    )(queries, extended, grad_mixed, mixed, probs)


GRAD_COLS = 128
AHEAD = 3


def owner_order(depth):
    return sorted(range(depth), key=lambda d: (d == 0, abs(2 * d - depth)))


class RowSum:
    def __init__(self, source, buffers, sems, where, go):
        self.source, self.go = source, go
        self.core, self.side, self.cross, self.along = buffers
        self.cs, self.cr, self.ys, self.yr, self.xs, self.xr, self.zs_, self.zr = sems
        self.x, self.y, self.c, self.zs, self.sib, self.ypeer, self.xpeer, self.zpeers = where
        self.depth, self.cols = len(self.zs), self.core.shape[-1]
        self.order = owner_order(self.depth)
        self.moved = {}

    def columns(self, y, c):
        return pl.ds(pl.multiple_of((2 * y + c) * self.cols, self.cols), self.cols)

    def first(self, d):
        for h in range(2):
            part = self.source.at[self.zs[d], :, :, self.columns(h, 1 - self.c)]
            self.moved["c", d, h] = self.go(part, self.core.at[d, h], self.cs.at[d, h], self.cr.at[d, h], self.sib)

    def second(self, d):
        for h in range(2):
            self.moved["c", d, h].wait_recv()
        far = 1 - self.y
        own = self.source[self.zs[d], :, :, self.columns(far, self.c)].astype(F32)
        self.core[d, far] = (own + self.core[d, far].astype(F32)).astype(BF16)
        self.moved["y", d] = self.go(self.core.at[d, far], self.side.at[d], self.ys.at[d], self.yr.at[d], self.ypeer)

    def kept(self, d, x):
        own = self.source[self.zs[d], x, :, self.columns(self.y, self.c)].astype(F32)
        return own + self.core[d, self.y, x].astype(F32) + self.side[d, x].astype(F32)

    def third(self, d):
        self.moved["y", d].wait_recv()
        self.side[d, 1 - self.x] = self.kept(d, 1 - self.x).astype(BF16)
        self.moved["x", d] = self.go(self.side.at[d, 1 - self.x], self.cross.at[d], self.xs.at[d], self.xr.at[d], self.xpeer)

    def fourth(self, d):
        self.moved["x", d].wait_recv()
        self.cross[d] = (self.kept(d, self.x) + self.cross[d].astype(F32)).astype(BF16)
        if d:
            self.moved["z", d] = self.go(
                self.cross.at[d], self.along.at[d - 1], self.zs_.at[d - 1], self.zr.at[d - 1], self.zpeers[d]
            )

    def total(self):
        value = self.cross[0].astype(F32)
        for d in range(1, self.depth):
            self.moved["z", d].wait_recv()
            value += self.along[d - 1].astype(F32)
        return value


def norm_back(values, grad, gain):
    r = lax.rsqrt(jnp.mean(values * values, axis=-1, keepdims=True) + EPSILON)
    scaled = grad * gain
    slope = r * r * r * jnp.mean(values * scaled, axis=-1, keepdims=True)
    return r * scaled - values * slope, jnp.sum(grad * values * r, axis=0, keepdims=True)


def finish_kernel(dh_hbm, cot_hbm, middle_hbm, w_out_hbm, w_attn_hbm, mixed_hbm, probs_hbm, qkv_hbm, ext_hbm, normed_hbm,
                  tokens_hbm, gd_hbm, gd_owner, gd_whole, gi_hbm, gain_attn, gain_ffn, squares,
                  grad_x, grad_d, grad_i, grad_qkv_out, grad_o, small_out,
                  dh, cot, middle, weight, mixed, probs, qkv, ext, normed, low, dmix, dkv, slabs, slabs_in,
                  gx, gz, own, staged, dx, dz, down, po, pa, ocore, oside, ocross, oalong, acore, aside, across, aalong, vb,
                  load, p_load, own_load, out_sem, slab_s, slab_r, ds, dr, gxs, gxr, gzs, gzr, o_sems, a_sems, vs, vr):
    z, x, y, c = places()
    depth, width = own.shape[1], own.shape[-1]
    rows, model_width = dh.shape
    units = gi_hbm.shape[-1]
    seq = 2 * depth
    me = 2 * z + x
    sib, ypeer, xpeer = device(z, x, y, 1 - c), device(z, x, 1 - y, c), device(z, 1 - x, y, c)
    zs = [lax.rem(z + d, depth) for d in range(depth)]
    zpeers = [device(zs[d], x, y, c) for d in range(depth)]
    wt = 2 * y + c
    diagonal = (lax.rem(me + seq - 1 + 2 * x, seq), wt)
    back = [(lax.rem(me + seq - step, seq), wt) for step in (1, 2)]

    def fetch(src, dst, sem):
        copy = pltpu.make_async_copy(src, dst, sem)
        copy.start()
        return copy

    loads = {}
    for n, (name, src, dst) in enumerate((
        ("dh", dh_hbm, dh), ("cot", cot_hbm, cot), ("w_out", w_out_hbm, weight.at[:, :model_width]), ("mixed", mixed_hbm, mixed),
        ("qkv", qkv_hbm, qkv), ("ext", ext_hbm, ext), ("normed", normed_hbm, normed))):
        loads[name] = fetch(src, dst, load.at[n])
    greet([sib, ypeer, xpeer, diagonal] + zpeers[1:])
    started = []

    def go(*args):
        started.append(remote(*args))
        return started[-1]

    spots = [(n, at) for n in range(2) for at in range(0, units, width)]
    chunks = len(spots)
    gxc, gzc, owned = {}, {}, {}

    def g_ref(k, side):
        n, at = spots[k]
        return gi_hbm.at[n, :, side, :, pl.ds(at, width)]

    def g_send(k):
        if k < chunks:
            gxc[k] = go(g_ref(k, 1 - x), gx.at[k], gxs.at[k], gxr.at[k], xpeer)

    def g_load(k):
        if k < chunks:
            owned[k] = fetch(g_ref(k, x), own.at[k % 2], own_load.at[k % 2])

    def g_step(k):
        gxc[k].wait_recv()
        g_send(k + AHEAD)
        owned[k].wait()
        for d in range(depth):
            gx[k, zs[d]] = (own[k % 2, zs[d]].astype(F32) + gx[k, zs[d]].astype(F32)).astype(BF16)
            if d:
                gzc[k, d] = go(gx.at[k, zs[d]], gz.at[k, d - 1], gzs.at[k, d - 1], gzr.at[k, d - 1], zpeers[d])
        g_load(k + 2)

    stores = {}

    def g_end(k):
        total = gx[k, z].astype(F32)
        for d in range(1, depth):
            gzc[k, d].wait_recv()
            total += gz[k, d - 1].astype(F32)
        if k >= 2:
            stores[k - 2].wait()
        staged[k % 2] = total
        n, at = spots[k]
        stores[k] = fetch(staged.at[k % 2], grad_i.at[n, :, pl.ds(at, width)], out_sem.at[k % 2])

    last = owner_order(depth)[2]
    sent_down = [
        go(gd_owner, dz, ds.at[0], dr.at[0], zpeers[last]),
        go(gd_whole.at[1 - x], dx, ds.at[1], dr.at[1], xpeer),
    ]
    loads["dw"] = fetch(gd_whole.at[x], down, load.at[10])
    loads["da"] = fetch(gd_hbm, grad_d, load.at[11])
    for k in range(AHEAD):
        g_send(k)
    g_load(0)
    g_load(1)
    where = (x, y, c, zs, sib, ypeer, xpeer, zpeers)
    sum_o = RowSum(po, (ocore, oside, ocross, oalong), o_sems, where, go)
    sum_a = RowSum(pa, (acore, aside, across, aalong), a_sems, where, go)

    step = middle.shape[1]
    steps = rows // step
    mids = [None] * steps

    def mid_load(n):
        if n < steps:
            mids[n] = fetch(middle_hbm.at[pl.ds(n * step, step)], middle.at[n % 2], load.at[8 + n % 2])

    mid_load(0)
    mid_load(1)
    loads["dh"].wait()
    loads["cot"].wait()
    gain_grad = jnp.zeros((1, model_width), F32)
    for n in range(steps):
        mids[n].wait()
        r = pl.ds(n * step, step)
        grad, part = norm_back(middle[n % 2], dh[r, :], gain_ffn[...])
        grad = cot[r, :] + grad
        cot[r, :] = grad
        low[r, :model_width] = grad.astype(BF16)
        gain_grad += part
        mid_load(n + 2)
    vb[0] = jnp.zeros(vb.shape[1:], F32)
    vb[0, 1:2] = gain_grad
    vb[0, 2:3] = jnp.broadcast_to(squares[0:1, 0:1], (1, model_width))
    loads["w_out"].wait()
    loads["mixed"].wait()
    rows_low = lambda: low[:, :model_width]

    def out_back(cols):
        dmix[:, cols] = contract(rows_low(), weight[cols, :model_width], 1, 1).astype(BF16)

    tiles(model_width, 512, out_back)
    loads["w_attn"] = fetch(w_attn_hbm, weight, load.at[7])

    def out_grad(d, _):
        cols = pl.ds(pl.multiple_of(d * 2 * po.shape[2], 128), 2 * po.shape[2])
        po[d] = contract(low[:, cols], mixed[...], 0, 0).astype(BF16).reshape(po.shape[1:])
        return 0

    lax.fori_loop(0, depth, out_grad, 0)
    for d in sum_o.order:
        sum_o.first(d)
    g_step(0)
    g_step(1)
    blocks, pairs, reach = probs_hbm.shape[0], probs_hbm.shape[1], probs.shape[-1]
    count = blocks * pairs

    def p_fetch(t):
        return pltpu.make_async_copy(probs_hbm.at[t // pairs, t % pairs], probs.at[t % 2], p_load.at[t % 2])

    p_fetch(0).start()
    p_fetch(1).start()
    dkv[...] = jnp.zeros_like(dkv)
    loads["qkv"].wait()
    loads["ext"].wait()
    for i in range(blocks):
        q_rows, keys = pl.ds(i * QROWS, QROWS), pl.ds(i * QROWS, reach)

        def one(pair, _):
            t = i * pairs + pair
            cols = pl.ds(pl.multiple_of(pair * 2 * HD, 2 * HD), 2 * HD)
            queries, grads = pair_rows(qkv[q_rows, cols]), pair_rows(dmix[q_rows, cols])
            outs = pair_rows(mixed[q_rows, cols])
            dots = jnp.sum(grads.astype(F32) * outs.astype(F32), axis=-1, keepdims=True)
            slot = lax.rem(t, 2)
            p_fetch(t).wait()
            weights = flat(probs[slot])
            steep = contract(grads, ext[keys, HD:], 1, 1) - dots
            steep = (weights.astype(F32) * steep).astype(BF16)
            low[q_rows, cols] = (pair_columns(contract(steep, ext[keys, :HD], 1, 0)) * (1.0 / math.sqrt(HD))).astype(BF16)
            dkv[keys, :HD] += contract(steep, queries, 0, 0)
            dkv[keys, HD:] += contract(weights, grads, 0, 0)

            @pl.when(t + 2 < count)
            def _():
                p_fetch(t + 2).start()

            return 0

        lax.fori_loop(0, pairs // 2, one, 0)
        if i == 0:
            for d in sum_o.order:
                sum_o.second(d)
        g_step(2 + 2 * i)
        lax.fori_loop(pairs // 2, pairs, one, 0)
        g_step(3 + 2 * i)
    for n in range(2):
        slabs[n] = dkv[(1 - n) * rows : (2 - n) * rows, :].astype(BF16)
    returned = [go(slabs.at[n], slabs_in.at[n], slab_s.at[n], slab_r.at[n], back[n]) for n in range(2)]
    loads["normed"].wait()
    slot_rows = model_width // seq

    def query_grad(d, _):
        cols = pl.ds(pl.multiple_of(d * 2 * slot_rows, 128), 2 * slot_rows)
        pa[d, :, :slot_rows] = contract(low[:, cols], normed[...], 0, 0).astype(BF16).reshape(2, slot_rows, model_width)
        return 0

    lax.fori_loop(0, depth, query_grad, 0)
    g_step(6)
    for one in returned:
        one.wait_recv()
    summed = dkv[2 * rows :, :] + slabs_in[0].astype(F32) + slabs_in[1].astype(F32)
    low[:, model_width : model_width + HD] = (summed[:, :HD] * (1.0 / math.sqrt(HD))).astype(BF16)
    low[:, model_width + HD :] = summed[:, HD:].astype(BF16)
    kv_grad = contract(low[:, model_width:], normed[...], 0, 0).astype(BF16)
    kv_rows = HD // seq
    for n in range(2):
        part = kv_grad[n * HD : (n + 1) * HD].reshape(depth, 2, kv_rows, model_width)
        pa[:, :, slot_rows + n * kv_rows : slot_rows + (n + 1) * kv_rows] = part
    for d in sum_a.order:
        sum_a.first(d)
    loads["tokens"] = fetch(tokens_hbm, mixed, load.at[3])
    loads["w_attn"].wait()

    def attn_back(cols):
        dh[:, cols] = contract(low[...], weight[cols, :], 1, 1)

    tiles(model_width, 512, attn_back)
    g_step(7)
    loads["tokens"].wait()

    def last_norm(n, so_far):
        r = pl.ds(pl.multiple_of(n * step, step), step)
        grad, part = norm_back(mixed[r, :].astype(F32), dh[r, :], gain_attn[...])
        cot[r, :] += grad
        return so_far + part

    vb[0, 0:1] = lax.fori_loop(0, steps, last_norm, jnp.zeros((1, model_width), F32))
    saved = fetch(cot, grad_x, load.at[0])

    vc = {}

    def v_first():
        vc[0] = go(vb.at[0], vb.at[1], vs.at[0], vr.at[0], sib)

    def v_swap(n, to):
        vc[n - 1].wait_recv()
        vb[2 * n] = vb[2 * n - 2] + vb[2 * n - 1]
        vc[n] = go(vb.at[2 * n], vb.at[2 * n + 1], vs.at[n], vr.at[n], to)

    def v_along():
        vc[2].wait_recv()
        vb[6] = vb[4] + vb[5]
        for d in range(1, depth):
            vc[2 + d] = go(vb.at[6], vb.at[6 + d], vs.at[2 + d], vr.at[2 + d], zpeers[d])

    def v_end():
        for d in range(1, depth):
            vc[2 + d].wait_recv()
        total = vb[6 + z]
        for n in range(1, depth):
            total += vb[6 + lax.rem(z - n + depth, depth)]
        small_out[...] = total

    v_first()
    o, a = sum_o.order, sum_a.order
    after = {
        8: [lambda: sum_a.second(a[0]), lambda: sum_o.third(o[0]), lambda: sum_o.third(o[1]), lambda: v_swap(1, ypeer)],
        9: [lambda: sum_o.third(o[2]), lambda: sum_o.third(o[3])],
        10: [lambda: sum_a.second(a[1]), lambda: sum_a.third(a[0]), lambda: sum_o.fourth(o[0]), lambda: v_swap(2, xpeer)],
        11: [lambda: sum_o.fourth(o[1])],
        12: [lambda: sum_a.second(a[2]), lambda: sum_a.third(a[1]), lambda: sum_a.fourth(a[0]), lambda: sum_o.fourth(o[2]), v_along],
        13: [lambda: sum_o.fourth(o[3])],
        14: [lambda: sum_a.second(a[3]), lambda: sum_a.third(a[2]), lambda: sum_a.fourth(a[1])],
        15: [v_end],
        16: [lambda: sum_a.third(a[3]), lambda: sum_a.fourth(a[2])],
    }
    ended = 0
    for k in range(8, chunks):
        g_step(k)
        for step in after.pop(k, ()):
            step()
        while ended < k - 4:
            g_end(ended)
            ended += 1
    for key in sorted(after):
        for step in after[key]:
            step()
    sum_a.fourth(a[3])
    for k in range(ended, chunks):
        g_end(k)
    grad_o[...] = sum_o.total()
    for one in sent_down:
        one.wait_recv()
    loads["dw"].wait()
    loads["da"].wait()
    grad_d[...] += dz[...].astype(F32) + dx[...].astype(F32) + down[...].astype(F32)
    grad_qkv_out[...] = sum_a.total()
    for copy in started:
        copy.wait_send()
    saved.wait()
    stores[chunks - 2].wait()
    stores[chunks - 1].wait()


def finish(dh, cot, middle, w_out, w_attn, mixed, probs, qkv, ext, normed, tokens, gd, gd_rest, gi, gain_attn, gain_ffn, squares, seq):
    rows, model_width = dh.shape
    depth, slot, units = seq // 2, model_width // seq, gi.shape[-1]
    kv_rows, cols = 2 * HD // seq, model_width // 4
    blocks, _, _, _, reach = probs.shape
    chunks = 2 * units // GRAD_COLS
    qkv_slot = slot + kv_rows
    step = 128
    dma = pltpu.SemaphoreType.DMA
    hbm, vm = pl.BlockSpec(memory_space=pl.ANY), pl.BlockSpec(memory_space=pltpu.VMEM)

    def sum_buffers(n):
        return [
            pltpu.VMEM((depth, 2, 2, n, cols), BF16),
            pltpu.VMEM((depth, 2, n, cols), BF16),
            pltpu.VMEM((depth, n, cols), BF16),
            pltpu.VMEM((depth - 1, n, cols), BF16),
        ]

    sum_sems = [dma((depth, 2)), dma((depth, 2)), dma((depth,)), dma((depth,)), dma((depth,)), dma((depth,)), dma((depth - 1,)), dma((depth - 1,))]

    def kernel(*refs):
        refs = list(refs)
        at = len(refs) - 18
        o_sems, a_sems = refs[at : at + 8], refs[at + 8 : at + 16]
        finish_kernel(*refs[:at], o_sems, a_sems, *refs[at + 16 :])

    return pl.pallas_call(
        kernel,
        name="finish",
        out_shape=[
            jax.ShapeDtypeStruct((rows, model_width), F32),
            jax.ShapeDtypeStruct((slot, units), F32),
            jax.ShapeDtypeStruct((2, slot, units), F32),
            jax.ShapeDtypeStruct((qkv_slot, cols), F32),
            jax.ShapeDtypeStruct((slot, cols), F32),
            jax.ShapeDtypeStruct((8, model_width), F32),
        ],
        in_specs=[hbm] * 15 + [vm] * 3,
        out_specs=[hbm, vm, hbm] + [vm] * 3,
        scratch_shapes=[
            pltpu.VMEM((rows, model_width), F32),
            pltpu.VMEM((rows, model_width), F32),
            pltpu.VMEM((2, step, model_width), F32),
            pltpu.VMEM(w_attn.shape, BF16),
            pltpu.VMEM((rows, model_width), BF16),
            pltpu.VMEM((2, 2, QROWS, reach), BF16),
            pltpu.VMEM(qkv.shape, BF16),
            pltpu.VMEM(ext.shape, BF16),
            pltpu.VMEM((rows, model_width), BF16),
            pltpu.VMEM(qkv.shape, BF16),
            pltpu.VMEM((rows, model_width), BF16),
            pltpu.VMEM(ext.shape, F32),
            pltpu.VMEM((2, rows, 2 * HD), BF16),
            pltpu.VMEM((2, rows, 2 * HD), BF16),
            pltpu.VMEM((chunks, depth, slot, GRAD_COLS), BF16),
            pltpu.VMEM((chunks, depth - 1, slot, GRAD_COLS), BF16),
            pltpu.VMEM((2, depth, slot, GRAD_COLS), BF16),
            pltpu.VMEM((2, slot, GRAD_COLS), F32),
            pltpu.VMEM((slot, units), BF16),
            pltpu.VMEM((slot, units), BF16),
            pltpu.VMEM((slot, units), BF16),
            pltpu.VMEM((depth, 2, slot, model_width), BF16),
            pltpu.VMEM((depth, 2, qkv_slot, model_width), BF16),
        ]
        + sum_buffers(slot)
        + sum_buffers(qkv_slot)
        + [pltpu.VMEM((6 + depth, 8, model_width), F32)]
        + [
            dma((12,)), dma((2,)), dma((2,)), dma((2,)), dma((2,)), dma((2,)), dma((2,)), dma((2,)),
            dma((chunks,)), dma((chunks,)), dma((chunks, depth - 1)), dma((chunks, depth - 1)),
        ]
        + sum_sems
        + sum_sems
        + [dma((2 + depth,)), dma((2 + depth,))],
        compiler_params=pltpu.CompilerParams(collective_id=1, has_side_effects=True, vmem_limit_bytes=63 << 20),
    )(
        dh, cot, middle, w_out, w_attn, mixed, probs, qkv, ext, normed, tokens,
        gd, *gd_rest, gi.reshape(2, depth, 2, slot, units),
        gain_attn.reshape(1, -1), gain_ffn.reshape(1, -1), squares,
    )


SHARERS = 8


def begin_kernel(lengths, tokens_hbm, w_attn_hbm, w_out_hbm, gain_attn, gain_ffn,
                 attn_out, out_out, qkv_out, ext_out, normed_out, mixed_out, probs_out, middle_out, low_out, valid_out, count_out,
                 tokens, normed, w_attn, w_out, qkv, ext, mixed, probs, bias, acc, counts,
                 load, c_send, c_recv, o_send, o_recv, s_send, s_recv, h_send, h_recv, n_send, n_recv, p_store, store):
    seq, wt = lax.axis_index("seq"), lax.axis_index("wt")
    n_seq = lax.axis_size("seq")
    y, c = wt // 2, wt % 2
    w_sib, w_peer, w_far = 2 * y + 1 - c, 2 * (1 - y) + c, 2 * (1 - y) + 1 - c
    sib, peer = (seq, w_sib), (seq, w_peer)
    rows, width = tokens.shape
    depth = w_attn_hbm.shape[0]
    pairs = width // (2 * HD)
    blocks, reach = rows // QROWS, WINDOW + QROWS
    slabs = WINDOW // rows
    first = seq // SHARERS * SHARERS
    place = lax.rem(seq, SHARERS)
    others = [(first + lax.rem(place + n, SHARERS), wt) for n in range(1, SHARERS)]
    ahead = [(lax.rem(seq + n, n_seq), wt) for n in range(1, slabs + 1)]
    behind = [(lax.rem(seq + n_seq - n, n_seq), wt) for n in range(1, slabs + 1)]

    def fetch(src, dst, sem):
        copy = pltpu.make_async_copy(src, dst, sem)
        copy.start()
        return copy

    def shard(w, size=None, at=0):
        return pl.ds(pl.multiple_of(w * depth + at, 16), depth if size is None else size)

    loads = [
        fetch(tokens_hbm, tokens, load.at[0]),
        fetch(w_attn_hbm, w_attn.at[shard(wt)], load.at[1]),
        fetch(w_out_hbm, w_out.at[shard(wt)], load.at[2]),
    ]
    greet([sib, peer] + others + (ahead + behind if n_seq > SHARERS else []))
    started = []

    def go(*args):
        started.append(remote(*args))
        return started[-1]

    def chunk(k):
        return pl.ds(pl.multiple_of(lax.rem(k + pairs, pairs + 1) * 2 * HD, 2 * HD), 2 * HD)

    def chunk_copy(kind, k):
        at = chunk(k)
        w, to = ((wt, peer), (wt, sib), (w_peer, sib))[kind]
        src = w_attn_hbm.at[:, at] if kind < 2 else w_attn.at[shard(w), at]
        return pltpu.make_async_remote_copy(
            src_ref=src, dst_ref=w_attn.at[shard(w), at], send_sem=c_send.at[kind, k], recv_sem=c_recv.at[kind, k],
            device_id=to, device_id_type=MESH)

    def arrived(kind, k):
        w = (w_peer, w_sib, w_far)[kind]
        at = chunk(k)
        here = w_attn.at[shard(w), at]
        pltpu.make_async_copy(here, here, c_recv.at[kind, k]).wait()

    chunk_copy(0, 0).start()
    slice_rows = depth // SHARERS

    def slice_at(w, n):
        return shard(w, slice_rows, n * slice_rows)

    mine = pl.ds(pl.multiple_of(place * slice_rows, 16), slice_rows)
    for k in range(pairs + 1):
        chunk_copy(1, k).start()
    whole = go(w_out_hbm, w_out.at[shard(wt)], o_send.at[1], o_recv.at[1], sib)

    def send_after(k):
        chunk_copy(0, k).wait_send()
        chunk_copy(0, k + 1).start()

    n_len = lengths.shape[1]
    ends = [lengths[0, 0]]
    for n in range(1, n_len):
        ends.append(ends[-1] + lengths[0, n])
    stream = n_seq * rows

    def ids(positions):
        number = jnp.zeros(positions.shape, jnp.int32) - 1
        for n in range(n_len):
            start = ends[n - 1] if n else 0
            number += (positions >= start).astype(jnp.int32)
        inside = (positions >= 0) & (positions < ends[-1])
        return jnp.where(inside, number, -(positions + 2 * stream))

    base = seq * rows
    q_ids = ids(lax.broadcasted_iota(jnp.int32, (rows, 1), 0) + base)
    k_ids = ids(lax.broadcasted_iota(jnp.int32, (1, rows + WINDOW), 1) + (base - WINDOW))
    valid_out[...] = (q_ids >= 0).astype(F32)
    counts[0] = jnp.full(counts.shape[1:], ends[-1]).astype(F32)
    number = go(counts.at[0], counts.at[1], n_send.at[0], n_recv.at[0], sib)

    loads[0].wait()
    part = 128

    def norm_rows(n, _):
        r = pl.ds(pl.multiple_of(n * part, part), part)
        values = tokens[r, :].astype(F32)
        scale = lax.rsqrt(jnp.mean(values * values, axis=-1, keepdims=True) + EPSILON)
        normed[r, :] = (values * scale * gain_attn[...]).astype(BF16)
        return 0

    lax.fori_loop(0, rows // part, norm_rows, 0)
    stores = [fetch(normed, normed_out, store.at[0])]
    for i in range(blocks):
        row = lax.broadcasted_iota(jnp.int32, (QROWS, reach), 0)
        offset = lax.broadcasted_iota(jnp.int32, (QROWS, reach), 1) - WINDOW - row
        here, there = q_ids[i * QROWS : (i + 1) * QROWS], k_ids[:, i * QROWS : i * QROWS + reach]
        bias[i] = jnp.where((offset <= 0) & (offset > -WINDOW) & (here == there), 0.0, NEGATIVE)
    number.wait_recv()
    counts[2] = counts[0] + counts[1]
    send_after(0)

    def relay(k):
        arrived(0, k)
        chunk_copy(2, k).start()

    loads[1].wait()
    relay(0)
    arrived(1, 0)
    arrived(2, 0)
    kv_cols = slice(width, width + 2 * HD)
    key_value = contract(normed[...], w_attn[:, kv_cols], 1, 0).astype(BF16)
    qkv[:, kv_cols] = key_value
    ext[WINDOW:, :] = key_value
    halo = {}

    def halo_send(half):
        for n in range(slabs):
            cols, at = pl.ds(half * HD, HD), half * slabs + n
            dst = ext.at[pl.ds(WINDOW - (n + 1) * rows, rows), cols]
            halo[half, n] = remote(ext.at[pl.ds(WINDOW, rows), cols], dst, h_send.at[at], h_recv.at[at], ahead[n])

    halo_send(0)

    def project_queries(p):
        cols = pl.ds(pl.multiple_of(p * 2 * HD, 2 * HD), 2 * HD)
        arrived(1, p + 1)
        arrived(2, p + 1)
        qkv[:, cols] = contract(normed[...], w_attn[:, cols], 1, 0).astype(BF16)

    send_after(1)
    relay(1)
    number = go(counts.at[2], counts.at[3], n_send.at[1], n_recv.at[1], peer)
    eighth = go(w_out_hbm.at[mine], w_out.at[slice_at(wt, place)], o_send.at[0], o_recv.at[0], peer)
    project_queries(0)
    for n in range(slabs):
        halo[0, n].wait_send()
    halo_send(1)
    send_after(2)
    relay(2)
    for n in range(slabs):
        halo[0, n].wait_recv()
    eighth.wait_recv()
    spread = [
        go(w_out.at[slice_at(w_peer, place)], w_out.at[slice_at(w_peer, place)], s_send.at[n], s_recv.at[n], others[n])
        for n in range(SHARERS - 1)
    ]
    number.wait_recv()
    count_out[...] = counts[2] + counts[3]
    factor = math.log2(math.e) / math.sqrt(HD)

    def p_copy(i, p):
        return pltpu.make_async_copy(probs.at[i], probs_out.at[i, p], p_store.at[i])

    def heads(p, _, values=None):
        @pl.when(jnp.asarray(p) + 3 <= pairs)
        def _():
            relay(p + 3)

        @pl.when(jnp.asarray(p) + 4 <= pairs)
        def _():
            send_after(p + 3)

        @pl.when(jnp.asarray(p) + 1 < pairs)
        def _():
            project_queries(p + 1)

        cols = pl.ds(pl.multiple_of(p * 2 * HD, 2 * HD), 2 * HD)
        for i in range(blocks):
            q_rows, keys = pl.ds(i * QROWS, QROWS), pl.ds(i * QROWS, reach)
            scores = contract(pair_rows(qkv[q_rows, cols]), ext[keys, :HD], 1, 1) * factor
            shifted = scores.reshape(2, QROWS, reach) + bias[i][None]
            powers = jnp.exp2(shifted - jnp.max(shifted, axis=-1, keepdims=True))
            weights = (powers * (1.0 / jnp.sum(powers, axis=-1, keepdims=True))).astype(BF16)

            @pl.when(jnp.asarray(p) > 0)
            def _():
                p_copy(i, p - 1).wait()

            probs[i] = weights
            p_copy(i, p).start()
            if values is not None and i == 0:
                for one in values:
                    one.wait_recv()
            outs = contract(weights.reshape(2 * QROWS, reach), ext[keys, HD:], 1, 0)
            mixed[q_rows, cols] = pair_columns(outs).astype(BF16)
        return 0

    heads(0, 0, [halo[1, n] for n in range(slabs)])
    stores.append(fetch(ext, ext_out, store.at[1]))
    lax.fori_loop(1, pairs - 1, heads, 0)
    for one in spread:
        one.wait_recv()
    passed = go(w_out.at[shard(w_peer)], w_out.at[shard(w_peer)], o_send.at[2], o_recv.at[2], sib)
    heads(pairs - 1, 0)
    stores += [fetch(qkv, qkv_out, store.at[2]), fetch(mixed, mixed_out, store.at[3]), fetch(w_attn, attn_out, store.at[4])]
    loads[2].wait()
    whole.wait_recv()
    passed.wait_recv()
    stores.append(fetch(w_out, out_out, store.at[5]))

    def project(cols):
        acc[:, cols] = tokens[:, cols].astype(F32) + contract(mixed[...], w_out[:, cols], 1, 0)

    tiles(width, 512, project)
    stores.append(fetch(acc, middle_out, store.at[6]))
    stores[0].wait()

    def norm_again(n, _):
        r = pl.ds(pl.multiple_of(n * part, part), part)
        values = acc[r, :]
        scale = lax.rsqrt(jnp.mean(values * values, axis=-1, keepdims=True) + EPSILON)
        normed[r, :] = (values * scale * gain_ffn[...]).astype(BF16)
        return 0

    lax.fori_loop(0, rows // part, norm_again, 0)
    stores.append(fetch(normed, low_out, store.at[0]))
    for i in range(blocks):
        p_copy(i, pairs - 1).wait()
    for one in stores[1:]:
        one.wait()
    chunk_copy(0, pairs).wait_send()
    for k in range(pairs + 1):
        for kind in range(1, 3):
            chunk_copy(kind, k).wait_send()
    for one in started + [halo[1, n] for n in range(slabs)]:
        one.wait_send()


def begin(lengths, tokens, w_attn, w_out, gain_attn, gain_ffn):
    rows, width = tokens.shape
    shards = 4
    depth = w_out.shape[0]
    pairs, blocks, reach = width // (2 * HD), rows // QROWS, WINDOW + QROWS
    columns = width + 2 * HD
    dma = pltpu.SemaphoreType.DMA
    hbm, vm = pl.BlockSpec(memory_space=pl.ANY), pl.BlockSpec(memory_space=pltpu.VMEM)
    shape = jax.ShapeDtypeStruct
    return pl.pallas_call(
        begin_kernel,
        name="begin",
        out_shape=[
            shape((width, columns), BF16),
            shape((width, width), BF16),
            shape((rows, columns), BF16),
            shape((rows + WINDOW, 2 * HD), BF16),
            shape((rows, width), BF16),
            shape((rows, width), BF16),
            shape((blocks, pairs, 2, QROWS, reach), BF16),
            shape((rows, width), F32),
            shape((rows, width), BF16),
            shape((rows, 1), F32),
            shape((8, 128), F32),
        ],
        in_specs=[pl.BlockSpec(memory_space=pltpu.SMEM)] + [hbm] * 3 + [vm] * 2,
        out_specs=[hbm] * 9 + [vm] * 2,
        scratch_shapes=[
            pltpu.VMEM((rows, width), BF16),
            pltpu.VMEM((rows, width), BF16),
            pltpu.VMEM((shards * depth, columns), BF16),
            pltpu.VMEM((shards * depth, width), BF16),
            pltpu.VMEM((rows, columns), BF16),
            pltpu.VMEM((rows + WINDOW, 2 * HD), BF16),
            pltpu.VMEM((rows, width), BF16),
            pltpu.VMEM((blocks, 2, QROWS, reach), BF16),
            pltpu.VMEM((blocks, QROWS, reach), F32),
            pltpu.VMEM((rows, width), F32),
            pltpu.VMEM((4, 8, 128), F32),
            dma((3,)), dma((3, pairs + 1)), dma((3, pairs + 1)), dma((3,)), dma((3,)), dma((SHARERS - 1,)), dma((SHARERS - 1,)),
            dma((2 * WINDOW // rows,)), dma((2 * WINDOW // rows,)), dma((2,)), dma((2,)), dma((blocks,)), dma((7,)),
        ],
        compiler_params=pltpu.CompilerParams(collective_id=3, has_side_effects=True, vmem_limit_bytes=60 << 20),
    )(lengths, tokens, w_attn, w_out, gain_attn.reshape(1, -1), gain_ffn.reshape(1, -1))


def passed_along(block, axis, distance):
    devices = range(lax.axis_size(axis))
    route = [(i - distance, i) for i in devices if i - distance in devices]
    return lax.ppermute(block, axis, route)


def rms_scale(values, gain):
    return values * lax.rsqrt(jnp.mean(values * values, axis=-1, keepdims=True) + EPSILON) * gain


def per_device(tokens, teacher, seq_lengths, w_attn, w_out, w_in, w_down, gain_attn, gain_ffn):
    tok_rows = tokens.shape[1]
    model_width = tokens.shape[2]
    seq_devices = lax.axis_size("seq")
    all_slots = tok_rows * seq_devices * lax.axis_size("wt")
    (attn_full, out_full, qkv, extended, normed, mixed_b, probs, middle, normed_two, valid, count) = begin(
        seq_lengths, tokens[0], w_attn, w_out, gain_attn, gain_ffn
    )
    valid_total = count[0, 0]
    scale_up = all_slots / count[:1, :1]
    w_pair = jnp.swapaxes(w_in, 0, 1)
    slot, kv_slot = model_width // seq_devices, HD // seq_devices
    aligned = seq_devices == 8 and slot % 16 == 0 and kv_slot % 16 == 0
    output, cotangent, grad_norm_two, grad_down, grad_in, squares, grad_down_rest = ffn(
        normed_two, w_pair, w_down, middle, teacher[0], seq_lengths, scale_up, seq_devices if aligned else 0
    )
    if aligned:
        grad_inputs, grad_down, grad_in, grad_attn, grad_out, small = finish(
            grad_norm_two, cotangent, middle, out_full, attn_full, mixed_b, probs, qkv, extended, normed, tokens[0],
            grad_down, grad_down_rest, grad_in, gain_attn, gain_ffn, squares, seq_devices,
        )
    else:
        _, norm_one_pull = jax.vjp(rms_scale, tokens[0].astype(jnp.float32), gain_attn)
        _, norm_two_pull = jax.vjp(rms_scale, middle, gain_ffn)
        grad_middle_norm, grad_gain_ffn = norm_two_pull(grad_norm_two)
        grad_middle = cotangent + grad_middle_norm
        grad_mid_low = grad_middle.astype(jnp.bfloat16)
        grad_out = jnp.einsum("te,td->ed", grad_mid_low, mixed_b, preferred_element_type=jnp.float32)
        grad_mixed = jnp.einsum("te,de->td", grad_mid_low, out_full, preferred_element_type=jnp.float32)
        grad_query, grad_ext = attend_back(qkv, extended, grad_mixed.astype(jnp.bfloat16), mixed_b, probs)
        edge_rows = WINDOW
        grad_kv = grad_ext[edge_rows:]
        for back_step in range(1, WINDOW // tok_rows + 1):
            slab_rows = grad_ext[
                edge_rows - back_step * tok_rows : edge_rows - (back_step - 1) * tok_rows
            ]
            grad_kv = grad_kv + passed_along(slab_rows, "seq", -back_step)
        grad_key = (grad_kv[:, :HD] * (1.0 / math.sqrt(HD))).astype(jnp.bfloat16)
        grad_qkv = jnp.concatenate([grad_query, grad_key, grad_kv[:, HD:].astype(jnp.bfloat16)], axis=1)
        grad_attn = jnp.einsum("te,td->ed", grad_qkv, normed, preferred_element_type=jnp.float32)
        grad_normed = jnp.einsum("te,de->td", grad_qkv, attn_full, preferred_element_type=jnp.float32)
        grad_input_norm, grad_gain_attn = norm_one_pull(grad_normed)
        grad_inputs = grad_middle + grad_input_norm
        grad_attn = grad_attn.astype(jnp.bfloat16)
        grad_key, grad_value = (
            grad_attn[model_width + at : model_width + at + HD].reshape(seq_devices, kv_slot, model_width) for at in (0, HD)
        )
        packed = jnp.concatenate(
            [
                grad_attn[:model_width].reshape(seq_devices, slot, model_width),
                grad_key,
                grad_value,
                grad_out.astype(jnp.bfloat16).reshape(seq_devices, slot, model_width),
            ],
            axis=1,
        )
        small = jnp.stack([grad_gain_attn, grad_gain_ffn, jnp.full((model_width,), squares[0, 0])] + [jnp.zeros_like(grad_gain_attn)] * 5)
        grad_down, grad_in = grad_down.reshape(seq_devices, slot, -1), grad_in.reshape(2, seq_devices, slot, -1)
        grad_down, grad_in, packed, small = reduce_plain(grad_down, grad_in, packed, small)
        grad_attn, grad_out = packed[:-slot], packed[-slot:]
    grad_queries = grad_attn[:slot].T
    grad_keyvals = grad_attn[slot:].T.reshape(-1, 2, kv_slot)
    grad_out = grad_out.T
    grad_down = grad_down.T
    grad_in = jnp.swapaxes(grad_in, 0, 1)
    gain_attn_all, gain_ffn_all, squares_all = small[0], small[1], small[2, 0]
    loss = squares_all / (valid_total * model_width)
    return (
        output[None],
        loss,
        grad_inputs[None],
        grad_queries,
        grad_keyvals,
        grad_out,
        grad_in,
        grad_down,
        gain_attn_all,
        gain_ffn_all,
    )


def solution(mesh):
    in_specs = (
        P("wt", "seq", None),
        P("wt", "seq", None),
        P("wt", None),
        P("wt", None),
        P("wt", None),
        P(None, None, "wt"),
        P("wt", None),
        P(),
        P(),
    )
    out_specs = (
        P("wt", "seq", None),
        P(),
        P("wt", "seq", None),
        P("wt", "seq"),
        P("wt", None, "seq"),
        P("wt", "seq"),
        P("seq", None, "wt"),
        P("wt", "seq"),
        P(),
        P(),
    )
    return jax.shard_map(
        per_device, mesh=mesh, in_specs=in_specs, out_specs=out_specs, check_vma=False
    )
```

```python
import functools
import math

import jax
import jax.numpy as jnp
from jax import lax
from jax.experimental import pallas as pl
from jax.experimental.pallas import tpu as pltpu
from jax.sharding import PartitionSpec as P

HEADS = 12
HD = 128
WINDOW = 1024
QROWS = 256


EPSILON = 1e-06
NEGATIVE = -1e30

MESH = pl.DeviceIdType.MESH
F32 = jnp.float32
BF16 = jnp.bfloat16


def places():
    seq, wt = lax.axis_index("seq"), lax.axis_index("wt")
    return seq // 2, seq % 2, wt // 2, wt % 2


def device(z, x, y, c):
    return (z * 2 + x, y * 2 + c)


def remote(src, dst, send, recv, to):
    copy = pltpu.make_async_remote_copy(
        src_ref=src, dst_ref=dst, send_sem=send, recv_sem=recv, device_id=to, device_id_type=MESH
    )
    copy.start()
    return copy


def greet(devices):
    barrier = pltpu.get_barrier_semaphore()
    for one in devices:
        pl.semaphore_signal(barrier, inc=1, device_id=one, device_id_type=MESH)
    pl.semaphore_wait(barrier, len(devices))


def reduce_plain(gd, gi, p, v):
    gd = lax.psum_scatter(gd, "seq", scatter_dimension=0, tiled=False).astype(F32)
    gi = lax.psum_scatter(gi, "seq", scatter_dimension=1, tiled=False).astype(F32)
    p = lax.psum_scatter(p, "seq", scatter_dimension=0, tiled=False)
    p = lax.psum_scatter(p, "wt", scatter_dimension=1, tiled=True).astype(F32)
    return gd, gi, p, lax.psum(v, ("seq", "wt"))


def contract(a, b, dim_a, dim_b):
    return lax.dot_general(a, b, (((dim_a,), (dim_b,)), ((), ())), preferred_element_type=F32)


def tiles(total, width, body):
    def step(i, _):
        body(pl.ds(pl.multiple_of(i * width, width), width))
        return 0

    lax.fori_loop(0, total // width, step, 0)


def flat(block):
    return block.reshape(-1, block.shape[-1])


def ffn_kernel(share, h, wi_hbm, wd_hbm, mid_hbm, teacher_hbm, lengths, count, out, cot, dh, gd, gi, squares, gd_owner, gd_whole,
               wi, wd, mid, teacher, hall, dall, act, hid, acc, far, out_low, sent, got,
               load, h_send, h_recv, d_send, d_recv, p_send, p_recv, store, g_store, *sharing):
    z, x, y, c = places()
    sib, peer = device(z, x, y, 1 - c), device(z, x, 1 - y, c)
    half, width = h.shape[1:]
    units = wd.shape[0]

    def fetch(src, dst, sem):
        copy = pltpu.make_async_copy(src, dst, sem)
        copy.start()
        return copy

    loads = [fetch(*pair, load.at[n]) for n, pair in enumerate(
        ((h, hall.at[0]), (wi_hbm, wi), (wd_hbm, wd), (teacher_hbm, teacher)))]
    if share:
        gx, gz, gxs, gxr, gzs, gzr, end = sharing
        depth, slot = lax.axis_size("seq") // 2, gx.shape[1]
        zs = [lax.rem(z + d, depth) for d in range(depth)]
        xpeer, zpeers = device(z, 1 - x, y, c), [device(zs[d], x, y, c) for d in range(depth)]
    greet([sib, peer] + ([xpeer] + zpeers[1:] if share else []))
    pending = []

    def go(*args):
        nonlocal pending
        pending.append(remote(*args))
        return pending[-1]

    def spread(src, dst, send, recv, j):
        a = go(src.at[j], dst.at[2, j], send.at[0, j], recv.at[0, j], peer)
        b = go(src.at[j], dst.at[1, j], send.at[1, j], recv.at[1, j], sib)
        return a, b

    def relay(dst, send, recv, j):
        return go(dst.at[2, j], dst.at[3, j], send.at[2, j], recv.at[2, j], sib)

    def group(ref, g):
        return ref.at[2:4, g - 2] if g >= 2 else ref.at[g]

    h_copies = [spread(h, hall, h_send, h_recv, j) for j in range(2)]

    def gated(g):
        rows = flat(group(hall, g)[...])

        def body(cols):
            mid[:, :, :384] = contract(rows, wi[0, :, cols], 1, 0).reshape(2, half, -1)
            mid[:, :, 384:768] = contract(rows, wi[1, :, cols], 1, 0).reshape(2, half, -1)
            block = half // 2

            def finish_rows(i, _):
                j, r = i // 2, pl.ds(pl.multiple_of(lax.rem(i, 2) * block, block), block)
                gate, up = mid[j, r, :384], mid[j, r, 384:768]
                square = gate * gate
                turn = jnp.tanh(gate * (0.7978845608028654 + 0.035677408136300125 * square))
                upper = 0.5 + 0.5 * turn
                value = gate * upper
                slope = upper + 0.5 * gate * (1.0 - turn * turn) * (0.7978845608028654 + 0.10703222440890038 * square)
                group(hid, g)[j, r, cols] = (value * up).astype(BF16)
                group(act.at[0], g)[j, r, cols] = (slope * up).astype(BF16)
                group(act.at[1], g)[j, r, cols] = value.astype(BF16)
                return 0

            lax.fori_loop(0, 4, finish_rows, 0)

        tiles(units, 384, body)

    def emit(g, cols, part):
        if g == 0:
            acc[:, :, cols] = part.reshape(2, half, -1)
        elif g == 1:
            sent[0, :, :, cols] = part.astype(BF16).reshape(2, half, -1)
        else:
            far[:, cols] = part[:half]
            sent[1, g - 2, :, cols] = part[half:].astype(BF16)

    def down(g):
        rows = flat(group(hid, g)[...])
        tiles(width, 512, lambda cols: emit(g, cols, contract(rows, wd[:, cols], 1, 0)))

    def push(phase, kind, j):
        return go(sent.at[kind, j], got.at[kind, j], p_send.at[phase, kind, j], p_recv.at[phase, kind, j], peer if kind == 2 else sib)

    def sums(phase, compute, copies, buffer, send, recv, before):
        kept = {}
        compute(0)
        for j in range(2):
            copies[j][1].wait_recv()
        compute(1)
        for j in range(2):
            kept[0, j] = push(phase, 0, j)
        for j in range(2):
            copies[j][0].wait_recv()
            passed = relay(buffer, send, recv, j)
            passed.wait_recv()
            if phase == 1 and j == 1 and share:
                down_tile(0)
            compute(2 + j)
            kept[1, j] = push(phase, 1, j)
            kept[1, j].wait_recv()
            sent[2, j] = (far[...] + got[1, j].astype(F32)).astype(BF16)
            kept[2, j] = push(phase, 2, j)
        return kept

    def forward(g):
        gated(g)
        down(g)

    for one in loads[:3]:
        one.wait()
    kept = sums(0, forward, h_copies, hall, h_send, h_recv, None)
    first, pending = pending, []
    loads.append(fetch(mid_hbm, mid, load.at[4]))
    loads[3].wait()
    loads[4].wait()
    total = jnp.zeros((), F32)
    d_copies, saves = [], []
    factor = (8.0 * half * lax.axis_size("seq")) / count[0:1, 0:1]
    first_row = lax.axis_index("seq") * 2 * half
    used = lengths[0, 0]
    for n in range(1, lengths.shape[1]):
        used += lengths[0, n]
    for j in range(2):
        kept[0, j].wait_recv()
        kept[2, j].wait_recv()
        step = half // 4

        def rows_of(i, so_far):
            r = pl.ds(pl.multiple_of(i * step, step), step)
            value = mid[j, r, :] + acc[j, r, :] + got[0, j, r, :].astype(F32) + got[2, j, r, :].astype(F32)
            out_low[j, r, :] = value.astype(BF16)
            diff = value - teacher[j, r, :].astype(F32)
            place = lax.broadcasted_iota(jnp.int32, (step, 1), 0) + (first_row + j * half + i * step)
            masked = (place < used).astype(F32) * diff
            grad = masked * factor
            mid[j, r, :] = grad
            dall[0, j, r, :] = grad.astype(BF16)
            return so_far + jnp.sum(masked * diff)

        total = lax.fori_loop(0, 4, rows_of, total)
        d_copies.append(spread(dall.at[0], dall, d_send, d_recv, j))
        saves.append(fetch(out_low.at[j], out.at[j], store.at[0, j]))
        saves.append(fetch(mid.at[j], cot.at[j], store.at[1, j]))
    squares[...] = jnp.full(squares.shape, total)

    def backward(g):
        rows = flat(group(dall, g)[...])

        def body(cols):
            grad = contract(rows, wd[cols, :], 1, 1).reshape(2, half, -1)
            for n in range(2):
                part = group(act.at[n], g)
                part[:, :, cols] = (grad * part[:, :, cols].astype(F32)).astype(BF16)

        tiles(units, 384, body)
        gate, up = flat(group(act.at[0], g)[...]), flat(group(act.at[1], g)[...])
        tiles(width, 512, lambda cols: emit(g, cols, contract(gate, wi[0, cols, :], 1, 1) + contract(up, wi[1, cols, :], 1, 1)))

    for copy in first:
        copy.wait_send()
    order = sorted(range(depth), key=lambda d: (d == 0, abs(2 * d - depth))) if share else []
    parts = [teacher.at[:, :slot, :units], out_low.at[:, :slot, :units]] if share else []
    stage = [wd.at[pl.ds(n * 256, 256), :units] for n in range(2)]
    swaps, owners = {}, {}

    def down_tile(n):
        if n >= 2:
            swaps[n - 2].wait_send()
        else:
            saves[2 * n].wait()
        cols = pl.ds(pl.multiple_of(zs[order[n]] * 2 * slot, 128), 2 * slot)
        left = dall[:, :, :, cols].reshape(8 * half, 2 * slot)

        parts[n % 2][...] = contract(left, hid[...].reshape(8 * half, units), 0, 0).astype(BF16).reshape(2, slot, units)
        if n == 0:
            down_swap(0)

    def down_swap(n):
        swaps[n] = remote(parts[n % 2].at[1 - x], gx.at[n], gxs.at[n], gxr.at[n], xpeer)

    def down_owner(n):
        swaps[n].wait_recv()
        gx[n] = (parts[n % 2][x].astype(F32) + gx[n].astype(F32)).astype(BF16)
        if n < 2:
            owners[n] = go(gx.at[n], gz.at[n], gzs.at[n], gzr.at[n], zpeers[order[n]])

    kept = sums(1, backward, d_copies, dall, d_send, d_recv, None)
    count = 0
    blocks = width // 256
    left, right = {}, {}

    def weight(left, right, target):
        def body(i, _):
            for n in range(2):
                at = pl.ds(pl.multiple_of(i * 512 + n * 256, 256), 256)

                @pl.when(i > 0)
                def _():
                    pltpu.make_async_copy(stage[n], target.at[at], g_store.at[n]).wait()

                stage[n][...] = contract(left(at), right(), 0, 0).astype(BF16)
                pltpu.make_async_copy(stage[n], target.at[at], g_store.at[n]).start()
            return 0

        lax.fori_loop(0, width // 512, body, 0)
        for n in range(2):
            pltpu.make_async_copy(stage[n], target.at[pl.ds(0, 256)], g_store.at[n]).wait()

    if not share:
        weight(lambda at: flat(dall[:, :, :, at].reshape(4, 2 * half, 256)), lambda: flat(hid[...].reshape(4, 2 * half, units)), gd)
    for n in range(2):
        if share:
            down_tile(n + 1)
            down_swap(n + 1)
        weight(lambda at: flat(hall[:, :, :, at].reshape(4, 2 * half, 256)), lambda n=n: flat(act[n].reshape(4, 2 * half, units)), gi.at[n])
        if share:
            down_owner(n)
    if share:
        down_tile(3)
        ends = [fetch(parts[1], gd_whole, end.at[0])]
    for j in range(2):
        kept[0, j].wait_recv()
        kept[2, j].wait_recv()
        saves[2 * j + 1].wait()

        def sum_rows(i, _):
            r = pl.ds(pl.multiple_of(i * step, step), step)
            mid[j, r, :] = acc[j, r, :] + got[0, j, r, :].astype(F32) + got[2, j, r, :].astype(F32)
            return 0

        lax.fori_loop(0, 4, sum_rows, 0)
        saves.append(fetch(mid.at[j], dh.at[j], store.at[2, j]))
    if share:
        down_owner(2)
        ends.append(fetch(gx.at[2], gd_owner, end.at[1]))
        for n in range(2):
            owners[n].wait_recv()
        far[:slot, :units] = gz[0].astype(F32) + gz[1].astype(F32)
        ends.append(fetch(far.at[:slot, :units], gd, end.at[2]))
        swaps[2].wait_send()
        for one in ends:
            one.wait()
    for copy in pending:
        copy.wait_send()
    for n in (4, 5) if share else (0, 2, 4, 5):
        saves[n].wait()


def ffn(h, wi, wd, mid, teacher, lengths, count, seq):
    rows, width = h.shape
    depth, slot = (seq // 2, width // seq) if seq else (0, 0)
    units = wd.shape[0]
    half = rows // 2
    split = lambda a: a.reshape(2, half, a.shape[-1])
    dma = pltpu.SemaphoreType.DMA
    hbm, vm = pl.BlockSpec(memory_space=pl.ANY), pl.BlockSpec(memory_space=pltpu.VMEM)
    def kernel(*refs):
        ffn_kernel(bool(seq), *(refs if seq else refs[:13] + (None, None) + refs[13:]))

    sharing = []
    if seq:
        sharing = [
            pltpu.VMEM((3, slot, units), BF16), pltpu.VMEM((2, slot, units), BF16),
            dma((3,)), dma((3,)), dma((2,)), dma((2,)), dma((3,)),
        ]
    out, cot, dh, gd, gi, squares, *rest = pl.pallas_call(
        kernel,
        name="ffn",
        out_shape=[
            jax.ShapeDtypeStruct((2, half, width), BF16),
            jax.ShapeDtypeStruct((2, half, width), F32),
            jax.ShapeDtypeStruct((2, half, width), F32),
            jax.ShapeDtypeStruct((slot, units), F32) if seq else jax.ShapeDtypeStruct((width, units), BF16),
            jax.ShapeDtypeStruct((2, width, units), BF16),
            jax.ShapeDtypeStruct((8, 128), F32),
        ]
        + [jax.ShapeDtypeStruct((slot, units), BF16), jax.ShapeDtypeStruct((2, slot, units), BF16)] * bool(seq),
        in_specs=[hbm] * 5 + [pl.BlockSpec(memory_space=pltpu.SMEM), vm],
        out_specs=[hbm] * 5 + [vm] + [hbm, hbm] * bool(seq),
        scratch_shapes=[
            pltpu.VMEM((2, width, units), BF16),
            pltpu.VMEM((units, width), BF16),
            pltpu.VMEM((2, half, width), F32),
            pltpu.VMEM((2, half, width), BF16),
            pltpu.VMEM((4, 2, half, width), BF16),
            pltpu.VMEM((4, 2, half, width), BF16),
            pltpu.VMEM((2, 4, 2, half, units), BF16),
            pltpu.VMEM((4, 2, half, units), BF16),
            pltpu.VMEM((2, half, width), F32),
            pltpu.VMEM((half, width), F32),
            pltpu.VMEM((2, half, width), BF16),
            pltpu.VMEM((3, 2, half, width), BF16),
            pltpu.VMEM((3, 2, half, width), BF16),
            dma((5,)), dma((3, 2)), dma((3, 2)), dma((3, 2)), dma((3, 2)),
            dma((2, 3, 2)), dma((2, 3, 2)), dma((3, 2)), dma((2,)),
        ]
        + sharing,
        compiler_params=pltpu.CompilerParams(collective_id=2, has_side_effects=True, vmem_limit_bytes=63 << 20),
    )(split(h), wi, wd, split(mid), split(teacher), lengths, count)
    return out.reshape(rows, width), cot.reshape(rows, width), dh.reshape(rows, width), gd, gi, squares, rest


def pair_rows(block):
    return jnp.concatenate([block[:, :HD], block[:, HD:]], axis=0)


def pair_columns(block):
    rows = block.shape[0] // 2
    return jnp.concatenate([block[:rows], block[rows:]], axis=1)


def attend_back_kernel(q, kv, grad, mixed, probs, grad_q, grad_kv):
    i, pair = pl.program_id(0), pl.program_id(1)
    reach = WINDOW + QROWS
    keys = pl.ds(pl.multiple_of(i * QROWS, QROWS), reach)

    @pl.when((i == 0) & (pair == 0))
    def _():
        grad_kv[...] = jnp.zeros_like(grad_kv)

    queries, grads = pair_rows(q[...]), pair_rows(grad[...])
    weights = probs[0, 0].reshape(2 * QROWS, reach)
    dots = jnp.sum(grads.astype(F32) * pair_rows(mixed[...]).astype(F32), axis=-1, keepdims=True)
    steep = contract(grads, kv[keys, HD:], 1, 1) - dots
    steep = (weights.astype(F32) * steep).astype(BF16)
    grad_q[...] = (pair_columns(contract(steep, kv[keys, :HD], 1, 0)) * (1.0 / math.sqrt(HD))).astype(BF16)
    grad_kv[keys, :HD] += contract(steep, queries, 0, 0)
    grad_kv[keys, HD:] += contract(weights, grads, 0, 0)


def attend_back(queries, extended, grad_mixed, mixed, probs):
    rows, width = mixed.shape
    blocks, pairs, reach = rows // QROWS, width // (2 * HD), WINDOW + QROWS
    block = pl.BlockSpec((QROWS, 2 * HD), lambda i, p: (i, p))
    whole = pl.BlockSpec(extended.shape, lambda i, p: (0, 0))
    return pl.pallas_call(
        attend_back_kernel,
        name="attend_back",
        grid=(blocks, pairs),
        out_shape=[jax.ShapeDtypeStruct((rows, width), BF16), jax.ShapeDtypeStruct(extended.shape, F32)],
        in_specs=[block, whole, block, block, pl.BlockSpec((1, 1, 2, QROWS, reach), lambda i, p: (i, p, 0, 0, 0))],
        out_specs=[block, whole],
        compiler_params=pltpu.CompilerParams(vmem_limit_bytes=48 << 20),
    )(queries, extended, grad_mixed, mixed, probs)


GRAD_COLS = 128
AHEAD = 3


def owner_order(depth):
    return sorted(range(depth), key=lambda d: (d == 0, abs(2 * d - depth)))


class RowSum:
    def __init__(self, source, buffers, sems, where, go):
        self.source, self.go = source, go
        self.core, self.side, self.cross, self.along = buffers
        self.cs, self.cr, self.ys, self.yr, self.xs, self.xr, self.zs_, self.zr = sems
        self.x, self.y, self.c, self.zs, self.sib, self.ypeer, self.xpeer, self.zpeers = where
        self.depth, self.cols = len(self.zs), self.core.shape[-1]
        self.order = owner_order(self.depth)
        self.moved = {}

    def columns(self, y, c):
        return pl.ds(pl.multiple_of((2 * y + c) * self.cols, self.cols), self.cols)

    def first(self, d):
        for h in range(2):
            part = self.source.at[self.zs[d], :, :, self.columns(h, 1 - self.c)]
            self.moved["c", d, h] = self.go(part, self.core.at[d, h], self.cs.at[d, h], self.cr.at[d, h], self.sib)

    def second(self, d):
        for h in range(2):
            self.moved["c", d, h].wait_recv()
        far = 1 - self.y
        own = self.source[self.zs[d], :, :, self.columns(far, self.c)].astype(F32)
        self.core[d, far] = (own + self.core[d, far].astype(F32)).astype(BF16)
        self.moved["y", d] = self.go(self.core.at[d, far], self.side.at[d], self.ys.at[d], self.yr.at[d], self.ypeer)

    def kept(self, d, x):
        own = self.source[self.zs[d], x, :, self.columns(self.y, self.c)].astype(F32)
        return own + self.core[d, self.y, x].astype(F32) + self.side[d, x].astype(F32)

    def third(self, d):
        self.moved["y", d].wait_recv()
        self.side[d, 1 - self.x] = self.kept(d, 1 - self.x).astype(BF16)
        self.moved["x", d] = self.go(self.side.at[d, 1 - self.x], self.cross.at[d], self.xs.at[d], self.xr.at[d], self.xpeer)

    def fourth(self, d):
        self.moved["x", d].wait_recv()
        self.cross[d] = (self.kept(d, self.x) + self.cross[d].astype(F32)).astype(BF16)
        if d:
            self.moved["z", d] = self.go(
                self.cross.at[d], self.along.at[d - 1], self.zs_.at[d - 1], self.zr.at[d - 1], self.zpeers[d]
            )

    def total(self):
        value = self.cross[0].astype(F32)
        for d in range(1, self.depth):
            self.moved["z", d].wait_recv()
            value += self.along[d - 1].astype(F32)
        return value


def norm_back(values, grad, gain):
    r = lax.rsqrt(jnp.mean(values * values, axis=-1, keepdims=True) + EPSILON)
    scaled = grad * gain
    slope = r * r * r * jnp.mean(values * scaled, axis=-1, keepdims=True)
    return r * scaled - values * slope, jnp.sum(grad * values * r, axis=0, keepdims=True)


def finish_kernel(dh_hbm, cot_hbm, middle_hbm, w_out_hbm, w_attn_hbm, mixed_hbm, probs_hbm, qkv_hbm, ext_hbm, normed_hbm,
                  tokens_hbm, gd_hbm, gd_owner, gd_whole, gi_hbm, gain_attn, gain_ffn, squares, count,
                  grad_x, grad_d, grad_i, grad_qkv_out, grad_o, gain_attn_out, gain_ffn_out, loss_out,
                  dh, cot, middle, weight, mixed, probs, qkv, ext, normed, low, dmix, dkv, slabs, slabs_in,
                  gx, gz, gr, own, staged, dx, dz, down, po, pa, ocore, oside, ocross, oalong, acore, aside, across, aalong, vb,
                  load, p_load, own_load, out_sem, slab_s, slab_r, ds, dr, gxs, gxr, gzs, gzr, grr, o_sems, a_sems, vs, vr):
    z, x, y, c = places()
    depth, width = own.shape[1], own.shape[-1]
    rows, model_width = dh.shape
    units = gi_hbm.shape[-1]
    seq = 2 * depth
    me = 2 * z + x
    sib, ypeer, xpeer = device(z, x, y, 1 - c), device(z, x, 1 - y, c), device(z, 1 - x, y, c)
    zs = [lax.rem(z + d, depth) for d in range(depth)]
    zpeers = [device(zs[d], x, y, c) for d in range(depth)]
    wt = 2 * y + c
    diagonal = (lax.rem(me + seq - 1 + 2 * x, seq), wt)
    back = [(lax.rem(me + seq - step, seq), wt) for step in (1, 2)]

    def fetch(src, dst, sem):
        copy = pltpu.make_async_copy(src, dst, sem)
        copy.start()
        return copy

    loads = {}
    for n, (name, src, dst) in enumerate((
        ("dh", dh_hbm, dh), ("cot", cot_hbm, cot), ("w_out", w_out_hbm, weight.at[:, :model_width]), ("mixed", mixed_hbm, mixed),
        ("qkv", qkv_hbm, qkv), ("ext", ext_hbm, ext), ("normed", normed_hbm, normed))):
        loads[name] = fetch(src, dst, load.at[n])
    greet([sib, ypeer, xpeer, diagonal] + zpeers[1:])
    started = []

    def go(*args):
        started.append(remote(*args))
        return started[-1]

    spots = [(n, at) for n in range(2) for at in range(0, units, width)]
    chunks = len(spots)
    gxc, gzc, owned = {}, {}, {}

    def g_ref(k, side):
        n, at = spots[k]
        return gi_hbm.at[n, :, side, :, pl.ds(at, width)]

    def g_send(k):
        if k < chunks:
            gxc[k] = go(g_ref(k, 1 - x), gx.at[k], gxs.at[k], gxr.at[k], xpeer)

    def g_load(k):
        if k < chunks:
            owned[k] = fetch(g_ref(k, x), own.at[k % 2], own_load.at[k % 2])

    def at_end(d):
        return ((z == 0) & (d == depth - 1)) | ((z == depth - 1) & (d == 1))

    def g_copy(k, d, dst, recv, to):
        return pltpu.make_async_remote_copy(
            src_ref=gx.at[k, zs[d]], dst_ref=dst, send_sem=gzs.at[k, d - 1], recv_sem=recv, device_id=to, device_id_type=MESH)

    def g_owner(k, d):
        return g_copy(k, d, gz.at[k, d - 1], gzr.at[k, d - 1], zpeers[d])

    def g_neighbour(k, d):
        return g_copy(k, d, gr.at[k], grr.at[k], zpeers[depth - d])

    def g_step(k):
        gxc[k].wait_recv()
        g_send(k + AHEAD)
        owned[k].wait()
        for d in range(depth):
            gx[k, zs[d]] = (own[k % 2, zs[d]].astype(F32) + gx[k, zs[d]].astype(F32)).astype(BF16)
            if d == 1 or d == depth - 1:
                pl.when(at_end(d))(lambda d=d: g_neighbour(k, d).start())
                pl.when(jnp.logical_not(at_end(d)))(lambda d=d: g_owner(k, d).start())
        g_load(k + 2)
        if k >= 2:
            g_relay(k - 2)

    def g_relay(k):
        @pl.when((z > 0) & (z < depth - 1))
        def _():
            g_copy(k, 2, gr.at[k], grr.at[k], zpeers[2]).wait_recv()
            gx[k, zs[2]] = (gx[k, zs[2]].astype(F32) + gr[k].astype(F32)).astype(BF16)

        g_owner(k, 2).start()

    stores = {}

    def g_end(k):
        if k >= 2:
            stores[k - 2].wait()
        at = k % 2
        staged[at] = gx[k, z].astype(F32)
        for d in range(1, depth):
            missing = ((z == depth - 1) & (d == depth - 1)) | ((z == 0) & (d == 1))

            @pl.when(jnp.logical_not(missing))
            def _():
                g_owner(k, d).wait_recv()
                staged[at] += gz[k, d - 1].astype(F32)

        n, column = spots[k]
        stores[k] = fetch(staged.at[at], grad_i.at[n, :, pl.ds(column, width)], out_sem.at[at])

    last = owner_order(depth)[2]
    sent_down = [
        go(gd_owner, dz, ds.at[0], dr.at[0], zpeers[last]),
        go(gd_whole.at[1 - x], dx, ds.at[1], dr.at[1], xpeer),
    ]
    loads["dw"] = fetch(gd_whole.at[x], down, load.at[10])
    loads["da"] = fetch(gd_hbm, grad_d, load.at[11])
    for k in range(AHEAD):
        g_send(k)
    g_load(0)
    g_load(1)
    where = (x, y, c, zs, sib, ypeer, xpeer, zpeers)
    sum_o = RowSum(po, (ocore, oside, ocross, oalong), o_sems, where, go)
    sum_a = RowSum(pa, (acore, aside, across, aalong), a_sems, where, go)

    step = middle.shape[1]
    steps = rows // step
    mids = [None] * steps

    def mid_load(n):
        if n < steps:
            mids[n] = fetch(middle_hbm.at[pl.ds(n * step, step)], middle.at[n % 2], load.at[8 + n % 2])

    mid_load(0)
    mid_load(1)
    loads["dh"].wait()
    loads["cot"].wait()
    gain_grad = jnp.zeros((1, model_width), F32)
    scale_ffn, scale_attn = as_row(gain_ffn), as_row(gain_attn)
    for n in range(steps):
        mids[n].wait()
        r = pl.ds(n * step, step)
        grad, part = norm_back(middle[n % 2], dh[r, :], scale_ffn)
        grad = cot[r, :] + grad
        cot[r, :] = grad
        low[r, :model_width] = grad.astype(BF16)
        gain_grad += part
        mid_load(n + 2)
    vb[0] = jnp.zeros(vb.shape[1:], F32)
    vb[0, 1:2] = gain_grad
    vb[0, 2:3] = jnp.broadcast_to(squares[0:1, 0:1], (1, model_width))
    loads["w_out"].wait()
    loads["mixed"].wait()
    rows_low = lambda: low[:, :model_width]

    def out_back(cols):
        dmix[:, cols] = contract(rows_low(), weight[cols, :model_width], 1, 1).astype(BF16)

    tiles(model_width, 512, out_back)
    loads["w_attn"] = fetch(w_attn_hbm, weight, load.at[7])

    def out_grad(d, _):
        cols = pl.ds(pl.multiple_of(d * 2 * po.shape[2], 128), 2 * po.shape[2])
        po[d] = contract(low[:, cols], mixed[...], 0, 0).astype(BF16).reshape(po.shape[1:])
        return 0

    lax.fori_loop(0, depth, out_grad, 0)
    for d in sum_o.order:
        sum_o.first(d)
    g_step(0)
    g_step(1)
    blocks, pairs, reach = probs_hbm.shape[0], probs_hbm.shape[1], probs.shape[-1]
    turns = blocks * pairs

    def p_fetch(t):
        return pltpu.make_async_copy(probs_hbm.at[t // pairs, t % pairs], probs.at[t % 2], p_load.at[t % 2])

    p_fetch(0).start()
    p_fetch(1).start()
    dkv[...] = jnp.zeros_like(dkv)
    loads["qkv"].wait()
    loads["ext"].wait()
    for i in range(blocks):
        q_rows, keys = pl.ds(i * QROWS, QROWS), pl.ds(i * QROWS, reach)

        def one(pair, _):
            t = i * pairs + pair
            cols = pl.ds(pl.multiple_of(pair * 2 * HD, 2 * HD), 2 * HD)
            queries, grads = pair_rows(qkv[q_rows, cols]), pair_rows(dmix[q_rows, cols])
            outs = pair_rows(mixed[q_rows, cols])
            dots = jnp.sum(grads.astype(F32) * outs.astype(F32), axis=-1, keepdims=True)
            slot = lax.rem(t, 2)
            p_fetch(t).wait()
            weights = flat(probs[slot])
            steep = contract(grads, ext[keys, HD:], 1, 1) - dots
            steep = (weights.astype(F32) * steep).astype(BF16)
            low[q_rows, cols] = (pair_columns(contract(steep, ext[keys, :HD], 1, 0)) * (1.0 / math.sqrt(HD))).astype(BF16)
            dkv[keys, :HD] += contract(steep, queries, 0, 0)
            dkv[keys, HD:] += contract(weights, grads, 0, 0)

            @pl.when(t + 2 < turns)
            def _():
                p_fetch(t + 2).start()

            return 0

        lax.fori_loop(0, pairs // 2, one, 0)
        if i == 0:
            for d in sum_o.order:
                sum_o.second(d)
        g_step(2 + 2 * i)
        lax.fori_loop(pairs // 2, pairs, one, 0)
        g_step(3 + 2 * i)
    for n in range(2):
        slabs[n] = dkv[(1 - n) * rows : (2 - n) * rows, :].astype(BF16)
    returned = [go(slabs.at[n], slabs_in.at[n], slab_s.at[n], slab_r.at[n], back[n]) for n in range(2)]
    loads["normed"].wait()
    slot_rows = model_width // seq

    def query_grad(d, _):
        cols = pl.ds(pl.multiple_of(d * 2 * slot_rows, 128), 2 * slot_rows)
        pa[d, :, :slot_rows] = contract(low[:, cols], normed[...], 0, 0).astype(BF16).reshape(2, slot_rows, model_width)
        return 0

    lax.fori_loop(0, depth, query_grad, 0)
    g_step(6)
    for one in returned:
        one.wait_recv()
    summed = dkv[2 * rows :, :] + slabs_in[0].astype(F32) + slabs_in[1].astype(F32)
    low[:, model_width : model_width + HD] = (summed[:, :HD] * (1.0 / math.sqrt(HD))).astype(BF16)
    low[:, model_width + HD :] = summed[:, HD:].astype(BF16)
    kv_grad = contract(low[:, model_width:], normed[...], 0, 0).astype(BF16)
    kv_rows = HD // seq
    for n in range(2):
        part = kv_grad[n * HD : (n + 1) * HD].reshape(depth, 2, kv_rows, model_width)
        pa[:, :, slot_rows + n * kv_rows : slot_rows + (n + 1) * kv_rows] = part
    for d in sum_a.order:
        sum_a.first(d)
    loads["tokens"] = fetch(tokens_hbm, mixed, load.at[3])
    loads["w_attn"].wait()

    def attn_back(cols):
        dh[:, cols] = contract(low[...], weight[cols, :], 1, 1)

    tiles(model_width, 512, attn_back)
    g_step(7)
    loads["tokens"].wait()

    def last_norm(n, so_far):
        r = pl.ds(pl.multiple_of(n * step, step), step)
        grad, part = norm_back(mixed[r, :].astype(F32), dh[r, :], scale_attn)
        cot[r, :] += grad
        return so_far + part

    vb[0, 0:1] = lax.fori_loop(0, steps, last_norm, jnp.zeros((1, model_width), F32))
    saved = fetch(cot, grad_x, load.at[0])

    vc = {}

    def v_first():
        vc[0] = go(vb.at[0], vb.at[1], vs.at[0], vr.at[0], sib)

    def v_swap(n, to):
        vc[n - 1].wait_recv()
        vb[2 * n] = vb[2 * n - 2] + vb[2 * n - 1]
        vc[n] = go(vb.at[2 * n], vb.at[2 * n + 1], vs.at[n], vr.at[n], to)

    def v_along():
        vc[2].wait_recv()
        vb[6] = vb[4] + vb[5]
        for d in range(1, depth):
            vc[2 + d] = go(vb.at[6], vb.at[6 + d], vs.at[2 + d], vr.at[2 + d], zpeers[d])

    def v_end():
        for d in range(1, depth):
            vc[2 + d].wait_recv()
        total = vb[6 + z]
        for n in range(1, depth):
            total += vb[6 + lax.rem(z - n + depth, depth)]
        gain_attn_out[...] = as_lines(total[0:1])
        gain_ffn_out[...] = as_lines(total[1:2])
        loss_out[...] = total[2:3, 0:1] / (count[0:1, 0:1] * model_width)

    v_first()
    o, a = sum_o.order, sum_a.order
    after = {
        8: [lambda: sum_a.second(a[0]), lambda: sum_o.third(o[0]), lambda: sum_o.third(o[1]), lambda: v_swap(1, ypeer)],
        9: [lambda: sum_o.third(o[2]), lambda: sum_o.third(o[3])],
        10: [lambda: sum_a.second(a[1]), lambda: sum_a.third(a[0]), lambda: sum_o.fourth(o[0]), lambda: v_swap(2, xpeer)],
        11: [lambda: sum_o.fourth(o[1])],
        12: [lambda: sum_a.second(a[2]), lambda: sum_a.third(a[1]), lambda: sum_a.fourth(a[0]), lambda: sum_o.fourth(o[2]), v_along],
        13: [lambda: sum_o.fourth(o[3])],
        14: [lambda: sum_a.second(a[3]), lambda: sum_a.third(a[2]), lambda: sum_a.fourth(a[1])],
        15: [v_end],
        16: [lambda: sum_a.third(a[3]), lambda: sum_a.fourth(a[2])],
    }
    ended = 0
    for k in range(8, chunks):
        g_step(k)
        for step in after.pop(k, ()):
            step()
        while ended < k - 4:
            g_end(ended)
            ended += 1
    g_relay(chunks - 2)
    g_relay(chunks - 1)
    for key in sorted(after):
        for step in after[key]:
            step()
    sum_a.fourth(a[3])
    for k in range(ended, chunks):
        g_end(k)
    grad_o[...] = sum_o.total()
    for one in sent_down:
        one.wait_recv()
    loads["dw"].wait()
    loads["da"].wait()
    grad_d[...] += dz[...].astype(F32) + dx[...].astype(F32) + down[...].astype(F32)
    grad_qkv_out[...] = sum_a.total()
    for copy in started:
        copy.wait_send()
    for k in range(chunks):
        for d in range(1, depth):
            g_owner(k, d).wait_send()
    saved.wait()
    stores[chunks - 2].wait()
    stores[chunks - 1].wait()


def finish(dh, cot, middle, w_out, w_attn, mixed, probs, qkv, ext, normed, tokens, gd, gd_rest, gi, gain_attn, gain_ffn, squares, count, seq):
    rows, model_width = dh.shape
    depth, slot, units = seq // 2, model_width // seq, gi.shape[-1]
    kv_rows, cols = 2 * HD // seq, model_width // 4
    blocks, _, _, _, reach = probs.shape
    chunks = 2 * units // GRAD_COLS
    qkv_slot = slot + kv_rows
    step = 128
    dma = pltpu.SemaphoreType.DMA
    hbm, vm = pl.BlockSpec(memory_space=pl.ANY), pl.BlockSpec(memory_space=pltpu.VMEM)

    def sum_buffers(n):
        return [
            pltpu.VMEM((depth, 2, 2, n, cols), BF16),
            pltpu.VMEM((depth, 2, n, cols), BF16),
            pltpu.VMEM((depth, n, cols), BF16),
            pltpu.VMEM((depth - 1, n, cols), BF16),
        ]

    sum_sems = [dma((depth, 2)), dma((depth, 2)), dma((depth,)), dma((depth,)), dma((depth,)), dma((depth,)), dma((depth - 1,)), dma((depth - 1,))]

    def kernel(*refs):
        refs = list(refs)
        at = len(refs) - 18
        o_sems, a_sems = refs[at : at + 8], refs[at + 8 : at + 16]
        finish_kernel(*refs[:at], o_sems, a_sems, *refs[at + 16 :])

    return pl.pallas_call(
        kernel,
        name="finish",
        out_shape=[
            jax.ShapeDtypeStruct((rows, model_width), F32),
            jax.ShapeDtypeStruct((slot, units), F32),
            jax.ShapeDtypeStruct((2, slot, units), F32),
            jax.ShapeDtypeStruct((qkv_slot, cols), F32),
            jax.ShapeDtypeStruct((slot, cols), F32),
            jax.ShapeDtypeStruct((model_width // 128, 128), F32),
            jax.ShapeDtypeStruct((model_width // 128, 128), F32),
            jax.ShapeDtypeStruct((1, 1), F32),
        ],
        in_specs=[hbm] * 15 + [vm] * 4,
        out_specs=[hbm, vm, hbm] + [vm] * 5,
        scratch_shapes=[
            pltpu.VMEM((rows, model_width), F32),
            pltpu.VMEM((rows, model_width), F32),
            pltpu.VMEM((2, step, model_width), F32),
            pltpu.VMEM(w_attn.shape, BF16),
            pltpu.VMEM((rows, model_width), BF16),
            pltpu.VMEM((2, 2, QROWS, reach), BF16),
            pltpu.VMEM(qkv.shape, BF16),
            pltpu.VMEM(ext.shape, BF16),
            pltpu.VMEM((rows, model_width), BF16),
            pltpu.VMEM(qkv.shape, BF16),
            pltpu.VMEM((rows, model_width), BF16),
            pltpu.VMEM(ext.shape, F32),
            pltpu.VMEM((2, rows, 2 * HD), BF16),
            pltpu.VMEM((2, rows, 2 * HD), BF16),
            pltpu.VMEM((chunks, depth, slot, GRAD_COLS), BF16),
            pltpu.VMEM((chunks, depth - 1, slot, GRAD_COLS), BF16),
            pltpu.VMEM((chunks, slot, GRAD_COLS), BF16),
            pltpu.VMEM((2, depth, slot, GRAD_COLS), BF16),
            pltpu.VMEM((2, slot, GRAD_COLS), F32),
            pltpu.VMEM((slot, units), BF16),
            pltpu.VMEM((slot, units), BF16),
            pltpu.VMEM((slot, units), BF16),
            pltpu.VMEM((depth, 2, slot, model_width), BF16),
            pltpu.VMEM((depth, 2, qkv_slot, model_width), BF16),
        ]
        + sum_buffers(slot)
        + sum_buffers(qkv_slot)
        + [pltpu.VMEM((6 + depth, 8, model_width), F32)]
        + [
            dma((12,)), dma((2,)), dma((2,)), dma((2,)), dma((2,)), dma((2,)), dma((2,)), dma((2,)),
            dma((chunks,)), dma((chunks,)), dma((chunks, depth - 1)), dma((chunks, depth - 1)), dma((chunks,)),
        ]
        + sum_sems
        + sum_sems
        + [dma((2 + depth,)), dma((2 + depth,))],
        compiler_params=pltpu.CompilerParams(collective_id=1, has_side_effects=True, vmem_limit_bytes=63 << 20),
    )(
        dh, cot, middle, w_out, w_attn, mixed, probs, qkv, ext, normed, tokens,
        gd, *gd_rest, gi.reshape(2, depth, 2, slot, units),
        gain_attn.reshape(-1, 128), gain_ffn.reshape(-1, 128), squares, count,
    )


SHARERS = 8


def as_row(ref):
    return jnp.concatenate([ref[n : n + 1, :] for n in range(ref.shape[0])], axis=1)


def as_lines(row):
    return jnp.concatenate([row[:, n : n + 128] for n in range(0, row.shape[1], 128)], axis=0)


def begin_kernel(lengths, tokens_hbm, w_attn_hbm, w_out_hbm, gain_attn, gain_ffn,
                 attn_out, out_out, qkv_out, ext_out, normed_out, mixed_out, probs_out, middle_out, low_out, count_out,
                 tokens, normed, w_attn, w_out, qkv, ext, mixed, probs, bias, acc, counts,
                 load, c_send, c_recv, o_send, o_recv, s_send, s_recv, h_send, h_recv, n_send, n_recv, p_store, store):
    seq, wt = lax.axis_index("seq"), lax.axis_index("wt")
    n_seq = lax.axis_size("seq")
    y, c = wt // 2, wt % 2
    w_sib, w_peer, w_far = 2 * y + 1 - c, 2 * (1 - y) + c, 2 * (1 - y) + 1 - c
    sib, peer = (seq, w_sib), (seq, w_peer)
    rows, width = tokens.shape
    depth = w_attn_hbm.shape[0]
    pairs = width // (2 * HD)
    blocks, reach = rows // QROWS, WINDOW + QROWS
    slabs = WINDOW // rows
    first = seq // SHARERS * SHARERS
    place = lax.rem(seq, SHARERS)
    others = [(first + lax.rem(place + n, SHARERS), wt) for n in range(1, SHARERS)]
    ahead = [(lax.rem(seq + n, n_seq), wt) for n in range(1, slabs + 1)]
    behind = [(lax.rem(seq + n_seq - n, n_seq), wt) for n in range(1, slabs + 1)]

    def fetch(src, dst, sem):
        copy = pltpu.make_async_copy(src, dst, sem)
        copy.start()
        return copy

    def shard(w, size=None, at=0):
        return pl.ds(pl.multiple_of(w * depth + at, 16), depth if size is None else size)

    loads = [
        fetch(tokens_hbm, tokens, load.at[0]),
        fetch(w_attn_hbm, w_attn.at[shard(wt)], load.at[1]),
        fetch(w_out_hbm, w_out.at[shard(wt)], load.at[2]),
    ]
    greet([sib, peer] + others + (ahead + behind if n_seq > SHARERS else []))
    started = []

    def go(*args):
        started.append(remote(*args))
        return started[-1]

    def chunk(k):
        return pl.ds(pl.multiple_of(lax.rem(k + pairs, pairs + 1) * 2 * HD, 2 * HD), 2 * HD)

    def chunk_copy(kind, k):
        at = chunk(k)
        w, to = ((wt, peer), (wt, sib), (w_peer, sib))[kind]
        src = w_attn_hbm.at[:, at] if kind < 2 else w_attn.at[shard(w), at]
        return pltpu.make_async_remote_copy(
            src_ref=src, dst_ref=w_attn.at[shard(w), at], send_sem=c_send.at[kind, k], recv_sem=c_recv.at[kind, k],
            device_id=to, device_id_type=MESH)

    def arrived(kind, k):
        w = (w_peer, w_sib, w_far)[kind]
        at = chunk(k)
        here = w_attn.at[shard(w), at]
        pltpu.make_async_copy(here, here, c_recv.at[kind, k]).wait()

    chunk_copy(0, 0).start()
    slice_rows = depth // SHARERS

    def slice_at(w, n):
        return shard(w, slice_rows, n * slice_rows)

    mine = pl.ds(pl.multiple_of(place * slice_rows, 16), slice_rows)
    for k in range(pairs + 1):
        chunk_copy(1, k).start()
    whole = go(w_out_hbm, w_out.at[shard(wt)], o_send.at[1], o_recv.at[1], sib)

    def send_after(k):
        chunk_copy(0, k).wait_send()
        chunk_copy(0, k + 1).start()

    n_len = lengths.shape[1]
    ends = [lengths[0, 0]]
    for n in range(1, n_len):
        ends.append(ends[-1] + lengths[0, n])
    stream = n_seq * rows

    def ids(positions):
        number = jnp.zeros(positions.shape, jnp.int32) - 1
        for n in range(n_len):
            start = ends[n - 1] if n else 0
            number += (positions >= start).astype(jnp.int32)
        inside = (positions >= 0) & (positions < ends[-1])
        return jnp.where(inside, number, -(positions + 2 * stream))

    base = seq * rows
    q_ids = ids(lax.broadcasted_iota(jnp.int32, (rows, 1), 0) + base)
    k_ids = ids(lax.broadcasted_iota(jnp.int32, (1, rows + WINDOW), 1) + (base - WINDOW))
    counts[0] = jnp.full(counts.shape[1:], ends[-1]).astype(F32)
    number = go(counts.at[0], counts.at[1], n_send.at[0], n_recv.at[0], sib)

    loads[0].wait()
    scale_attn = as_row(gain_attn)
    part = 128

    def norm_rows(n, _):
        r = pl.ds(pl.multiple_of(n * part, part), part)
        values = tokens[r, :].astype(F32)
        scale = lax.rsqrt(jnp.mean(values * values, axis=-1, keepdims=True) + EPSILON)
        normed[r, :] = (values * scale * scale_attn).astype(BF16)
        return 0

    lax.fori_loop(0, rows // part, norm_rows, 0)
    stores = [fetch(normed, normed_out, store.at[0])]
    for i in range(blocks):
        row = lax.broadcasted_iota(jnp.int32, (QROWS, reach), 0)
        offset = lax.broadcasted_iota(jnp.int32, (QROWS, reach), 1) - WINDOW - row
        here, there = q_ids[i * QROWS : (i + 1) * QROWS], k_ids[:, i * QROWS : i * QROWS + reach]
        bias[i] = jnp.where((offset <= 0) & (offset > -WINDOW) & (here == there), 0.0, NEGATIVE)
    number.wait_recv()
    counts[2] = counts[0] + counts[1]
    send_after(0)

    def relay(k):
        arrived(0, k)
        chunk_copy(2, k).start()

    loads[1].wait()
    relay(0)
    arrived(1, 0)
    arrived(2, 0)
    kv_cols = slice(width, width + 2 * HD)
    key_value = contract(normed[...], w_attn[:, kv_cols], 1, 0).astype(BF16)
    qkv[:, kv_cols] = key_value
    ext[WINDOW:, :] = key_value
    halo = {}

    def halo_send(half):
        for n in range(slabs):
            cols, at = pl.ds(half * HD, HD), half * slabs + n
            dst = ext.at[pl.ds(WINDOW - (n + 1) * rows, rows), cols]
            halo[half, n] = remote(ext.at[pl.ds(WINDOW, rows), cols], dst, h_send.at[at], h_recv.at[at], ahead[n])

    halo_send(0)

    def project_queries(p):
        cols = pl.ds(pl.multiple_of(p * 2 * HD, 2 * HD), 2 * HD)
        arrived(1, p + 1)
        arrived(2, p + 1)
        qkv[:, cols] = contract(normed[...], w_attn[:, cols], 1, 0).astype(BF16)

    send_after(1)
    relay(1)
    number = go(counts.at[2], counts.at[3], n_send.at[1], n_recv.at[1], peer)
    eighth = go(w_out_hbm.at[mine], w_out.at[slice_at(wt, place)], o_send.at[0], o_recv.at[0], peer)
    project_queries(0)
    for n in range(slabs):
        halo[0, n].wait_send()
    halo_send(1)
    send_after(2)
    relay(2)
    for n in range(slabs):
        halo[0, n].wait_recv()
    eighth.wait_recv()
    spread = [
        go(w_out.at[slice_at(w_peer, place)], w_out.at[slice_at(w_peer, place)], s_send.at[n], s_recv.at[n], others[n])
        for n in range(SHARERS - 1)
    ]
    number.wait_recv()
    count_out[...] = counts[2] + counts[3]
    factor = math.log2(math.e) / math.sqrt(HD)

    def p_copy(i, p):
        return pltpu.make_async_copy(probs.at[i], probs_out.at[i, p], p_store.at[i])

    def heads(p, _, values=None):
        @pl.when(jnp.asarray(p) + 3 <= pairs)
        def _():
            relay(p + 3)

        @pl.when(jnp.asarray(p) + 4 <= pairs)
        def _():
            send_after(p + 3)

        @pl.when(jnp.asarray(p) + 1 < pairs)
        def _():
            project_queries(p + 1)

        cols = pl.ds(pl.multiple_of(p * 2 * HD, 2 * HD), 2 * HD)
        for i in range(blocks):
            q_rows, keys = pl.ds(i * QROWS, QROWS), pl.ds(i * QROWS, reach)
            scores = contract(pair_rows(qkv[q_rows, cols]), ext[keys, :HD], 1, 1) * factor
            shifted = scores.reshape(2, QROWS, reach) + bias[i][None]
            powers = jnp.exp2(shifted - jnp.max(shifted, axis=-1, keepdims=True))
            weights = (powers * (1.0 / jnp.sum(powers, axis=-1, keepdims=True))).astype(BF16)

            @pl.when(jnp.asarray(p) > 0)
            def _():
                p_copy(i, p - 1).wait()

            probs[i] = weights
            p_copy(i, p).start()
            if values is not None and i == 0:
                for one in values:
                    one.wait_recv()
            outs = contract(weights.reshape(2 * QROWS, reach), ext[keys, HD:], 1, 0)
            mixed[q_rows, cols] = pair_columns(outs).astype(BF16)
        return 0

    heads(0, 0, [halo[1, n] for n in range(slabs)])
    stores.append(fetch(ext, ext_out, store.at[1]))
    lax.fori_loop(1, pairs - 1, heads, 0)
    for one in spread:
        one.wait_recv()
    passed = go(w_out.at[shard(w_peer)], w_out.at[shard(w_peer)], o_send.at[2], o_recv.at[2], sib)
    heads(pairs - 1, 0)
    stores += [fetch(qkv, qkv_out, store.at[2]), fetch(mixed, mixed_out, store.at[3]), fetch(w_attn, attn_out, store.at[4])]
    loads[2].wait()
    whole.wait_recv()
    passed.wait_recv()
    stores.append(fetch(w_out, out_out, store.at[5]))

    def project(cols):
        acc[:, cols] = tokens[:, cols].astype(F32) + contract(mixed[...], w_out[:, cols], 1, 0)

    tiles(width, 512, project)
    stores.append(fetch(acc, middle_out, store.at[6]))
    stores[0].wait()

    scale_ffn = as_row(gain_ffn)

    def norm_again(n, _):
        r = pl.ds(pl.multiple_of(n * part, part), part)
        values = acc[r, :]
        scale = lax.rsqrt(jnp.mean(values * values, axis=-1, keepdims=True) + EPSILON)
        normed[r, :] = (values * scale * scale_ffn).astype(BF16)
        return 0

    lax.fori_loop(0, rows // part, norm_again, 0)
    stores.append(fetch(normed, low_out, store.at[0]))
    for i in range(blocks):
        p_copy(i, pairs - 1).wait()
    for one in stores[1:]:
        one.wait()
    chunk_copy(0, pairs).wait_send()
    for k in range(pairs + 1):
        for kind in range(1, 3):
            chunk_copy(kind, k).wait_send()
    for one in started + [halo[1, n] for n in range(slabs)]:
        one.wait_send()


def begin(lengths, tokens, w_attn, w_out, gain_attn, gain_ffn):
    rows, width = tokens.shape
    shards = 4
    depth = w_out.shape[0]
    pairs, blocks, reach = width // (2 * HD), rows // QROWS, WINDOW + QROWS
    columns = width + 2 * HD
    dma = pltpu.SemaphoreType.DMA
    hbm, vm = pl.BlockSpec(memory_space=pl.ANY), pl.BlockSpec(memory_space=pltpu.VMEM)
    shape = jax.ShapeDtypeStruct
    return pl.pallas_call(
        begin_kernel,
        name="begin",
        out_shape=[
            shape((width, columns), BF16),
            shape((width, width), BF16),
            shape((rows, columns), BF16),
            shape((rows + WINDOW, 2 * HD), BF16),
            shape((rows, width), BF16),
            shape((rows, width), BF16),
            shape((blocks, pairs, 2, QROWS, reach), BF16),
            shape((rows, width), F32),
            shape((rows, width), BF16),
            shape((8, 128), F32),
        ],
        in_specs=[pl.BlockSpec(memory_space=pltpu.SMEM)] + [hbm] * 3 + [vm] * 2,
        out_specs=[hbm] * 9 + [vm],
        scratch_shapes=[
            pltpu.VMEM((rows, width), BF16),
            pltpu.VMEM((rows, width), BF16),
            pltpu.VMEM((shards * depth, columns), BF16),
            pltpu.VMEM((shards * depth, width), BF16),
            pltpu.VMEM((rows, columns), BF16),
            pltpu.VMEM((rows + WINDOW, 2 * HD), BF16),
            pltpu.VMEM((rows, width), BF16),
            pltpu.VMEM((blocks, 2, QROWS, reach), BF16),
            pltpu.VMEM((blocks, QROWS, reach), F32),
            pltpu.VMEM((rows, width), F32),
            pltpu.VMEM((4, 8, 128), F32),
            dma((3,)), dma((3, pairs + 1)), dma((3, pairs + 1)), dma((3,)), dma((3,)), dma((SHARERS - 1,)), dma((SHARERS - 1,)),
            dma((2 * WINDOW // rows,)), dma((2 * WINDOW // rows,)), dma((2,)), dma((2,)), dma((blocks,)), dma((7,)),
        ],
        compiler_params=pltpu.CompilerParams(collective_id=3, has_side_effects=True, vmem_limit_bytes=60 << 20),
    )(lengths, tokens, w_attn, w_out, gain_attn.reshape(-1, 128), gain_ffn.reshape(-1, 128))


def passed_along(block, axis, distance):
    devices = range(lax.axis_size(axis))
    route = [(i - distance, i) for i in devices if i - distance in devices]
    return lax.ppermute(block, axis, route)


def rms_scale(values, gain):
    return values * lax.rsqrt(jnp.mean(values * values, axis=-1, keepdims=True) + EPSILON) * gain


def per_device(tokens, teacher, seq_lengths, w_attn, w_out, w_in, w_down, gain_attn, gain_ffn):
    tok_rows = tokens.shape[1]
    model_width = tokens.shape[2]
    seq_devices = lax.axis_size("seq")
    (attn_full, out_full, qkv, extended, normed, mixed_b, probs, middle, normed_two, count) = begin(
        seq_lengths, tokens[0], w_attn, w_out, gain_attn, gain_ffn
    )
    w_pair = jnp.swapaxes(w_in, 0, 1)
    slot, kv_slot = model_width // seq_devices, HD // seq_devices
    aligned = seq_devices == 8 and slot % 16 == 0 and kv_slot % 16 == 0
    output, cotangent, grad_norm_two, grad_down, grad_in, squares, grad_down_rest = ffn(
        normed_two, w_pair, w_down, middle, teacher[0], seq_lengths, count, seq_devices if aligned else 0
    )
    if aligned:
        grad_inputs, grad_down, grad_in, grad_attn, grad_out, gain_attn_all, gain_ffn_all, loss = finish(
            grad_norm_two, cotangent, middle, out_full, attn_full, mixed_b, probs, qkv, extended, normed, tokens[0],
            grad_down, grad_down_rest, grad_in, gain_attn, gain_ffn, squares, count, seq_devices,
        )
    else:
        _, norm_one_pull = jax.vjp(rms_scale, tokens[0].astype(jnp.float32), gain_attn)
        _, norm_two_pull = jax.vjp(rms_scale, middle, gain_ffn)
        grad_middle_norm, grad_gain_ffn = norm_two_pull(grad_norm_two)
        grad_middle = cotangent + grad_middle_norm
        grad_mid_low = grad_middle.astype(jnp.bfloat16)
        grad_out = jnp.einsum("te,td->ed", grad_mid_low, mixed_b, preferred_element_type=jnp.float32)
        grad_mixed = jnp.einsum("te,de->td", grad_mid_low, out_full, preferred_element_type=jnp.float32)
        grad_query, grad_ext = attend_back(qkv, extended, grad_mixed.astype(jnp.bfloat16), mixed_b, probs)
        edge_rows = WINDOW
        grad_kv = grad_ext[edge_rows:]
        for back_step in range(1, WINDOW // tok_rows + 1):
            slab_rows = grad_ext[
                edge_rows - back_step * tok_rows : edge_rows - (back_step - 1) * tok_rows
            ]
            grad_kv = grad_kv + passed_along(slab_rows, "seq", -back_step)
        grad_key = (grad_kv[:, :HD] * (1.0 / math.sqrt(HD))).astype(jnp.bfloat16)
        grad_qkv = jnp.concatenate([grad_query, grad_key, grad_kv[:, HD:].astype(jnp.bfloat16)], axis=1)
        grad_attn = jnp.einsum("te,td->ed", grad_qkv, normed, preferred_element_type=jnp.float32)
        grad_normed = jnp.einsum("te,de->td", grad_qkv, attn_full, preferred_element_type=jnp.float32)
        grad_input_norm, grad_gain_attn = norm_one_pull(grad_normed)
        grad_inputs = grad_middle + grad_input_norm
        grad_attn = grad_attn.astype(jnp.bfloat16)
        grad_key, grad_value = (
            grad_attn[model_width + at : model_width + at + HD].reshape(seq_devices, kv_slot, model_width) for at in (0, HD)
        )
        packed = jnp.concatenate(
            [
                grad_attn[:model_width].reshape(seq_devices, slot, model_width),
                grad_key,
                grad_value,
                grad_out.astype(jnp.bfloat16).reshape(seq_devices, slot, model_width),
            ],
            axis=1,
        )
        small = jnp.stack([grad_gain_attn, grad_gain_ffn, jnp.full((model_width,), squares[0, 0])] + [jnp.zeros_like(grad_gain_attn)] * 5)
        grad_down, grad_in = grad_down.reshape(seq_devices, slot, -1), grad_in.reshape(2, seq_devices, slot, -1)
        grad_down, grad_in, packed, small = reduce_plain(grad_down, grad_in, packed, small)
        grad_attn, grad_out = packed[:-slot], packed[-slot:]
        gain_attn_all, gain_ffn_all = small[0], small[1]
        loss = small[2, 0] / (count[0, 0] * model_width)
    grad_queries = grad_attn[:slot].T
    grad_keyvals = grad_attn[slot:].T.reshape(-1, 2, kv_slot)
    grad_out = grad_out.T
    grad_down = grad_down.T
    grad_in = jnp.swapaxes(grad_in, 0, 1)
    return (
        output[None],
        loss.reshape(()),
        grad_inputs[None],
        grad_queries,
        grad_keyvals,
        grad_out,
        grad_in,
        grad_down,
        gain_attn_all.reshape(-1),
        gain_ffn_all.reshape(-1),
    )


def solution(mesh):
    in_specs = (
        P("wt", "seq", None),
        P("wt", "seq", None),
        P("wt", None),
        P("wt", None),
        P("wt", None),
        P(None, None, "wt"),
        P("wt", None),
        P(),
        P(),
    )
    out_specs = (
        P("wt", "seq", None),
        P(),
        P("wt", "seq", None),
        P("wt", "seq"),
        P("wt", None, "seq"),
        P("wt", "seq"),
        P("seq", None, "wt"),
        P("wt", "seq"),
        P(),
        P(),
    )
    return jax.shard_map(
        per_device, mesh=mesh, in_specs=in_specs, out_specs=out_specs, check_vma=False
    )
```

```python
import functools
import math

import jax
import jax.numpy as jnp
from jax import lax
from jax.experimental import pallas as pl
from jax.experimental.pallas import tpu as pltpu
from jax.sharding import PartitionSpec as P

HEADS = 12
HD = 128
WINDOW = 1024
QROWS = 256


EPSILON = 1e-06
NEGATIVE = -1e30

MESH = pl.DeviceIdType.MESH
F32 = jnp.float32
BF16 = jnp.bfloat16


def places():
    seq, wt = lax.axis_index("seq"), lax.axis_index("wt")
    return seq // 2, seq % 2, wt // 2, wt % 2


def device(z, x, y, c):
    return (z * 2 + x, y * 2 + c)


def remote(src, dst, send, recv, to):
    copy = pltpu.make_async_remote_copy(
        src_ref=src, dst_ref=dst, send_sem=send, recv_sem=recv, device_id=to, device_id_type=MESH
    )
    copy.start()
    return copy


def greet(devices):
    barrier = pltpu.get_barrier_semaphore()
    for one in devices:
        pl.semaphore_signal(barrier, inc=1, device_id=one, device_id_type=MESH)
    pl.semaphore_wait(barrier, len(devices))


def reduce_plain(gd, gi, p, v):
    gd = lax.psum_scatter(gd, "seq", scatter_dimension=0, tiled=False).astype(F32)
    gi = lax.psum_scatter(gi, "seq", scatter_dimension=1, tiled=False).astype(F32)
    p = lax.psum_scatter(p, "seq", scatter_dimension=0, tiled=False)
    p = lax.psum_scatter(p, "wt", scatter_dimension=1, tiled=True).astype(F32)
    return gd, gi, p, lax.psum(v, ("seq", "wt"))


def contract(a, b, dim_a, dim_b):
    return lax.dot_general(a, b, (((dim_a,), (dim_b,)), ((), ())), preferred_element_type=F32)


def tiles(total, width, body):
    def step(i, _):
        body(pl.ds(pl.multiple_of(i * width, width), width))
        return 0

    lax.fori_loop(0, total // width, step, 0)


def flat(block):
    return block.reshape(-1, block.shape[-1])


def ffn_kernel(share, h, wi_hbm, wd_hbm, mid_hbm, teacher_hbm, lengths, count, out, cot, dh, gd, gi, squares, gd_owner,
               wi, wd, mid, teacher, hall, dall, act, hid, acc, far, out_low, sent, got,
               load, h_send, h_recv, d_send, d_recv, p_send, p_recv, store, g_store, *sharing):
    z, x, y, c = places()
    sib, peer = device(z, x, y, 1 - c), device(z, x, 1 - y, c)
    half, width = h.shape[1:]
    units = wd.shape[0]

    def fetch(src, dst, sem):
        copy = pltpu.make_async_copy(src, dst, sem)
        copy.start()
        return copy

    loads = [fetch(*pair, load.at[n]) for n, pair in enumerate(
        ((h, hall.at[0]), (wi_hbm, wi), (wd_hbm, wd), (teacher_hbm, teacher)))]
    if share:
        gx, gz, gxs, gxr, gzs, gzr, end = sharing
        depth, slot = lax.axis_size("seq") // 2, gx.shape[1]
        zs = [lax.rem(z + d, depth) for d in range(depth)]
        xpeer, zpeers = device(z, 1 - x, y, c), [device(zs[d], x, y, c) for d in range(depth)]
    greet([sib, peer] + ([xpeer] + zpeers[1:] if share else []))
    pending = []

    def go(*args):
        nonlocal pending
        pending.append(remote(*args))
        return pending[-1]

    def spread(src, dst, send, recv, j):
        a = go(src.at[j], dst.at[2, j], send.at[0, j], recv.at[0, j], peer)
        b = go(src.at[j], dst.at[1, j], send.at[1, j], recv.at[1, j], sib)
        return a, b

    def relay(dst, send, recv, j):
        return go(dst.at[2, j], dst.at[3, j], send.at[2, j], recv.at[2, j], sib)

    def group(ref, g):
        return ref.at[2:4, g - 2] if g >= 2 else ref.at[g]

    h_copies = [spread(h, hall, h_send, h_recv, j) for j in range(2)]

    def gated(g):
        rows = flat(group(hall, g)[...])

        def body(cols):
            mid[:, :, :384] = contract(rows, wi[0, :, cols], 1, 0).reshape(2, half, -1)
            mid[:, :, 384:768] = contract(rows, wi[1, :, cols], 1, 0).reshape(2, half, -1)
            block = half // 2

            def finish_rows(i, _):
                j, r = i // 2, pl.ds(pl.multiple_of(lax.rem(i, 2) * block, block), block)
                gate, up = mid[j, r, :384], mid[j, r, 384:768]
                square = gate * gate
                turn = jnp.tanh(gate * (0.7978845608028654 + 0.035677408136300125 * square))
                upper = 0.5 + 0.5 * turn
                value = gate * upper
                slope = upper + 0.5 * gate * (1.0 - turn * turn) * (0.7978845608028654 + 0.10703222440890038 * square)
                group(hid, g)[j, r, cols] = (value * up).astype(BF16)
                group(act.at[0], g)[j, r, cols] = (slope * up).astype(BF16)
                group(act.at[1], g)[j, r, cols] = value.astype(BF16)
                return 0

            lax.fori_loop(0, 4, finish_rows, 0)

        tiles(units, 384, body)

    def emit(g, cols, part):
        if g == 0:
            acc[:, :, cols] = part.reshape(2, half, -1)
        elif g == 1:
            sent[0, :, :, cols] = part.astype(BF16).reshape(2, half, -1)
        else:
            far[:, cols] = part[:half]
            sent[1, g - 2, :, cols] = part[half:].astype(BF16)

    def down(g):
        rows = flat(group(hid, g)[...])
        tiles(width, 512, lambda cols: emit(g, cols, contract(rows, wd[:, cols], 1, 0)))

    def push(phase, kind, j):
        return go(sent.at[kind, j], got.at[kind, j], p_send.at[phase, kind, j], p_recv.at[phase, kind, j], peer if kind == 2 else sib)

    def sums(phase, compute, copies, buffer, send, recv, before):
        kept = {}
        compute(0)
        for j in range(2):
            copies[j][1].wait_recv()
        compute(1)
        for j in range(2):
            kept[0, j] = push(phase, 0, j)
        for j in range(2):
            copies[j][0].wait_recv()
            passed = relay(buffer, send, recv, j)
            passed.wait_recv()
            if phase == 1 and j == 1 and share:
                down_tile(0)
            compute(2 + j)
            kept[1, j] = push(phase, 1, j)
            kept[1, j].wait_recv()
            sent[2, j] = (far[...] + got[1, j].astype(F32)).astype(BF16)
            kept[2, j] = push(phase, 2, j)
        return kept

    def forward(g):
        gated(g)
        down(g)

    for one in loads[:3]:
        one.wait()
    kept = sums(0, forward, h_copies, hall, h_send, h_recv, None)
    first, pending = pending, []
    loads.append(fetch(mid_hbm, mid, load.at[4]))
    loads[3].wait()
    loads[4].wait()
    total = jnp.zeros((), F32)
    d_copies, saves = [], []
    factor = (8.0 * half * lax.axis_size("seq")) / count[0:1, 0:1]
    first_row = lax.axis_index("seq") * 2 * half
    used = lengths[0, 0]
    for n in range(1, lengths.shape[1]):
        used += lengths[0, n]
    for j in range(2):
        kept[0, j].wait_recv()
        kept[2, j].wait_recv()
        step = half // 4

        def rows_of(i, so_far):
            r = pl.ds(pl.multiple_of(i * step, step), step)
            value = mid[j, r, :] + acc[j, r, :] + got[0, j, r, :].astype(F32) + got[2, j, r, :].astype(F32)
            out_low[j, r, :] = value.astype(BF16)
            diff = value - teacher[j, r, :].astype(F32)
            place = lax.broadcasted_iota(jnp.int32, (step, 1), 0) + (first_row + j * half + i * step)
            masked = (place < used).astype(F32) * diff
            grad = masked * factor
            mid[j, r, :] = grad
            dall[0, j, r, :] = grad.astype(BF16)
            return so_far + jnp.sum(masked * diff)

        total = lax.fori_loop(0, 4, rows_of, total)
        d_copies.append(spread(dall.at[0], dall, d_send, d_recv, j))
        saves.append(fetch(out_low.at[j], out.at[j], store.at[0, j]))
        saves.append(fetch(mid.at[j], cot.at[j], store.at[1, j]))
    squares[...] = jnp.full(squares.shape, total)

    def backward(g):
        rows = flat(group(dall, g)[...])

        def body(cols):
            grad = contract(rows, wd[cols, :], 1, 1).reshape(2, half, -1)
            for n in range(2):
                part = group(act.at[n], g)
                part[:, :, cols] = (grad * part[:, :, cols].astype(F32)).astype(BF16)

        tiles(units, 384, body)
        gate, up = flat(group(act.at[0], g)[...]), flat(group(act.at[1], g)[...])
        tiles(width, 512, lambda cols: emit(g, cols, contract(gate, wi[0, cols, :], 1, 1) + contract(up, wi[1, cols, :], 1, 1)))

    for copy in first:
        copy.wait_send()
    order = sorted(range(depth), key=lambda d: (d == 0, abs(2 * d - depth))) if share else []
    parts = [teacher.at[:, :slot, :units], out_low.at[:, :slot, :units]] if share else []
    stage = [wd.at[pl.ds(n * 256, 256), :units] for n in range(2)]
    swaps, owners = {}, {}

    def down_tile(n):
        if n >= 2:
            swaps[n - 2].wait_send()
        else:
            saves[2 * n].wait()
        cols = pl.ds(pl.multiple_of(zs[order[n]] * 2 * slot, 128), 2 * slot)
        left = dall[:, :, :, cols].reshape(8 * half, 2 * slot)

        parts[n % 2][...] = contract(left, hid[...].reshape(8 * half, units), 0, 0).astype(BF16).reshape(2, slot, units)
        if n == 0:
            down_swap(0)

    def down_swap(n):
        swaps[n] = remote(parts[n % 2].at[1 - x], gx.at[n], gxs.at[n], gxr.at[n], xpeer)

    def down_owner(n):
        swaps[n].wait_recv()
        gx[n] = (parts[n % 2][x].astype(F32) + gx[n].astype(F32)).astype(BF16)
        if n < 2:
            owners[n] = go(gx.at[n], gz.at[n], gzs.at[n], gzr.at[n], zpeers[order[n]])

    kept = sums(1, backward, d_copies, dall, d_send, d_recv, None)
    count = 0
    blocks = width // 256
    left, right = {}, {}

    def weight(left, right, target):
        def body(i, _):
            for n in range(2):
                at = pl.ds(pl.multiple_of(i * 512 + n * 256, 256), 256)

                @pl.when(i > 0)
                def _():
                    pltpu.make_async_copy(stage[n], target.at[at], g_store.at[n]).wait()

                stage[n][...] = contract(left(at), right(), 0, 0).astype(BF16)
                pltpu.make_async_copy(stage[n], target.at[at], g_store.at[n]).start()
            return 0

        lax.fori_loop(0, width // 512, body, 0)
        for n in range(2):
            pltpu.make_async_copy(stage[n], target.at[pl.ds(0, 256)], g_store.at[n]).wait()

    if not share:
        weight(lambda at: flat(dall[:, :, :, at].reshape(4, 2 * half, 256)), lambda: flat(hid[...].reshape(4, 2 * half, units)), gd)
    for n in range(2):
        if share:
            down_tile(n + 1)
            down_swap(n + 1)
            if n == 1:
                down_owner(1)
                down_tile(3)
                down_swap(3)
        weight(lambda at: flat(hall[:, :, :, at].reshape(4, 2 * half, 256)), lambda n=n: flat(act[n].reshape(4, 2 * half, units)), gi.at[n])
        if share and n == 0:
            down_owner(0)
    for j in range(2):
        kept[0, j].wait_recv()
        kept[2, j].wait_recv()
        saves[2 * j + 1].wait()

        def sum_rows(i, _):
            r = pl.ds(pl.multiple_of(i * step, step), step)
            mid[j, r, :] = acc[j, r, :] + got[0, j, r, :].astype(F32) + got[2, j, r, :].astype(F32)
            return 0

        lax.fori_loop(0, 4, sum_rows, 0)
        saves.append(fetch(mid.at[j], dh.at[j], store.at[2, j]))
    if share:
        down_owner(2)
        ends = [fetch(gx.at[2], gd_owner, end.at[0])]
        for n in range(2):
            owners[n].wait_recv()
        down_owner(3)
        far[:slot, :units] = gx[3].astype(F32) + gz[0].astype(F32) + gz[1].astype(F32)
        ends.append(fetch(far.at[:slot, :units], gd, end.at[1]))
        for n in range(2, 4):
            swaps[n].wait_send()
        for one in ends:
            one.wait()
    for copy in pending:
        copy.wait_send()
    for n in (4, 5) if share else (0, 2, 4, 5):
        saves[n].wait()


def ffn(h, wi, wd, mid, teacher, lengths, count, seq):
    rows, width = h.shape
    depth, slot = (seq // 2, width // seq) if seq else (0, 0)
    units = wd.shape[0]
    half = rows // 2
    split = lambda a: a.reshape(2, half, a.shape[-1])
    dma = pltpu.SemaphoreType.DMA
    hbm, vm = pl.BlockSpec(memory_space=pl.ANY), pl.BlockSpec(memory_space=pltpu.VMEM)
    def kernel(*refs):
        ffn_kernel(bool(seq), *(refs if seq else refs[:13] + (None,) + refs[13:]))

    sharing = []
    if seq:
        sharing = [
            pltpu.VMEM((4, slot, units), BF16), pltpu.VMEM((2, slot, units), BF16),
            dma((4,)), dma((4,)), dma((2,)), dma((2,)), dma((2,)),
        ]
    out, cot, dh, gd, gi, squares, *rest = pl.pallas_call(
        kernel,
        name="ffn",
        out_shape=[
            jax.ShapeDtypeStruct((2, half, width), BF16),
            jax.ShapeDtypeStruct((2, half, width), F32),
            jax.ShapeDtypeStruct((2, half, width), F32),
            jax.ShapeDtypeStruct((slot, units), F32) if seq else jax.ShapeDtypeStruct((width, units), BF16),
            jax.ShapeDtypeStruct((2, width, units), BF16),
            jax.ShapeDtypeStruct((8, 128), F32),
        ]
        + [jax.ShapeDtypeStruct((slot, units), BF16)] * bool(seq),
        in_specs=[hbm] * 5 + [pl.BlockSpec(memory_space=pltpu.SMEM), vm],
        out_specs=[hbm] * 5 + [vm] + [hbm] * bool(seq),
        scratch_shapes=[
            pltpu.VMEM((2, width, units), BF16),
            pltpu.VMEM((units, width), BF16),
            pltpu.VMEM((2, half, width), F32),
            pltpu.VMEM((2, half, width), BF16),
            pltpu.VMEM((4, 2, half, width), BF16),
            pltpu.VMEM((4, 2, half, width), BF16),
            pltpu.VMEM((2, 4, 2, half, units), BF16),
            pltpu.VMEM((4, 2, half, units), BF16),
            pltpu.VMEM((2, half, width), F32),
            pltpu.VMEM((half, width), F32),
            pltpu.VMEM((2, half, width), BF16),
            pltpu.VMEM((3, 2, half, width), BF16),
            pltpu.VMEM((3, 2, half, width), BF16),
            dma((5,)), dma((3, 2)), dma((3, 2)), dma((3, 2)), dma((3, 2)),
            dma((2, 3, 2)), dma((2, 3, 2)), dma((3, 2)), dma((2,)),
        ]
        + sharing,
        compiler_params=pltpu.CompilerParams(collective_id=2, has_side_effects=True, vmem_limit_bytes=63 << 20),
    )(split(h), wi, wd, split(mid), split(teacher), lengths, count)
    return out.reshape(rows, width), cot.reshape(rows, width), dh.reshape(rows, width), gd, gi, squares, rest


def pair_rows(block):
    return jnp.concatenate([block[:, :HD], block[:, HD:]], axis=0)


def pair_columns(block):
    rows = block.shape[0] // 2
    return jnp.concatenate([block[:rows], block[rows:]], axis=1)


def attend_back_kernel(q, kv, grad, mixed, probs, grad_q, grad_kv):
    i, pair = pl.program_id(0), pl.program_id(1)
    reach = WINDOW + QROWS
    keys = pl.ds(pl.multiple_of(i * QROWS, QROWS), reach)

    @pl.when((i == 0) & (pair == 0))
    def _():
        grad_kv[...] = jnp.zeros_like(grad_kv)

    queries, grads = pair_rows(q[...]), pair_rows(grad[...])
    weights = probs[0, 0].reshape(2 * QROWS, reach)
    dots = jnp.sum(grads.astype(F32) * pair_rows(mixed[...]).astype(F32), axis=-1, keepdims=True)
    steep = contract(grads, kv[keys, HD:], 1, 1) - dots
    steep = (weights.astype(F32) * steep).astype(BF16)
    grad_q[...] = (pair_columns(contract(steep, kv[keys, :HD], 1, 0)) * (1.0 / math.sqrt(HD))).astype(BF16)
    grad_kv[keys, :HD] += contract(steep, queries, 0, 0)
    grad_kv[keys, HD:] += contract(weights, grads, 0, 0)


def attend_back(queries, extended, grad_mixed, mixed, probs):
    rows, width = mixed.shape
    blocks, pairs, reach = rows // QROWS, width // (2 * HD), WINDOW + QROWS
    block = pl.BlockSpec((QROWS, 2 * HD), lambda i, p: (i, p))
    whole = pl.BlockSpec(extended.shape, lambda i, p: (0, 0))
    return pl.pallas_call(
        attend_back_kernel,
        name="attend_back",
        grid=(blocks, pairs),
        out_shape=[jax.ShapeDtypeStruct((rows, width), BF16), jax.ShapeDtypeStruct(extended.shape, F32)],
        in_specs=[block, whole, block, block, pl.BlockSpec((1, 1, 2, QROWS, reach), lambda i, p: (i, p, 0, 0, 0))],
        out_specs=[block, whole],
        compiler_params=pltpu.CompilerParams(vmem_limit_bytes=48 << 20),
    )(queries, extended, grad_mixed, mixed, probs)


GRAD_COLS = 128
AHEAD = 3


def owner_order(depth):
    return sorted(range(depth), key=lambda d: (d == 0, abs(2 * d - depth)))


class RowSum:
    def __init__(self, source, buffers, sems, where, go):
        self.source, self.go = source, go
        self.core, self.side, self.cross, self.along = buffers
        self.cs, self.cr, self.ys, self.yr, self.xs, self.xr, self.zs_, self.zr = sems
        self.x, self.y, self.c, self.zs, self.sib, self.ypeer, self.xpeer, self.zpeers = where
        self.depth, self.cols = len(self.zs), self.core.shape[-1]
        self.order = owner_order(self.depth)
        self.moved = {}

    def columns(self, y, c):
        return pl.ds(pl.multiple_of((2 * y + c) * self.cols, self.cols), self.cols)

    def first(self, d):
        for h in range(2):
            part = self.source.at[self.zs[d], :, :, self.columns(h, 1 - self.c)]
            self.moved["c", d, h] = self.go(part, self.core.at[d, h], self.cs.at[d, h], self.cr.at[d, h], self.sib)

    def second(self, d):
        for h in range(2):
            self.moved["c", d, h].wait_recv()
        far = 1 - self.y
        own = self.source[self.zs[d], :, :, self.columns(far, self.c)].astype(F32)
        self.core[d, far] = (own + self.core[d, far].astype(F32)).astype(BF16)
        self.moved["y", d] = self.go(self.core.at[d, far], self.side.at[d], self.ys.at[d], self.yr.at[d], self.ypeer)

    def kept(self, d, x):
        own = self.source[self.zs[d], x, :, self.columns(self.y, self.c)].astype(F32)
        return own + self.core[d, self.y, x].astype(F32) + self.side[d, x].astype(F32)

    def third(self, d):
        self.moved["y", d].wait_recv()
        self.side[d, 1 - self.x] = self.kept(d, 1 - self.x).astype(BF16)
        self.moved["x", d] = self.go(self.side.at[d, 1 - self.x], self.cross.at[d], self.xs.at[d], self.xr.at[d], self.xpeer)

    def fourth(self, d):
        self.moved["x", d].wait_recv()
        self.cross[d] = (self.kept(d, self.x) + self.cross[d].astype(F32)).astype(BF16)
        if d:
            self.moved["z", d] = self.go(
                self.cross.at[d], self.along.at[d - 1], self.zs_.at[d - 1], self.zr.at[d - 1], self.zpeers[d]
            )

    def total(self):
        value = self.cross[0].astype(F32)
        for d in range(1, self.depth):
            self.moved["z", d].wait_recv()
            value += self.along[d - 1].astype(F32)
        return value


def norm_back(values, grad, gain):
    r = lax.rsqrt(jnp.mean(values * values, axis=-1, keepdims=True) + EPSILON)
    scaled = grad * gain
    slope = r * r * r * jnp.mean(values * scaled, axis=-1, keepdims=True)
    return r * scaled - values * slope, jnp.sum(grad * values * r, axis=0, keepdims=True)


def finish_kernel(dh_hbm, cot_hbm, middle_hbm, w_out_hbm, w_attn_hbm, mixed_hbm, probs_hbm, qkv_hbm, ext_hbm, normed_hbm,
                  tokens_hbm, gd_hbm, gd_owner, gi_hbm, gain_attn, gain_ffn, squares, count,
                  grad_x, grad_d, grad_i, grad_qkv_out, grad_o, gain_attn_out, gain_ffn_out, loss_out,
                  dh, cot, middle, weight, mixed, probs, qkv, ext, normed, low, dmix, dkv, slabs, slabs_in,
                  gx, gz, gr, own, staged, joined, dz, po, pa, ocore, oside, ocross, oalong, acore, aside, across, aalong, vb,
                  load, p_load, own_load, out_sem, slab_s, slab_r, ds, dr, gxs, gxr, gzs, gzr, grr, o_sems, a_sems, vs, vr):
    z, x, y, c = places()
    depth, width = own.shape[1], own.shape[-1]
    rows, model_width = dh.shape
    units = gi_hbm.shape[-1]
    seq = 2 * depth
    me = 2 * z + x
    sib, ypeer, xpeer = device(z, x, y, 1 - c), device(z, x, 1 - y, c), device(z, 1 - x, y, c)
    zs = [lax.rem(z + d, depth) for d in range(depth)]
    zpeers = [device(zs[d], x, y, c) for d in range(depth)]
    wt = 2 * y + c
    diagonal = (lax.rem(me + seq - 1 + 2 * x, seq), wt)
    back = [(lax.rem(me + seq - step, seq), wt) for step in (1, 2)]

    def fetch(src, dst, sem):
        copy = pltpu.make_async_copy(src, dst, sem)
        copy.start()
        return copy

    loads = {}
    for n, (name, src, dst) in enumerate((
        ("dh", dh_hbm, dh), ("cot", cot_hbm, cot), ("w_out", w_out_hbm, weight.at[:, :model_width]), ("mixed", mixed_hbm, mixed),
        ("qkv", qkv_hbm, qkv), ("ext", ext_hbm, ext), ("normed", normed_hbm, normed))):
        loads[name] = fetch(src, dst, load.at[n])
    greet([sib, ypeer, xpeer, diagonal] + zpeers[1:])
    started = []

    def go(*args):
        started.append(remote(*args))
        return started[-1]

    spots = [(n, at) for at in range(0, units, width) for n in range(2)]
    chunks = len(spots)
    gxc, gzc, owned = {}, {}, {}

    def g_ref(k, side):
        n, at = spots[k]
        return gi_hbm.at[n, :, side, :, pl.ds(at, width)]

    def g_send(k):
        if k < chunks:
            gxc[k] = go(g_ref(k, 1 - x), gx.at[k], gxs.at[k], gxr.at[k], xpeer)

    def g_load(k):
        if k < chunks:
            owned[k] = fetch(g_ref(k, x), own.at[k % 2], own_load.at[k % 2])

    def at_end(d):
        return ((z == 0) & (d == depth - 1)) | ((z == depth - 1) & (d == 1))

    def g_copy(k, d, dst, recv, to):
        return pltpu.make_async_remote_copy(
            src_ref=gx.at[k, zs[d]], dst_ref=dst, send_sem=gzs.at[k, d - 1], recv_sem=recv, device_id=to, device_id_type=MESH)

    def g_owner(k, d):
        return g_copy(k, d, gz.at[k, d - 1], gzr.at[k, d - 1], zpeers[d])

    def g_neighbour(k, d):
        return g_copy(k, d, gr.at[k], grr.at[k], zpeers[depth - d])

    def g_step(k):
        gxc[k].wait_recv()
        g_send(k + AHEAD)
        owned[k].wait()
        for d in range(depth):
            gx[k, zs[d]] = (own[k % 2, zs[d]].astype(F32) + gx[k, zs[d]].astype(F32)).astype(BF16)
            if d == 1 or d == depth - 1:
                pl.when(at_end(d))(lambda d=d: g_neighbour(k, d).start())
                pl.when(jnp.logical_not(at_end(d)))(lambda d=d: g_owner(k, d).start())
        g_load(k + 2)
        if k >= 2:
            g_relay(k - 2)

    def g_relay(k):
        @pl.when((z > 0) & (z < depth - 1))
        def _():
            g_copy(k, 2, gr.at[k], grr.at[k], zpeers[2]).wait_recv()
            gx[k, zs[2]] = (gx[k, zs[2]].astype(F32) + gr[k].astype(F32)).astype(BF16)

        g_owner(k, 2).start()

    stores = {}

    def g_end(k):
        at = k % 2
        staged[at] = gx[k, z].astype(F32)
        for d in range(1, depth):
            missing = ((z == depth - 1) & (d == depth - 1)) | ((z == 0) & (d == 1))

            @pl.when(jnp.logical_not(missing))
            def _():
                g_owner(k, d).wait_recv()
                staged[at] += gz[k, d - 1].astype(F32)

        if at == 1:
            turn = k // 2
            if turn >= 2:
                stores[turn - 2].wait()
            joined[turn % 2] = jnp.stack([staged[0], staged[1]], axis=1)
            stores[turn] = fetch(joined.at[turn % 2], grad_i.at[:, :, pl.ds(spots[k][1], width)], out_sem.at[turn % 2])

    last = owner_order(depth)[2]
    sent_down = [
        go(gd_owner, dz, ds.at[0], dr.at[0], zpeers[last]),
    ]
    loads["da"] = fetch(gd_hbm, grad_d, load.at[11])
    for k in range(AHEAD):
        g_send(k)
    g_load(0)
    g_load(1)
    where = (x, y, c, zs, sib, ypeer, xpeer, zpeers)
    sum_o = RowSum(po, (ocore, oside, ocross, oalong), o_sems, where, go)
    sum_a = RowSum(pa, (acore, aside, across, aalong), a_sems, where, go)

    step = middle.shape[1]
    steps = rows // step
    mids = [None] * steps

    def mid_load(n):
        if n < steps:
            mids[n] = fetch(middle_hbm.at[pl.ds(n * step, step)], middle.at[n % 2], load.at[8 + n % 2])

    mid_load(0)
    mid_load(1)
    loads["dh"].wait()
    loads["cot"].wait()
    gain_grad = jnp.zeros((1, model_width), F32)
    scale_ffn, scale_attn = as_row(gain_ffn), as_row(gain_attn)
    for n in range(steps):
        mids[n].wait()
        r = pl.ds(n * step, step)
        grad, part = norm_back(middle[n % 2], dh[r, :], scale_ffn)
        grad = cot[r, :] + grad
        cot[r, :] = grad
        low[r, :model_width] = grad.astype(BF16)
        gain_grad += part
        mid_load(n + 2)
    vb[0] = jnp.zeros(vb.shape[1:], F32)
    vb[0, 1:2] = gain_grad
    vb[0, 2:3] = jnp.broadcast_to(squares[0:1, 0:1], (1, model_width))
    loads["w_out"].wait()
    loads["mixed"].wait()
    rows_low = lambda: low[:, :model_width]

    def out_back(cols):
        dmix[:, cols] = contract(rows_low(), weight[cols, :model_width], 1, 1).astype(BF16)

    tiles(model_width, 512, out_back)
    loads["w_attn"] = fetch(w_attn_hbm, weight, load.at[7])

    def out_grad(d, _):
        cols = pl.ds(pl.multiple_of(d * 2 * po.shape[2], 128), 2 * po.shape[2])
        po[d] = contract(low[:, cols], mixed[...], 0, 0).astype(BF16).reshape(po.shape[1:])
        return 0

    lax.fori_loop(0, depth, out_grad, 0)
    for d in sum_o.order:
        sum_o.first(d)
    g_step(0)
    g_step(1)
    blocks, pairs, reach = probs_hbm.shape[0], probs_hbm.shape[1], probs.shape[-1]
    turns = blocks * pairs

    def p_fetch(t):
        return pltpu.make_async_copy(probs_hbm.at[t // pairs, t % pairs], probs.at[t % 2], p_load.at[t % 2])

    p_fetch(0).start()
    p_fetch(1).start()
    dkv[...] = jnp.zeros_like(dkv)
    loads["qkv"].wait()
    loads["ext"].wait()
    for i in range(blocks):
        q_rows, keys = pl.ds(i * QROWS, QROWS), pl.ds(i * QROWS, reach)

        def one(pair, _):
            t = i * pairs + pair
            cols = pl.ds(pl.multiple_of(pair * 2 * HD, 2 * HD), 2 * HD)
            queries, grads = pair_rows(qkv[q_rows, cols]), pair_rows(dmix[q_rows, cols])
            outs = pair_rows(mixed[q_rows, cols])
            dots = jnp.sum(grads.astype(F32) * outs.astype(F32), axis=-1, keepdims=True)
            slot = lax.rem(t, 2)
            p_fetch(t).wait()
            weights = flat(probs[slot])
            steep = contract(grads, ext[keys, HD:], 1, 1) - dots
            steep = (weights.astype(F32) * steep).astype(BF16)
            low[q_rows, cols] = (pair_columns(contract(steep, ext[keys, :HD], 1, 0)) * (1.0 / math.sqrt(HD))).astype(BF16)
            dkv[keys, :HD] += contract(steep, queries, 0, 0)
            dkv[keys, HD:] += contract(weights, grads, 0, 0)

            @pl.when(t + 2 < turns)
            def _():
                p_fetch(t + 2).start()

            return 0

        lax.fori_loop(0, pairs // 2, one, 0)
        if i == 0:
            for d in sum_o.order:
                sum_o.second(d)
        g_step(2 + 2 * i)
        lax.fori_loop(pairs // 2, pairs, one, 0)
        g_step(3 + 2 * i)
    for n in range(2):
        slabs[n] = dkv[(1 - n) * rows : (2 - n) * rows, :].astype(BF16)
    returned = [go(slabs.at[n], slabs_in.at[n], slab_s.at[n], slab_r.at[n], back[n]) for n in range(2)]
    loads["normed"].wait()
    slot_rows = model_width // seq

    def query_grad(d, _):
        cols = pl.ds(pl.multiple_of(d * 2 * slot_rows, 128), 2 * slot_rows)
        pa[d, :, :slot_rows] = contract(low[:, cols], normed[...], 0, 0).astype(BF16).reshape(2, slot_rows, model_width)
        return 0

    lax.fori_loop(0, depth, query_grad, 0)
    g_step(6)
    for one in returned:
        one.wait_recv()
    summed = dkv[2 * rows :, :] + slabs_in[0].astype(F32) + slabs_in[1].astype(F32)
    low[:, model_width : model_width + HD] = (summed[:, :HD] * (1.0 / math.sqrt(HD))).astype(BF16)
    low[:, model_width + HD :] = summed[:, HD:].astype(BF16)
    kv_grad = contract(low[:, model_width:], normed[...], 0, 0).astype(BF16)
    kv_rows = HD // seq
    for n in range(2):
        part = kv_grad[n * HD : (n + 1) * HD].reshape(depth, 2, kv_rows, model_width)
        pa[:, :, slot_rows + n * kv_rows : slot_rows + (n + 1) * kv_rows] = part
    for d in sum_a.order:
        sum_a.first(d)
    loads["tokens"] = fetch(tokens_hbm, mixed, load.at[3])
    loads["w_attn"].wait()

    def attn_back(cols):
        dh[:, cols] = contract(low[...], weight[cols, :], 1, 1)

    tiles(model_width, 512, attn_back)
    g_step(7)
    loads["tokens"].wait()

    def last_norm(n, so_far):
        r = pl.ds(pl.multiple_of(n * step, step), step)
        grad, part = norm_back(mixed[r, :].astype(F32), dh[r, :], scale_attn)
        cot[r, :] += grad
        return so_far + part

    vb[0, 0:1] = lax.fori_loop(0, steps, last_norm, jnp.zeros((1, model_width), F32))
    saved = fetch(cot, grad_x, load.at[0])

    vc = {}

    def v_first():
        vc[0] = go(vb.at[0], vb.at[1], vs.at[0], vr.at[0], sib)

    def v_swap(n, to):
        vc[n - 1].wait_recv()
        vb[2 * n] = vb[2 * n - 2] + vb[2 * n - 1]
        vc[n] = go(vb.at[2 * n], vb.at[2 * n + 1], vs.at[n], vr.at[n], to)

    def v_along():
        vc[2].wait_recv()
        vb[6] = vb[4] + vb[5]
        for d in range(1, depth):
            vc[2 + d] = go(vb.at[6], vb.at[6 + d], vs.at[2 + d], vr.at[2 + d], zpeers[d])

    def v_end():
        for d in range(1, depth):
            vc[2 + d].wait_recv()
        total = vb[6 + z]
        for n in range(1, depth):
            total += vb[6 + lax.rem(z - n + depth, depth)]
        gain_attn_out[...] = as_lines(total[0:1])
        gain_ffn_out[...] = as_lines(total[1:2])
        loss_out[...] = total[2:3, 0:1] / (count[0:1, 0:1] * model_width)

    v_first()
    o, a = sum_o.order, sum_a.order
    after = {
        8: [lambda: sum_a.second(a[0]), lambda: sum_o.third(o[0]), lambda: sum_o.third(o[1]), lambda: v_swap(1, ypeer)],
        9: [lambda: sum_o.third(o[2]), lambda: sum_o.third(o[3])],
        10: [lambda: sum_a.second(a[1]), lambda: sum_a.third(a[0]), lambda: sum_o.fourth(o[0]), lambda: v_swap(2, xpeer)],
        11: [lambda: sum_o.fourth(o[1])],
        12: [lambda: sum_a.second(a[2]), lambda: sum_a.third(a[1]), lambda: sum_a.fourth(a[0]), lambda: sum_o.fourth(o[2]), v_along],
        13: [lambda: sum_o.fourth(o[3])],
        14: [lambda: sum_a.second(a[3]), lambda: sum_a.third(a[2]), lambda: sum_a.fourth(a[1])],
        15: [v_end],
        16: [lambda: sum_a.third(a[3]), lambda: sum_a.fourth(a[2])],
    }
    ended = 0
    for k in range(8, chunks):
        g_step(k)
        for step in after.pop(k, ()):
            step()
        while ended < k - 4:
            g_end(ended)
            ended += 1
    g_relay(chunks - 2)
    g_relay(chunks - 1)
    for key in sorted(after):
        for step in after[key]:
            step()
    sum_a.fourth(a[3])
    for k in range(ended, chunks):
        g_end(k)
    grad_o[...] = sum_o.total()
    for one in sent_down:
        one.wait_recv()
    loads["da"].wait()
    grad_d[...] += dz[...].astype(F32)
    grad_qkv_out[...] = sum_a.total()
    for copy in started:
        copy.wait_send()
    for k in range(chunks):
        for d in range(1, depth):
            g_owner(k, d).wait_send()
    saved.wait()
    stores[chunks // 2 - 2].wait()
    stores[chunks // 2 - 1].wait()


def finish(dh, cot, middle, w_out, w_attn, mixed, probs, qkv, ext, normed, tokens, gd, gd_rest, gi, gain_attn, gain_ffn, squares, count, seq):
    rows, model_width = dh.shape
    depth, slot, units = seq // 2, model_width // seq, gi.shape[-1]
    kv_rows, cols = 2 * HD // seq, model_width // 4
    blocks, _, _, _, reach = probs.shape
    chunks = 2 * units // GRAD_COLS
    qkv_slot = slot + kv_rows
    step = 128
    dma = pltpu.SemaphoreType.DMA
    hbm, vm = pl.BlockSpec(memory_space=pl.ANY), pl.BlockSpec(memory_space=pltpu.VMEM)

    def sum_buffers(n):
        return [
            pltpu.VMEM((depth, 2, 2, n, cols), BF16),
            pltpu.VMEM((depth, 2, n, cols), BF16),
            pltpu.VMEM((depth, n, cols), BF16),
            pltpu.VMEM((depth - 1, n, cols), BF16),
        ]

    sum_sems = [dma((depth, 2)), dma((depth, 2)), dma((depth,)), dma((depth,)), dma((depth,)), dma((depth,)), dma((depth - 1,)), dma((depth - 1,))]

    def kernel(*refs):
        refs = list(refs)
        at = len(refs) - 18
        o_sems, a_sems = refs[at : at + 8], refs[at + 8 : at + 16]
        finish_kernel(*refs[:at], o_sems, a_sems, *refs[at + 16 :])

    return pl.pallas_call(
        kernel,
        name="finish",
        out_shape=[
            jax.ShapeDtypeStruct((rows, model_width), F32),
            jax.ShapeDtypeStruct((slot, units), F32),
            jax.ShapeDtypeStruct((slot, 2, units), F32),
            jax.ShapeDtypeStruct((qkv_slot, cols), F32),
            jax.ShapeDtypeStruct((slot, cols), F32),
            jax.ShapeDtypeStruct((model_width // 128, 128), F32),
            jax.ShapeDtypeStruct((model_width // 128, 128), F32),
            jax.ShapeDtypeStruct((1, 1), F32),
        ],
        in_specs=[hbm] * 14 + [vm] * 4,
        out_specs=[hbm, vm, hbm] + [vm] * 5,
        scratch_shapes=[
            pltpu.VMEM((rows, model_width), F32),
            pltpu.VMEM((rows, model_width), F32),
            pltpu.VMEM((2, step, model_width), F32),
            pltpu.VMEM(w_attn.shape, BF16),
            pltpu.VMEM((rows, model_width), BF16),
            pltpu.VMEM((2, 2, QROWS, reach), BF16),
            pltpu.VMEM(qkv.shape, BF16),
            pltpu.VMEM(ext.shape, BF16),
            pltpu.VMEM((rows, model_width), BF16),
            pltpu.VMEM(qkv.shape, BF16),
            pltpu.VMEM((rows, model_width), BF16),
            pltpu.VMEM(ext.shape, F32),
            pltpu.VMEM((2, rows, 2 * HD), BF16),
            pltpu.VMEM((2, rows, 2 * HD), BF16),
            pltpu.VMEM((chunks, depth, slot, GRAD_COLS), BF16),
            pltpu.VMEM((chunks, depth - 1, slot, GRAD_COLS), BF16),
            pltpu.VMEM((chunks, slot, GRAD_COLS), BF16),
            pltpu.VMEM((2, depth, slot, GRAD_COLS), BF16),
            pltpu.VMEM((2, slot, GRAD_COLS), F32),
            pltpu.VMEM((2, slot, 2, GRAD_COLS), F32),
            pltpu.VMEM((slot, units), BF16),
            pltpu.VMEM((depth, 2, slot, model_width), BF16),
            pltpu.VMEM((depth, 2, qkv_slot, model_width), BF16),
        ]
        + sum_buffers(slot)
        + sum_buffers(qkv_slot)
        + [pltpu.VMEM((6 + depth, 8, model_width), F32)]
        + [
            dma((12,)), dma((2,)), dma((2,)), dma((2,)), dma((2,)), dma((2,)), dma((1,)), dma((1,)),
            dma((chunks,)), dma((chunks,)), dma((chunks, depth - 1)), dma((chunks, depth - 1)), dma((chunks,)),
        ]
        + sum_sems
        + sum_sems
        + [dma((2 + depth,)), dma((2 + depth,))],
        compiler_params=pltpu.CompilerParams(collective_id=1, has_side_effects=True, vmem_limit_bytes=63 << 20),
    )(
        dh, cot, middle, w_out, w_attn, mixed, probs, qkv, ext, normed, tokens,
        gd, *gd_rest, gi.reshape(2, depth, 2, slot, units),
        gain_attn.reshape(-1, 128), gain_ffn.reshape(-1, 128), squares, count,
    )


SHARERS = 8


def as_row(ref):
    return jnp.concatenate([ref[n : n + 1, :] for n in range(ref.shape[0])], axis=1)


def as_lines(row):
    return jnp.concatenate([row[:, n : n + 128] for n in range(0, row.shape[1], 128)], axis=0)


def begin_kernel(lengths, tokens_hbm, w_attn_hbm, w_out_hbm, gain_attn, gain_ffn,
                 attn_out, out_out, qkv_out, ext_out, normed_out, mixed_out, probs_out, middle_out, low_out, count_out,
                 tokens, normed, w_attn, w_out, qkv, ext, mixed, probs, bias, acc, counts,
                 load, c_send, c_recv, o_send, o_recv, s_send, s_recv, h_send, h_recv, n_send, n_recv, p_store, store):
    seq, wt = lax.axis_index("seq"), lax.axis_index("wt")
    n_seq = lax.axis_size("seq")
    y, c = wt // 2, wt % 2
    w_sib, w_peer, w_far = 2 * y + 1 - c, 2 * (1 - y) + c, 2 * (1 - y) + 1 - c
    sib, peer = (seq, w_sib), (seq, w_peer)
    rows, width = tokens.shape
    depth = w_attn_hbm.shape[0]
    pairs = width // (2 * HD)
    blocks, reach = rows // QROWS, WINDOW + QROWS
    slabs = WINDOW // rows
    first = seq // SHARERS * SHARERS
    place = lax.rem(seq, SHARERS)
    others = [(first + lax.rem(place + n, SHARERS), wt) for n in range(1, SHARERS)]
    ahead = [(lax.rem(seq + n, n_seq), wt) for n in range(1, slabs + 1)]
    behind = [(lax.rem(seq + n_seq - n, n_seq), wt) for n in range(1, slabs + 1)]

    def fetch(src, dst, sem):
        copy = pltpu.make_async_copy(src, dst, sem)
        copy.start()
        return copy

    def shard(w, size=None, at=0):
        return pl.ds(pl.multiple_of(w * depth + at, 16), depth if size is None else size)

    loads = [
        fetch(tokens_hbm, tokens, load.at[0]),
        fetch(w_attn_hbm, w_attn.at[shard(wt)], load.at[1]),
        fetch(w_out_hbm, w_out.at[shard(wt)], load.at[2]),
    ]
    greet([sib, peer] + others + (ahead + behind if n_seq > SHARERS else []))
    started = []

    def go(*args):
        started.append(remote(*args))
        return started[-1]

    def chunk(k):
        return pl.ds(pl.multiple_of(lax.rem(k + pairs, pairs + 1) * 2 * HD, 2 * HD), 2 * HD)

    def chunk_copy(kind, k):
        at = chunk(k)
        w, to = ((wt, peer), (wt, sib), (w_peer, sib))[kind]
        src = w_attn_hbm.at[:, at] if kind < 2 else w_attn.at[shard(w), at]
        return pltpu.make_async_remote_copy(
            src_ref=src, dst_ref=w_attn.at[shard(w), at], send_sem=c_send.at[kind, k], recv_sem=c_recv.at[kind, k],
            device_id=to, device_id_type=MESH)

    def arrived(kind, k):
        w = (w_peer, w_sib, w_far)[kind]
        at = chunk(k)
        here = w_attn.at[shard(w), at]
        pltpu.make_async_copy(here, here, c_recv.at[kind, k]).wait()

    chunk_copy(0, 0).start()
    slice_rows = depth // SHARERS

    def slice_at(w, n):
        return shard(w, slice_rows, n * slice_rows)

    mine = pl.ds(pl.multiple_of(place * slice_rows, 16), slice_rows)
    for k in range(pairs + 1):
        chunk_copy(1, k).start()
    whole = go(w_out_hbm, w_out.at[shard(wt)], o_send.at[1], o_recv.at[1], sib)

    def send_after(k):
        chunk_copy(0, k).wait_send()
        chunk_copy(0, k + 2).start()

    n_len = lengths.shape[1]
    ends = [lengths[0, 0]]
    for n in range(1, n_len):
        ends.append(ends[-1] + lengths[0, n])
    stream = n_seq * rows

    def ids(positions):
        number = jnp.zeros(positions.shape, jnp.int32) - 1
        for n in range(n_len):
            start = ends[n - 1] if n else 0
            number += (positions >= start).astype(jnp.int32)
        inside = (positions >= 0) & (positions < ends[-1])
        return jnp.where(inside, number, -(positions + 2 * stream))

    base = seq * rows
    q_ids = ids(lax.broadcasted_iota(jnp.int32, (rows, 1), 0) + base)
    k_ids = ids(lax.broadcasted_iota(jnp.int32, (1, rows + WINDOW), 1) + (base - WINDOW))
    counts[0] = jnp.full(counts.shape[1:], ends[-1]).astype(F32)
    number = go(counts.at[0], counts.at[1], n_send.at[0], n_recv.at[0], sib)

    loads[0].wait()
    scale_attn = as_row(gain_attn)
    part = 128

    def norm_rows(n, _):
        r = pl.ds(pl.multiple_of(n * part, part), part)
        values = tokens[r, :].astype(F32)
        scale = lax.rsqrt(jnp.mean(values * values, axis=-1, keepdims=True) + EPSILON)
        normed[r, :] = (values * scale * scale_attn).astype(BF16)
        return 0

    lax.fori_loop(0, rows // part, norm_rows, 0)
    stores = [fetch(normed, normed_out, store.at[0])]
    for i in range(blocks):
        row = lax.broadcasted_iota(jnp.int32, (QROWS, reach), 0)
        offset = lax.broadcasted_iota(jnp.int32, (QROWS, reach), 1) - WINDOW - row
        here, there = q_ids[i * QROWS : (i + 1) * QROWS], k_ids[:, i * QROWS : i * QROWS + reach]
        bias[i] = jnp.where((offset <= 0) & (offset > -WINDOW) & (here == there), 0.0, NEGATIVE)
    number.wait_recv()
    counts[2] = counts[0] + counts[1]
    chunk_copy(0, 0).wait_send()
    chunk_copy(0, 1).start()
    chunk_copy(0, 2).start()

    def relay(k):
        arrived(0, k)
        chunk_copy(2, k).start()

    loads[1].wait()
    relay(0)
    arrived(1, 0)
    arrived(2, 0)
    kv_cols = slice(width, width + 2 * HD)
    key_value = contract(normed[...], w_attn[:, kv_cols], 1, 0).astype(BF16)
    qkv[:, kv_cols] = key_value
    ext[WINDOW:, :] = key_value
    halo = {}

    def halo_send(half):
        for n in range(slabs):
            cols, at = pl.ds(half * HD, HD), half * slabs + n
            dst = ext.at[pl.ds(WINDOW - (n + 1) * rows, rows), cols]
            halo[half, n] = remote(ext.at[pl.ds(WINDOW, rows), cols], dst, h_send.at[at], h_recv.at[at], ahead[n])

    halo_send(0)

    def project_queries(p):
        cols = pl.ds(pl.multiple_of(p * 2 * HD, 2 * HD), 2 * HD)
        arrived(1, p + 1)
        arrived(2, p + 1)
        qkv[:, cols] = contract(normed[...], w_attn[:, cols], 1, 0).astype(BF16)

    send_after(1)
    relay(1)
    number = go(counts.at[2], counts.at[3], n_send.at[1], n_recv.at[1], peer)
    eighth = go(w_out_hbm.at[mine], w_out.at[slice_at(wt, place)], o_send.at[0], o_recv.at[0], peer)
    project_queries(0)
    for n in range(slabs):
        halo[0, n].wait_send()
    halo_send(1)
    send_after(2)
    relay(2)
    for n in range(slabs):
        halo[0, n].wait_recv()
    eighth.wait_recv()
    spread = [
        go(w_out.at[slice_at(w_peer, place)], w_out.at[slice_at(w_peer, place)], s_send.at[n], s_recv.at[n], others[n])
        for n in range(SHARERS - 1)
    ]
    number.wait_recv()
    count_out[...] = counts[2] + counts[3]
    factor = math.log2(math.e) / math.sqrt(HD)

    def p_copy(i, p):
        return pltpu.make_async_copy(probs.at[i], probs_out.at[i, p], p_store.at[i])

    def heads(p, _, values=None):
        @pl.when(jnp.asarray(p) + 3 <= pairs)
        def _():
            relay(p + 3)

        @pl.when(jnp.asarray(p) + 5 <= pairs)
        def _():
            send_after(p + 3)

        @pl.when(jnp.asarray(p) + 1 < pairs)
        def _():
            project_queries(p + 1)

        cols = pl.ds(pl.multiple_of(p * 2 * HD, 2 * HD), 2 * HD)
        for i in range(blocks):
            q_rows, keys = pl.ds(i * QROWS, QROWS), pl.ds(i * QROWS, reach)
            scores = contract(pair_rows(qkv[q_rows, cols]), ext[keys, :HD], 1, 1) * factor
            shifted = scores.reshape(2, QROWS, reach) + bias[i][None]
            powers = jnp.exp2(shifted - jnp.max(shifted, axis=-1, keepdims=True))
            weights = (powers * (1.0 / jnp.sum(powers, axis=-1, keepdims=True))).astype(BF16)

            @pl.when(jnp.asarray(p) > 0)
            def _():
                p_copy(i, p - 1).wait()

            probs[i] = weights
            p_copy(i, p).start()
            if values is not None and i == 0:
                for one in values:
                    one.wait_recv()
            outs = contract(weights.reshape(2 * QROWS, reach), ext[keys, HD:], 1, 0)
            mixed[q_rows, cols] = pair_columns(outs).astype(BF16)
        return 0

    heads(0, 0, [halo[1, n] for n in range(slabs)])

    def keep_shard(w, n):
        return fetch(w_out.at[shard(w)], out_out.at[shard(w)], store.at[n])

    loads[2].wait()
    whole.wait_recv()
    stores += [keep_shard(wt, 5), keep_shard(w_sib, 7)]
    stores.append(fetch(ext, ext_out, store.at[1]))
    lax.fori_loop(1, pairs - 1, heads, 0)
    stores.append(fetch(w_attn, attn_out, store.at[4]))
    for one in spread:
        one.wait_recv()
    stores.append(keep_shard(w_peer, 8))
    passed = go(w_out.at[shard(w_peer)], w_out.at[shard(w_peer)], o_send.at[2], o_recv.at[2], sib)
    heads(pairs - 1, 0)
    stores += [fetch(qkv, qkv_out, store.at[2]), fetch(mixed, mixed_out, store.at[3])]
    passed.wait_recv()
    stores.append(keep_shard(w_far, 9))

    def project(cols):
        acc[:, cols] = tokens[:, cols].astype(F32) + contract(mixed[...], w_out[:, cols], 1, 0)

    tiles(width, 512, project)
    stores.append(fetch(acc, middle_out, store.at[6]))
    stores[0].wait()

    scale_ffn = as_row(gain_ffn)

    def norm_again(n, _):
        r = pl.ds(pl.multiple_of(n * part, part), part)
        values = acc[r, :]
        scale = lax.rsqrt(jnp.mean(values * values, axis=-1, keepdims=True) + EPSILON)
        normed[r, :] = (values * scale * scale_ffn).astype(BF16)
        return 0

    lax.fori_loop(0, rows // part, norm_again, 0)
    stores.append(fetch(normed, low_out, store.at[0]))
    for i in range(blocks):
        p_copy(i, pairs - 1).wait()
    for one in stores[1:]:
        one.wait()
    chunk_copy(0, pairs - 1).wait_send()
    chunk_copy(0, pairs).wait_send()
    for k in range(pairs + 1):
        for kind in range(1, 3):
            chunk_copy(kind, k).wait_send()
    for one in started + [halo[1, n] for n in range(slabs)]:
        one.wait_send()


def begin(lengths, tokens, w_attn, w_out, gain_attn, gain_ffn):
    rows, width = tokens.shape
    shards = 4
    depth = w_out.shape[0]
    pairs, blocks, reach = width // (2 * HD), rows // QROWS, WINDOW + QROWS
    columns = width + 2 * HD
    dma = pltpu.SemaphoreType.DMA
    hbm, vm = pl.BlockSpec(memory_space=pl.ANY), pl.BlockSpec(memory_space=pltpu.VMEM)
    shape = jax.ShapeDtypeStruct
    return pl.pallas_call(
        begin_kernel,
        name="begin",
        out_shape=[
            shape((width, columns), BF16),
            shape((width, width), BF16),
            shape((rows, columns), BF16),
            shape((rows + WINDOW, 2 * HD), BF16),
            shape((rows, width), BF16),
            shape((rows, width), BF16),
            shape((blocks, pairs, 2, QROWS, reach), BF16),
            shape((rows, width), F32),
            shape((rows, width), BF16),
            shape((8, 128), F32),
        ],
        in_specs=[pl.BlockSpec(memory_space=pltpu.SMEM)] + [hbm] * 3 + [vm] * 2,
        out_specs=[hbm] * 9 + [vm],
        scratch_shapes=[
            pltpu.VMEM((rows, width), BF16),
            pltpu.VMEM((rows, width), BF16),
            pltpu.VMEM((shards * depth, columns), BF16),
            pltpu.VMEM((shards * depth, width), BF16),
            pltpu.VMEM((rows, columns), BF16),
            pltpu.VMEM((rows + WINDOW, 2 * HD), BF16),
            pltpu.VMEM((rows, width), BF16),
            pltpu.VMEM((blocks, 2, QROWS, reach), BF16),
            pltpu.VMEM((blocks, QROWS, reach), F32),
            pltpu.VMEM((rows, width), F32),
            pltpu.VMEM((4, 8, 128), F32),
            dma((3,)), dma((3, pairs + 1)), dma((3, pairs + 1)), dma((3,)), dma((3,)), dma((SHARERS - 1,)), dma((SHARERS - 1,)),
            dma((2 * WINDOW // rows,)), dma((2 * WINDOW // rows,)), dma((2,)), dma((2,)), dma((blocks,)), dma((10,)),
        ],
        compiler_params=pltpu.CompilerParams(collective_id=3, has_side_effects=True, vmem_limit_bytes=60 << 20),
    )(lengths, tokens, w_attn, w_out, gain_attn.reshape(-1, 128), gain_ffn.reshape(-1, 128))


def passed_along(block, axis, distance):
    devices = range(lax.axis_size(axis))
    route = [(i - distance, i) for i in devices if i - distance in devices]
    return lax.ppermute(block, axis, route)


def rms_scale(values, gain):
    return values * lax.rsqrt(jnp.mean(values * values, axis=-1, keepdims=True) + EPSILON) * gain


def per_device(tokens, teacher, seq_lengths, w_attn, w_out, w_in, w_down, gain_attn, gain_ffn):
    tok_rows = tokens.shape[1]
    model_width = tokens.shape[2]
    seq_devices = lax.axis_size("seq")
    (attn_full, out_full, qkv, extended, normed, mixed_b, probs, middle, normed_two, count) = begin(
        seq_lengths, tokens[0], w_attn, w_out, gain_attn, gain_ffn
    )
    w_pair = jnp.swapaxes(w_in, 0, 1)
    slot, kv_slot = model_width // seq_devices, HD // seq_devices
    aligned = seq_devices == 8 and slot % 16 == 0 and kv_slot % 16 == 0
    output, cotangent, grad_norm_two, grad_down, grad_in, squares, grad_down_rest = ffn(
        normed_two, w_pair, w_down, middle, teacher[0], seq_lengths, count, seq_devices if aligned else 0
    )
    if aligned:
        grad_inputs, grad_down, grad_in, grad_attn, grad_out, gain_attn_all, gain_ffn_all, loss = finish(
            grad_norm_two, cotangent, middle, out_full, attn_full, mixed_b, probs, qkv, extended, normed, tokens[0],
            grad_down, grad_down_rest, grad_in, gain_attn, gain_ffn, squares, count, seq_devices,
        )
    else:
        _, norm_one_pull = jax.vjp(rms_scale, tokens[0].astype(jnp.float32), gain_attn)
        _, norm_two_pull = jax.vjp(rms_scale, middle, gain_ffn)
        grad_middle_norm, grad_gain_ffn = norm_two_pull(grad_norm_two)
        grad_middle = cotangent + grad_middle_norm
        grad_mid_low = grad_middle.astype(jnp.bfloat16)
        grad_out = jnp.einsum("te,td->ed", grad_mid_low, mixed_b, preferred_element_type=jnp.float32)
        grad_mixed = jnp.einsum("te,de->td", grad_mid_low, out_full, preferred_element_type=jnp.float32)
        grad_query, grad_ext = attend_back(qkv, extended, grad_mixed.astype(jnp.bfloat16), mixed_b, probs)
        edge_rows = WINDOW
        grad_kv = grad_ext[edge_rows:]
        for back_step in range(1, WINDOW // tok_rows + 1):
            slab_rows = grad_ext[
                edge_rows - back_step * tok_rows : edge_rows - (back_step - 1) * tok_rows
            ]
            grad_kv = grad_kv + passed_along(slab_rows, "seq", -back_step)
        grad_key = (grad_kv[:, :HD] * (1.0 / math.sqrt(HD))).astype(jnp.bfloat16)
        grad_qkv = jnp.concatenate([grad_query, grad_key, grad_kv[:, HD:].astype(jnp.bfloat16)], axis=1)
        grad_attn = jnp.einsum("te,td->ed", grad_qkv, normed, preferred_element_type=jnp.float32)
        grad_normed = jnp.einsum("te,de->td", grad_qkv, attn_full, preferred_element_type=jnp.float32)
        grad_input_norm, grad_gain_attn = norm_one_pull(grad_normed)
        grad_inputs = grad_middle + grad_input_norm
        grad_attn = grad_attn.astype(jnp.bfloat16)
        grad_key, grad_value = (
            grad_attn[model_width + at : model_width + at + HD].reshape(seq_devices, kv_slot, model_width) for at in (0, HD)
        )
        packed = jnp.concatenate(
            [
                grad_attn[:model_width].reshape(seq_devices, slot, model_width),
                grad_key,
                grad_value,
                grad_out.astype(jnp.bfloat16).reshape(seq_devices, slot, model_width),
            ],
            axis=1,
        )
        small = jnp.stack([grad_gain_attn, grad_gain_ffn, jnp.full((model_width,), squares[0, 0])] + [jnp.zeros_like(grad_gain_attn)] * 5)
        grad_down, grad_in = grad_down.reshape(seq_devices, slot, -1), grad_in.reshape(2, seq_devices, slot, -1)
        grad_down, grad_in, packed, small = reduce_plain(grad_down, grad_in, packed, small)
        grad_attn, grad_out = packed[:-slot], packed[-slot:]
        grad_in = jnp.swapaxes(grad_in, 0, 1)
        gain_attn_all, gain_ffn_all = small[0], small[1]
        loss = small[2, 0] / (count[0, 0] * model_width)
    grad_queries = grad_attn[:slot].T
    grad_keyvals = grad_attn[slot:].T.reshape(-1, 2, kv_slot)
    grad_out = grad_out.T
    grad_down = grad_down.T
    return (
        output[None],
        loss.reshape(()),
        grad_inputs[None],
        grad_queries,
        grad_keyvals,
        grad_out,
        grad_in,
        grad_down,
        gain_attn_all.reshape(-1),
        gain_ffn_all.reshape(-1),
    )


def solution(mesh):
    in_specs = (
        P("wt", "seq", None),
        P("wt", "seq", None),
        P("wt", None),
        P("wt", None),
        P("wt", None),
        P(None, None, "wt"),
        P("wt", None),
        P(),
        P(),
    )
    out_specs = (
        P("wt", "seq", None),
        P(),
        P("wt", "seq", None),
        P("wt", "seq"),
        P("wt", None, "seq"),
        P("wt", "seq"),
        P("seq", None, "wt"),
        P("wt", "seq"),
        P(),
        P(),
    )
    return jax.shard_map(
        per_device, mesh=mesh, in_specs=in_specs, out_specs=out_specs, check_vma=False
    )
```

```python
import functools
import math

import jax
import jax.numpy as jnp
from jax import lax
from jax.experimental import pallas as pl
from jax.experimental.pallas import tpu as pltpu
from jax.sharding import PartitionSpec as P

HEADS = 12
HD = 128
WINDOW = 1024
QROWS = 256


EPSILON = 1e-06
NEGATIVE = -1e30

MESH = pl.DeviceIdType.MESH
F32 = jnp.float32
BF16 = jnp.bfloat16


def places():
    seq, wt = lax.axis_index("seq"), lax.axis_index("wt")
    return seq // 2, seq % 2, wt // 2, wt % 2


def device(z, x, y, c):
    return (z * 2 + x, y * 2 + c)


def remote(src, dst, send, recv, to):
    copy = pltpu.make_async_remote_copy(
        src_ref=src, dst_ref=dst, send_sem=send, recv_sem=recv, device_id=to, device_id_type=MESH
    )
    copy.start()
    return copy


def greet(devices):
    barrier = pltpu.get_barrier_semaphore()
    for one in devices:
        pl.semaphore_signal(barrier, inc=1, device_id=one, device_id_type=MESH)
    pl.semaphore_wait(barrier, len(devices))


def reduce_plain(gd, gi, p, v):
    gd = lax.psum_scatter(gd, "seq", scatter_dimension=0, tiled=False).astype(F32)
    gi = lax.psum_scatter(gi, "seq", scatter_dimension=1, tiled=False).astype(F32)
    p = lax.psum_scatter(p, "seq", scatter_dimension=0, tiled=False)
    p = lax.psum_scatter(p, "wt", scatter_dimension=1, tiled=True).astype(F32)
    return gd, gi, p, lax.psum(v, ("seq", "wt"))


def contract(a, b, dim_a, dim_b):
    return lax.dot_general(a, b, (((dim_a,), (dim_b,)), ((), ())), preferred_element_type=F32)


def tiles(total, width, body):
    def step(i, _):
        body(pl.ds(pl.multiple_of(i * width, width), width))
        return 0

    lax.fori_loop(0, total // width, step, 0)


def flat(block):
    return block.reshape(-1, block.shape[-1])


def ffn_kernel(share, h, wi_hbm, wd_hbm, mid_hbm, teacher_hbm, lengths, count, out, cot, dh, gd, gi, squares, gd_owner,
               wi, wd, mid, teacher, hall, dall, act, hid, acc, far, out_low, sent, got,
               load, h_send, h_recv, d_send, d_recv, p_send, p_recv, store, g_store, w_load, *sharing):
    z, x, y, c = places()
    sib, peer = device(z, x, y, 1 - c), device(z, x, 1 - y, c)
    half, width = h.shape[1:]
    units = wd.shape[0]

    def fetch(src, dst, sem):
        copy = pltpu.make_async_copy(src, dst, sem)
        copy.start()
        return copy

    loads = [fetch(*pair, load.at[n]) for n, pair in enumerate(
        ((h, hall.at[0]), (wd_hbm, wd), (teacher_hbm, teacher)))]
    lanes = [fetch(wi_hbm.at[n % 2, :, pl.ds(n // 2 * 128, 128)], wi.at[:, pl.ds(n * 128, 128)], w_load.at[n]) for n in range(units // 64)]
    if share:
        gx, gz, gxs, gxr, gzs, gzr, end = sharing
        depth, slot = lax.axis_size("seq") // 2, gx.shape[1]
        zs = [lax.rem(z + d, depth) for d in range(depth)]
        xpeer, zpeers = device(z, 1 - x, y, c), [device(zs[d], x, y, c) for d in range(depth)]
    greet([sib, peer] + ([xpeer] + zpeers[1:] if share else []))
    pending = []

    def go(*args):
        nonlocal pending
        pending.append(remote(*args))
        return pending[-1]

    def spread(src, dst, send, recv, j):
        a = go(src.at[j], dst.at[2, j], send.at[0, j], recv.at[0, j], peer)
        b = go(src.at[j], dst.at[1, j], send.at[1, j], recv.at[1, j], sib)
        return a, b

    def relay(dst, send, recv, j):
        return go(dst.at[2, j], dst.at[3, j], send.at[2, j], recv.at[2, j], sib)

    def group(ref, g):
        return ref.at[2:4, g - 2] if g >= 2 else ref.at[g]

    h_copies = [spread(h, hall, h_send, h_recv, j) for j in range(2)]

    def third(start, n):
        return pl.ds(pl.multiple_of(start + 128 * n, 128), 128)

    def gated(g):
        rows = flat(group(hall, g)[...])

        def body(cols):
            mid[:, :, :768] = contract(rows, wi[:, cols], 1, 0).reshape(2, half, -1)
            block = half // 2

            def finish_rows(i, _):
                j, r = i // 2, pl.ds(pl.multiple_of(lax.rem(i, 2) * block, block), block)
                for n in range(3):
                    gate, up = mid[j, r, 256 * n : 256 * n + 128], mid[j, r, 256 * n + 128 : 256 * n + 256]
                    square = gate * gate
                    turn = jnp.tanh(gate * (0.7978845608028654 + 0.035677408136300125 * square))
                    upper = 0.5 + 0.5 * turn
                    value = gate * upper
                    slope = upper + 0.5 * gate * (1.0 - turn * turn) * (0.7978845608028654 + 0.10703222440890038 * square)
                    group(hid, g)[j, r, third(cols.start // 2, n)] = (value * up).astype(BF16)
                    group(act, g)[j, r, third(cols.start, 2 * n)] = (slope * up).astype(BF16)
                    group(act, g)[j, r, third(cols.start, 2 * n + 1)] = value.astype(BF16)
                return 0

            lax.fori_loop(0, 4, finish_rows, 0)

        tiles(2 * units, 768, body)

    def emit(g, cols, part):
        if g == 0:
            acc[:, :, cols] = part.reshape(2, half, -1)
        elif g == 1:
            sent[0, :, :, cols] = part.astype(BF16).reshape(2, half, -1)
        else:
            far[:, cols] = part[:half]
            sent[1, g - 2, :, cols] = part[half:].astype(BF16)

    def down(g):
        rows = flat(group(hid, g)[...])
        tiles(width, 512, lambda cols: emit(g, cols, contract(rows, wd[:, cols], 1, 0)))

    def push(phase, kind, j):
        return go(sent.at[kind, j], got.at[kind, j], p_send.at[phase, kind, j], p_recv.at[phase, kind, j], peer if kind == 2 else sib)

    def sums(phase, compute, copies, buffer, send, recv, before):
        kept = {}
        compute(0)
        for j in range(2):
            copies[j][1].wait_recv()
        compute(1)
        for j in range(2):
            kept[0, j] = push(phase, 0, j)
        for j in range(2):
            copies[j][0].wait_recv()
            passed = relay(buffer, send, recv, j)
            passed.wait_recv()
            if phase == 1 and j == 1 and share:
                down_tile(0)
                down_tile(1)
                down_swap(1)
            compute(2 + j)
            kept[1, j] = push(phase, 1, j)
            kept[1, j].wait_recv()
            sent[2, j] = (far[...] + got[1, j].astype(F32)).astype(BF16)
            kept[2, j] = push(phase, 2, j)
        return kept

    def forward(g):
        gated(g)
        down(g)

    for one in loads[:2] + lanes:
        one.wait()
    kept = sums(0, forward, h_copies, hall, h_send, h_recv, None)
    first, pending = pending, []
    loads.append(fetch(mid_hbm, mid, load.at[4]))
    loads[2].wait()
    loads[3].wait()
    total = jnp.zeros((), F32)
    d_copies, saves = [], []
    factor = (8.0 * half * lax.axis_size("seq")) / count[0:1, 0:1]
    first_row = lax.axis_index("seq") * 2 * half
    used = lengths[0, 0]
    for n in range(1, lengths.shape[1]):
        used += lengths[0, n]
    for j in range(2):
        kept[0, j].wait_recv()
        kept[2, j].wait_recv()
        step = half // 4

        def rows_of(i, so_far):
            r = pl.ds(pl.multiple_of(i * step, step), step)
            value = mid[j, r, :] + acc[j, r, :] + got[0, j, r, :].astype(F32) + got[2, j, r, :].astype(F32)
            out_low[j, r, :] = value.astype(BF16)
            diff = value - teacher[j, r, :].astype(F32)
            place = lax.broadcasted_iota(jnp.int32, (step, 1), 0) + (first_row + j * half + i * step)
            masked = (place < used).astype(F32) * diff
            grad = masked * factor
            mid[j, r, :] = grad
            dall[0, j, r, :] = grad.astype(BF16)
            return so_far + jnp.sum(masked * diff)

        total = lax.fori_loop(0, 4, rows_of, total)
        d_copies.append(spread(dall.at[0], dall, d_send, d_recv, j))
        saves.append(fetch(out_low.at[j], out.at[j], store.at[0, j]))
        saves.append(fetch(mid.at[j], cot.at[j], store.at[1, j]))
    squares[...] = jnp.full(squares.shape, total)

    def backward(g):
        rows = flat(group(dall, g)[...])

        def body(cols):
            grad = contract(rows, wd[cols, :], 1, 1).reshape(2, half, -1)
            part = group(act, g)
            for n in range(6):
                at = third(2 * cols.start, n)
                piece = grad[:, :, 128 * (n // 2) : 128 * (n // 2) + 128]
                part[:, :, at] = (piece * part[:, :, at].astype(F32)).astype(BF16)

        tiles(units, 384, body)
        both = flat(group(act, g)[...])
        tiles(width, 512, lambda cols: emit(g, cols, contract(both, wi[cols, :], 1, 1)))

    for copy in first:
        copy.wait_send()
    order = sorted(range(depth), key=lambda d: (d == 0, abs(2 * d - depth))) if share else []
    parts = [teacher.at[:, :slot, :units], out_low.at[:, :slot, :units]] if share else []
    stage = [wd.at[pl.ds(n * 256, 256)] for n in range(2)]
    swaps, owners = {}, {}

    def down_tile(n):
        if n >= 2:
            swaps[n - 2].wait_send()
        else:
            saves[2 * n].wait()
        cols = pl.ds(pl.multiple_of(zs[order[n]] * 2 * slot, 128), 2 * slot)
        left = dall[:, :, :, cols].reshape(8 * half, 2 * slot)

        parts[n % 2][...] = contract(left, hid[...].reshape(8 * half, units), 0, 0).astype(BF16).reshape(2, slot, units)
        if n == 0:
            down_swap(0)

    def down_swap(n):
        swaps[n] = remote(parts[n % 2].at[1 - x], gx.at[n], gxs.at[n], gxr.at[n], xpeer)

    def down_owner(n):
        swaps[n].wait_recv()
        gx[n] = (parts[n % 2][x].astype(F32) + gx[n].astype(F32)).astype(BF16)
        if n < 2:
            owners[n] = go(gx.at[n], gz.at[n], gzs.at[n], gzr.at[n], zpeers[order[n]])

    kept = sums(1, backward, d_copies, dall, d_send, d_recv, None)
    count = 0
    blocks = width // 256
    left, right = {}, {}

    def weight(left, right, target, start, size):
        held = [one.at[:, :size] for one in stage]

        def store_rows(n, at):
            return pltpu.make_async_copy(held[n], target.at[at, start : start + size], g_store.at[n])

        def body(i, _):
            for n in range(2):
                at = pl.ds(pl.multiple_of(i * 512 + n * 256, 256), 256)

                @pl.when(i > 0)
                def _():
                    store_rows(n, at).wait()

                held[n][...] = contract(left(at), right(start, size), 0, 0).astype(BF16)
                store_rows(n, at).start()
            return 0

        lax.fori_loop(0, width // 512, body, 0)
        for n in range(2):
            store_rows(n, pl.ds(0, 256)).wait()

    if not share:
        weight(lambda at: dall[:, :, :, at].reshape(8 * half, 256), lambda start, size: hid[...].reshape(8 * half, units), gd, 0, units)
    cut = (units + 255) // 256 * 256
    for n in range(2):
        if share:
            down_owner(n)
            down_tile(n + 2)
            down_swap(n + 2)
        start, size = ((0, cut), (cut, 2 * units - cut))[n]
        weight(lambda at: hall[:, :, :, at].reshape(8 * half, 256), lambda start, size: act[:, :, :, start : start + size].reshape(8 * half, size), gi, start, size)
    for j in range(2):
        kept[0, j].wait_recv()
        kept[2, j].wait_recv()
        saves[2 * j + 1].wait()

        def sum_rows(i, _):
            r = pl.ds(pl.multiple_of(i * step, step), step)
            mid[j, r, :] = acc[j, r, :] + got[0, j, r, :].astype(F32) + got[2, j, r, :].astype(F32)
            return 0

        lax.fori_loop(0, 4, sum_rows, 0)
        saves.append(fetch(mid.at[j], dh.at[j], store.at[2, j]))
    if share:
        down_owner(2)
        ends = [fetch(gx.at[2], gd_owner, end.at[0])]
        for n in range(2):
            owners[n].wait_recv()
        down_owner(3)
        far[:slot, :units] = gx[3].astype(F32) + gz[0].astype(F32) + gz[1].astype(F32)
        ends.append(fetch(far.at[:slot, :units], gd, end.at[1]))
        for n in range(2, 4):
            swaps[n].wait_send()
        for one in ends:
            one.wait()
    for copy in pending:
        copy.wait_send()
    for n in (4, 5) if share else (0, 2, 4, 5):
        saves[n].wait()


def ffn(h, wi, wd, mid, teacher, lengths, count, seq):
    rows, width = h.shape
    depth, slot = (seq // 2, width // seq) if seq else (0, 0)
    units = wd.shape[0]
    half = rows // 2
    split = lambda a: a.reshape(2, half, a.shape[-1])
    dma = pltpu.SemaphoreType.DMA
    hbm, vm = pl.BlockSpec(memory_space=pl.ANY), pl.BlockSpec(memory_space=pltpu.VMEM)
    def kernel(*refs):
        ffn_kernel(bool(seq), *(refs if seq else refs[:13] + (None,) + refs[13:]))

    sharing = []
    if seq:
        sharing = [
            pltpu.VMEM((4, slot, units), BF16), pltpu.VMEM((2, slot, units), BF16),
            dma((4,)), dma((4,)), dma((2,)), dma((2,)), dma((2,)),
        ]
    out, cot, dh, gd, gi, squares, *rest = pl.pallas_call(
        kernel,
        name="ffn",
        out_shape=[
            jax.ShapeDtypeStruct((2, half, width), BF16),
            jax.ShapeDtypeStruct((2, half, width), F32),
            jax.ShapeDtypeStruct((2, half, width), F32),
            jax.ShapeDtypeStruct((slot, units), F32) if seq else jax.ShapeDtypeStruct((width, units), BF16),
            jax.ShapeDtypeStruct((width, 2 * units), BF16),
            jax.ShapeDtypeStruct((8, 128), F32),
        ]
        + [jax.ShapeDtypeStruct((slot, units), BF16)] * bool(seq),
        in_specs=[hbm] * 5 + [pl.BlockSpec(memory_space=pltpu.SMEM), vm],
        out_specs=[hbm] * 5 + [vm] + [hbm] * bool(seq),
        scratch_shapes=[
            pltpu.VMEM((width, 2 * units), BF16),
            pltpu.VMEM((units, width), BF16),
            pltpu.VMEM((2, half, width), F32),
            pltpu.VMEM((2, half, width), BF16),
            pltpu.VMEM((4, 2, half, width), BF16),
            pltpu.VMEM((4, 2, half, width), BF16),
            pltpu.VMEM((4, 2, half, 2 * units), BF16),
            pltpu.VMEM((4, 2, half, units), BF16),
            pltpu.VMEM((2, half, width), F32),
            pltpu.VMEM((half, width), F32),
            pltpu.VMEM((2, half, width), BF16),
            pltpu.VMEM((3, 2, half, width), BF16),
            pltpu.VMEM((3, 2, half, width), BF16),
            dma((5,)), dma((3, 2)), dma((3, 2)), dma((3, 2)), dma((3, 2)),
            dma((2, 3, 2)), dma((2, 3, 2)), dma((3, 2)), dma((2,)), dma((units // 64,)),
        ]
        + sharing,
        compiler_params=pltpu.CompilerParams(collective_id=2, has_side_effects=True, vmem_limit_bytes=63 << 20),
    )(split(h), wi, wd, split(mid), split(teacher), lengths, count)
    return out.reshape(rows, width), cot.reshape(rows, width), dh.reshape(rows, width), gd, gi, squares, rest


def pair_rows(block):
    return jnp.concatenate([block[:, :HD], block[:, HD:]], axis=0)


def pair_columns(block):
    rows = block.shape[0] // 2
    return jnp.concatenate([block[:rows], block[rows:]], axis=1)


def attend_back_kernel(q, kv, grad, mixed, probs, grad_q, grad_kv):
    i, pair = pl.program_id(0), pl.program_id(1)
    reach = WINDOW + QROWS
    keys = pl.ds(pl.multiple_of(i * QROWS, QROWS), reach)

    @pl.when((i == 0) & (pair == 0))
    def _():
        grad_kv[...] = jnp.zeros_like(grad_kv)

    queries, grads = pair_rows(q[...]), pair_rows(grad[...])
    weights = probs[0, 0].reshape(2 * QROWS, reach)
    dots = jnp.sum(grads.astype(F32) * pair_rows(mixed[...]).astype(F32), axis=-1, keepdims=True)
    steep = contract(grads, kv[keys, HD:], 1, 1) - dots
    steep = (weights.astype(F32) * steep).astype(BF16)
    grad_q[...] = (pair_columns(contract(steep, kv[keys, :HD], 1, 0)) * (1.0 / math.sqrt(HD))).astype(BF16)
    grad_kv[keys, :HD] += contract(steep, queries, 0, 0)
    grad_kv[keys, HD:] += contract(weights, grads, 0, 0)


def attend_back(queries, extended, grad_mixed, mixed, probs):
    rows, width = mixed.shape
    blocks, pairs, reach = rows // QROWS, width // (2 * HD), WINDOW + QROWS
    block = pl.BlockSpec((QROWS, 2 * HD), lambda i, p: (i, p))
    whole = pl.BlockSpec(extended.shape, lambda i, p: (0, 0))
    return pl.pallas_call(
        attend_back_kernel,
        name="attend_back",
        grid=(blocks, pairs),
        out_shape=[jax.ShapeDtypeStruct((rows, width), BF16), jax.ShapeDtypeStruct(extended.shape, F32)],
        in_specs=[block, whole, block, block, pl.BlockSpec((1, 1, 2, QROWS, reach), lambda i, p: (i, p, 0, 0, 0))],
        out_specs=[block, whole],
        compiler_params=pltpu.CompilerParams(vmem_limit_bytes=48 << 20),
    )(queries, extended, grad_mixed, mixed, probs)


GRAD_COLS = 128
AHEAD = 3


def owner_order(depth):
    return sorted(range(depth), key=lambda d: (d == 0, abs(2 * d - depth)))


class RowSum:
    def __init__(self, source, buffers, sems, where, go):
        self.source, self.go = source, go
        self.core, self.side, self.cross, self.along = buffers
        self.cs, self.cr, self.ys, self.yr, self.xs, self.xr, self.zs_, self.zr = sems
        self.x, self.y, self.c, self.zs, self.sib, self.ypeer, self.xpeer, self.zpeers = where
        self.depth, self.cols = len(self.zs), self.core.shape[-1]
        self.order = owner_order(self.depth)
        self.moved = {}

    def columns(self, y, c):
        return pl.ds(pl.multiple_of((2 * y + c) * self.cols, self.cols), self.cols)

    def first(self, d):
        for h in range(2):
            part = self.source.at[self.zs[d], :, :, self.columns(h, 1 - self.c)]
            self.moved["c", d, h] = self.go(part, self.core.at[d, h], self.cs.at[d, h], self.cr.at[d, h], self.sib)

    def second(self, d):
        for h in range(2):
            self.moved["c", d, h].wait_recv()
        far = 1 - self.y
        own = self.source[self.zs[d], :, :, self.columns(far, self.c)].astype(F32)
        self.core[d, far] = (own + self.core[d, far].astype(F32)).astype(BF16)
        self.moved["y", d] = self.go(self.core.at[d, far], self.side.at[d], self.ys.at[d], self.yr.at[d], self.ypeer)

    def kept(self, d, x):
        own = self.source[self.zs[d], x, :, self.columns(self.y, self.c)].astype(F32)
        return own + self.core[d, self.y, x].astype(F32) + self.side[d, x].astype(F32)

    def third(self, d):
        self.moved["y", d].wait_recv()
        self.side[d, 1 - self.x] = self.kept(d, 1 - self.x).astype(BF16)
        self.moved["x", d] = self.go(self.side.at[d, 1 - self.x], self.cross.at[d], self.xs.at[d], self.xr.at[d], self.xpeer)

    def fourth(self, d):
        self.moved["x", d].wait_recv()
        self.cross[d] = (self.kept(d, self.x) + self.cross[d].astype(F32)).astype(BF16)
        if d:
            self.moved["z", d] = self.go(
                self.cross.at[d], self.along.at[d - 1], self.zs_.at[d - 1], self.zr.at[d - 1], self.zpeers[d]
            )

    def total(self):
        value = self.cross[0].astype(F32)
        for d in range(1, self.depth):
            self.moved["z", d].wait_recv()
            value += self.along[d - 1].astype(F32)
        return value


def norm_back(values, grad, gain):
    r = lax.rsqrt(jnp.mean(values * values, axis=-1, keepdims=True) + EPSILON)
    scaled = grad * gain
    slope = r * r * r * jnp.mean(values * scaled, axis=-1, keepdims=True)
    return r * scaled - values * slope, jnp.sum(grad * values * r, axis=0, keepdims=True)


def finish_kernel(dh_hbm, cot_hbm, middle_hbm, w_out_hbm, w_attn_hbm, mixed_hbm, probs_hbm, qkv_hbm, ext_hbm, normed_hbm,
                  tokens_hbm, gd_hbm, gd_owner, gi_hbm, gain_attn, gain_ffn, squares, count,
                  grad_x, grad_d, grad_i, grad_qkv_out, grad_o, gain_attn_out, gain_ffn_out, loss_out,
                  dh, cot, middle, weight, mixed, probs, qkv, ext, normed, low, dmix, dkv, slabs, slabs_in,
                  gx, gz, gr, own, staged, joined, dz, po, pa, ocore, oside, ocross, oalong, acore, aside, across, aalong, vb,
                  load, p_load, own_load, out_sem, slab_s, slab_r, ds, dr, gxs, gxr, gzs, gzr, grr, o_sems, a_sems, vs, vr):
    z, x, y, c = places()
    depth, width = own.shape[1], own.shape[-1]
    rows, model_width = dh.shape
    seq = 2 * depth
    me = 2 * z + x
    sib, ypeer, xpeer = device(z, x, y, 1 - c), device(z, x, 1 - y, c), device(z, 1 - x, y, c)
    zs = [lax.rem(z + d, depth) for d in range(depth)]
    zpeers = [device(zs[d], x, y, c) for d in range(depth)]
    wt = 2 * y + c
    diagonal = (lax.rem(me + seq - 1 + 2 * x, seq), wt)
    back = [(lax.rem(me + seq - step, seq), wt) for step in (1, 2)]

    def fetch(src, dst, sem):
        copy = pltpu.make_async_copy(src, dst, sem)
        copy.start()
        return copy

    loads = {}
    for n, (name, src, dst) in enumerate((
        ("dh", dh_hbm, dh), ("cot", cot_hbm, cot), ("w_out", w_out_hbm, weight.at[:, :model_width]), ("mixed", mixed_hbm, mixed),
        ("qkv", qkv_hbm, qkv), ("ext", ext_hbm, ext), ("normed", normed_hbm, normed))):
        loads[name] = fetch(src, dst, load.at[n])
    greet([sib, ypeer, xpeer, diagonal] + zpeers[1:])
    started = []

    def go(*args):
        started.append(remote(*args))
        return started[-1]

    chunks = gi_hbm.shape[-1] // width
    gxc, gzc, owned = {}, {}, {}

    def g_ref(k, side):
        return gi_hbm.at[:, side, :, pl.ds(k * width, width)]

    def g_send(k):
        if k < chunks:
            gxc[k] = go(g_ref(k, 1 - x), gx.at[k], gxs.at[k], gxr.at[k], xpeer)

    def g_load(k):
        if k < chunks:
            owned[k] = fetch(g_ref(k, x), own.at[k % 2], own_load.at[k % 2])

    def at_end(d):
        return ((z == 0) & (d == depth - 1)) | ((z == depth - 1) & (d == 1))

    def g_copy(k, d, dst, recv, to):
        return pltpu.make_async_remote_copy(
            src_ref=gx.at[k, zs[d]], dst_ref=dst, send_sem=gzs.at[k, d - 1], recv_sem=recv, device_id=to, device_id_type=MESH)

    def g_owner(k, d):
        return g_copy(k, d, gz.at[k, d - 1], gzr.at[k, d - 1], zpeers[d])

    def g_neighbour(k, d):
        return g_copy(k, d, gr.at[k], grr.at[k], zpeers[depth - d])

    def g_step(k):
        gxc[k].wait_recv()
        g_send(k + AHEAD)
        owned[k].wait()
        for d in range(depth):
            gx[k, zs[d]] = (own[k % 2, zs[d]].astype(F32) + gx[k, zs[d]].astype(F32)).astype(BF16)
            if d == 1 or d == depth - 1:
                pl.when(at_end(d))(lambda d=d: g_neighbour(k, d).start())
                pl.when(jnp.logical_not(at_end(d)))(lambda d=d: g_owner(k, d).start())
        g_load(k + 2)
        if k >= 2:
            g_relay(k - 2)

    def g_relay(k):
        @pl.when((z > 0) & (z < depth - 1))
        def _():
            g_copy(k, 2, gr.at[k], grr.at[k], zpeers[2]).wait_recv()
            gx[k, zs[2]] = (gx[k, zs[2]].astype(F32) + gr[k].astype(F32)).astype(BF16)

        g_owner(k, 2).start()

    stores = {}

    def g_end(k):
        at = k % 2
        staged[at] = gx[k, z].astype(F32)
        for d in range(1, depth):
            missing = ((z == depth - 1) & (d == depth - 1)) | ((z == 0) & (d == 1))

            @pl.when(jnp.logical_not(missing))
            def _():
                g_owner(k, d).wait_recv()
                staged[at] += gz[k, d - 1].astype(F32)

        if at == 1:
            turn = k // 2
            if turn >= 2:
                stores[turn - 2].wait()
            joined[turn % 2] = jnp.stack([staged[0], staged[1]], axis=1)
            stores[turn] = fetch(joined.at[turn % 2], grad_i.at[:, :, pl.ds(turn * width, width)], out_sem.at[turn % 2])

    last = owner_order(depth)[2]
    sent_down = [
        go(gd_owner, dz, ds.at[0], dr.at[0], zpeers[last]),
    ]
    loads["da"] = fetch(gd_hbm, grad_d, load.at[11])
    for k in range(AHEAD):
        g_send(k)
    g_load(0)
    g_load(1)
    where = (x, y, c, zs, sib, ypeer, xpeer, zpeers)
    sum_o = RowSum(po, (ocore, oside, ocross, oalong), o_sems, where, go)
    sum_a = RowSum(pa, (acore, aside, across, aalong), a_sems, where, go)

    step = middle.shape[1]
    steps = rows // step
    mids = [None] * steps

    def mid_load(n):
        if n < steps:
            mids[n] = fetch(middle_hbm.at[pl.ds(n * step, step)], middle.at[n % 2], load.at[8 + n % 2])

    mid_load(0)
    mid_load(1)
    loads["dh"].wait()
    loads["cot"].wait()
    gain_grad = jnp.zeros((1, model_width), F32)
    scale_ffn, scale_attn = as_row(gain_ffn), as_row(gain_attn)
    for n in range(steps):
        mids[n].wait()
        r = pl.ds(n * step, step)
        grad, part = norm_back(middle[n % 2], dh[r, :], scale_ffn)
        grad = cot[r, :] + grad
        cot[r, :] = grad
        low[r, :model_width] = grad.astype(BF16)
        gain_grad += part
        mid_load(n + 2)
    vb[0] = jnp.zeros(vb.shape[1:], F32)
    vb[0, 1:2] = gain_grad
    vb[0, 2:3] = jnp.broadcast_to(squares[0:1, 0:1], (1, model_width))
    loads["w_out"].wait()
    loads["mixed"].wait()
    rows_low = lambda: low[:, :model_width]

    def out_back(cols):
        dmix[:, cols] = contract(rows_low(), weight[cols, :model_width], 1, 1).astype(BF16)

    tiles(model_width, 512, out_back)
    loads["w_attn"] = fetch(w_attn_hbm, weight, load.at[7])

    def out_grad(d, _):
        cols = pl.ds(pl.multiple_of(d * 2 * po.shape[2], 128), 2 * po.shape[2])
        po[d] = contract(low[:, cols], mixed[...], 0, 0).astype(BF16).reshape(po.shape[1:])
        return 0

    lax.fori_loop(0, depth, out_grad, 0)
    for d in sum_o.order:
        sum_o.first(d)
    g_step(0)
    g_step(1)
    blocks, pairs, reach = probs_hbm.shape[0], probs_hbm.shape[1], probs.shape[-1]
    turns = blocks * pairs

    def p_fetch(t):
        return pltpu.make_async_copy(probs_hbm.at[t // pairs, t % pairs], probs.at[t % 2], p_load.at[t % 2])

    p_fetch(0).start()
    p_fetch(1).start()
    dkv[...] = jnp.zeros_like(dkv)
    loads["qkv"].wait()
    loads["ext"].wait()
    for i in range(blocks):
        q_rows, keys = pl.ds(i * QROWS, QROWS), pl.ds(i * QROWS, reach)

        def one(pair, _):
            t = i * pairs + pair
            cols = pl.ds(pl.multiple_of(pair * 2 * HD, 2 * HD), 2 * HD)
            queries, grads = pair_rows(qkv[q_rows, cols]), pair_rows(dmix[q_rows, cols])
            outs = pair_rows(mixed[q_rows, cols])
            dots = jnp.sum(grads.astype(F32) * outs.astype(F32), axis=-1, keepdims=True)
            slot = lax.rem(t, 2)
            p_fetch(t).wait()
            weights = flat(probs[slot])
            steep = contract(grads, ext[keys, HD:], 1, 1) - dots
            steep = (weights.astype(F32) * steep).astype(BF16)
            low[q_rows, cols] = (pair_columns(contract(steep, ext[keys, :HD], 1, 0)) * (1.0 / math.sqrt(HD))).astype(BF16)
            dkv[keys, :HD] += contract(steep, queries, 0, 0)
            dkv[keys, HD:] += contract(weights, grads, 0, 0)

            @pl.when(t + 2 < turns)
            def _():
                p_fetch(t + 2).start()

            return 0

        lax.fori_loop(0, pairs // 2, one, 0)
        if i == 0:
            for d in sum_o.order:
                sum_o.second(d)
        g_step(2 + 2 * i)
        lax.fori_loop(pairs // 2, pairs, one, 0)
        g_step(3 + 2 * i)
    for n in range(2):
        slabs[n] = dkv[(1 - n) * rows : (2 - n) * rows, :].astype(BF16)
    returned = [go(slabs.at[n], slabs_in.at[n], slab_s.at[n], slab_r.at[n], back[n]) for n in range(2)]
    loads["normed"].wait()
    slot_rows = model_width // seq

    def query_grad(d, _):
        cols = pl.ds(pl.multiple_of(d * 2 * slot_rows, 128), 2 * slot_rows)
        pa[d, :, :slot_rows] = contract(low[:, cols], normed[...], 0, 0).astype(BF16).reshape(2, slot_rows, model_width)
        return 0

    lax.fori_loop(0, depth, query_grad, 0)
    g_step(6)
    for one in returned:
        one.wait_recv()
    summed = dkv[2 * rows :, :] + slabs_in[0].astype(F32) + slabs_in[1].astype(F32)
    low[:, model_width : model_width + HD] = (summed[:, :HD] * (1.0 / math.sqrt(HD))).astype(BF16)
    low[:, model_width + HD :] = summed[:, HD:].astype(BF16)
    kv_grad = contract(low[:, model_width:], normed[...], 0, 0).astype(BF16)
    kv_rows = HD // seq
    for n in range(2):
        part = kv_grad[n * HD : (n + 1) * HD].reshape(depth, 2, kv_rows, model_width)
        pa[:, :, slot_rows + n * kv_rows : slot_rows + (n + 1) * kv_rows] = part
    for d in sum_a.order:
        sum_a.first(d)
    loads["tokens"] = fetch(tokens_hbm, mixed, load.at[3])
    loads["w_attn"].wait()

    def attn_back(cols):
        dh[:, cols] = contract(low[...], weight[cols, :], 1, 1)

    tiles(model_width, 512, attn_back)
    g_step(7)
    loads["tokens"].wait()

    def last_norm(n, so_far):
        r = pl.ds(pl.multiple_of(n * step, step), step)
        grad, part = norm_back(mixed[r, :].astype(F32), dh[r, :], scale_attn)
        cot[r, :] += grad
        return so_far + part

    vb[0, 0:1] = lax.fori_loop(0, steps, last_norm, jnp.zeros((1, model_width), F32))
    saved = fetch(cot, grad_x, load.at[0])

    vc = {}

    def v_first():
        vc[0] = go(vb.at[0], vb.at[1], vs.at[0], vr.at[0], sib)

    def v_swap(n, to):
        vc[n - 1].wait_recv()
        vb[2 * n] = vb[2 * n - 2] + vb[2 * n - 1]
        vc[n] = go(vb.at[2 * n], vb.at[2 * n + 1], vs.at[n], vr.at[n], to)

    def v_along():
        vc[2].wait_recv()
        vb[6] = vb[4] + vb[5]
        for d in range(1, depth):
            vc[2 + d] = go(vb.at[6], vb.at[6 + d], vs.at[2 + d], vr.at[2 + d], zpeers[d])

    def v_end():
        for d in range(1, depth):
            vc[2 + d].wait_recv()
        total = vb[6 + z]
        for n in range(1, depth):
            total += vb[6 + lax.rem(z - n + depth, depth)]
        gain_attn_out[...] = as_lines(total[0:1])
        gain_ffn_out[...] = as_lines(total[1:2])
        loss_out[...] = total[2:3, 0:1] / (count[0:1, 0:1] * model_width)

    v_first()
    o, a = sum_o.order, sum_a.order
    after = {
        8: [lambda: sum_a.second(a[0]), lambda: sum_o.third(o[0]), lambda: sum_o.third(o[1]), lambda: v_swap(1, ypeer)],
        9: [lambda: sum_o.third(o[2]), lambda: sum_o.third(o[3])],
        10: [lambda: sum_a.second(a[1]), lambda: sum_a.third(a[0]), lambda: sum_o.fourth(o[0]), lambda: v_swap(2, xpeer)],
        11: [lambda: sum_o.fourth(o[1])],
        12: [lambda: sum_a.second(a[2]), lambda: sum_a.third(a[1]), lambda: sum_a.fourth(a[0]), lambda: sum_o.fourth(o[2]), v_along],
        13: [lambda: sum_o.fourth(o[3])],
        14: [lambda: sum_a.second(a[3]), lambda: sum_a.third(a[2]), lambda: sum_a.fourth(a[1])],
        15: [v_end],
        16: [lambda: sum_a.third(a[3]), lambda: sum_a.fourth(a[2])],
    }
    ended = 0
    for k in range(8, chunks):
        g_step(k)
        for step in after.pop(k, ()):
            step()
        while ended < k - 4:
            g_end(ended)
            ended += 1
    g_relay(chunks - 2)
    g_relay(chunks - 1)
    for key in sorted(after):
        for step in after[key]:
            step()
    sum_a.fourth(a[3])
    for k in range(ended, chunks):
        g_end(k)
    grad_o[...] = sum_o.total()
    for one in sent_down:
        one.wait_recv()
    loads["da"].wait()
    grad_d[...] += dz[...].astype(F32)
    grad_qkv_out[...] = sum_a.total()
    for copy in started:
        copy.wait_send()
    for k in range(chunks):
        for d in range(1, depth):
            g_owner(k, d).wait_send()
    saved.wait()
    stores[chunks // 2 - 2].wait()
    stores[chunks // 2 - 1].wait()


def finish(dh, cot, middle, w_out, w_attn, mixed, probs, qkv, ext, normed, tokens, gd, gd_rest, gi, gain_attn, gain_ffn, squares, count, seq):
    rows, model_width = dh.shape
    depth, slot, units = seq // 2, model_width // seq, gi.shape[-1] // 2
    kv_rows, cols = 2 * HD // seq, model_width // 4
    blocks, _, _, _, reach = probs.shape
    chunks = 2 * units // GRAD_COLS
    qkv_slot = slot + kv_rows
    step = 128
    dma = pltpu.SemaphoreType.DMA
    hbm, vm = pl.BlockSpec(memory_space=pl.ANY), pl.BlockSpec(memory_space=pltpu.VMEM)

    def sum_buffers(n):
        return [
            pltpu.VMEM((depth, 2, 2, n, cols), BF16),
            pltpu.VMEM((depth, 2, n, cols), BF16),
            pltpu.VMEM((depth, n, cols), BF16),
            pltpu.VMEM((depth - 1, n, cols), BF16),
        ]

    sum_sems = [dma((depth, 2)), dma((depth, 2)), dma((depth,)), dma((depth,)), dma((depth,)), dma((depth,)), dma((depth - 1,)), dma((depth - 1,))]

    def kernel(*refs):
        refs = list(refs)
        at = len(refs) - 18
        o_sems, a_sems = refs[at : at + 8], refs[at + 8 : at + 16]
        finish_kernel(*refs[:at], o_sems, a_sems, *refs[at + 16 :])

    return pl.pallas_call(
        kernel,
        name="finish",
        out_shape=[
            jax.ShapeDtypeStruct((rows, model_width), F32),
            jax.ShapeDtypeStruct((slot, units), F32),
            jax.ShapeDtypeStruct((slot, 2, units), F32),
            jax.ShapeDtypeStruct((qkv_slot, cols), F32),
            jax.ShapeDtypeStruct((slot, cols), F32),
            jax.ShapeDtypeStruct((model_width // 128, 128), F32),
            jax.ShapeDtypeStruct((model_width // 128, 128), F32),
            jax.ShapeDtypeStruct((1, 1), F32),
        ],
        in_specs=[hbm] * 14 + [vm] * 4,
        out_specs=[hbm, vm, hbm] + [vm] * 5,
        scratch_shapes=[
            pltpu.VMEM((rows, model_width), F32),
            pltpu.VMEM((rows, model_width), F32),
            pltpu.VMEM((2, step, model_width), F32),
            pltpu.VMEM(w_attn.shape, BF16),
            pltpu.VMEM((rows, model_width), BF16),
            pltpu.VMEM((2, 2, QROWS, reach), BF16),
            pltpu.VMEM(qkv.shape, BF16),
            pltpu.VMEM(ext.shape, BF16),
            pltpu.VMEM((rows, model_width), BF16),
            pltpu.VMEM(qkv.shape, BF16),
            pltpu.VMEM((rows, model_width), BF16),
            pltpu.VMEM(ext.shape, F32),
            pltpu.VMEM((2, rows, 2 * HD), BF16),
            pltpu.VMEM((2, rows, 2 * HD), BF16),
            pltpu.VMEM((chunks, depth, slot, GRAD_COLS), BF16),
            pltpu.VMEM((chunks, depth - 1, slot, GRAD_COLS), BF16),
            pltpu.VMEM((chunks, slot, GRAD_COLS), BF16),
            pltpu.VMEM((2, depth, slot, GRAD_COLS), BF16),
            pltpu.VMEM((2, slot, GRAD_COLS), F32),
            pltpu.VMEM((2, slot, 2, GRAD_COLS), F32),
            pltpu.VMEM((slot, units), BF16),
            pltpu.VMEM((depth, 2, slot, model_width), BF16),
            pltpu.VMEM((depth, 2, qkv_slot, model_width), BF16),
        ]
        + sum_buffers(slot)
        + sum_buffers(qkv_slot)
        + [pltpu.VMEM((6 + depth, 8, model_width), F32)]
        + [
            dma((12,)), dma((2,)), dma((2,)), dma((2,)), dma((2,)), dma((2,)), dma((1,)), dma((1,)),
            dma((chunks,)), dma((chunks,)), dma((chunks, depth - 1)), dma((chunks, depth - 1)), dma((chunks,)),
        ]
        + sum_sems
        + sum_sems
        + [dma((2 + depth,)), dma((2 + depth,))],
        compiler_params=pltpu.CompilerParams(collective_id=1, has_side_effects=True, vmem_limit_bytes=63 << 20),
    )(
        dh, cot, middle, w_out, w_attn, mixed, probs, qkv, ext, normed, tokens,
        gd, *gd_rest, gi.reshape(depth, 2, slot, 2 * units),
        gain_attn.reshape(-1, 128), gain_ffn.reshape(-1, 128), squares, count,
    )


SHARERS = 8


def as_row(ref):
    return jnp.concatenate([ref[n : n + 1, :] for n in range(ref.shape[0])], axis=1)


def as_lines(row):
    return jnp.concatenate([row[:, n : n + 128] for n in range(0, row.shape[1], 128)], axis=0)


def begin_kernel(lengths, tokens_hbm, w_attn_hbm, w_out_hbm, gain_attn, gain_ffn,
                 attn_out, out_out, qkv_out, ext_out, normed_out, mixed_out, probs_out, middle_out, low_out, count_out,
                 tokens, normed, w_attn, w_out, qkv, ext, mixed, probs, bias, acc, counts,
                 load, c_send, c_recv, o_send, o_recv, s_send, s_recv, h_send, h_recv, n_send, n_recv, p_store, store):
    seq, wt = lax.axis_index("seq"), lax.axis_index("wt")
    n_seq = lax.axis_size("seq")
    y, c = wt // 2, wt % 2
    w_sib, w_peer, w_far = 2 * y + 1 - c, 2 * (1 - y) + c, 2 * (1 - y) + 1 - c
    sib, peer = (seq, w_sib), (seq, w_peer)
    rows, width = tokens.shape
    depth = w_attn_hbm.shape[0]
    pairs = width // (2 * HD)
    blocks, reach = rows // QROWS, WINDOW + QROWS
    slabs = WINDOW // rows
    first = seq // SHARERS * SHARERS
    place = lax.rem(seq, SHARERS)
    others = [(first + lax.rem(place + n, SHARERS), wt) for n in range(1, SHARERS)]
    ahead = [(lax.rem(seq + n, n_seq), wt) for n in range(1, slabs + 1)]
    behind = [(lax.rem(seq + n_seq - n, n_seq), wt) for n in range(1, slabs + 1)]

    def fetch(src, dst, sem):
        copy = pltpu.make_async_copy(src, dst, sem)
        copy.start()
        return copy

    def shard(w, size=None, at=0):
        return pl.ds(pl.multiple_of(w * depth + at, 16), depth if size is None else size)

    loads = [
        fetch(tokens_hbm, tokens, load.at[0]),
        fetch(w_attn_hbm, w_attn.at[shard(wt)], load.at[1]),
        fetch(w_out_hbm, w_out.at[shard(wt)], load.at[2]),
    ]
    greet([sib, peer] + others + (ahead + behind if n_seq > SHARERS else []))
    started = []

    def go(*args):
        started.append(remote(*args))
        return started[-1]

    def chunk(k):
        return pl.ds(pl.multiple_of(lax.rem(k + pairs, pairs + 1) * 2 * HD, 2 * HD), 2 * HD)

    def chunk_copy(kind, k):
        at = chunk(k)
        w, to = ((wt, peer), (wt, sib), (w_peer, sib))[kind]
        src = w_attn_hbm.at[:, at] if kind < 2 else w_attn.at[shard(w), at]
        return pltpu.make_async_remote_copy(
            src_ref=src, dst_ref=w_attn.at[shard(w), at], send_sem=c_send.at[kind, k], recv_sem=c_recv.at[kind, k],
            device_id=to, device_id_type=MESH)

    def arrived(kind, k):
        w = (w_peer, w_sib, w_far)[kind]
        at = chunk(k)
        here = w_attn.at[shard(w), at]
        pltpu.make_async_copy(here, here, c_recv.at[kind, k]).wait()

    chunk_copy(0, 0).start()
    slice_rows = depth // SHARERS

    def slice_at(w, n):
        return shard(w, slice_rows, n * slice_rows)

    mine = pl.ds(pl.multiple_of(place * slice_rows, 16), slice_rows)
    for k in range(pairs + 1):
        chunk_copy(1, k).start()
    whole = go(w_out_hbm, w_out.at[shard(wt)], o_send.at[1], o_recv.at[1], sib)

    def send_after(k):
        chunk_copy(0, k).wait_send()
        chunk_copy(0, k + 2).start()

    n_len = lengths.shape[1]
    ends = [lengths[0, 0]]
    for n in range(1, n_len):
        ends.append(ends[-1] + lengths[0, n])
    stream = n_seq * rows

    def ids(positions):
        number = jnp.zeros(positions.shape, jnp.int32) - 1
        for n in range(n_len):
            start = ends[n - 1] if n else 0
            number += (positions >= start).astype(jnp.int32)
        inside = (positions >= 0) & (positions < ends[-1])
        return jnp.where(inside, number, -(positions + 2 * stream))

    base = seq * rows
    q_ids = ids(lax.broadcasted_iota(jnp.int32, (rows, 1), 0) + base)
    k_ids = ids(lax.broadcasted_iota(jnp.int32, (1, rows + WINDOW), 1) + (base - WINDOW))
    counts[0] = jnp.full(counts.shape[1:], ends[-1]).astype(F32)
    number = go(counts.at[0], counts.at[1], n_send.at[0], n_recv.at[0], sib)

    loads[0].wait()
    scale_attn = as_row(gain_attn)
    part = 128

    def norm_rows(n, _):
        r = pl.ds(pl.multiple_of(n * part, part), part)
        values = tokens[r, :].astype(F32)
        scale = lax.rsqrt(jnp.mean(values * values, axis=-1, keepdims=True) + EPSILON)
        normed[r, :] = (values * scale * scale_attn).astype(BF16)
        return 0

    lax.fori_loop(0, rows // part, norm_rows, 0)
    stores = [fetch(normed, normed_out, store.at[0])]
    for i in range(blocks):
        row = lax.broadcasted_iota(jnp.int32, (QROWS, reach), 0)
        offset = lax.broadcasted_iota(jnp.int32, (QROWS, reach), 1) - WINDOW - row
        here, there = q_ids[i * QROWS : (i + 1) * QROWS], k_ids[:, i * QROWS : i * QROWS + reach]
        bias[i] = jnp.where((offset <= 0) & (offset > -WINDOW) & (here == there), 0.0, NEGATIVE)
    number.wait_recv()
    counts[2] = counts[0] + counts[1]
    chunk_copy(0, 0).wait_send()
    chunk_copy(0, 1).start()
    chunk_copy(0, 2).start()

    def relay(k):
        arrived(0, k)
        chunk_copy(2, k).start()

    loads[1].wait()
    relay(0)
    arrived(1, 0)
    arrived(2, 0)
    kv_cols = slice(width, width + 2 * HD)
    key_value = contract(normed[...], w_attn[:, kv_cols], 1, 0).astype(BF16)
    qkv[:, kv_cols] = key_value
    ext[WINDOW:, :] = key_value
    halo = {}

    def halo_send(half):
        for n in range(slabs):
            cols, at = pl.ds(half * HD, HD), half * slabs + n
            dst = ext.at[pl.ds(WINDOW - (n + 1) * rows, rows), cols]
            halo[half, n] = remote(ext.at[pl.ds(WINDOW, rows), cols], dst, h_send.at[at], h_recv.at[at], ahead[n])

    halo_send(0)

    def project_queries(p):
        cols = pl.ds(pl.multiple_of(p * 2 * HD, 2 * HD), 2 * HD)
        arrived(1, p + 1)
        arrived(2, p + 1)
        qkv[:, cols] = contract(normed[...], w_attn[:, cols], 1, 0).astype(BF16)

    send_after(1)
    relay(1)
    number = go(counts.at[2], counts.at[3], n_send.at[1], n_recv.at[1], peer)
    eighth = go(w_out_hbm.at[mine], w_out.at[slice_at(wt, place)], o_send.at[0], o_recv.at[0], peer)
    project_queries(0)
    for n in range(slabs):
        halo[0, n].wait_send()
    halo_send(1)
    send_after(2)
    relay(2)
    for n in range(slabs):
        halo[0, n].wait_recv()
    eighth.wait_recv()
    spread = [
        go(w_out.at[slice_at(w_peer, place)], w_out.at[slice_at(w_peer, place)], s_send.at[n], s_recv.at[n], others[n])
        for n in range(SHARERS - 1)
    ]
    number.wait_recv()
    count_out[...] = counts[2] + counts[3]
    factor = math.log2(math.e) / math.sqrt(HD)

    def p_copy(i, p):
        return pltpu.make_async_copy(probs.at[i], probs_out.at[i, p], p_store.at[i])

    def heads(p, _, values=None):
        @pl.when(jnp.asarray(p) + 3 <= pairs)
        def _():
            relay(p + 3)

        @pl.when(jnp.asarray(p) + 5 <= pairs)
        def _():
            send_after(p + 3)

        @pl.when(jnp.asarray(p) + 1 < pairs)
        def _():
            project_queries(p + 1)

        cols = pl.ds(pl.multiple_of(p * 2 * HD, 2 * HD), 2 * HD)
        for i in range(blocks):
            q_rows, keys = pl.ds(i * QROWS, QROWS), pl.ds(i * QROWS, reach)
            scores = contract(pair_rows(qkv[q_rows, cols]), ext[keys, :HD], 1, 1) * factor
            shifted = scores.reshape(2, QROWS, reach) + bias[i][None]
            powers = jnp.exp2(shifted - jnp.max(shifted, axis=-1, keepdims=True))
            weights = (powers * (1.0 / jnp.sum(powers, axis=-1, keepdims=True))).astype(BF16)

            @pl.when(jnp.asarray(p) > 0)
            def _():
                p_copy(i, p - 1).wait()

            probs[i] = weights
            p_copy(i, p).start()
            if values is not None and i == 0:
                for one in values:
                    one.wait_recv()
            outs = contract(weights.reshape(2 * QROWS, reach), ext[keys, HD:], 1, 0)
            mixed[q_rows, cols] = pair_columns(outs).astype(BF16)
        return 0

    heads(0, 0, [halo[1, n] for n in range(slabs)])

    def keep_shard(w, n):
        return fetch(w_out.at[shard(w)], out_out.at[shard(w)], store.at[n])

    loads[2].wait()
    whole.wait_recv()
    stores += [keep_shard(wt, 5), keep_shard(w_sib, 7)]
    stores.append(fetch(ext, ext_out, store.at[1]))
    lax.fori_loop(1, pairs - 1, heads, 0)
    stores.append(fetch(w_attn, attn_out, store.at[4]))
    for one in spread:
        one.wait_recv()
    stores.append(keep_shard(w_peer, 8))
    passed = go(w_out.at[shard(w_peer)], w_out.at[shard(w_peer)], o_send.at[2], o_recv.at[2], sib)
    heads(pairs - 1, 0)
    stores += [fetch(qkv, qkv_out, store.at[2]), fetch(mixed, mixed_out, store.at[3])]
    passed.wait_recv()
    stores.append(keep_shard(w_far, 9))

    def project(cols):
        acc[:, cols] = tokens[:, cols].astype(F32) + contract(mixed[...], w_out[:, cols], 1, 0)

    tiles(width, 512, project)
    stores.append(fetch(acc, middle_out, store.at[6]))
    stores[0].wait()

    scale_ffn = as_row(gain_ffn)

    def norm_again(n, _):
        r = pl.ds(pl.multiple_of(n * part, part), part)
        values = acc[r, :]
        scale = lax.rsqrt(jnp.mean(values * values, axis=-1, keepdims=True) + EPSILON)
        normed[r, :] = (values * scale * scale_ffn).astype(BF16)
        return 0

    lax.fori_loop(0, rows // part, norm_again, 0)
    stores.append(fetch(normed, low_out, store.at[0]))
    for i in range(blocks):
        p_copy(i, pairs - 1).wait()
    for one in stores[1:]:
        one.wait()
    chunk_copy(0, pairs - 1).wait_send()
    chunk_copy(0, pairs).wait_send()
    for k in range(pairs + 1):
        for kind in range(1, 3):
            chunk_copy(kind, k).wait_send()
    for one in started + [halo[1, n] for n in range(slabs)]:
        one.wait_send()


def begin(lengths, tokens, w_attn, w_out, gain_attn, gain_ffn):
    rows, width = tokens.shape
    shards = 4
    depth = w_out.shape[0]
    pairs, blocks, reach = width // (2 * HD), rows // QROWS, WINDOW + QROWS
    columns = width + 2 * HD
    dma = pltpu.SemaphoreType.DMA
    hbm, vm = pl.BlockSpec(memory_space=pl.ANY), pl.BlockSpec(memory_space=pltpu.VMEM)
    shape = jax.ShapeDtypeStruct
    return pl.pallas_call(
        begin_kernel,
        name="begin",
        out_shape=[
            shape((width, columns), BF16),
            shape((width, width), BF16),
            shape((rows, columns), BF16),
            shape((rows + WINDOW, 2 * HD), BF16),
            shape((rows, width), BF16),
            shape((rows, width), BF16),
            shape((blocks, pairs, 2, QROWS, reach), BF16),
            shape((rows, width), F32),
            shape((rows, width), BF16),
            shape((8, 128), F32),
        ],
        in_specs=[pl.BlockSpec(memory_space=pltpu.SMEM)] + [hbm] * 3 + [vm] * 2,
        out_specs=[hbm] * 9 + [vm],
        scratch_shapes=[
            pltpu.VMEM((rows, width), BF16),
            pltpu.VMEM((rows, width), BF16),
            pltpu.VMEM((shards * depth, columns), BF16),
            pltpu.VMEM((shards * depth, width), BF16),
            pltpu.VMEM((rows, columns), BF16),
            pltpu.VMEM((rows + WINDOW, 2 * HD), BF16),
            pltpu.VMEM((rows, width), BF16),
            pltpu.VMEM((blocks, 2, QROWS, reach), BF16),
            pltpu.VMEM((blocks, QROWS, reach), F32),
            pltpu.VMEM((rows, width), F32),
            pltpu.VMEM((4, 8, 128), F32),
            dma((3,)), dma((3, pairs + 1)), dma((3, pairs + 1)), dma((3,)), dma((3,)), dma((SHARERS - 1,)), dma((SHARERS - 1,)),
            dma((2 * WINDOW // rows,)), dma((2 * WINDOW // rows,)), dma((2,)), dma((2,)), dma((blocks,)), dma((10,)),
        ],
        compiler_params=pltpu.CompilerParams(collective_id=3, has_side_effects=True, vmem_limit_bytes=60 << 20),
    )(lengths, tokens, w_attn, w_out, gain_attn.reshape(-1, 128), gain_ffn.reshape(-1, 128))


def passed_along(block, axis, distance):
    devices = range(lax.axis_size(axis))
    route = [(i - distance, i) for i in devices if i - distance in devices]
    return lax.ppermute(block, axis, route)


def rms_scale(values, gain):
    return values * lax.rsqrt(jnp.mean(values * values, axis=-1, keepdims=True) + EPSILON) * gain


def per_device(tokens, teacher, seq_lengths, w_attn, w_out, w_in, w_down, gain_attn, gain_ffn):
    tok_rows = tokens.shape[1]
    model_width = tokens.shape[2]
    seq_devices = lax.axis_size("seq")
    (attn_full, out_full, qkv, extended, normed, mixed_b, probs, middle, normed_two, count) = begin(
        seq_lengths, tokens[0], w_attn, w_out, gain_attn, gain_ffn
    )
    units = w_down.shape[0]
    w_pair = jnp.swapaxes(w_in, 0, 1)
    slot, kv_slot = model_width // seq_devices, HD // seq_devices
    aligned = seq_devices == 8 and slot % 16 == 0 and kv_slot % 16 == 0
    output, cotangent, grad_norm_two, grad_down, grad_in, squares, grad_down_rest = ffn(
        normed_two, w_pair, w_down, middle, teacher[0], seq_lengths, count, seq_devices if aligned else 0
    )
    if aligned:
        grad_inputs, grad_down, grad_in, grad_attn, grad_out, gain_attn_all, gain_ffn_all, loss = finish(
            grad_norm_two, cotangent, middle, out_full, attn_full, mixed_b, probs, qkv, extended, normed, tokens[0],
            grad_down, grad_down_rest, grad_in, gain_attn, gain_ffn, squares, count, seq_devices,
        )
    else:
        _, norm_one_pull = jax.vjp(rms_scale, tokens[0].astype(jnp.float32), gain_attn)
        _, norm_two_pull = jax.vjp(rms_scale, middle, gain_ffn)
        grad_middle_norm, grad_gain_ffn = norm_two_pull(grad_norm_two)
        grad_middle = cotangent + grad_middle_norm
        grad_mid_low = grad_middle.astype(jnp.bfloat16)
        grad_out = jnp.einsum("te,td->ed", grad_mid_low, mixed_b, preferred_element_type=jnp.float32)
        grad_mixed = jnp.einsum("te,de->td", grad_mid_low, out_full, preferred_element_type=jnp.float32)
        grad_query, grad_ext = attend_back(qkv, extended, grad_mixed.astype(jnp.bfloat16), mixed_b, probs)
        edge_rows = WINDOW
        grad_kv = grad_ext[edge_rows:]
        for back_step in range(1, WINDOW // tok_rows + 1):
            slab_rows = grad_ext[
                edge_rows - back_step * tok_rows : edge_rows - (back_step - 1) * tok_rows
            ]
            grad_kv = grad_kv + passed_along(slab_rows, "seq", -back_step)
        grad_key = (grad_kv[:, :HD] * (1.0 / math.sqrt(HD))).astype(jnp.bfloat16)
        grad_qkv = jnp.concatenate([grad_query, grad_key, grad_kv[:, HD:].astype(jnp.bfloat16)], axis=1)
        grad_attn = jnp.einsum("te,td->ed", grad_qkv, normed, preferred_element_type=jnp.float32)
        grad_normed = jnp.einsum("te,de->td", grad_qkv, attn_full, preferred_element_type=jnp.float32)
        grad_input_norm, grad_gain_attn = norm_one_pull(grad_normed)
        grad_inputs = grad_middle + grad_input_norm
        grad_attn = grad_attn.astype(jnp.bfloat16)
        grad_key, grad_value = (
            grad_attn[model_width + at : model_width + at + HD].reshape(seq_devices, kv_slot, model_width) for at in (0, HD)
        )
        packed = jnp.concatenate(
            [
                grad_attn[:model_width].reshape(seq_devices, slot, model_width),
                grad_key,
                grad_value,
                grad_out.astype(jnp.bfloat16).reshape(seq_devices, slot, model_width),
            ],
            axis=1,
        )
        small = jnp.stack([grad_gain_attn, grad_gain_ffn, jnp.full((model_width,), squares[0, 0])] + [jnp.zeros_like(grad_gain_attn)] * 5)
        grad_in = jnp.moveaxis(grad_in.reshape(model_width, units // 128, 2, 128), 2, 0)
        grad_down, grad_in = grad_down.reshape(seq_devices, slot, -1), grad_in.reshape(2, seq_devices, slot, -1)
        grad_down, grad_in, packed, small = reduce_plain(grad_down, grad_in, packed, small)
        grad_attn, grad_out = packed[:-slot], packed[-slot:]
        grad_in = jnp.swapaxes(grad_in, 0, 1)
        gain_attn_all, gain_ffn_all = small[0], small[1]
        loss = small[2, 0] / (count[0, 0] * model_width)
    grad_queries = grad_attn[:slot].T
    grad_keyvals = grad_attn[slot:].T.reshape(-1, 2, kv_slot)
    grad_out = grad_out.T
    grad_down = grad_down.T
    return (
        output[None],
        loss.reshape(()),
        grad_inputs[None],
        grad_queries,
        grad_keyvals,
        grad_out,
        grad_in,
        grad_down,
        gain_attn_all.reshape(-1),
        gain_ffn_all.reshape(-1),
    )


def solution(mesh):
    in_specs = (
        P("wt", "seq", None),
        P("wt", "seq", None),
        P("wt", None),
        P("wt", None),
        P("wt", None),
        P(None, None, "wt"),
        P("wt", None),
        P(),
        P(),
    )
    out_specs = (
        P("wt", "seq", None),
        P(),
        P("wt", "seq", None),
        P("wt", "seq"),
        P("wt", None, "seq"),
        P("wt", "seq"),
        P("seq", None, "wt"),
        P("wt", "seq"),
        P(),
        P(),
    )
    return jax.shard_map(
        per_device, mesh=mesh, in_specs=in_specs, out_specs=out_specs, check_vma=False
    )
```

```python
import functools
import math

import jax
import jax.numpy as jnp
from jax import lax
from jax.experimental import pallas as pl
from jax.experimental.pallas import tpu as pltpu
from jax.sharding import PartitionSpec as P

HEADS = 12
HD = 128
WINDOW = 1024
QROWS = 256


EPSILON = 1e-06
NEGATIVE = -1e30

MESH = pl.DeviceIdType.MESH
F32 = jnp.float32
BF16 = jnp.bfloat16


def places():
    seq, wt = lax.axis_index("seq"), lax.axis_index("wt")
    return seq // 2, seq % 2, wt // 2, wt % 2


def device(z, x, y, c):
    return (z * 2 + x, y * 2 + c)


def remote(src, dst, send, recv, to):
    copy = pltpu.make_async_remote_copy(
        src_ref=src, dst_ref=dst, send_sem=send, recv_sem=recv, device_id=to, device_id_type=MESH
    )
    copy.start()
    return copy


def greet(devices):
    barrier = pltpu.get_barrier_semaphore()
    for one in devices:
        pl.semaphore_signal(barrier, inc=1, device_id=one, device_id_type=MESH)
    pl.semaphore_wait(barrier, len(devices))


def reduce_plain(gd, gi, p, v):
    gd = lax.psum_scatter(gd, "seq", scatter_dimension=0, tiled=False).astype(F32)
    gi = lax.psum_scatter(gi, "seq", scatter_dimension=1, tiled=False).astype(F32)
    p = lax.psum_scatter(p, "seq", scatter_dimension=0, tiled=False)
    p = lax.psum_scatter(p, "wt", scatter_dimension=1, tiled=True).astype(F32)
    return gd, gi, p, lax.psum(v, ("seq", "wt"))


def contract(a, b, dim_a, dim_b):
    return lax.dot_general(a, b, (((dim_a,), (dim_b,)), ((), ())), preferred_element_type=F32)


def tiles(total, width, body):
    def step(i, _):
        body(pl.ds(pl.multiple_of(i * width, width), width))
        return 0

    lax.fori_loop(0, total // width, step, 0)


def flat(block):
    return block.reshape(-1, block.shape[-1])


def ffn_kernel(share, h, wi_hbm, wd_hbm, mid_hbm, teacher_hbm, lengths, count, out, cot, dh, gd, gi, squares, gd_owner,
               wi, wd, mid, teacher, hall, dall, act, hid, acc, far, out_low, sent, got,
               load, h_send, h_recv, d_send, d_recv, p_send, p_recv, store, g_store, w_load, *sharing):
    z, x, y, c = places()
    sib, peer = device(z, x, y, 1 - c), device(z, x, 1 - y, c)
    half, width = h.shape[1:]
    units = wd.shape[0]

    def fetch(src, dst, sem):
        copy = pltpu.make_async_copy(src, dst, sem)
        copy.start()
        return copy

    loads = [fetch(*pair, load.at[n]) for n, pair in enumerate(
        ((h, hall.at[0]), (wd_hbm, wd), (teacher_hbm, teacher)))]
    lanes = [fetch(wi_hbm.at[n % 2, :, pl.ds(n // 2 * 128, 128)], wi.at[:, pl.ds(n * 128, 128)], w_load.at[n]) for n in range(units // 64)]
    if share:
        gx, gz, gxs, gxr, gzs, gzr, end = sharing
        depth, slot = lax.axis_size("seq") // 2, gx.shape[1]
        zs = [lax.rem(z + d, depth) for d in range(depth)]
        xpeer, zpeers = device(z, 1 - x, y, c), [device(zs[d], x, y, c) for d in range(depth)]
    greet([sib, peer] + ([xpeer] + zpeers[1:] if share else []))
    pending = []

    def go(*args):
        nonlocal pending
        pending.append(remote(*args))
        return pending[-1]

    def spread(src, dst, send, recv, j):
        a = go(src.at[j], dst.at[2, j], send.at[0, j], recv.at[0, j], peer)
        b = go(src.at[j], dst.at[1, j], send.at[1, j], recv.at[1, j], sib)
        return a, b

    def relay(dst, send, recv, j):
        return go(dst.at[2, j], dst.at[3, j], send.at[2, j], recv.at[2, j], sib)

    def group(ref, g):
        return ref.at[2:4, g - 2] if g >= 2 else ref.at[g]

    h_copies = [spread(h, hall, h_send, h_recv, j) for j in range(2)]

    def third(start, n):
        return pl.ds(pl.multiple_of(start + 128 * n, 128), 128)

    def gated(g):
        rows = flat(group(hall, g)[...])

        def body(cols):
            mid[:, :, :768] = contract(rows, wi[:, cols], 1, 0).reshape(2, half, -1)
            block = half // 2

            def finish_rows(i, _):
                j, r = i // 2, pl.ds(pl.multiple_of(lax.rem(i, 2) * block, block), block)
                for n in range(3):
                    gate, up = mid[j, r, 256 * n : 256 * n + 128], mid[j, r, 256 * n + 128 : 256 * n + 256]
                    square = gate * gate
                    turn = jnp.tanh(gate * (0.7978845608028654 + 0.035677408136300125 * square))
                    upper = 0.5 + 0.5 * turn
                    value = gate * upper
                    slope = upper + 0.5 * gate * (1.0 - turn * turn) * (0.7978845608028654 + 0.10703222440890038 * square)
                    group(hid, g)[j, r, third(cols.start // 2, n)] = (value * up).astype(BF16)
                    group(act, g)[j, r, third(cols.start, 2 * n)] = (slope * up).astype(BF16)
                    group(act, g)[j, r, third(cols.start, 2 * n + 1)] = value.astype(BF16)
                return 0

            lax.fori_loop(0, 4, finish_rows, 0)

        tiles(2 * units, 768, body)

    def emit(g, cols, part):
        if g == 0:
            acc[:, :, cols] = part.reshape(2, half, -1)
        elif g == 1:
            sent[0, :, :, cols] = part.astype(BF16).reshape(2, half, -1)
        else:
            far[:, cols] = part[:half]
            sent[1, g - 2, :, cols] = part[half:].astype(BF16)

    def down(g):
        rows = flat(group(hid, g)[...])
        tiles(width, 512, lambda cols: emit(g, cols, contract(rows, wd[:, cols], 1, 0)))

    def push(phase, kind, j):
        return go(sent.at[kind, j], got.at[kind, j], p_send.at[phase, kind, j], p_recv.at[phase, kind, j], peer if kind == 2 else sib)

    def sums(phase, compute, copies, buffer, send, recv, before):
        kept = {}
        compute(0)
        for j in range(2):
            copies[j][1].wait_recv()
        compute(1)
        for j in range(2):
            kept[0, j] = push(phase, 0, j)
        for j in range(2):
            copies[j][0].wait_recv()
            passed = relay(buffer, send, recv, j)
            passed.wait_recv()
            if phase == 1 and j == 1 and share:
                down_tile(0)
                down_tile(1)
                down_swap(1)
            compute(2 + j)
            kept[1, j] = push(phase, 1, j)
            kept[1, j].wait_recv()
            sent[2, j] = (far[...] + got[1, j].astype(F32)).astype(BF16)
            kept[2, j] = push(phase, 2, j)
        return kept

    def forward(g):
        gated(g)
        down(g)

    for one in loads[:2] + lanes:
        one.wait()
    kept = sums(0, forward, h_copies, hall, h_send, h_recv, None)
    first, pending = pending, []
    loads.append(fetch(mid_hbm, mid, load.at[4]))
    loads[2].wait()
    loads[3].wait()
    total = jnp.zeros((), F32)
    d_copies, saves = [], []
    factor = (8.0 * half * lax.axis_size("seq")) / count[0:1, 0:1]
    first_row = lax.axis_index("seq") * 2 * half
    used = lengths[0, 0]
    for n in range(1, lengths.shape[1]):
        used += lengths[0, n]
    for j in range(2):
        kept[0, j].wait_recv()
        kept[2, j].wait_recv()
        step = half // 4

        def rows_of(i, so_far):
            r = pl.ds(pl.multiple_of(i * step, step), step)
            value = mid[j, r, :] + acc[j, r, :] + got[0, j, r, :].astype(F32) + got[2, j, r, :].astype(F32)
            out_low[j, r, :] = value.astype(BF16)
            diff = value - teacher[j, r, :].astype(F32)
            place = lax.broadcasted_iota(jnp.int32, (step, 1), 0) + (first_row + j * half + i * step)
            masked = (place < used).astype(F32) * diff
            grad = masked * factor
            mid[j, r, :] = grad
            dall[0, j, r, :] = grad.astype(BF16)
            return so_far + jnp.sum(masked * diff)

        total = lax.fori_loop(0, 4, rows_of, total)
        d_copies.append(spread(dall.at[0], dall, d_send, d_recv, j))
        saves.append(fetch(out_low.at[j], out.at[j], store.at[0, j]))
        saves.append(fetch(mid.at[j], cot.at[j], store.at[1, j]))
    squares[...] = jnp.full(squares.shape, total)

    def backward(g):
        rows = flat(group(dall, g)[...])

        def body(cols):
            grad = contract(rows, wd[cols, :], 1, 1).reshape(2, half, -1)
            part = group(act, g)
            for n in range(6):
                at = third(2 * cols.start, n)
                piece = grad[:, :, 128 * (n // 2) : 128 * (n // 2) + 128]
                part[:, :, at] = (piece * part[:, :, at].astype(F32)).astype(BF16)

        tiles(units, 384, body)
        both = flat(group(act, g)[...])
        tiles(width, 512, lambda cols: emit(g, cols, contract(both, wi[cols, :], 1, 1)))

    for copy in first:
        copy.wait_send()
    order = sorted(range(depth), key=lambda d: (d == 0, abs(2 * d - depth))) if share else []
    parts = [teacher.at[:, :slot, :units], out_low.at[:, :slot, :units]] if share else []
    stage = [wd.at[pl.ds(n * 256, 256)] for n in range(2)]
    swaps, owners = {}, {}

    def down_tile(n):
        if n >= 2:
            swaps[n - 2].wait_send()
        else:
            saves[2 * n].wait()
        cols = pl.ds(pl.multiple_of(zs[order[n]] * 2 * slot, 128), 2 * slot)
        left = dall[:, :, :, cols].reshape(8 * half, 2 * slot)

        parts[n % 2][...] = contract(left, hid[...].reshape(8 * half, units), 0, 0).astype(BF16).reshape(2, slot, units)
        if n == 0:
            down_swap(0)

    def down_swap(n):
        swaps[n] = remote(parts[n % 2].at[1 - x], gx.at[n], gxs.at[n], gxr.at[n], xpeer)

    def down_owner(n):
        swaps[n].wait_recv()
        gx[n] = (parts[n % 2][x].astype(F32) + gx[n].astype(F32)).astype(BF16)
        if n < 2:
            owners[n] = go(gx.at[n], gz.at[n], gzs.at[n], gzr.at[n], zpeers[order[n]])

    kept = sums(1, backward, d_copies, dall, d_send, d_recv, None)
    count = 0
    blocks = width // 256
    left, right = {}, {}

    def weight(left, right, target, start, size):
        held = [one.at[:, :size] for one in stage]

        def store_rows(n, at):
            return pltpu.make_async_copy(held[n], target.at[at, start : start + size], g_store.at[n])

        def body(i, _):
            for n in range(2):
                at = pl.ds(pl.multiple_of(i * 512 + n * 256, 256), 256)

                @pl.when(i > 0)
                def _():
                    store_rows(n, at).wait()

                held[n][...] = contract(left(at), right(start, size), 0, 0).astype(BF16)
                store_rows(n, at).start()
            return 0

        lax.fori_loop(0, width // 512, body, 0)
        for n in range(2):
            store_rows(n, pl.ds(0, 256)).wait()

    if not share:
        weight(lambda at: dall[:, :, :, at].reshape(8 * half, 256), lambda start, size: hid[...].reshape(8 * half, units), gd, 0, units)
    cut = (units + 255) // 256 * 256
    for n in range(2):
        if share:
            down_owner(n)
            down_tile(n + 2)
            down_swap(n + 2)
        start, size = ((0, cut), (cut, 2 * units - cut))[n]
        weight(lambda at: hall[:, :, :, at].reshape(8 * half, 256), lambda start, size: act[:, :, :, start : start + size].reshape(8 * half, size), gi, start, size)
    for j in range(2):
        kept[0, j].wait_recv()
        kept[2, j].wait_recv()
        saves[2 * j + 1].wait()

        def sum_rows(i, _):
            r = pl.ds(pl.multiple_of(i * step, step), step)
            mid[j, r, :] = acc[j, r, :] + got[0, j, r, :].astype(F32) + got[2, j, r, :].astype(F32)
            return 0

        lax.fori_loop(0, 4, sum_rows, 0)
        saves.append(fetch(mid.at[j], dh.at[j], store.at[2, j]))
    if share:
        down_owner(2)
        ends = [fetch(gx.at[2], gd_owner, end.at[0])]
        for n in range(2):
            owners[n].wait_recv()
        down_owner(3)
        far[:slot, :units] = gx[3].astype(F32) + gz[0].astype(F32) + gz[1].astype(F32)
        ends.append(fetch(far.at[:slot, :units], gd, end.at[1]))
        for n in range(2, 4):
            swaps[n].wait_send()
        for one in ends:
            one.wait()
    for copy in pending:
        copy.wait_send()
    for n in (4, 5) if share else (0, 2, 4, 5):
        saves[n].wait()


def ffn(h, wi, wd, mid, teacher, lengths, count, seq):
    rows, width = h.shape
    depth, slot = (seq // 2, width // seq) if seq else (0, 0)
    units = wd.shape[0]
    half = rows // 2
    split = lambda a: a.reshape(2, half, a.shape[-1])
    dma = pltpu.SemaphoreType.DMA
    hbm, vm = pl.BlockSpec(memory_space=pl.ANY), pl.BlockSpec(memory_space=pltpu.VMEM)
    def kernel(*refs):
        ffn_kernel(bool(seq), *(refs if seq else refs[:13] + (None,) + refs[13:]))

    sharing = []
    if seq:
        sharing = [
            pltpu.VMEM((4, slot, units), BF16), pltpu.VMEM((2, slot, units), BF16),
            dma((4,)), dma((4,)), dma((2,)), dma((2,)), dma((2,)),
        ]
    out, cot, dh, gd, gi, squares, *rest = pl.pallas_call(
        kernel,
        name="ffn",
        out_shape=[
            jax.ShapeDtypeStruct((2, half, width), BF16),
            jax.ShapeDtypeStruct((2, half, width), F32),
            jax.ShapeDtypeStruct((2, half, width), F32),
            jax.ShapeDtypeStruct((slot, units), F32) if seq else jax.ShapeDtypeStruct((width, units), BF16),
            jax.ShapeDtypeStruct((width, 2 * units), BF16),
            jax.ShapeDtypeStruct((8, 128), F32),
        ]
        + [jax.ShapeDtypeStruct((slot, units), BF16)] * bool(seq),
        in_specs=[hbm] * 5 + [pl.BlockSpec(memory_space=pltpu.SMEM), vm],
        out_specs=[hbm] * 5 + [vm] + [hbm] * bool(seq),
        scratch_shapes=[
            pltpu.VMEM((width, 2 * units), BF16),
            pltpu.VMEM((units, width), BF16),
            pltpu.VMEM((2, half, width), F32),
            pltpu.VMEM((2, half, width), BF16),
            pltpu.VMEM((4, 2, half, width), BF16),
            pltpu.VMEM((4, 2, half, width), BF16),
            pltpu.VMEM((4, 2, half, 2 * units), BF16),
            pltpu.VMEM((4, 2, half, units), BF16),
            pltpu.VMEM((2, half, width), F32),
            pltpu.VMEM((half, width), F32),
            pltpu.VMEM((2, half, width), BF16),
            pltpu.VMEM((3, 2, half, width), BF16),
            pltpu.VMEM((3, 2, half, width), BF16),
            dma((5,)), dma((3, 2)), dma((3, 2)), dma((3, 2)), dma((3, 2)),
            dma((2, 3, 2)), dma((2, 3, 2)), dma((3, 2)), dma((2,)), dma((units // 64,)),
        ]
        + sharing,
        compiler_params=pltpu.CompilerParams(collective_id=2, has_side_effects=True, vmem_limit_bytes=63 << 20),
    )(split(h), wi, wd, split(mid), split(teacher), lengths, count)
    return out.reshape(rows, width), cot.reshape(rows, width), dh.reshape(rows, width), gd, gi, squares, rest


def pair_rows(block):
    return jnp.concatenate([block[:, :HD], block[:, HD:]], axis=0)


def pair_columns(block):
    rows = block.shape[0] // 2
    return jnp.concatenate([block[:rows], block[rows:]], axis=1)


def attend_back_kernel(q, kv, grad, mixed, probs, grad_q, grad_kv):
    i, pair = pl.program_id(0), pl.program_id(1)
    reach = WINDOW + QROWS
    keys = pl.ds(pl.multiple_of(i * QROWS, QROWS), reach)

    @pl.when((i == 0) & (pair == 0))
    def _():
        grad_kv[...] = jnp.zeros_like(grad_kv)

    queries, grads = pair_rows(q[...]), pair_rows(grad[...])
    weights = probs[0, 0].reshape(2 * QROWS, reach)
    dots = jnp.sum(grads.astype(F32) * pair_rows(mixed[...]).astype(F32), axis=-1, keepdims=True)
    steep = contract(grads, kv[keys, HD:], 1, 1) - dots
    steep = (weights.astype(F32) * steep).astype(BF16)
    grad_q[...] = (pair_columns(contract(steep, kv[keys, :HD], 1, 0)) * (1.0 / math.sqrt(HD))).astype(BF16)
    grad_kv[keys, :HD] += contract(steep, queries, 0, 0)
    grad_kv[keys, HD:] += contract(weights, grads, 0, 0)


def attend_back(queries, extended, grad_mixed, mixed, probs):
    rows, width = mixed.shape
    blocks, pairs, reach = rows // QROWS, width // (2 * HD), WINDOW + QROWS
    block = pl.BlockSpec((QROWS, 2 * HD), lambda i, p: (i, p))
    whole = pl.BlockSpec(extended.shape, lambda i, p: (0, 0))
    return pl.pallas_call(
        attend_back_kernel,
        name="attend_back",
        grid=(blocks, pairs),
        out_shape=[jax.ShapeDtypeStruct((rows, width), BF16), jax.ShapeDtypeStruct(extended.shape, F32)],
        in_specs=[block, whole, block, block, pl.BlockSpec((1, 1, 2, QROWS, reach), lambda i, p: (i, p, 0, 0, 0))],
        out_specs=[block, whole],
        compiler_params=pltpu.CompilerParams(vmem_limit_bytes=48 << 20),
    )(queries, extended, grad_mixed, mixed, probs)


GRAD_COLS = 128
AHEAD = 3


def owner_order(depth):
    return sorted(range(depth), key=lambda d: (d == 0, abs(2 * d - depth)))


class RowSum:
    def __init__(self, source, buffers, sems, where, go):
        self.source, self.go = source, go
        self.core, self.side, self.cross, self.along = buffers
        self.cs, self.cr, self.ys, self.yr, self.xs, self.xr, self.zs_, self.zr = sems
        self.x, self.y, self.c, self.zs, self.sib, self.ypeer, self.xpeer, self.zpeers = where
        self.depth, self.cols = len(self.zs), self.core.shape[-1]
        self.order = owner_order(self.depth)
        self.moved = {}

    def columns(self, y, c):
        return pl.ds(pl.multiple_of((2 * y + c) * self.cols, self.cols), self.cols)

    def first(self, d):
        for h in range(2):
            part = self.source.at[self.zs[d], :, :, self.columns(h, 1 - self.c)]
            self.moved["c", d, h] = self.go(part, self.core.at[d, h], self.cs.at[d, h], self.cr.at[d, h], self.sib)

    def second(self, d):
        for h in range(2):
            self.moved["c", d, h].wait_recv()
        far = 1 - self.y
        own = self.source[self.zs[d], :, :, self.columns(far, self.c)].astype(F32)
        self.core[d, far] = (own + self.core[d, far].astype(F32)).astype(BF16)
        self.moved["y", d] = self.go(self.core.at[d, far], self.side.at[d], self.ys.at[d], self.yr.at[d], self.ypeer)

    def kept(self, d, x):
        own = self.source[self.zs[d], x, :, self.columns(self.y, self.c)].astype(F32)
        return own + self.core[d, self.y, x].astype(F32) + self.side[d, x].astype(F32)

    def third(self, d):
        self.moved["y", d].wait_recv()
        self.side[d, 1 - self.x] = self.kept(d, 1 - self.x).astype(BF16)
        self.moved["x", d] = self.go(self.side.at[d, 1 - self.x], self.cross.at[d], self.xs.at[d], self.xr.at[d], self.xpeer)

    def fourth(self, d):
        self.moved["x", d].wait_recv()
        self.cross[d] = (self.kept(d, self.x) + self.cross[d].astype(F32)).astype(BF16)
        if d:
            self.moved["z", d] = self.go(
                self.cross.at[d], self.along.at[d - 1], self.zs_.at[d - 1], self.zr.at[d - 1], self.zpeers[d]
            )

    def total(self):
        value = self.cross[0].astype(F32)
        for d in range(1, self.depth):
            self.moved["z", d].wait_recv()
            value += self.along[d - 1].astype(F32)
        return value


def norm_back(values, grad, gain):
    r = lax.rsqrt(jnp.mean(values * values, axis=-1, keepdims=True) + EPSILON)
    scaled = grad * gain
    slope = r * r * r * jnp.mean(values * scaled, axis=-1, keepdims=True)
    return r * scaled - values * slope, jnp.sum(grad * values * r, axis=0, keepdims=True)


def finish_kernel(dh_hbm, cot_hbm, middle_hbm, w_out_hbm, w_attn_hbm, mixed_hbm, probs_hbm, qkv_hbm, ext_hbm, normed_hbm,
                  tokens_hbm, gd_hbm, gd_owner, gi_hbm, gain_attn, gain_ffn, squares, count,
                  grad_x, grad_d, grad_i, grad_qkv_out, grad_o, gain_attn_out, gain_ffn_out, loss_out,
                  dh, cot, middle, weight, mixed, probs, qkv, ext, normed, low, dmix, dkv, slabs, slabs_in,
                  gx, gz, gr, own, staged, joined, dz, po, pa, ocore, oside, ocross, oalong, acore, aside, across, aalong, vb,
                  load, p_load, own_load, out_sem, slab_s, slab_r, ds, dr, gxs, gxr, gzs, gzr, grr, o_sems, a_sems, vs, vr):
    z, x, y, c = places()
    depth, width = own.shape[1], own.shape[-1]
    rows, model_width = dh.shape
    seq = 2 * depth
    me = 2 * z + x
    sib, ypeer, xpeer = device(z, x, y, 1 - c), device(z, x, 1 - y, c), device(z, 1 - x, y, c)
    zs = [lax.rem(z + d, depth) for d in range(depth)]
    zpeers = [device(zs[d], x, y, c) for d in range(depth)]
    wt = 2 * y + c
    diagonal = (lax.rem(me + seq - 1 + 2 * x, seq), wt)
    back = [(lax.rem(me + seq - step, seq), wt) for step in (1, 2)]

    def fetch(src, dst, sem):
        copy = pltpu.make_async_copy(src, dst, sem)
        copy.start()
        return copy

    loads = {}
    for n, (name, src, dst) in enumerate((
        ("dh", dh_hbm, dh), ("cot", cot_hbm, cot), ("w_out", w_out_hbm, weight.at[:, :model_width]), ("mixed", mixed_hbm, mixed),
        ("qkv", qkv_hbm, qkv), ("ext", ext_hbm, ext), ("normed", normed_hbm, normed))):
        loads[name] = fetch(src, dst, load.at[n])
    greet([sib, ypeer, xpeer, diagonal] + zpeers[1:])
    started = []

    def go(*args):
        started.append(remote(*args))
        return started[-1]

    chunks = gi_hbm.shape[-1] // width
    gxc, gzc, owned = {}, {}, {}

    def g_ref(k, side):
        return gi_hbm.at[:, side, :, pl.ds(k * width, width)]

    def g_send(k):
        if k < chunks:
            gxc[k] = go(g_ref(k, 1 - x), gx.at[k], gxs.at[k], gxr.at[k], xpeer)

    def g_load(k):
        if k < chunks:
            owned[k] = fetch(g_ref(k, x), own.at[k % 2], own_load.at[k % 2])

    def at_end(d):
        return ((z == 0) & (d == depth - 1)) | ((z == depth - 1) & (d == 1))

    def g_copy(k, d, dst, recv, to):
        return pltpu.make_async_remote_copy(
            src_ref=gx.at[k, zs[d]], dst_ref=dst, send_sem=gzs.at[k, d - 1], recv_sem=recv, device_id=to, device_id_type=MESH)

    def g_owner(k, d):
        return g_copy(k, d, gz.at[k, d - 1], gzr.at[k, d - 1], zpeers[d])

    def g_neighbour(k, d):
        return g_copy(k, d, gr.at[k], grr.at[k], zpeers[depth - d])

    def g_step(k):
        gxc[k].wait_recv()
        g_send(k + AHEAD)
        owned[k].wait()
        for d in range(depth):
            gx[k, zs[d]] = (own[k % 2, zs[d]].astype(F32) + gx[k, zs[d]].astype(F32)).astype(BF16)
            if d == 1 or d == depth - 1:
                pl.when(at_end(d))(lambda d=d: g_neighbour(k, d).start())
                pl.when(jnp.logical_not(at_end(d)))(lambda d=d: g_owner(k, d).start())
        g_load(k + 2)
        if k >= 2:
            g_relay(k - 2)

    def g_relay(k):
        @pl.when((z > 0) & (z < depth - 1))
        def _():
            g_copy(k, 2, gr.at[k], grr.at[k], zpeers[2]).wait_recv()
            gx[k, zs[2]] = (gx[k, zs[2]].astype(F32) + gr[k].astype(F32)).astype(BF16)

        g_owner(k, 2).start()

    stores = {}

    def g_end(k):
        at = k % 2
        staged[at] = gx[k, z].astype(F32)
        for d in range(1, depth):
            missing = ((z == depth - 1) & (d == depth - 1)) | ((z == 0) & (d == 1))

            @pl.when(jnp.logical_not(missing))
            def _():
                g_owner(k, d).wait_recv()
                staged[at] += gz[k, d - 1].astype(F32)

        if at == 1:
            turn = k // 2
            if turn >= 2:
                stores[turn - 2].wait()
            joined[turn % 2] = jnp.stack([staged[0], staged[1]], axis=1)
            stores[turn] = fetch(joined.at[turn % 2], grad_i.at[:, :, pl.ds(turn * width, width)], out_sem.at[turn % 2])

    last = owner_order(depth)[2]
    sent_down = [
        go(gd_owner, dz, ds.at[0], dr.at[0], zpeers[last]),
    ]
    loads["da"] = fetch(gd_hbm, grad_d, load.at[11])
    for k in range(AHEAD):
        g_send(k)
    g_load(0)
    g_load(1)
    where = (x, y, c, zs, sib, ypeer, xpeer, zpeers)
    sum_o = RowSum(po, (ocore, oside, ocross, oalong), o_sems, where, go)
    sum_a = RowSum(pa, (acore, aside, across, aalong), a_sems, where, go)

    step = middle.shape[1]
    steps = rows // step
    mids = [None] * steps

    def mid_load(n):
        if n < steps:
            mids[n] = fetch(middle_hbm.at[pl.ds(n * step, step)], middle.at[n % 2], load.at[8 + n % 2])

    mid_load(0)
    mid_load(1)
    loads["dh"].wait()
    loads["cot"].wait()
    gain_grad = jnp.zeros((1, model_width), F32)
    scale_ffn, scale_attn = as_row(gain_ffn), as_row(gain_attn)
    for n in range(steps):
        mids[n].wait()
        r = pl.ds(n * step, step)
        grad, part = norm_back(middle[n % 2], dh[r, :], scale_ffn)
        grad = cot[r, :] + grad
        cot[r, :] = grad
        low[r, :model_width] = grad.astype(BF16)
        gain_grad += part
        mid_load(n + 2)
    vb[0] = jnp.zeros(vb.shape[1:], F32)
    vb[0, 1:2] = gain_grad
    vb[0, 2:3] = jnp.broadcast_to(squares[0:1, 0:1], (1, model_width))
    loads["w_out"].wait()
    loads["mixed"].wait()
    rows_low = lambda: low[:, :model_width]

    def out_back(cols):
        dmix[:, cols] = contract(rows_low(), weight[cols, :model_width], 1, 1).astype(BF16)

    tiles(model_width, 512, out_back)
    loads["w_attn"] = fetch(w_attn_hbm, weight, load.at[7])

    def out_grad(d, _):
        cols = pl.ds(pl.multiple_of(d * 2 * po.shape[2], 128), 2 * po.shape[2])
        po[d] = contract(low[:, cols], mixed[...], 0, 0).astype(BF16).reshape(po.shape[1:])
        return 0

    lax.fori_loop(0, depth, out_grad, 0)
    for d in sum_o.order:
        sum_o.first(d)
    g_step(0)
    g_step(1)
    blocks, pairs, reach = probs_hbm.shape[0], probs_hbm.shape[1], probs.shape[-1]
    turns = blocks * pairs

    def p_fetch(t):
        return pltpu.make_async_copy(probs_hbm.at[t // pairs, t % pairs], probs.at[t % 2], p_load.at[t % 2])

    p_fetch(0).start()
    p_fetch(1).start()
    dkv[...] = jnp.zeros_like(dkv)
    loads["qkv"].wait()
    loads["ext"].wait()
    for i in range(blocks):
        q_rows, keys = pl.ds(i * QROWS, QROWS), pl.ds(i * QROWS, reach)

        def one(pair, _):
            t = i * pairs + pair
            cols = pl.ds(pl.multiple_of(pair * 2 * HD, 2 * HD), 2 * HD)
            queries, grads = pair_rows(qkv[q_rows, cols]), pair_rows(dmix[q_rows, cols])
            outs = pair_rows(mixed[q_rows, cols])
            dots = jnp.sum(grads.astype(F32) * outs.astype(F32), axis=-1, keepdims=True)
            slot = lax.rem(t, 2)
            p_fetch(t).wait()
            weights = flat(probs[slot])
            steep = contract(grads, ext[keys, HD:], 1, 1) - dots
            steep = (weights.astype(F32) * steep).astype(BF16)
            low[q_rows, cols] = (pair_columns(contract(steep, ext[keys, :HD], 1, 0)) * (1.0 / math.sqrt(HD))).astype(BF16)
            dkv[keys, :HD] += contract(steep, queries, 0, 0)
            dkv[keys, HD:] += contract(weights, grads, 0, 0)

            @pl.when(t + 2 < turns)
            def _():
                p_fetch(t + 2).start()

            return 0

        lax.fori_loop(0, pairs // 2, one, 0)
        if i == 0:
            for d in sum_o.order:
                sum_o.second(d)
        g_step(2 + 3 * i)
        lax.fori_loop(pairs // 2, pairs, one, 0)
        g_step(3 + 3 * i)
        if i == 0:
            g_step(4)
    for n in range(2):
        slabs[n] = dkv[(1 - n) * rows : (2 - n) * rows, :].astype(BF16)
    returned = [go(slabs.at[n], slabs_in.at[n], slab_s.at[n], slab_r.at[n], back[n]) for n in range(2)]
    loads["normed"].wait()
    slot_rows = model_width // seq

    def query_grad(d, _):
        cols = pl.ds(pl.multiple_of(d * 2 * slot_rows, 128), 2 * slot_rows)
        pa[d, :, :slot_rows] = contract(low[:, cols], normed[...], 0, 0).astype(BF16).reshape(2, slot_rows, model_width)
        return 0

    lax.fori_loop(0, depth, query_grad, 0)
    g_step(7)
    for one in returned:
        one.wait_recv()
    summed = dkv[2 * rows :, :] + slabs_in[0].astype(F32) + slabs_in[1].astype(F32)
    low[:, model_width : model_width + HD] = (summed[:, :HD] * (1.0 / math.sqrt(HD))).astype(BF16)
    low[:, model_width + HD :] = summed[:, HD:].astype(BF16)
    kv_grad = contract(low[:, model_width:], normed[...], 0, 0).astype(BF16)
    kv_rows = HD // seq
    for n in range(2):
        part = kv_grad[n * HD : (n + 1) * HD].reshape(depth, 2, kv_rows, model_width)
        pa[:, :, slot_rows + n * kv_rows : slot_rows + (n + 1) * kv_rows] = part
    for d in sum_a.order:
        sum_a.first(d)
    loads["tokens"] = fetch(tokens_hbm, mixed, load.at[3])
    loads["w_attn"].wait()

    def attn_back(cols):
        dh[:, cols] = contract(low[...], weight[cols, :], 1, 1)

    tiles(model_width, 512, attn_back)
    g_step(8)
    loads["tokens"].wait()

    def last_norm(n, so_far):
        r = pl.ds(pl.multiple_of(n * step, step), step)
        grad, part = norm_back(mixed[r, :].astype(F32), dh[r, :], scale_attn)
        cot[r, :] += grad
        return so_far + part

    vb[0, 0:1] = lax.fori_loop(0, steps, last_norm, jnp.zeros((1, model_width), F32))
    saved = fetch(cot, grad_x, load.at[0])

    vc = {}

    def v_first():
        vc[0] = go(vb.at[0], vb.at[1], vs.at[0], vr.at[0], sib)

    def v_swap(n, to):
        vc[n - 1].wait_recv()
        vb[2 * n] = vb[2 * n - 2] + vb[2 * n - 1]
        vc[n] = go(vb.at[2 * n], vb.at[2 * n + 1], vs.at[n], vr.at[n], to)

    def v_along():
        vc[2].wait_recv()
        vb[6] = vb[4] + vb[5]
        for d in range(1, depth):
            vc[2 + d] = go(vb.at[6], vb.at[6 + d], vs.at[2 + d], vr.at[2 + d], zpeers[d])

    def v_end():
        for d in range(1, depth):
            vc[2 + d].wait_recv()
        total = vb[6 + z]
        for n in range(1, depth):
            total += vb[6 + lax.rem(z - n + depth, depth)]
        gain_attn_out[...] = as_lines(total[0:1])
        gain_ffn_out[...] = as_lines(total[1:2])
        loss_out[...] = total[2:3, 0:1] / (count[0:1, 0:1] * model_width)

    v_first()
    o, a = sum_o.order, sum_a.order
    after = {
        8: [lambda: sum_a.second(a[0]), lambda: sum_o.third(o[0]), lambda: sum_o.third(o[1]), lambda: v_swap(1, ypeer)],
        9: [lambda: sum_o.third(o[2]), lambda: sum_o.third(o[3])],
        10: [lambda: sum_a.second(a[1]), lambda: sum_a.third(a[0]), lambda: sum_o.fourth(o[0]), lambda: v_swap(2, xpeer)],
        11: [lambda: sum_o.fourth(o[1])],
        12: [lambda: sum_a.second(a[2]), lambda: sum_a.third(a[1]), lambda: sum_a.fourth(a[0]), lambda: sum_o.fourth(o[2]), v_along],
        13: [lambda: sum_o.fourth(o[3])],
        14: [lambda: sum_a.second(a[3]), lambda: sum_a.third(a[2]), lambda: sum_a.fourth(a[1])],
        15: [v_end],
        16: [lambda: sum_a.third(a[3]), lambda: sum_a.fourth(a[2])],
    }
    ended = 0
    for k in range(9, chunks):
        g_step(k)
        for step in after.pop(k - 1, ()):
            step()
        while ended < k - 4:
            g_end(ended)
            ended += 1
    g_relay(chunks - 2)
    g_relay(chunks - 1)
    for key in sorted(after):
        for step in after[key]:
            step()
    sum_a.fourth(a[3])
    for k in range(ended, chunks):
        g_end(k)
    grad_o[...] = sum_o.total()
    for one in sent_down:
        one.wait_recv()
    loads["da"].wait()
    grad_d[...] += dz[...].astype(F32)
    grad_qkv_out[...] = sum_a.total()
    for copy in started:
        copy.wait_send()
    for k in range(chunks):
        for d in range(1, depth):
            g_owner(k, d).wait_send()
    saved.wait()
    stores[chunks // 2 - 2].wait()
    stores[chunks // 2 - 1].wait()


def finish(dh, cot, middle, w_out, w_attn, mixed, probs, qkv, ext, normed, tokens, gd, gd_rest, gi, gain_attn, gain_ffn, squares, count, seq):
    rows, model_width = dh.shape
    depth, slot, units = seq // 2, model_width // seq, gi.shape[-1] // 2
    kv_rows, cols = 2 * HD // seq, model_width // 4
    blocks, _, _, _, reach = probs.shape
    chunks = 2 * units // GRAD_COLS
    qkv_slot = slot + kv_rows
    step = 128
    dma = pltpu.SemaphoreType.DMA
    hbm, vm = pl.BlockSpec(memory_space=pl.ANY), pl.BlockSpec(memory_space=pltpu.VMEM)

    def sum_buffers(n):
        return [
            pltpu.VMEM((depth, 2, 2, n, cols), BF16),
            pltpu.VMEM((depth, 2, n, cols), BF16),
            pltpu.VMEM((depth, n, cols), BF16),
            pltpu.VMEM((depth - 1, n, cols), BF16),
        ]

    sum_sems = [dma((depth, 2)), dma((depth, 2)), dma((depth,)), dma((depth,)), dma((depth,)), dma((depth,)), dma((depth - 1,)), dma((depth - 1,))]

    def kernel(*refs):
        refs = list(refs)
        at = len(refs) - 18
        o_sems, a_sems = refs[at : at + 8], refs[at + 8 : at + 16]
        finish_kernel(*refs[:at], o_sems, a_sems, *refs[at + 16 :])

    return pl.pallas_call(
        kernel,
        name="finish",
        out_shape=[
            jax.ShapeDtypeStruct((rows, model_width), F32),
            jax.ShapeDtypeStruct((slot, units), F32),
            jax.ShapeDtypeStruct((slot, 2, units), F32),
            jax.ShapeDtypeStruct((qkv_slot, cols), F32),
            jax.ShapeDtypeStruct((slot, cols), F32),
            jax.ShapeDtypeStruct((model_width // 128, 128), F32),
            jax.ShapeDtypeStruct((model_width // 128, 128), F32),
            jax.ShapeDtypeStruct((1, 1), F32),
        ],
        in_specs=[hbm] * 14 + [vm] * 4,
        out_specs=[hbm, vm, hbm] + [vm] * 5,
        scratch_shapes=[
            pltpu.VMEM((rows, model_width), F32),
            pltpu.VMEM((rows, model_width), F32),
            pltpu.VMEM((2, step, model_width), F32),
            pltpu.VMEM(w_attn.shape, BF16),
            pltpu.VMEM((rows, model_width), BF16),
            pltpu.VMEM((2, 2, QROWS, reach), BF16),
            pltpu.VMEM(qkv.shape, BF16),
            pltpu.VMEM(ext.shape, BF16),
            pltpu.VMEM((rows, model_width), BF16),
            pltpu.VMEM(qkv.shape, BF16),
            pltpu.VMEM((rows, model_width), BF16),
            pltpu.VMEM(ext.shape, F32),
            pltpu.VMEM((2, rows, 2 * HD), BF16),
            pltpu.VMEM((2, rows, 2 * HD), BF16),
            pltpu.VMEM((chunks, depth, slot, GRAD_COLS), BF16),
            pltpu.VMEM((chunks, depth - 1, slot, GRAD_COLS), BF16),
            pltpu.VMEM((chunks, slot, GRAD_COLS), BF16),
            pltpu.VMEM((2, depth, slot, GRAD_COLS), BF16),
            pltpu.VMEM((2, slot, GRAD_COLS), F32),
            pltpu.VMEM((2, slot, 2, GRAD_COLS), F32),
            pltpu.VMEM((slot, units), BF16),
            pltpu.VMEM((depth, 2, slot, model_width), BF16),
            pltpu.VMEM((depth, 2, qkv_slot, model_width), BF16),
        ]
        + sum_buffers(slot)
        + sum_buffers(qkv_slot)
        + [pltpu.VMEM((6 + depth, 8, model_width), F32)]
        + [
            dma((12,)), dma((2,)), dma((2,)), dma((2,)), dma((2,)), dma((2,)), dma((1,)), dma((1,)),
            dma((chunks,)), dma((chunks,)), dma((chunks, depth - 1)), dma((chunks, depth - 1)), dma((chunks,)),
        ]
        + sum_sems
        + sum_sems
        + [dma((2 + depth,)), dma((2 + depth,))],
        compiler_params=pltpu.CompilerParams(collective_id=1, has_side_effects=True, vmem_limit_bytes=63 << 20),
    )(
        dh, cot, middle, w_out, w_attn, mixed, probs, qkv, ext, normed, tokens,
        gd, *gd_rest, gi.reshape(depth, 2, slot, 2 * units),
        gain_attn.reshape(-1, 128), gain_ffn.reshape(-1, 128), squares, count,
    )


SHARERS = 8


def as_row(ref):
    return jnp.concatenate([ref[n : n + 1, :] for n in range(ref.shape[0])], axis=1)


def as_lines(row):
    return jnp.concatenate([row[:, n : n + 128] for n in range(0, row.shape[1], 128)], axis=0)


def begin_kernel(lengths, tokens_hbm, w_attn_hbm, w_out_hbm, gain_attn, gain_ffn,
                 attn_out, out_out, qkv_out, ext_out, normed_out, mixed_out, probs_out, middle_out, low_out, count_out,
                 tokens, normed, w_attn, w_out, qkv, ext, mixed, probs, bias, acc, counts,
                 load, c_send, c_recv, o_send, o_recv, s_send, s_recv, h_send, h_recv, n_send, n_recv, p_store, store):
    seq, wt = lax.axis_index("seq"), lax.axis_index("wt")
    n_seq = lax.axis_size("seq")
    y, c = wt // 2, wt % 2
    w_sib, w_peer, w_far = 2 * y + 1 - c, 2 * (1 - y) + c, 2 * (1 - y) + 1 - c
    sib, peer = (seq, w_sib), (seq, w_peer)
    rows, width = tokens.shape
    depth = w_attn_hbm.shape[0]
    pairs = width // (2 * HD)
    blocks, reach = rows // QROWS, WINDOW + QROWS
    slabs = WINDOW // rows
    first = seq // SHARERS * SHARERS
    place = lax.rem(seq, SHARERS)
    others = [(first + lax.rem(place + n, SHARERS), wt) for n in range(1, SHARERS)]
    ahead = [(lax.rem(seq + n, n_seq), wt) for n in range(1, slabs + 1)]
    behind = [(lax.rem(seq + n_seq - n, n_seq), wt) for n in range(1, slabs + 1)]

    def fetch(src, dst, sem):
        copy = pltpu.make_async_copy(src, dst, sem)
        copy.start()
        return copy

    def shard(w, size=None, at=0):
        return pl.ds(pl.multiple_of(w * depth + at, 16), depth if size is None else size)

    loads = [
        fetch(tokens_hbm, tokens, load.at[0]),
        fetch(w_attn_hbm, w_attn.at[shard(wt)], load.at[1]),
        fetch(w_out_hbm, w_out.at[shard(wt)], load.at[2]),
    ]
    greet([sib, peer] + others + (ahead + behind if n_seq > SHARERS else []))
    started = []

    def go(*args):
        started.append(remote(*args))
        return started[-1]

    def chunk(k):
        return pl.ds(pl.multiple_of(lax.rem(k + pairs, pairs + 1) * 2 * HD, 2 * HD), 2 * HD)

    def chunk_copy(kind, k):
        at = chunk(k)
        w, to = ((wt, peer), (wt, sib), (w_peer, sib))[kind]
        src = w_attn_hbm.at[:, at] if kind < 2 else w_attn.at[shard(w), at]
        return pltpu.make_async_remote_copy(
            src_ref=src, dst_ref=w_attn.at[shard(w), at], send_sem=c_send.at[kind, k], recv_sem=c_recv.at[kind, k],
            device_id=to, device_id_type=MESH)

    def arrived(kind, k):
        w = (w_peer, w_sib, w_far)[kind]
        at = chunk(k)
        here = w_attn.at[shard(w), at]
        pltpu.make_async_copy(here, here, c_recv.at[kind, k]).wait()

    chunk_copy(0, 0).start()
    slice_rows = depth // SHARERS

    def slice_at(w, n):
        return shard(w, slice_rows, n * slice_rows)

    mine = pl.ds(pl.multiple_of(place * slice_rows, 16), slice_rows)
    for k in range(pairs + 1):
        chunk_copy(1, k).start()
    whole = go(w_out_hbm, w_out.at[shard(wt)], o_send.at[1], o_recv.at[1], sib)

    def send_after(k):
        chunk_copy(0, k).wait_send()
        chunk_copy(0, k + 2).start()

    n_len = lengths.shape[1]
    ends = [lengths[0, 0]]
    for n in range(1, n_len):
        ends.append(ends[-1] + lengths[0, n])
    stream = n_seq * rows

    def ids(positions):
        number = jnp.zeros(positions.shape, jnp.int32) - 1
        for n in range(n_len):
            start = ends[n - 1] if n else 0
            number += (positions >= start).astype(jnp.int32)
        inside = (positions >= 0) & (positions < ends[-1])
        return jnp.where(inside, number, -(positions + 2 * stream))

    base = seq * rows
    q_ids = ids(lax.broadcasted_iota(jnp.int32, (rows, 1), 0) + base)
    k_ids = ids(lax.broadcasted_iota(jnp.int32, (1, rows + WINDOW), 1) + (base - WINDOW))
    counts[0] = jnp.full(counts.shape[1:], ends[-1]).astype(F32)
    number = go(counts.at[0], counts.at[1], n_send.at[0], n_recv.at[0], sib)

    loads[0].wait()
    scale_attn = as_row(gain_attn)
    part = 128

    def norm_rows(n, _):
        r = pl.ds(pl.multiple_of(n * part, part), part)
        values = tokens[r, :].astype(F32)
        scale = lax.rsqrt(jnp.mean(values * values, axis=-1, keepdims=True) + EPSILON)
        normed[r, :] = (values * scale * scale_attn).astype(BF16)
        return 0

    lax.fori_loop(0, rows // part, norm_rows, 0)
    stores = [fetch(normed, normed_out, store.at[0])]
    for i in range(blocks):
        row = lax.broadcasted_iota(jnp.int32, (QROWS, reach), 0)
        offset = lax.broadcasted_iota(jnp.int32, (QROWS, reach), 1) - WINDOW - row
        here, there = q_ids[i * QROWS : (i + 1) * QROWS], k_ids[:, i * QROWS : i * QROWS + reach]
        bias[i] = jnp.where((offset <= 0) & (offset > -WINDOW) & (here == there), 0.0, NEGATIVE)
    number.wait_recv()
    counts[2] = counts[0] + counts[1]
    chunk_copy(0, 0).wait_send()
    chunk_copy(0, 1).start()
    chunk_copy(0, 2).start()

    def relay(k):
        arrived(0, k)
        chunk_copy(2, k).start()

    loads[1].wait()
    relay(0)
    arrived(1, 0)
    arrived(2, 0)
    kv_cols = slice(width, width + 2 * HD)
    key_value = contract(normed[...], w_attn[:, kv_cols], 1, 0).astype(BF16)
    qkv[:, kv_cols] = key_value
    ext[WINDOW:, :] = key_value
    halo = {}

    def halo_send(half):
        for n in range(slabs):
            cols, at = pl.ds(half * HD, HD), half * slabs + n
            dst = ext.at[pl.ds(WINDOW - (n + 1) * rows, rows), cols]
            halo[half, n] = remote(ext.at[pl.ds(WINDOW, rows), cols], dst, h_send.at[at], h_recv.at[at], ahead[n])

    halo_send(0)

    def project_queries(p):
        cols = pl.ds(pl.multiple_of(p * 2 * HD, 2 * HD), 2 * HD)
        arrived(1, p + 1)
        arrived(2, p + 1)
        qkv[:, cols] = contract(normed[...], w_attn[:, cols], 1, 0).astype(BF16)

    send_after(1)
    relay(1)
    number = go(counts.at[2], counts.at[3], n_send.at[1], n_recv.at[1], peer)
    eighth = go(w_out_hbm.at[mine], w_out.at[slice_at(wt, place)], o_send.at[0], o_recv.at[0], peer)
    project_queries(0)
    for n in range(slabs):
        halo[0, n].wait_send()
    halo_send(1)
    send_after(2)
    relay(2)
    for n in range(slabs):
        halo[0, n].wait_recv()
    eighth.wait_recv()
    spread = [
        go(w_out.at[slice_at(w_peer, place)], w_out.at[slice_at(w_peer, place)], s_send.at[n], s_recv.at[n], others[n])
        for n in range(SHARERS - 1)
    ]
    number.wait_recv()
    count_out[...] = counts[2] + counts[3]
    factor = math.log2(math.e) / math.sqrt(HD)

    def p_copy(i, p):
        return pltpu.make_async_copy(probs.at[i], probs_out.at[i, p], p_store.at[i])

    def heads(p, _, values=None):
        @pl.when(jnp.asarray(p) + 3 <= pairs)
        def _():
            relay(p + 3)

        @pl.when(jnp.asarray(p) + 5 <= pairs)
        def _():
            send_after(p + 3)

        @pl.when(jnp.asarray(p) + 1 < pairs)
        def _():
            project_queries(p + 1)

        cols = pl.ds(pl.multiple_of(p * 2 * HD, 2 * HD), 2 * HD)
        for i in range(blocks):
            q_rows, keys = pl.ds(i * QROWS, QROWS), pl.ds(i * QROWS, reach)
            scores = contract(pair_rows(qkv[q_rows, cols]), ext[keys, :HD], 1, 1) * factor
            shifted = scores.reshape(2, QROWS, reach) + bias[i][None]
            powers = jnp.exp2(shifted - jnp.max(shifted, axis=-1, keepdims=True))
            weights = (powers * (1.0 / jnp.sum(powers, axis=-1, keepdims=True))).astype(BF16)

            @pl.when(jnp.asarray(p) > 0)
            def _():
                p_copy(i, p - 1).wait()

            probs[i] = weights
            p_copy(i, p).start()
            if values is not None and i == 0:
                for one in values:
                    one.wait_recv()
            outs = contract(weights.reshape(2 * QROWS, reach), ext[keys, HD:], 1, 0)
            mixed[q_rows, cols] = pair_columns(outs).astype(BF16)
        return 0

    heads(0, 0, [halo[1, n] for n in range(slabs)])

    def keep_shard(w, n):
        return fetch(w_out.at[shard(w)], out_out.at[shard(w)], store.at[n])

    loads[2].wait()
    whole.wait_recv()
    stores += [keep_shard(wt, 5), keep_shard(w_sib, 7)]
    stores.append(fetch(ext, ext_out, store.at[1]))
    lax.fori_loop(1, pairs - 1, heads, 0)
    stores.append(fetch(w_attn, attn_out, store.at[4]))
    for one in spread:
        one.wait_recv()
    stores.append(keep_shard(w_peer, 8))
    passed = go(w_out.at[shard(w_peer)], w_out.at[shard(w_peer)], o_send.at[2], o_recv.at[2], sib)
    heads(pairs - 1, 0)
    stores += [fetch(qkv, qkv_out, store.at[2]), fetch(mixed, mixed_out, store.at[3])]
    passed.wait_recv()
    stores.append(keep_shard(w_far, 9))

    def project(cols):
        acc[:, cols] = tokens[:, cols].astype(F32) + contract(mixed[...], w_out[:, cols], 1, 0)

    tiles(width, 512, project)
    stores.append(fetch(acc, middle_out, store.at[6]))
    stores[0].wait()

    scale_ffn = as_row(gain_ffn)

    def norm_again(n, _):
        r = pl.ds(pl.multiple_of(n * part, part), part)
        values = acc[r, :]
        scale = lax.rsqrt(jnp.mean(values * values, axis=-1, keepdims=True) + EPSILON)
        normed[r, :] = (values * scale * scale_ffn).astype(BF16)
        return 0

    lax.fori_loop(0, rows // part, norm_again, 0)
    stores.append(fetch(normed, low_out, store.at[0]))
    for i in range(blocks):
        p_copy(i, pairs - 1).wait()
    for one in stores[1:]:
        one.wait()
    chunk_copy(0, pairs - 1).wait_send()
    chunk_copy(0, pairs).wait_send()
    for k in range(pairs + 1):
        for kind in range(1, 3):
            chunk_copy(kind, k).wait_send()
    for one in started + [halo[1, n] for n in range(slabs)]:
        one.wait_send()


def begin(lengths, tokens, w_attn, w_out, gain_attn, gain_ffn):
    rows, width = tokens.shape
    shards = 4
    depth = w_out.shape[0]
    pairs, blocks, reach = width // (2 * HD), rows // QROWS, WINDOW + QROWS
    columns = width + 2 * HD
    dma = pltpu.SemaphoreType.DMA
    hbm, vm = pl.BlockSpec(memory_space=pl.ANY), pl.BlockSpec(memory_space=pltpu.VMEM)
    shape = jax.ShapeDtypeStruct
    return pl.pallas_call(
        begin_kernel,
        name="begin",
        out_shape=[
            shape((width, columns), BF16),
            shape((width, width), BF16),
            shape((rows, columns), BF16),
            shape((rows + WINDOW, 2 * HD), BF16),
            shape((rows, width), BF16),
            shape((rows, width), BF16),
            shape((blocks, pairs, 2, QROWS, reach), BF16),
            shape((rows, width), F32),
            shape((rows, width), BF16),
            shape((8, 128), F32),
        ],
        in_specs=[pl.BlockSpec(memory_space=pltpu.SMEM)] + [hbm] * 3 + [vm] * 2,
        out_specs=[hbm] * 9 + [vm],
        scratch_shapes=[
            pltpu.VMEM((rows, width), BF16),
            pltpu.VMEM((rows, width), BF16),
            pltpu.VMEM((shards * depth, columns), BF16),
            pltpu.VMEM((shards * depth, width), BF16),
            pltpu.VMEM((rows, columns), BF16),
            pltpu.VMEM((rows + WINDOW, 2 * HD), BF16),
            pltpu.VMEM((rows, width), BF16),
            pltpu.VMEM((blocks, 2, QROWS, reach), BF16),
            pltpu.VMEM((blocks, QROWS, reach), F32),
            pltpu.VMEM((rows, width), F32),
            pltpu.VMEM((4, 8, 128), F32),
            dma((3,)), dma((3, pairs + 1)), dma((3, pairs + 1)), dma((3,)), dma((3,)), dma((SHARERS - 1,)), dma((SHARERS - 1,)),
            dma((2 * WINDOW // rows,)), dma((2 * WINDOW // rows,)), dma((2,)), dma((2,)), dma((blocks,)), dma((10,)),
        ],
        compiler_params=pltpu.CompilerParams(collective_id=3, has_side_effects=True, vmem_limit_bytes=60 << 20),
    )(lengths, tokens, w_attn, w_out, gain_attn.reshape(-1, 128), gain_ffn.reshape(-1, 128))


def passed_along(block, axis, distance):
    devices = range(lax.axis_size(axis))
    route = [(i - distance, i) for i in devices if i - distance in devices]
    return lax.ppermute(block, axis, route)


def rms_scale(values, gain):
    return values * lax.rsqrt(jnp.mean(values * values, axis=-1, keepdims=True) + EPSILON) * gain


def per_device(tokens, teacher, seq_lengths, w_attn, w_out, w_in, w_down, gain_attn, gain_ffn):
    tok_rows = tokens.shape[1]
    model_width = tokens.shape[2]
    seq_devices = lax.axis_size("seq")
    (attn_full, out_full, qkv, extended, normed, mixed_b, probs, middle, normed_two, count) = begin(
        seq_lengths, tokens[0], w_attn, w_out, gain_attn, gain_ffn
    )
    units = w_down.shape[0]
    w_pair = jnp.swapaxes(w_in, 0, 1)
    slot, kv_slot = model_width // seq_devices, HD // seq_devices
    aligned = seq_devices == 8 and slot % 16 == 0 and kv_slot % 16 == 0
    output, cotangent, grad_norm_two, grad_down, grad_in, squares, grad_down_rest = ffn(
        normed_two, w_pair, w_down, middle, teacher[0], seq_lengths, count, seq_devices if aligned else 0
    )
    if aligned:
        grad_inputs, grad_down, grad_in, grad_attn, grad_out, gain_attn_all, gain_ffn_all, loss = finish(
            grad_norm_two, cotangent, middle, out_full, attn_full, mixed_b, probs, qkv, extended, normed, tokens[0],
            grad_down, grad_down_rest, grad_in, gain_attn, gain_ffn, squares, count, seq_devices,
        )
    else:
        _, norm_one_pull = jax.vjp(rms_scale, tokens[0].astype(jnp.float32), gain_attn)
        _, norm_two_pull = jax.vjp(rms_scale, middle, gain_ffn)
        grad_middle_norm, grad_gain_ffn = norm_two_pull(grad_norm_two)
        grad_middle = cotangent + grad_middle_norm
        grad_mid_low = grad_middle.astype(jnp.bfloat16)
        grad_out = jnp.einsum("te,td->ed", grad_mid_low, mixed_b, preferred_element_type=jnp.float32)
        grad_mixed = jnp.einsum("te,de->td", grad_mid_low, out_full, preferred_element_type=jnp.float32)
        grad_query, grad_ext = attend_back(qkv, extended, grad_mixed.astype(jnp.bfloat16), mixed_b, probs)
        edge_rows = WINDOW
        grad_kv = grad_ext[edge_rows:]
        for back_step in range(1, WINDOW // tok_rows + 1):
            slab_rows = grad_ext[
                edge_rows - back_step * tok_rows : edge_rows - (back_step - 1) * tok_rows
            ]
            grad_kv = grad_kv + passed_along(slab_rows, "seq", -back_step)
        grad_key = (grad_kv[:, :HD] * (1.0 / math.sqrt(HD))).astype(jnp.bfloat16)
        grad_qkv = jnp.concatenate([grad_query, grad_key, grad_kv[:, HD:].astype(jnp.bfloat16)], axis=1)
        grad_attn = jnp.einsum("te,td->ed", grad_qkv, normed, preferred_element_type=jnp.float32)
        grad_normed = jnp.einsum("te,de->td", grad_qkv, attn_full, preferred_element_type=jnp.float32)
        grad_input_norm, grad_gain_attn = norm_one_pull(grad_normed)
        grad_inputs = grad_middle + grad_input_norm
        grad_attn = grad_attn.astype(jnp.bfloat16)
        grad_key, grad_value = (
            grad_attn[model_width + at : model_width + at + HD].reshape(seq_devices, kv_slot, model_width) for at in (0, HD)
        )
        packed = jnp.concatenate(
            [
                grad_attn[:model_width].reshape(seq_devices, slot, model_width),
                grad_key,
                grad_value,
                grad_out.astype(jnp.bfloat16).reshape(seq_devices, slot, model_width),
            ],
            axis=1,
        )
        small = jnp.stack([grad_gain_attn, grad_gain_ffn, jnp.full((model_width,), squares[0, 0])] + [jnp.zeros_like(grad_gain_attn)] * 5)
        grad_in = jnp.moveaxis(grad_in.reshape(model_width, units // 128, 2, 128), 2, 0)
        grad_down, grad_in = grad_down.reshape(seq_devices, slot, -1), grad_in.reshape(2, seq_devices, slot, -1)
        grad_down, grad_in, packed, small = reduce_plain(grad_down, grad_in, packed, small)
        grad_attn, grad_out = packed[:-slot], packed[-slot:]
        grad_in = jnp.swapaxes(grad_in, 0, 1)
        gain_attn_all, gain_ffn_all = small[0], small[1]
        loss = small[2, 0] / (count[0, 0] * model_width)
    grad_queries = grad_attn[:slot].T
    grad_keyvals = grad_attn[slot:].T.reshape(-1, 2, kv_slot)
    grad_out = grad_out.T
    grad_down = grad_down.T
    return (
        output[None],
        loss.reshape(()),
        grad_inputs[None],
        grad_queries,
        grad_keyvals,
        grad_out,
        grad_in,
        grad_down,
        gain_attn_all.reshape(-1),
        gain_ffn_all.reshape(-1),
    )


def solution(mesh):
    in_specs = (
        P("wt", "seq", None),
        P("wt", "seq", None),
        P("wt", None),
        P("wt", None),
        P("wt", None),
        P(None, None, "wt"),
        P("wt", None),
        P(),
        P(),
    )
    out_specs = (
        P("wt", "seq", None),
        P(),
        P("wt", "seq", None),
        P("wt", "seq"),
        P("wt", None, "seq"),
        P("wt", "seq"),
        P("seq", None, "wt"),
        P("wt", "seq"),
        P(),
        P(),
    )
    return jax.shard_map(
        per_device, mesh=mesh, in_specs=in_specs, out_specs=out_specs, check_vma=False
    )
```
